32 devices in a mesh: section: 2 (over core), batch: 16 (over z, y, x).
Axes of the slice: x: 2, y: 2, z: 4, core: 2. Of those that a mesh axis runs over, the one named last changes fastest.
Arguments:
- inputs: bfloat16 [6, 32, 128, 512], P(None, 'batch'), may hold values from -6 to 6
- grad_out: bfloat16 [6, 32, 128, 512], P(None, 'batch'), may hold values from -6 to 6
- band_ids: int32 [6, 32], P(None, 'batch'), may hold values from 0 to 3
- conv_kernel: float32 [4, 7, 512], P('section'), may hold values from -2 to 2
- conv_bias: float32 [4, 512], P('section'), may hold values from -1.5 to 1.5
- band_scale: float32 [4, 4, 512], P('section'), may hold values from 0.25 to 1.75
- band_shift: float32 [4, 4, 512], P('section'), may hold values from -2.5 to 2.5
- up_weight: bfloat16 [4, 512, 1536], P('section'), may hold values from -0.25 to 0.25
- up_bias: float32 [4, 1536], P('section'), may hold values from -2.5 to 2.5
- down_weight: bfloat16 [4, 1536, 512], P('section'), may hold values from -0.15625 to 0.15625
- down_bias: float32 [4, 512], P('section'), may hold values from -1.5 to 1.5
- layer_scale: float32 [4, 512], P('section'), may hold values from 0.3 to 1
Outputs:
- ends: float32 [2, 6, 32, 128, 512], P('section', None, 'batch')
- grad_conv_kernel: float32 [4, 7, 512], P('section')
- grad_conv_bias: float32 [4, 512], P('section')
- grad_band_scale: float32 [4, 4, 512], P('section')
- grad_band_shift: float32 [4, 4, 512], P('section')
- grad_up_weight: float32 [4, 512, 1536], P('section')
- grad_up_bias: float32 [4, 1536], P('section')
- grad_down_weight: float32 [4, 1536, 512], P('section')
- grad_down_bias: float32 [4, 512], P('section')
- grad_layer_scale: float32 [4, 512], P('section')
The draws below stay inside these ranges and needn't reach their ends.
All inputs are finite; a program needn't handle non-finite values.
Results may differ from the reference program's by a relative error of at most 0.009.
Values sent between devices are 32-bit elements; how exact they have to be, the bound alone decides.
A program may use at most 192 MiB of HBM per device.

```python
import math
import jax
import jax.numpy as jnp
import numpy as np
from jax import lax

D = 512
FF = 1536
KERNEL = 7
BANDS = 4
F = 128
MB = 6
CLIPS = 32
BLOCKS = 4


def touch_ends(array, stream_key, least, high):
    extent = array.shape
    index_at = [jax.random.randint(jax.random.fold_in(stream_key, axis), (), 0, extent[axis]) for axis in range(len(extent))]
    array = array.at[tuple(index_at)].set(least)
    longest = extent.index(max(extent))
    index_at[longest] = (index_at[longest] + 1) % extent[longest]
    return array.at[tuple(index_at)].set(high)


def levels(own_key, dims, split, least, top_value):
    factor_of = 1.0
    for dim, parts in split:
        steps = jax.random.uniform(jax.random.fold_in(jax.random.fold_in(own_key, 6), dim), (parts,), jnp.float32, least / len(split), top_value / len(split))
        factor_of = factor_of * jnp.repeat(jnp.exp(steps), dims[dim] // parts).reshape((-1,) + (1,) * (len(dims) - 1 - dim))
    return factor_of


def rank_table(amount, skew):
    weights = [(1 << 20) // math.isqrt(rank ** skew) + 1 for rank in range(1, amount + 1)]
    spread = 1 + sum(weights) // (1 << 30)
    return np.cumsum(np.array([max(1, weight // spread) for weight in weights]))


def ranked_ids(stream_key, shape, count, skew):
    grid = rank_table(count, skew)
    ticket = jax.random.randint(jax.random.fold_in(stream_key, 1), shape, 0, int(grid[count - 1]))
    standing = jnp.searchsorted(jnp.asarray(grid, jnp.int32), ticket, side="right")
    return jax.random.permutation(jax.random.fold_in(stream_key, 2), count)[standing].astype(jnp.int32)


def noise(rng, shape, width, bound, split=(), held_as=jnp.bfloat16):
    array = width * jax.random.normal(rng, shape, jnp.float32)
    if split:
        array = array * levels(rng, shape, split, -0.22, 0.18)
    return jnp.clip(array, -bound, bound).astype(held_as)


def setup_inputs(seed: int = 0) -> dict:
    splits = jax.random.split(jax.random.key(seed), 13)
    inputs = noise(splits[0], (MB, CLIPS, F, D), 1.0, 6.0, ((1, 16),))
    grad_out = noise(splits[1], (MB, CLIPS, F, D), 1.0, 6.0, ((1, 16),))
    band_ids = touch_ends(ranked_ids(splits[2], (MB, CLIPS), BANDS, 2), jax.random.fold_in(splits[2], 3), 0, BANDS - 1).astype(jnp.int32)
    conv_kernel = noise(splits[3], (BLOCKS, KERNEL, D), KERNEL ** -0.5, 2.0, ((0, 2),), jnp.float32)
    conv_bias = noise(splits[4], (BLOCKS, D), 0.3, 1.5, ((0, 2),), jnp.float32)
    band_scale = jnp.clip(1.0 + 0.15 * jax.random.normal(splits[5], (BLOCKS, BANDS, D), jnp.float32), 0.25, 1.75)
    band_shift = noise(splits[6], (BLOCKS, BANDS, D), 0.5, 2.5, ((0, 2),), jnp.float32)
    up_weight = noise(splits[7], (BLOCKS, D, FF), D ** -0.5, 0.25, ((0, 2),))
    up_bias = noise(splits[8], (BLOCKS, FF), 0.5, 2.5, ((0, 2),), jnp.float32)
    down_weight = noise(splits[9], (BLOCKS, FF, D), FF ** -0.5, 0.15625, ((0, 2),))
    down_bias = noise(splits[10], (BLOCKS, D), 0.3, 1.5, ((0, 2),), jnp.float32)
    layer_scale = jnp.clip(jnp.exp(math.log(1.0) - 1.2039728 * jax.random.uniform(splits[11], (BLOCKS, D), jnp.float32) ** levels(splits[11], (BLOCKS, D), ((0, 2),), -0.2, 0.2)), 0.3, 1.0)
    return dict(inputs=inputs, grad_out=grad_out, band_ids=band_ids, conv_kernel=conv_kernel, conv_bias=conv_bias, band_scale=band_scale, band_shift=band_shift, up_weight=up_weight, up_bias=up_bias, down_weight=down_weight, down_bias=down_bias, layer_scale=layer_scale)


@jax.custom_vjp
def low(v):
    return lax.optimization_barrier(v.astype(jnp.bfloat16)).astype(jnp.float32)

@jax.custom_vjp
def low_back(v):
    return v

def low_keep(v):
    return (low(v), None)

def low_pass(kept, grad):
    return (grad,)

def back_keep(v):
    return (v, None)

def back_low(kept, grad):
    return (low(grad),)
low.defvjp(low_keep, low_pass)
low_back.defvjp(back_keep, back_low)
highest_precision = lax.Precision.HIGHEST
norm_epsilon = 1e-06

def time_conv(signal, kernel):
    frames = signal.shape[1]
    half_width = kernel.shape[0] // 2
    padded = jnp.pad(signal, ((0, 0), (half_width, half_width), (0, 0)))
    summed = jnp.zeros_like(signal)
    for offset in range(kernel.shape[0]):
        summed = summed + padded[:, offset:offset + frames, :] * kernel[offset]
    return summed

def convnext(signal, weights, onehot):
    conv_kernel, conv_bias, band_scale, band_shift, up_weight, up_bias, down_weight, down_bias, layer_scale = weights
    conv_out = time_conv(signal, conv_kernel) + conv_bias
    centered = conv_out - lax.optimization_barrier(jnp.mean(conv_out, axis=-1, keepdims=True))
    normed = centered * lax.rsqrt(lax.optimization_barrier(jnp.mean(centered * centered, axis=-1, keepdims=True)) + norm_epsilon)
    scale_rows = jnp.dot(onehot, band_scale, precision=highest_precision)[:, None, :]
    shift_rows = jnp.dot(onehot, band_shift, precision=highest_precision)[:, None, :]
    adapted = low(normed * scale_rows + shift_rows)
    upper_proj = low_back(jnp.einsum('cfd,dh->cfh', adapted, up_weight, precision=highest_precision) + up_bias)
    hidden = low(jax.nn.gelu(upper_proj, approximate=False))
    branch = low_back(jnp.einsum('cfh,hd->cfd', hidden, down_weight, precision=highest_precision) + down_bias)
    return signal + layer_scale * branch

def window(signal, weights, onehot):
    for layer in range(BLOCKS):
        signal = convnext(signal, tuple((weight[layer] for weight in weights)), onehot)
    return signal

def reference(inputs, grad_out, band_ids, conv_kernel, conv_bias, band_scale, band_shift, up_weight, up_bias, down_weight, down_bias, layer_scale):
    weights = tuple((weight.astype(jnp.float32) for weight in (conv_kernel, conv_bias, band_scale, band_shift, up_weight, up_bias, down_weight, down_bias, layer_scale)))
    group_size = 32
    signals = inputs.astype(jnp.float32).reshape(-1, group_size, F, D)
    cotangents = grad_out.astype(jnp.float32).reshape(-1, group_size, F, D)
    onehots = (band_ids.reshape(-1, group_size)[..., None] == jnp.arange(BANDS)[None, None, :]).astype(jnp.float32)

    def visit_group(totals, entries):
        signal, cotangent, onehot = entries
        result, pullback = jax.vjp(lambda signal_in, weight_in: window(signal_in, weight_in, onehot), signal, weights)
        grad_signal, grad_weights = pullback(cotangent)
        totals = tuple((total + grad for total, grad in zip(totals, grad_weights)))
        return (totals, (result, grad_signal))
    starts = tuple((jnp.zeros_like(weight) for weight in weights))
    totals, (results, grad_signals) = lax.scan(visit_group, starts, (signals, cotangents, onehots))
    full_shape = (MB, CLIPS, F, D)
    ends = jnp.stack([grad_signals.reshape(full_shape), results.reshape(full_shape)])
    return (ends, totals[0], totals[1], totals[2], totals[3], totals[4], totals[5], totals[6], totals[7], totals[8])
```

```python
import functools

import jax
import jax.numpy as jnp
from jax import lax
from jax.experimental import pallas as pl
from jax.experimental.pallas import tpu as pltpu
from jax.sharding import PartitionSpec as P

norm_epsilon = 1e-06
f32 = jnp.float32
bf16 = jnp.bfloat16

knee = 0.275
tail = (-0.00136932, 0.1279114, 0.01125887, 0.38387257, -0.37619095, 0.47368867, -0.11917123)

taps_row, conv_bias_row, scale_row, shift_row, up_bias_row, down_bias_row, gamma_row = 0, 7, 8, 12, 16, 19, 20
packed_rows = 24
pad = 8
chunk = 32


def gelu_and_slope(u):
    exponential = jnp.exp2(u * u * (-0.5 * 1.4426950408889634))
    t = pl.reciprocal(1.0 + knee * jnp.abs(u))
    poly = jnp.full_like(t, tail[6])
    for k in range(5, -1, -1):
        poly = poly * t + tail[k]
    below = exponential * poly
    cdf = jnp.where(u < 0.0, below, 1.0 - below)
    return u * cdf, cdf + u * (exponential * 0.3989422804014327)


def fold(values):
    rows, columns = values.shape
    return jnp.sum(values.reshape(rows // 8, 8, columns), axis=0)


def dot_rows(left, right):
    return lax.dot_general(left, right, (((0,), (0,)), ((), ())), preferred_element_type=f32)


def dot_plain(left, right):
    return lax.dot_general(left, right, (((1,), (0,)), ((), ())), preferred_element_type=f32)


def dot_cols(left, right):
    return lax.dot_general(left, right, (((1,), (1,)), ((), ())), preferred_element_type=f32)


class Plan:
    def __init__(self, batch, rows):
        self.bits = batch.bit_length() - 1
        third = rows // 3
        order = list(range(self.bits))
        swapped = order[:]
        if self.bits > 1:
            swapped[0], swapped[1] = 1, 0
        late, later = order[:], order[:]
        if self.bits > 2:
            late = [2, 0, 1] + order[3:]
            later = [2, 1, 0] + order[3:]
        self.lanes = [
            (0, third, order),
            (third, third, swapped),
            (2 * third, third // 2, late),
            (2 * third + third // 2, third // 2, later),
        ]
        self.kept = []
        self.halves = []
        self.slot_rows = []
        for _, size, _ in self.lanes:
            kept, halves = [size], []
            for _ in range(self.bits):
                halves.append(kept[-1] // 2 >= 8)
                kept.append(kept[-1] // 2 if halves[-1] else kept[-1])
            self.kept.append(kept)
            self.halves.append(halves)
        for stage in range(self.bits):
            begin, starts = 0, []
            for lane in range(len(self.lanes)):
                starts.append(begin)
                begin += self.kept[lane][stage + 1]
            self.slot_rows.append((starts, begin))


def step_kernel(
    plan,
    inputs,
    grad_out,
    onehot,
    packed,
    up_weight,
    down_weight,
    ends,
    up_out,
    down_out,
    small_out,
    spill,
    xs,
    normed,
    inv_std,
    adapted,
    hidden,
    slope,
    gb,
    g,
    gc,
    wup,
    wdn,
    params,
    scale_clip,
    shift_clip,
    sums,
    small,
    keep,
    outgo,
    income,
    small_sum,
    small_in,
    *rest,
):
    stage_in = rest[: plan.bits]
    (
        load_sem,
        wt_send,
        wt_recv,
        par_send,
        par_recv,
        ends_send,
        ends_recv,
        core_send,
        core_recv,
        rs_send,
        rs_recv,
        deliver_send,
        deliver_recv,
        ag_send,
        ag_recv,
        small_send,
        small_recv,
        spill_sem,
    ) = rest[plan.bits :]
    core = lax.axis_index("section")
    other = 1 - core
    batch = lax.axis_index("batch")
    clips, frames, width = g.shape
    rows = clips * frames
    layers = xs.shape[0] - 1
    per_core = layers // 2
    hidden_width = hidden.shape[2]
    tile = 2 * frames
    chunks = frames // chunk
    blocks = hidden_width // 256
    bits = plan.bits

    def bit_of(bit):
        return (batch // (1 << bit)) % 2

    def partner(bit):
        return batch + (1 - 2 * bit_of(bit)) * (1 << bit)

    def to_core(source, target, send, recv):
        return pltpu.make_async_remote_copy(
            src_ref=source,
            dst_ref=target,
            send_sem=send,
            recv_sem=recv,
            device_id={"section": other},
            device_id_type=pl.DeviceIdType.MESH,
        )

    def to_partner(source, target, send, recv, bit):
        return pltpu.make_async_remote_copy(
            src_ref=source,
            dst_ref=target,
            send_sem=send,
            recv_sem=recv,
            device_id={"batch": partner(bit)},
            device_id_type=pl.DeviceIdType.MESH,
        )

    own_up = pltpu.make_async_copy(up_weight, wup.at[pl.ds(per_core * core, per_core)], load_sem.at[0])
    own_dn = pltpu.make_async_copy(down_weight, wdn.at[pl.ds(per_core * core, per_core)], load_sem.at[1])
    own_par = pltpu.make_async_copy(packed, params.at[pl.ds(per_core * core, per_core)], load_sem.at[2])
    own_up.start()
    own_dn.start()
    own_par.start()
    loads = []
    for clip in range(clips):
        loads.append(
            pltpu.make_async_copy(
                inputs.at[clip, core], adapted.at[pl.ds(clip * frames, frames)], load_sem.at[3 + clip]
            )
        )
        loads.append(
            pltpu.make_async_copy(
                grad_out.at[clip, core], gb.at[pl.ds(clip * frames, frames)], load_sem.at[3 + clips + clip]
            )
        )
    for load in loads:
        load.start()

    barrier = pltpu.get_barrier_semaphore()
    pl.semaphore_signal(barrier, inc=1, device_id={"section": other}, device_id_type=pl.DeviceIdType.MESH)
    for bit in range(bits):
        pl.semaphore_signal(
            barrier, inc=1, device_id={"batch": partner(bit)}, device_id_type=pl.DeviceIdType.MESH
        )
    pl.semaphore_wait(barrier, 1 + bits)

    own_par.wait()
    par_copy = to_core(
        packed, params.at[pl.ds(per_core * core, per_core)], par_send.at[0], par_recv.at[0]
    )
    par_copy.start()

    stages = [
        xs.at[1, :, 0:frames],
        xs.at[2, :, 0:frames],
        xs.at[3, :, 0:frames],
        outgo.at[0],
        outgo.at[1],
        g,
        gc.at[:, 0:frames],
        xs.at[4, :, 0:frames],
    ]
    own_up.wait()
    own_dn.wait()
    for j in range(per_core):
        for kind in range(2):
            for half in range(2):
                k = 4 * j + 2 * kind + half
                stage = stages[k]
                for part in range(clips):

                    def cast(i, carry, j=j, kind=kind, half=half, part=part, stage=stage):
                        r = pl.multiple_of(i * chunk, chunk)
                        if kind == 0:
                            value = wup[
                                per_core * core + j,
                                pl.ds(half * (width // 2) + (part % 2) * frames + r, chunk),
                                (part // 2) * width : (part // 2 + 1) * width,
                            ]
                        else:
                            value = wdn[
                                per_core * core + j, pl.ds(half * rows + part * frames + r, chunk), :
                            ]
                        stage[part, pl.ds(r, chunk), :] = value.astype(f32)
                        return carry

                    lax.fori_loop(0, chunks, cast, 0)
                to_core(stage, keep.at[k], wt_send.at[k], wt_recv.at[k]).start()

    def weight_wait(k):
        return to_core(outgo.at[0], keep.at[k], wt_send.at[k], wt_recv.at[k])

    for load in loads:
        load.wait()

    def load_x(clip, carry):
        xs[0, clip, 0:pad, :] = jnp.zeros((pad, width), f32)
        xs[0, clip, pad + frames : 2 * pad + frames, :] = jnp.zeros((pad, width), f32)
        for j in range(chunks):
            xs[0, clip, pad + j * chunk : pad + (j + 1) * chunk, :] = adapted[
                pl.ds(pl.multiple_of(clip * frames + j * chunk, chunk), chunk), :
            ].astype(f32)
        return carry

    lax.fori_loop(0, clips, load_x, 0)
    par_copy.wait()

    def norm_phase(layer):
        for clip in range(clips):
            table = params[layer]
            choice = onehot[clip]
            scale_clip[clip] = jnp.sum(choice * table[scale_row : scale_row + 4], axis=0, keepdims=True)
            shift_clip[clip] = jnp.sum(choice * table[shift_row : shift_row + 4], axis=0, keepdims=True)

        def body(i, carry):
            clip, j = i // chunks, i % chunks
            r = pl.multiple_of(i * chunk, chunk)
            table = params[layer]
            window = xs[layer, clip, pl.ds(pl.multiple_of(j * chunk, chunk), chunk + 2 * pad), :]
            conv = window[pad : pad + chunk] * table[3:4] + table[conv_bias_row : conv_bias_row + 1]
            for k in (0, 1, 2, 4, 5, 6):
                conv = conv + window[pad - 3 + k : pad - 3 + k + chunk] * table[k : k + 1]
            centered = conv - jnp.mean(conv, axis=-1, keepdims=True)
            inv = lax.rsqrt(jnp.mean(centered * centered, axis=-1, keepdims=True) + norm_epsilon)
            value = centered * inv
            normed[pl.ds(r, chunk), :] = value
            inv_std[pl.ds(r, chunk), :] = inv
            adapted[pl.ds(r, chunk), :] = (value * scale_clip[clip] + shift_clip[clip]).astype(bf16)
            return carry

        lax.fori_loop(0, clips * chunks, body, 0)

    def spill_copy(layer, which):
        buffer = hidden if which == 0 else slope
        return pltpu.make_async_copy(buffer.at[layer % 2], spill.at[layer % 2, which], spill_sem.at[layer % 2, which])

    def fill_copy(layer, which):
        buffer = hidden if which == 0 else slope
        return pltpu.make_async_copy(spill.at[layer % 2, which], buffer.at[layer % 2], spill_sem.at[layer % 2, which])

    def forward(layer, carry):
        slot = layer % 2
        @pl.when(layer // per_core != core)
        def _():
            for kind in range(2):
                for half in range(2):
                    k = 4 * (layer % per_core) + 2 * kind + half
                    weight_wait(k).wait_recv()
                    for part in range(clips):

                        def cast(i, carry, kind=kind, half=half, part=part, k=k):
                            r = pl.multiple_of(i * chunk, chunk)
                            value = keep[k, part, pl.ds(r, chunk), :].astype(bf16)
                            if kind == 0:
                                wup[
                                    layer,
                                    pl.ds(half * (width // 2) + (part % 2) * frames + r, chunk),
                                    (part // 2) * width : (part // 2 + 1) * width,
                                ] = value
                            else:
                                wdn[layer, pl.ds(half * rows + part * frames + r, chunk), :] = value
                            return carry

                        lax.fori_loop(0, chunks, cast, 0)

        norm_phase(layer)

        @pl.when(layer >= 2)
        def _():
            for which in range(2):
                spill_copy(layer, which).wait()

        def up(i, carry):
            r = pl.multiple_of(i * tile, tile)
            table = params[layer]
            for block in range(blocks):
                columns = slice(block * 256, (block + 1) * 256)
                place = (block % 2) * 256
                row = up_bias_row + block // 2
                bias = table[row : row + 1, place : place + 256]
                value = dot_plain(adapted[pl.ds(r, tile), :], wup[layer, :, columns])
                for q in range(tile // chunk):
                    smooth, steep = gelu_and_slope(value[q * chunk : (q + 1) * chunk] + bias)
                    hidden[slot, pl.ds(r + q * chunk, chunk), columns] = smooth.astype(bf16)
                    slope[slot, pl.ds(r + q * chunk, chunk), columns] = steep.astype(bf16)
            return carry

        lax.fori_loop(0, rows // tile, up, 0)

        @pl.when(layer < 2)
        def _():
            for which in range(2):
                spill_copy(layer, which).start()

        for step in range(layers):

            @pl.when(layer == step)
            def _(step=step):
                for k in [step] if step < layers - 1 else range(layers - 1, 4 * per_core):
                    weight_wait(k).wait_send()

        def down(i, carry):
            r = pl.multiple_of(i * tile, tile)
            table = params[layer]
            for block in range(width // 256):
                columns = slice(block * 256, (block + 1) * 256)
                bias = table[down_bias_row : down_bias_row + 1, columns]
                gamma = table[gamma_row : gamma_row + 1, columns]
                value = dot_plain(hidden[slot, pl.ds(r, tile), :], wdn[layer, :, columns])
                for q in range(tile // chunk):
                    clip = 2 * i + q // chunks
                    begin = pad + (q % chunks) * chunk
                    xs[layer + 1, clip, begin : begin + chunk, columns] = xs[
                        layer, clip, begin : begin + chunk, columns
                    ] + gamma * (value[q * chunk : (q + 1) * chunk] + bias)
            return carry

        lax.fori_loop(0, rows // tile, down, 0)

        def zero_pads(clip, carry):
            xs[layer + 1, clip, 0:pad, :] = jnp.zeros((pad, width), f32)
            xs[layer + 1, clip, pad + frames : 2 * pad + frames, :] = jnp.zeros((pad, width), f32)
            return carry

        lax.fori_loop(0, clips, zero_pads, 0)
        return carry

    lax.fori_loop(0, layers, forward, 0)

    result = xs.at[layers, :, pad : pad + frames]
    result_remote = pltpu.make_async_remote_copy(
        src_ref=result,
        dst_ref=ends.at[0, :, 0],
        send_sem=ends_send.at[0],
        recv_sem=ends_recv.at[0],
        device_id={"section": other},
        device_id_type=pl.DeviceIdType.MESH,
    )
    result_local = pltpu.make_async_copy(result, ends.at[0, :, 1], ends_send.at[1])

    @pl.when(core == 0)
    def _():
        result_remote.start()

    @pl.when(core == 1)
    def _():
        result_local.start()

    def load_g(i, carry):
        clip, j = i // chunks, i % chunks
        r = pl.multiple_of(j * chunk, chunk)
        g[clip, pl.ds(r, chunk), :] = gb[pl.ds(pl.multiple_of(i * chunk, chunk), chunk), :].astype(f32)
        return carry

    lax.fori_loop(0, clips * chunks, load_g, 0)

    matrices = 2 * layers
    lane_count = len(plan.lanes)

    def core_copy(m, parity):
        return to_core(outgo.at[parity], income.at[parity], core_send.at[parity], core_recv.at[parity])

    keep_rows = keep.reshape(matrices, rows, width)
    income_rows = income.reshape(2, rows, width)

    def offset(lane, stage):
        start = 0
        for s in range(stage):
            if plan.halves[lane][s]:
                start = start + bit_of(plan.lanes[lane][2][s]) * plan.kept[lane][s + 1]
        return start

    def rs_copy(m, parity, lane, stage):
        begin, _, order = plan.lanes[lane]
        bit = order[stage]
        size = plan.kept[lane][stage + 1]
        at = begin + offset(lane, stage)
        if plan.halves[lane][stage]:
            at = at + (1 - bit_of(bit)) * size
        starts, _ = plan.slot_rows[stage]
        return to_partner(
            keep_rows.at[m, pl.ds(pl.multiple_of(at, 8), size)],
            stage_in[stage].at[parity, starts[lane] : starts[lane] + size],
            rs_send.at[stage, parity, lane],
            rs_recv.at[stage, parity, lane],
            bit,
        )

    def rs_add(m, parity, lane, stage):
        begin, _, _ = plan.lanes[lane]
        size = plan.kept[lane][stage + 1]
        at = begin + offset(lane, stage + 1)
        starts, _ = plan.slot_rows[stage]
        step = min(size, chunk)

        def body(i, carry):
            r = pl.multiple_of(at + i * step, 8)
            keep_rows[m, pl.ds(r, step), :] = (
                keep_rows[m, pl.ds(r, step), :]
                + stage_in[stage][parity, pl.ds(pl.multiple_of(starts[lane] + i * step, 8), step), :]
            )
            return carry

        lax.fori_loop(0, size // step, body, 0)

    def out_slice(kind, local, half, lane, at, size):
        begin, _, _ = plan.lanes[lane]
        third = rows // 3
        if kind == 0:
            return down_out.at[local, pl.ds(pl.multiple_of(half * rows + begin + at, 8), size), :]
        column = (begin // third) * width
        return up_out.at[
            local,
            pl.ds(pl.multiple_of(half * (width // 2) + begin % third + at, 8), size),
            column : column + width,
        ]

    def deliver_copy(m, kind, local, lane, near):
        begin, _, _ = plan.lanes[lane]
        size = plan.kept[lane][bits]
        at = offset(lane, bits)
        source = keep_rows.at[m, pl.ds(pl.multiple_of(begin + at, 8), size)]
        target = out_slice(kind, local, core, lane, at, size)
        if near:
            return pltpu.make_async_copy(source, target, deliver_recv.at[m % 4, core, lane])
        return to_core(source, target, deliver_send.at[m % 4, lane], deliver_recv.at[m % 4, core, lane])

    def deliver_wait(m, kind, local, lane):
        size = plan.kept[lane][bits]
        at = offset(lane, bits)
        source = keep_rows.at[m, pl.ds(0, size)]
        near = pltpu.make_async_copy(
            source, out_slice(kind, local, core, lane, at, size), deliver_recv.at[m % 4, core, lane]
        )
        far = to_core(
            source,
            out_slice(kind, local, other, lane, at, size),
            deliver_send.at[m % 4, lane],
            deliver_recv.at[m % 4, other, lane],
        )
        return near, far

    def ag_copy(kind, local, parity, half, lane, stage):
        size = plan.kept[lane][stage + 1]
        at = offset(lane, stage + 1)
        place = out_slice(kind, local, half, lane, at, size)
        return to_partner(
            place,
            place,
            ag_send.at[stage, parity, half, lane],
            ag_recv.at[stage, parity, half, lane],
            plan.lanes[lane][2][stage],
        )

    def ag_wait(kind, local, parity, half, lane, stage):
        copy = ag_copy(kind, local, parity, half, lane, stage)
        copy.wait_send()
        copy.wait_recv()

    def tick(pair, phase):
        for s in range(2 * bits + 2, -1, -1):
            m = 2 * pair + phase - s
            parity = (phase - s) % 2
            kind = parity
            layer = layers - 1 - (2 * pair + phase - s - kind) // 2
            owner = layer // per_core
            local = layer % per_core

            @pl.when((m >= 0) & (m < matrices))
            def _(s=s, m=m, parity=parity, kind=kind, owner=owner, local=local):
                if s == 0:
                    core_copy(m, parity).start()
                    return
                if s == 1:
                    core_copy(m, parity).wait()

                    def body(i, carry):
                        r = pl.multiple_of(i * chunk, chunk)
                        keep_rows[m, pl.ds(r, chunk), :] = (
                            keep_rows[m, pl.ds(r, chunk), :] + income_rows[parity, pl.ds(r, chunk), :]
                        )
                        return carry

                    lax.fori_loop(0, rows // chunk, body, 0)
                elif s <= bits + 1:
                    for lane in range(lane_count):
                        rs_copy(m, parity, lane, s - 2).wait()
                        rs_add(m, parity, lane, s - 2)
                if s <= bits:
                    for lane in range(lane_count):
                        rs_copy(m, parity, lane, s - 1).start()
                elif s == bits + 1:

                    @pl.when(owner == core)
                    def _():
                        for lane in range(lane_count):
                            deliver_copy(m, kind, local, lane, True).start()

                    @pl.when(owner != core)
                    def _():
                        for lane in range(lane_count):
                            deliver_copy(m, kind, local, lane, False).start()

                else:

                    @pl.when(owner == core)
                    def _():
                        if s == bits + 2:
                            for lane in range(lane_count):
                                near, far = deliver_wait(m, kind, local, lane)
                                near.wait()
                                far.wait_recv()
                        else:
                            stage = 2 * bits + 2 - s
                            for half in range(2):
                                for lane in range(lane_count):
                                    if plan.halves[lane][stage]:
                                        ag_wait(kind, local, parity, half, lane, stage)
                        if s < 2 * bits + 2:
                            stage = 2 * bits + 1 - s
                            for half in range(2):
                                for lane in range(lane_count):
                                    if plan.halves[lane][stage]:
                                        ag_copy(kind, local, parity, half, lane, stage).start()

                    if s == bits + 2:

                        @pl.when(owner != core)
                        def _():
                            for lane in range(lane_count):
                                deliver_copy(m, kind, local, lane, False).wait_send()

    def partial_down(m, slot):
        for second in range(2):
            half = other if second == 0 else core
            for block in range(clips // 2):
                value = dot_rows(
                    hidden[slot, :, pl.ds(pl.multiple_of(half * rows + block * tile, tile), tile)], gb[...]
                )
                for q in range(2):
                    piece = value[q * frames : (q + 1) * frames]
                    if second == 0:
                        outgo[0, 2 * block + q] = piece
                    else:
                        keep[m, 2 * block + q] = piece

    def partial_up(m, slot):
        for second in range(2):
            half = other if second == 0 else core
            for block in range(clips // 2):
                value = dot_rows(
                    adapted[:, pl.ds(pl.multiple_of(half * (width // 2), width // 2), width // 2)],
                    slope[slot, :, block * width : (block + 1) * width],
                )
                for q in range(2):
                    piece = value[q * frames : (q + 1) * frames]
                    if second == 0:
                        outgo[1, 2 * block + q] = piece
                    else:
                        keep[m, 2 * block + q] = piece

    def backward(pair, carry):
        layer = layers - 1 - pair
        slot = layer % 2

        @pl.when(pair > 0)
        def _():
            norm_phase(layer)

        sums[...] = jnp.zeros(sums.shape, f32)
        small[layer] = jnp.zeros(small.shape[1:], f32)

        def scale_down(i, carry):
            clip, j = i // chunks, i % chunks
            r = pl.multiple_of(j * chunk, chunk)
            table = params[layer]
            here = g[clip, pl.ds(r, chunk), :]
            begin = pl.multiple_of(pad + j * chunk, 8)
            change = xs[layer + 1, clip, pl.ds(begin, chunk), :] - xs[layer, clip, pl.ds(begin, chunk), :]
            sums[0] += fold(here * change)
            value = (table[gamma_row : gamma_row + 1] * here).astype(bf16)
            gb[pl.ds(pl.multiple_of(i * chunk, chunk), chunk), :] = value
            sums[1] += fold(value.astype(f32))
            return carry

        lax.fori_loop(0, clips * chunks, scale_down, 0)

        @pl.when(layer < 2)
        def _():
            for which in range(2):
                fill_copy(layer, which).wait()

        partial_down(2 * pair, slot)
        tick(pair, 0)

        def up_grad(i, carry):
            r = pl.multiple_of(i * tile, tile)
            for block in range(blocks):
                columns = slice(block * 256, (block + 1) * 256)
                place = (block % 2) * 256
                value = dot_cols(gb[pl.ds(r, tile), :], wdn[layer, columns, :])
                total = jnp.zeros((8, 256), f32)
                for q in range(tile // chunk):
                    at = pl.ds(r + q * chunk, chunk)
                    piece = (value[q * chunk : (q + 1) * chunk] * slope[slot, at, columns].astype(f32)).astype(bf16)
                    slope[slot, at, columns] = piece
                    total = total + fold(piece.astype(f32))
                sums[2 + block // 2, :, place : place + 256] += total
            return carry

        lax.fori_loop(0, rows // tile, up_grad, 0)
        partial_up(2 * pair + 1, slot)
        tick(pair, 1)

        def pads(clip, carry):
            gc[clip, 0:pad, :] = jnp.zeros((pad, width), f32)
            gc[clip, pad + frames : 2 * pad + frames, :] = jnp.zeros((pad, width), f32)
            return carry

        lax.fori_loop(0, clips, pads, 0)

        def adapted_grad(i, carry):
            r = pl.multiple_of(i * tile, tile)
            for block in range(width // 256):
                columns = slice(block * 256, (block + 1) * 256)
                value = dot_cols(slope[slot, pl.ds(r, tile), :], wup[layer, columns, :])
                for q in range(2):
                    gc[2 * i + q, pad : pad + frames, columns] = value[q * frames : (q + 1) * frames]
            return carry

        lax.fori_loop(0, rows // tile, adapted_grad, 0)

        @pl.when(layer >= 2)
        def _():
            for which in range(2):
                fill_copy(layer, which).start()

        def norm_back(clip, carry):
            scale = scale_clip[clip]
            for q in range(2):
                sums[13 + q] = jnp.zeros((8, width), f32)

            def body(j, carry):
                r = pl.multiple_of(clip * frames + j * chunk, chunk)
                at = pl.ds(pl.multiple_of(pad + j * chunk, 8), chunk)
                ga = gc[clip, at, :]
                value = normed[pl.ds(r, chunk), :]
                product = ga * value
                sums[13] += fold(product)
                sums[14] += fold(ga)
                first = jnp.mean(ga * scale, axis=-1, keepdims=True)
                second = jnp.mean(product * scale, axis=-1, keepdims=True)
                result = inv_std[pl.ds(r, chunk), :] * (ga * scale - first - value * second)
                gc[clip, at, :] = result
                sums[12] += fold(result)
                return carry

            lax.fori_loop(0, chunks, body, 0)
            choice = onehot[clip]
            small[layer, scale_row : scale_row + 4, :] += choice * jnp.sum(sums[13], axis=0, keepdims=True)
            small[layer, shift_row : shift_row + 4, :] += choice * jnp.sum(sums[14], axis=0, keepdims=True)
            return carry

        lax.fori_loop(0, clips, norm_back, 0)

        def conv_back(i, carry):
            clip, j = i // chunks, i % chunks
            table = params[layer]
            around = pl.ds(pl.multiple_of(j * chunk, chunk), chunk + 2 * pad)
            signal = xs[layer, clip, around, :]
            grads = gc[clip, around, :]
            here = grads[pad : pad + chunk]
            at = pl.ds(pl.multiple_of(j * chunk, chunk), chunk)
            total = g[clip, at, :] + here * table[3:4]
            sums[5 + 3] += fold(signal[pad : pad + chunk] * here)
            for k in (0, 1, 2, 4, 5, 6):
                total = total + grads[pad + 3 - k : pad + 3 - k + chunk] * table[k : k + 1]
                sums[5 + k] += fold(signal[pad - 3 + k : pad - 3 + k + chunk] * here)
            g[clip, at, :] = total
            return carry

        lax.fori_loop(0, clips * chunks, conv_back, 0)
        gamma = params[layer, gamma_row : gamma_row + 1, :]
        small[layer, gamma_row : gamma_row + 1, :] = jnp.sum(sums[0], axis=0, keepdims=True) / gamma
        small[layer, down_bias_row : down_bias_row + 1, :] = jnp.sum(sums[1], axis=0, keepdims=True)
        for q in range(3):
            row = up_bias_row + q
            small[layer, row : row + 1, :] = jnp.sum(sums[2 + q], axis=0, keepdims=True)
        for q in range(7):
            small[layer, taps_row + q : taps_row + q + 1, :] = jnp.sum(sums[5 + q], axis=0, keepdims=True)
        small[layer, conv_bias_row : conv_bias_row + 1, :] = jnp.sum(sums[12], axis=0, keepdims=True)
        return carry

    lax.fori_loop(0, layers, backward, 0)

    grad_remote = pltpu.make_async_remote_copy(
        src_ref=g,
        dst_ref=ends.at[0, :, 1],
        send_sem=ends_send.at[2],
        recv_sem=ends_recv.at[1],
        device_id={"section": other},
        device_id_type=pl.DeviceIdType.MESH,
    )
    grad_local = pltpu.make_async_copy(g, ends.at[0, :, 0], ends_send.at[3])

    @pl.when(core == 0)
    def _():
        grad_local.start()

    @pl.when(core == 1)
    def _():
        grad_remote.start()

    small_core = to_core(
        small.at[pl.ds(per_core * other, per_core)], small_in.at[bits], small_send.at[bits], small_recv.at[bits]
    )
    small_core.start()

    def small_copy(bit):
        return to_partner(small_sum, small_in.at[bit], small_send.at[bit], small_recv.at[bit], bit)

    def drain(pair, carry):
        for phase in range(2):
            tick(pair, phase)
            for step in range(bits + 1):

                @pl.when(2 * pair + phase - matrices == step)
                def _(step=step):
                    if step == 0:
                        small_core.wait()
                        small_sum[...] = small[pl.ds(per_core * core, per_core)] + small_in[bits]
                    else:
                        small_copy(step - 1).wait()
                        small_sum[...] = small_sum[...] + small_in[step - 1]
                    if step < bits:
                        small_copy(step).start()

        return carry

    lax.fori_loop(layers, layers + bits + 1, drain, 0)
    small_out[...] = small_sum[...]

    @pl.when(core == 0)
    def _():
        grad_local.wait()
        result_remote.wait_send()
        grad_remote.wait_recv()

    @pl.when(core == 1)
    def _():
        result_local.wait()
        result_remote.wait_recv()
        grad_remote.wait_send()


def body(
    inputs,
    grad_out,
    band_ids,
    conv_kernel,
    conv_bias,
    band_scale,
    band_shift,
    up_weight,
    up_bias,
    down_weight,
    down_bias,
    layer_scale,
):
    sections = lax.axis_size("section")
    batch = lax.axis_size("batch")
    core = lax.axis_index("section")
    clips, local_clips, frames, width = inputs.shape
    per_core, _, hidden_width = up_weight.shape
    layers = per_core * sections
    bands = band_scale.shape[1]
    rows = clips * frames
    assert sections == 2 and local_clips == 2 and batch & (batch - 1) == 0
    assert hidden_width == 3 * width and bands == 4 and layers == 4 and rows == 3 * width // 2
    plan = Plan(batch, rows)
    bits = plan.bits
    ids = lax.dynamic_index_in_dim(band_ids, core, 1, keepdims=False)
    onehot = (ids[:, None, None] == jnp.arange(bands)[None, :, None]).astype(f32)
    onehot = jnp.broadcast_to(onehot, (clips, bands, width))
    packed = jnp.concatenate(
        [
            conv_kernel,
            conv_bias[:, None],
            band_scale,
            band_shift,
            up_bias.reshape(per_core, 3, width),
            down_bias[:, None],
            layer_scale[:, None],
            jnp.zeros((per_core, packed_rows - 21, width), f32),
        ],
        axis=1,
    )
    hbm = pl.BlockSpec(memory_space=pl.ANY)
    vmem = pl.BlockSpec(memory_space=pltpu.VMEM)
    padded = frames + 2 * pad
    dma = pltpu.SemaphoreType.DMA
    outs = pl.pallas_call(
        functools.partial(step_kernel, plan),
        out_shape=[
            jax.ShapeDtypeStruct((1, clips, local_clips, frames, width), f32),
            jax.ShapeDtypeStruct((per_core, width, hidden_width), f32),
            jax.ShapeDtypeStruct((per_core, hidden_width, width), f32),
            jax.ShapeDtypeStruct((per_core, packed_rows, width), f32),
            jax.ShapeDtypeStruct((2, 2, rows, hidden_width), bf16),
        ],
        in_specs=[hbm, hbm, vmem, vmem, hbm, hbm],
        out_specs=[hbm, hbm, hbm, vmem, hbm],
        scratch_shapes=[
            pltpu.VMEM((layers + 1, clips, padded, width), f32),
            pltpu.VMEM((rows, width), f32),
            pltpu.VMEM((rows, 1), f32),
            pltpu.VMEM((rows, width), bf16),
            pltpu.VMEM((2, rows, hidden_width), bf16),
            pltpu.VMEM((2, rows, hidden_width), bf16),
            pltpu.VMEM((rows, width), bf16),
            pltpu.VMEM((clips, frames, width), f32),
            pltpu.VMEM((clips, padded, width), f32),
            pltpu.VMEM((layers, width, hidden_width), bf16),
            pltpu.VMEM((layers, hidden_width, width), bf16),
            pltpu.VMEM((layers, packed_rows, width), f32),
            pltpu.VMEM((clips, 1, width), f32),
            pltpu.VMEM((clips, 1, width), f32),
            pltpu.VMEM((15, 8, width), f32),
            pltpu.VMEM((layers, packed_rows, width), f32),
            pltpu.VMEM((2 * layers, clips, frames, width), f32),
            pltpu.VMEM((2, clips, frames, width), f32),
            pltpu.VMEM((2, clips, frames, width), f32),
            pltpu.VMEM((per_core, packed_rows, width), f32),
            pltpu.VMEM((bits + 1, per_core, packed_rows, width), f32),
            *[pltpu.VMEM((2, plan.slot_rows[stage][1], width), f32) for stage in range(bits)],
            dma((3 + 2 * clips,)),
            dma((4 * per_core,)),
            dma((4 * per_core,)),
            dma((1,)),
            dma((1,)),
            dma((4,)),
            dma((2,)),
            dma((2,)),
            dma((2,)),
            dma((bits, 2, len(plan.lanes))),
            dma((bits, 2, len(plan.lanes))),
            dma((4, len(plan.lanes))),
            dma((4, 2, len(plan.lanes))),
            dma((bits, 2, 2, len(plan.lanes))),
            dma((bits, 2, 2, len(plan.lanes))),
            dma((bits + 1,)),
            dma((bits + 1,)),
            dma((2, 2)),
        ],
        compiler_params=pltpu.CompilerParams(
            collective_id=0, has_side_effects=True, vmem_limit_bytes=63 * 2**20
        ),
        cost_estimate=pl.CostEstimate(
            flops=24 * rows * width * hidden_width * 2, bytes_accessed=2**26, transcendentals=2**24
        ),
        name="blocks_step",
    )(inputs, grad_out, onehot, packed, up_weight, down_weight)
    ends, up_grad, down_grad, small, _ = outs
    return (
        ends,
        small[:, 0:7],
        small[:, 7],
        small[:, 8:12],
        small[:, 12:16],
        up_grad,
        small[:, 16:19].reshape(per_core, hidden_width),
        down_grad,
        small[:, 19],
        small[:, 20],
    )


def solution(mesh):
    in_specs = (
        P(None, "batch", None, None),
        P(None, "batch", None, None),
        P(None, "batch"),
        P("section", None, None),
        P("section", None),
        P("section", None, None),
        P("section", None, None),
        P("section", None, None),
        P("section", None),
        P("section", None, None),
        P("section", None),
        P("section", None),
    )
    out_specs = (
        P("section", None, "batch", None, None),
        P("section", None, None),
        P("section", None),
        P("section", None, None),
        P("section", None, None),
        P("section", None, None),
        P("section", None),
        P("section", None, None),
        P("section", None),
        P("section", None),
    )
    return jax.shard_map(body, mesh=mesh, in_specs=in_specs, out_specs=out_specs, check_vma=False)
```

```python
import functools

import jax
import jax.numpy as jnp
from jax import lax
from jax.experimental import pallas as pl
from jax.experimental.pallas import tpu as pltpu
from jax.sharding import PartitionSpec as P

norm_epsilon = 1e-06
f32 = jnp.float32
bf16 = jnp.bfloat16

knee = 1.0 / 0.325
tail = tuple(
    value * knee**power
    for power, value in enumerate((0.0023193, 0.10197519, 0.25681865, -0.17643491, 0.43540795, -0.12008618))
)

taps_row, conv_bias_row, scale_row, shift_row, up_bias_row, down_bias_row, gamma_row = 0, 7, 8, 12, 16, 19, 20
packed_rows = 24
pad = 8
chunk = 32


def gelu_and_slope(u):
    size = jnp.abs(u)
    exponential = jnp.exp2(u * (u * (-0.5 * 1.4426950408889634)))
    base = size + knee
    t = pl.reciprocal(base, approx=True)
    t = t * (2.0 - base * t)
    poly = tail[5] * t + tail[4]
    for k in range(3, -1, -1):
        poly = poly * t + tail[k]
    smooth = jnp.maximum(u, 0.0) - size * (exponential * poly)
    below = exponential * (poly - 0.3989422804014327 * size)
    return smooth, jnp.where(u < 0.0, below, 1.0 - below)


def fold(values):
    rows, columns = values.shape
    return jnp.sum(values.reshape(rows // 8, 8, columns), axis=0)


def dot_rows(left, right):
    return lax.dot_general(left, right, (((0,), (0,)), ((), ())), preferred_element_type=f32)


def dot_plain(left, right):
    return lax.dot_general(left, right, (((1,), (0,)), ((), ())), preferred_element_type=f32)


def dot_cols(left, right):
    return lax.dot_general(left, right, (((1,), (1,)), ((), ())), preferred_element_type=f32)


class Plan:
    def __init__(self, batch, rows):
        self.bits = batch.bit_length() - 1
        third = rows // 3
        order = list(range(self.bits))
        swapped = order[:]
        if self.bits > 1:
            swapped[0], swapped[1] = 1, 0
        late, later = order[:], order[:]
        if self.bits > 2:
            late = [2, 0, 1] + order[3:]
            later = [2, 1, 0] + order[3:]
        self.lanes = [
            (0, third, order),
            (third, third, swapped),
            (2 * third, third // 2, late),
            (2 * third + third // 2, third // 2, later),
        ]
        self.kept = []
        self.halves = []
        self.slot_rows = []
        for _, size, _ in self.lanes:
            kept, halves = [size], []
            for _ in range(self.bits):
                halves.append(kept[-1] // 2 >= 8)
                kept.append(kept[-1] // 2 if halves[-1] else kept[-1])
            self.kept.append(kept)
            self.halves.append(halves)
        for stage in range(self.bits):
            begin, starts = 0, []
            for lane in range(len(self.lanes)):
                starts.append(begin)
                begin += self.kept[lane][stage + 1]
            self.slot_rows.append((starts, begin))


def step_kernel(
    plan,
    inputs,
    grad_out,
    band_ids,
    conv_kernel,
    conv_bias,
    band_scale,
    band_shift,
    up_weight,
    up_bias,
    down_weight,
    down_bias,
    layer_scale,
    ends,
    conv_kernel_out,
    conv_bias_out,
    band_scale_out,
    band_shift_out,
    up_out,
    up_bias_out,
    down_out,
    down_bias_out,
    layer_scale_out,
    spill,
    xs,
    normed,
    inv_std,
    adapted,
    hidden,
    slope,
    gb,
    g,
    gc,
    wup,
    wdn,
    packed,
    params,
    up_bias_row_of,
    onehot,
    sums,
    up_sums,
    small,
    keep,
    outgo,
    income,
    small_sum,
    small_in,
    *rest,
):
    stage_in = rest[: plan.bits]
    (
        load_sem,
        wt_send,
        wt_recv,
        par_send,
        par_recv,
        ends_send,
        ends_recv,
        core_send,
        core_recv,
        rs_send,
        rs_recv,
        deliver_send,
        deliver_recv,
        ag_send,
        ag_recv,
        small_send,
        small_recv,
        spill_sem,
    ) = rest[plan.bits :]
    core = lax.axis_index("section")
    other = 1 - core
    batch = lax.axis_index("batch")
    clips, frames, width = g.shape
    rows = clips * frames
    layers = xs.shape[0] - 1
    per_core = layers // 2
    hidden_width = hidden.shape[2]
    tile = 2 * frames
    chunks = frames // chunk
    blocks = hidden_width // tile
    bits = plan.bits
    mesh_id = pl.DeviceIdType.MESH

    def bit_of(bit):
        return (batch // (1 << bit)) % 2

    def partner(bit):
        return batch + (1 - 2 * bit_of(bit)) * (1 << bit)

    def to_core(source, target, send, recv):
        return pltpu.make_async_remote_copy(source, target, send, recv, {"section": other}, mesh_id)

    def to_partner(source, target, send, recv, bit):
        return pltpu.make_async_remote_copy(source, target, send, recv, {"batch": partner(bit)}, mesh_id)

    own_blocks = pl.ds(per_core * core, per_core)
    own_up = pltpu.make_async_copy(up_weight, wup.at[own_blocks], load_sem.at[0])
    own_dn = pltpu.make_async_copy(down_weight, wdn.at[own_blocks], load_sem.at[1])
    own_up.start()
    own_dn.start()
    loads = []
    for source, target in ((inputs, adapted), (grad_out, gb)):
        for clip in range(clips):
            loads.append(
                pltpu.make_async_copy(
                    source.at[clip, core], target.at[pl.ds(clip * frames, frames)], load_sem.at[2 + len(loads)]
                )
            )
    for load in loads:
        load.start()

    for j in range(per_core):
        packed[j, taps_row : taps_row + 7] = conv_kernel[j]
        packed[j, conv_bias_row : conv_bias_row + 1] = conv_bias[j : j + 1]
        packed[j, scale_row : scale_row + 4] = band_scale[j]
        packed[j, shift_row : shift_row + 4] = band_shift[j]
        for q in range(3):
            row = up_bias_row + q
            packed[j, row : row + 1] = up_bias[j : j + 1, q * width : (q + 1) * width]
        packed[j, down_bias_row : down_bias_row + 1] = down_bias[j : j + 1]
        packed[j, gamma_row : gamma_row + 1] = layer_scale[j : j + 1]
        packed[j, gamma_row + 1 : packed_rows] = jnp.zeros((packed_rows - gamma_row - 1, width), f32)

    barrier = pltpu.get_barrier_semaphore()
    pl.semaphore_signal(barrier, inc=1, device_id={"section": other}, device_id_type=mesh_id)
    for bit in range(bits):
        pl.semaphore_signal(barrier, inc=1, device_id={"batch": partner(bit)}, device_id_type=mesh_id)
    pl.semaphore_wait(barrier, 1 + bits)

    par_copy = to_core(packed, params.at[own_blocks], par_send.at[0], par_recv.at[0])
    par_copy.start()
    params[own_blocks] = packed[...]

    stages = [
        xs.at[1, :, 0:frames],
        xs.at[2, :, 0:frames],
        xs.at[3, :, 0:frames],
        outgo.at[0],
        outgo.at[1],
        g,
        gc.at[:, 0:frames],
        xs.at[4, :, 0:frames],
    ]

    def weight_part(kind, layer, half, part):
        if kind == 0:
            return wup.at[
                layer,
                pl.ds(pl.multiple_of(half * (width // 2) + (part % 2) * frames, frames), frames),
                pl.ds(pl.multiple_of((part // 2) * width, width), width),
            ]
        return wdn.at[layer, pl.ds(pl.multiple_of(half * rows + part * frames, frames), frames), :]

    def weight_wait(k):
        return to_core(outgo.at[0], keep.at[k], wt_send.at[k], wt_recv.at[k])

    def send_weights(j):
        for kind in range(2):
            for half in range(2):
                k = 4 * j + 2 * kind + half

                def cast(part, carry, kind=kind, half=half, k=k):
                    stages[k][part] = weight_part(kind, per_core * core + j, half, part)[...].astype(f32)
                    return carry

                lax.fori_loop(0, clips, cast, 0)
                to_core(stages[k], keep.at[k], wt_send.at[k], wt_recv.at[k]).start()

    def take_weights(layer, kind):
        @pl.when(layer // per_core != core)
        def _():
            for half in range(2):
                k = 4 * (layer % per_core) + 2 * kind + half
                weight_wait(k).wait_recv()

                def cast(part, carry, half=half, k=k):
                    weight_part(kind, layer, half, part)[...] = keep[k, part].astype(bf16)
                    return carry

                lax.fori_loop(0, clips, cast, 0)

    own_up.wait()
    own_dn.wait()
    for j in range(per_core):
        send_weights(j)

    for load in loads:
        load.wait()

    def load_x(clip, carry):
        xs[0, clip, 0:pad, :] = jnp.zeros((pad, width), f32)
        xs[0, clip, pad + frames : 2 * pad + frames, :] = jnp.zeros((pad, width), f32)
        xs[0, clip, pad : pad + frames, :] = adapted[
            pl.ds(pl.multiple_of(clip * frames, frames), frames), :
        ].astype(f32)
        for band in range(4):
            chosen = jnp.where(band_ids[clip, core] == band, 1.0, 0.0).astype(f32)
            onehot[clip, band : band + 1] = jnp.zeros((1, width), f32) + chosen
        return carry

    lax.fori_loop(0, clips, load_x, 0)
    par_copy.wait()
    for layer in range(layers):
        for block in range(blocks):
            row = up_bias_row + block // 2
            place = (block % 2) * tile
            up_bias_row_of[layer, block] = params[layer, row : row + 1, place : place + tile]

    def chosen_row(layer, clip, first):
        return jnp.sum(onehot[clip] * params[layer, first : first + 4], axis=0, keepdims=True)

    def norm_clip(layer, clip):
        table = params[layer]
        scale = chosen_row(layer, clip, scale_row)
        shift = chosen_row(layer, clip, shift_row)
        for j in range(chunks):
            window = xs[layer, clip, j * chunk : (j + 1) * chunk + 2 * pad, :]
            conv = window[pad : pad + chunk] * table[3:4] + table[conv_bias_row : conv_bias_row + 1]
            for k in (0, 1, 2, 4, 5, 6):
                conv = conv + window[pad - 3 + k : pad - 3 + k + chunk] * table[k : k + 1]
            centered = conv - jnp.mean(conv, axis=-1, keepdims=True)
            inv = lax.rsqrt(jnp.mean(centered * centered, axis=-1, keepdims=True) + norm_epsilon)
            value = centered * inv
            at = pl.ds(pl.multiple_of(clip * frames + j * chunk, chunk), chunk)
            normed[at, :] = value
            inv_std[at, :] = inv
            adapted[at, :] = (value * scale + shift).astype(bf16)

    def saved_copy(layer, which, back):
        buffer = (hidden if which == 0 else slope).at[layer % 2]
        away = spill.at[layer % 2, which]
        source, target = (away, buffer) if back else (buffer, away)
        return pltpu.make_async_copy(source, target, spill_sem.at[layer % 2, which])

    def forward(layer, carry):
        slot = layer % 2

        def norm_body(clip, carry):
            norm_clip(layer, clip)
            return carry

        lax.fori_loop(0, clips, norm_body, 0)
        take_weights(layer, 0)

        @pl.when(layer >= 2)
        def _():
            for which in range(2):
                saved_copy(layer, which, False).wait()

        def up(block, carry):
            columns = pl.ds(pl.multiple_of(block * tile, tile), tile)
            bias = up_bias_row_of[layer, block]
            value = dot_plain(adapted[...], wup[layer, :, columns])
            for q in range(rows // chunk):
                smooth, steep = gelu_and_slope(value[q * chunk : (q + 1) * chunk] + bias)
                hidden[slot, q * chunk : (q + 1) * chunk, columns] = smooth.astype(bf16)
                slope[slot, q * chunk : (q + 1) * chunk, columns] = steep.astype(bf16)
            return carry

        lax.fori_loop(0, blocks, up, 0)

        @pl.when(layer < 2)
        def _():
            for which in range(2):
                saved_copy(layer, which, False).start()

        take_weights(layer, 1)

        for step in range(layers):

            @pl.when(layer == step)
            def _(step=step):
                for k in [step] if step < layers - 1 else range(layers - 1, 4 * per_core):
                    weight_wait(k).wait_send()

        for block in range(width // tile):
            columns = slice(block * tile, (block + 1) * tile)
            bias = params[layer, down_bias_row : down_bias_row + 1, columns]
            gamma = params[layer, gamma_row : gamma_row + 1, columns]
            value = dot_plain(hidden[slot], wdn[layer, :, columns])
            for q in range(rows // chunk):
                clip = q // chunks
                begin = pad + (q % chunks) * chunk
                xs[layer + 1, clip, begin : begin + chunk, columns] = xs[
                    layer, clip, begin : begin + chunk, columns
                ] + gamma * (value[q * chunk : (q + 1) * chunk] + bias)

        def zero_pads(clip, carry):
            xs[layer + 1, clip, 0:pad, :] = jnp.zeros((pad, width), f32)
            xs[layer + 1, clip, pad + frames : 2 * pad + frames, :] = jnp.zeros((pad, width), f32)
            return carry

        lax.fori_loop(0, clips, zero_pads, 0)
        return carry

    lax.fori_loop(0, layers, forward, 0)

    result = xs.at[layers, :, pad : pad + frames]
    result_remote = to_core(result, ends.at[0, :, 0], ends_send.at[0], ends_recv.at[0])
    result_local = pltpu.make_async_copy(result, ends.at[0, :, 1], ends_send.at[1])

    @pl.when(core == 0)
    def _():
        result_remote.start()

    @pl.when(core == 1)
    def _():
        result_local.start()

    def load_g(clip, carry):
        g[clip] = gb[pl.ds(pl.multiple_of(clip * frames, frames), frames), :].astype(f32)
        gc[clip, 0:pad, :] = jnp.zeros((pad, width), f32)
        gc[clip, pad + frames : 2 * pad + frames, :] = jnp.zeros((pad, width), f32)
        return carry

    lax.fori_loop(0, clips, load_g, 0)

    matrices = 2 * layers
    lane_count = len(plan.lanes)

    def core_copy(m, parity):
        return to_core(outgo.at[parity], income.at[parity], core_send.at[parity], core_recv.at[parity])

    keep_rows = keep.reshape(matrices, rows, width)

    def offset(lane, stage):
        start = 0
        for s in range(stage):
            if plan.halves[lane][s]:
                start = start + bit_of(plan.lanes[lane][2][s]) * plan.kept[lane][s + 1]
        return start

    def rs_copy(m, parity, lane, stage):
        begin, _, order = plan.lanes[lane]
        bit = order[stage]
        size = plan.kept[lane][stage + 1]
        at = begin + offset(lane, stage)
        if plan.halves[lane][stage]:
            at = at + (1 - bit_of(bit)) * size
        starts, _ = plan.slot_rows[stage]
        return to_partner(
            keep_rows.at[m, pl.ds(pl.multiple_of(at, 8), size)],
            stage_in[stage].at[parity, starts[lane] : starts[lane] + size],
            rs_send.at[stage, parity, lane],
            rs_recv.at[stage, parity, lane],
            bit,
        )

    def rs_add(m, parity, lane, stage):
        begin, _, _ = plan.lanes[lane]
        size = plan.kept[lane][stage + 1]
        at = begin + offset(lane, stage + 1)
        starts, _ = plan.slot_rows[stage]
        step = min(size, 2 * chunk)

        def body(i, carry):
            r = pl.multiple_of(at + i * step, 8)
            keep_rows[m, pl.ds(r, step), :] = (
                keep_rows[m, pl.ds(r, step), :]
                + stage_in[stage][parity, pl.ds(pl.multiple_of(starts[lane] + i * step, 8), step), :]
            )
            return carry

        lax.fori_loop(0, size // step, body, 0)

    def out_slice(kind, local, half, lane, at, size):
        begin, _, _ = plan.lanes[lane]
        third = rows // 3
        if kind == 0:
            return down_out.at[local, half, pl.ds(pl.multiple_of(begin + at, 8), size), :]
        column = (begin // third) * width
        return up_out.at[
            local, half, pl.ds(pl.multiple_of(begin % third + at, 8), size), column : column + width
        ]

    def deliver_copy(m, kind, local, lane, near):
        begin, _, _ = plan.lanes[lane]
        size = plan.kept[lane][bits]
        at = offset(lane, bits)
        source = keep_rows.at[m, pl.ds(pl.multiple_of(begin + at, 8), size)]
        target = out_slice(kind, local, core, lane, at, size)
        if near:
            return pltpu.make_async_copy(source, target, deliver_recv.at[m % 4, core, lane])
        return to_core(source, target, deliver_send.at[m % 4, lane], deliver_recv.at[m % 4, core, lane])

    def deliver_wait(m, kind, local, lane):
        size = plan.kept[lane][bits]
        at = offset(lane, bits)
        source = keep_rows.at[m, pl.ds(0, size)]
        near = pltpu.make_async_copy(
            source, out_slice(kind, local, core, lane, at, size), deliver_recv.at[m % 4, core, lane]
        )
        far = to_core(
            source,
            out_slice(kind, local, other, lane, at, size),
            deliver_send.at[m % 4, lane],
            deliver_recv.at[m % 4, other, lane],
        )
        return near, far

    def ag_copy(kind, local, parity, lane, stage):
        size = plan.kept[lane][stage + 1]
        at = offset(lane, stage + 1)
        place = out_slice(kind, local, slice(None), lane, at, size)
        return to_partner(
            place,
            place,
            ag_send.at[stage, parity, lane],
            ag_recv.at[stage, parity, lane],
            plan.lanes[lane][2][stage],
        )

    def tick(pair, phase):
        for s in range(2 * bits + 2, -1, -1):
            m = 2 * pair + phase - s
            parity = (phase - s) % 2
            kind = parity
            layer = layers - 1 - (2 * pair + phase - s - kind) // 2
            owner = layer // per_core
            local = layer % per_core

            @pl.when((m >= 0) & (m < matrices))
            def _(s=s, m=m, parity=parity, kind=kind, owner=owner, local=local):
                if s == 0:
                    core_copy(m, parity).start()
                    return
                if s == 1:
                    core_copy(m, parity).wait()

                    def body(clip, carry):
                        keep[m, clip] = keep[m, clip] + income[parity, clip]
                        return carry

                    lax.fori_loop(0, clips, body, 0)
                elif s <= bits + 1:
                    for lane in range(lane_count):
                        rs_copy(m, parity, lane, s - 2).wait()
                        rs_add(m, parity, lane, s - 2)
                if s <= bits:
                    for lane in range(lane_count):
                        rs_copy(m, parity, lane, s - 1).start()
                elif s == bits + 1:

                    @pl.when(owner == core)
                    def _():
                        for lane in range(lane_count):
                            deliver_copy(m, kind, local, lane, True).start()

                    @pl.when(owner != core)
                    def _():
                        for lane in range(lane_count):
                            deliver_copy(m, kind, local, lane, False).start()

                else:

                    @pl.when(owner == core)
                    def _():
                        if s == bits + 2:
                            for lane in range(lane_count):
                                near, far = deliver_wait(m, kind, local, lane)
                                near.wait()
                                far.wait_recv()
                        else:
                            stage = 2 * bits + 2 - s
                            for lane in range(lane_count):
                                if plan.halves[lane][stage]:
                                    ag_copy(kind, local, parity, lane, stage).wait()
                        if s < 2 * bits + 2:
                            stage = 2 * bits + 1 - s
                            for lane in range(lane_count):
                                if plan.halves[lane][stage]:
                                    ag_copy(kind, local, parity, lane, stage).start()

                    if s == bits + 2:

                        @pl.when(owner != core)
                        def _():
                            for lane in range(lane_count):
                                deliver_copy(m, kind, local, lane, False).wait_send()

    def store_block(m, phase, second, block, value):
        for q in range(2):
            piece = value[q * frames : (q + 1) * frames]
            if second == 0:
                outgo[phase, 2 * block + q] = piece
            else:
                keep[m, 2 * block + q] = piece

    def scale_clip(layer, clip):
        gamma = params[layer, gamma_row : gamma_row + 1]
        gamma_sum = bias_sum = jnp.zeros((8, width), f32)
        for j in range(chunks):
            here = g[clip, j * chunk : (j + 1) * chunk, :]
            at = slice(pad + j * chunk, pad + (j + 1) * chunk)
            gamma_sum = gamma_sum + fold(here * (xs[layer + 1, clip, at, :] - xs[layer, clip, at, :]))
            value = (gamma * here).astype(bf16)
            gb[pl.ds(pl.multiple_of(clip * frames + j * chunk, chunk), chunk), :] = value
            bias_sum = bias_sum + fold(value.astype(f32))
        sums[0] += gamma_sum
        sums[1] += bias_sum

    def norm_back(layer, clip):
        scale = chosen_row(layer, clip, scale_row)
        scale_sum = shift_sum = conv_sum = jnp.zeros((8, width), f32)
        for j in range(chunks):
            row = pl.ds(pl.multiple_of(clip * frames + j * chunk, chunk), chunk)
            at = slice(pad + j * chunk, pad + (j + 1) * chunk)
            ga = gc[clip, at, :]
            value = normed[row, :]
            scale_sum = scale_sum + fold(ga * value)
            shift_sum = shift_sum + fold(ga)
            dn = ga * scale
            first = jnp.mean(dn, axis=-1, keepdims=True)
            second = jnp.mean(dn * value, axis=-1, keepdims=True)
            result = inv_std[row, :] * (dn - first - value * second)
            gc[clip, at, :] = result
            conv_sum = conv_sum + fold(result)
        sums[9] += conv_sum
        choice = onehot[clip]
        small[layer, scale_row : scale_row + 4, :] += choice * jnp.sum(scale_sum, axis=0, keepdims=True)
        small[layer, shift_row : shift_row + 4, :] += choice * jnp.sum(shift_sum, axis=0, keepdims=True)

    def conv_back(layer, clip):
        table = params[layer]
        totals = [jnp.zeros((8, width), f32) for _ in range(7)]
        for j in range(chunks):
            around = slice(j * chunk, (j + 1) * chunk + 2 * pad)
            signal = xs[layer, clip, around, :]
            grads = gc[clip, around, :]
            here = grads[pad : pad + chunk]
            at = slice(j * chunk, (j + 1) * chunk)
            total = g[clip, at, :] + here * table[3:4]
            totals[3] = totals[3] + fold(signal[pad : pad + chunk] * here)
            for k in (0, 1, 2, 4, 5, 6):
                total = total + grads[pad + 3 - k : pad + 3 - k + chunk] * table[k : k + 1]
                totals[k] = totals[k] + fold(signal[pad - 3 + k : pad - 3 + k + chunk] * here)
            g[clip, at, :] = total
        for k in range(7):
            sums[2 + k] += totals[k]

    def backward(pair, carry):
        layer = layers - 1 - pair
        slot = layer % 2
        sums[...] = jnp.zeros(sums.shape, f32)
        small[layer] = jnp.zeros(small.shape[1:], f32)

        def scale_body(clip, carry):
            scale_clip(layer, clip)
            return carry

        lax.fori_loop(0, clips, scale_body, 0)

        @pl.when(layer < 2)
        def _():
            for which in range(2):
                saved_copy(layer, which, True).wait()

        for second in range(2):
            half = other if second == 0 else core

            def down_body(block, carry, second=second, half=half):
                at = pl.ds(pl.multiple_of(half * rows + block * tile, tile), tile)
                store_block(2 * pair, 0, second, block, dot_rows(hidden[slot, :, at], gb[...]))
                norm_clip(layer, block + 3 * second)
                return carry

            lax.fori_loop(0, clips // 2, down_body, 0)

        def up_grad(block, carry):
            columns = pl.ds(pl.multiple_of(block * tile, tile), tile)
            value = dot_cols(gb[...], wdn[layer, columns, :])
            total = jnp.zeros((8, tile), f32)
            for q in range(rows // chunk):
                at = slice(q * chunk, (q + 1) * chunk)
                piece = (value[at] * slope[slot, at, columns].astype(f32)).astype(bf16)
                slope[slot, at, columns] = piece
                total = total + fold(piece.astype(f32))
            up_sums[block] = total
            return carry

        lax.fori_loop(0, blocks, up_grad, 0)
        tick(pair, 0)

        for block in range(width // tile):
            columns = slice(block * tile, (block + 1) * tile)
            value = dot_cols(slope[slot], wup[layer, columns, :])
            for clip in range(clips):
                gc[clip, pad : pad + frames, columns] = value[clip * frames : (clip + 1) * frames]

        for second in range(2):
            half = other if second == 0 else core

            def up_body(block, carry, second=second, half=half):
                at = pl.ds(pl.multiple_of(half * (width // 2), width // 2), width // 2)
                columns = pl.ds(pl.multiple_of(block * width, width), width)
                store_block(2 * pair + 1, 1, second, block, dot_rows(adapted[:, at], slope[slot, :, columns]))
                norm_back(layer, block + 3 * second)
                conv_back(layer, block + 3 * second)
                return carry

            lax.fori_loop(0, clips // 2, up_body, 0)

        @pl.when(layer >= 2)
        def _():
            for which in range(2):
                saved_copy(layer, which, True).start()

        gamma = params[layer, gamma_row : gamma_row + 1, :]
        small[layer, gamma_row : gamma_row + 1, :] = jnp.sum(sums[0], axis=0, keepdims=True) / gamma
        small[layer, down_bias_row : down_bias_row + 1, :] = jnp.sum(sums[1], axis=0, keepdims=True)
        for block in range(blocks):
            row = up_bias_row + block // 2
            place = (block % 2) * tile
            small[layer, row : row + 1, place : place + tile] = jnp.sum(up_sums[block], axis=0, keepdims=True)
        for k in range(7):
            small[layer, taps_row + k : taps_row + k + 1, :] = jnp.sum(sums[2 + k], axis=0, keepdims=True)
        small[layer, conv_bias_row : conv_bias_row + 1, :] = jnp.sum(sums[9], axis=0, keepdims=True)
        tick(pair, 1)
        return carry

    lax.fori_loop(0, layers, backward, 0)

    grad_remote = to_core(g, ends.at[0, :, 1], ends_send.at[2], ends_recv.at[1])
    grad_local = pltpu.make_async_copy(g, ends.at[0, :, 0], ends_send.at[3])

    @pl.when(core == 0)
    def _():
        grad_local.start()

    @pl.when(core == 1)
    def _():
        grad_remote.start()

    small_core = to_core(
        small.at[pl.ds(per_core * other, per_core)], small_in.at[bits], small_send.at[bits], small_recv.at[bits]
    )
    small_core.start()

    def small_copy(bit):
        return to_partner(small_sum, small_in.at[bit], small_send.at[bit], small_recv.at[bit], bit)

    def drain(pair, carry):
        for phase in range(2):
            tick(pair, phase)
            for step in range(bits + 1):

                @pl.when(2 * pair + phase - matrices == step)
                def _(step=step):
                    if step == 0:
                        small_core.wait()
                        small_sum[...] = small[pl.ds(per_core * core, per_core)] + small_in[bits]
                    else:
                        small_copy(step - 1).wait()
                        small_sum[...] = small_sum[...] + small_in[step - 1]
                    if step < bits:
                        small_copy(step).start()

        return carry

    lax.fori_loop(layers, layers + bits + 1, drain, 0)
    for j in range(per_core):
        conv_kernel_out[j] = small_sum[j, taps_row : taps_row + 7]
        conv_bias_out[j : j + 1] = small_sum[j, conv_bias_row : conv_bias_row + 1]
        band_scale_out[j] = small_sum[j, scale_row : scale_row + 4]
        band_shift_out[j] = small_sum[j, shift_row : shift_row + 4]
        for q in range(3):
            row = up_bias_row + q
            up_bias_out[j : j + 1, q * width : (q + 1) * width] = small_sum[j, row : row + 1]
        down_bias_out[j : j + 1] = small_sum[j, down_bias_row : down_bias_row + 1]
        layer_scale_out[j : j + 1] = small_sum[j, gamma_row : gamma_row + 1]

    @pl.when(core == 0)
    def _():
        grad_local.wait()
        result_remote.wait_send()
        grad_remote.wait_recv()

    @pl.when(core == 1)
    def _():
        result_local.wait()
        result_remote.wait_recv()
        grad_remote.wait_send()


def body(
    inputs,
    grad_out,
    band_ids,
    conv_kernel,
    conv_bias,
    band_scale,
    band_shift,
    up_weight,
    up_bias,
    down_weight,
    down_bias,
    layer_scale,
):
    sections = lax.axis_size("section")
    batch = lax.axis_size("batch")
    clips, local_clips, frames, width = inputs.shape
    per_core, _, hidden_width = up_weight.shape
    layers = per_core * sections
    bands = band_scale.shape[1]
    rows = clips * frames
    assert sections == 2 and local_clips == 2 and batch & (batch - 1) == 0
    assert hidden_width == 3 * width and bands == 4 and layers == 4 and rows == 3 * width // 2
    plan = Plan(batch, rows)
    bits = plan.bits
    hbm = pl.BlockSpec(memory_space=pl.ANY)
    vmem = pl.BlockSpec(memory_space=pltpu.VMEM)
    smem = pl.BlockSpec(memory_space=pltpu.SMEM)
    padded = frames + 2 * pad
    dma = pltpu.SemaphoreType.DMA
    lanes = len(plan.lanes)
    tile = 2 * frames
    outs = pl.pallas_call(
        functools.partial(step_kernel, plan),
        out_shape=[
            jax.ShapeDtypeStruct((1, clips, local_clips, frames, width), f32),
            jax.ShapeDtypeStruct(conv_kernel.shape, f32),
            jax.ShapeDtypeStruct(conv_bias.shape, f32),
            jax.ShapeDtypeStruct(band_scale.shape, f32),
            jax.ShapeDtypeStruct(band_shift.shape, f32),
            jax.ShapeDtypeStruct((per_core, 2, width // 2, hidden_width), f32),
            jax.ShapeDtypeStruct(up_bias.shape, f32),
            jax.ShapeDtypeStruct((per_core, 2, hidden_width // 2, width), f32),
            jax.ShapeDtypeStruct(down_bias.shape, f32),
            jax.ShapeDtypeStruct(layer_scale.shape, f32),
            jax.ShapeDtypeStruct((2, 2, rows, hidden_width), bf16),
        ],
        in_specs=[hbm, hbm, smem, vmem, vmem, vmem, vmem, hbm, vmem, hbm, vmem, vmem],
        out_specs=[hbm, vmem, vmem, vmem, vmem, hbm, vmem, hbm, vmem, vmem, hbm],
        scratch_shapes=[
            pltpu.VMEM((layers + 1, clips, padded, width), f32),
            pltpu.VMEM((rows, width), f32),
            pltpu.VMEM((rows, 1), f32),
            pltpu.VMEM((rows, width), bf16),
            pltpu.VMEM((2, rows, hidden_width), bf16),
            pltpu.VMEM((2, rows, hidden_width), bf16),
            pltpu.VMEM((rows, width), bf16),
            pltpu.VMEM((clips, frames, width), f32),
            pltpu.VMEM((clips, padded, width), f32),
            pltpu.VMEM((layers, width, hidden_width), bf16),
            pltpu.VMEM((layers, hidden_width, width), bf16),
            pltpu.VMEM((per_core, packed_rows, width), f32),
            pltpu.VMEM((layers, packed_rows, width), f32),
            pltpu.VMEM((layers, hidden_width // tile, 1, tile), f32),
            pltpu.VMEM((clips, bands, width), f32),
            pltpu.VMEM((10, 8, width), f32),
            pltpu.VMEM((hidden_width // tile, 8, tile), f32),
            pltpu.VMEM((layers, packed_rows, width), f32),
            pltpu.VMEM((2 * layers, clips, frames, width), f32),
            pltpu.VMEM((2, clips, frames, width), f32),
            pltpu.VMEM((2, clips, frames, width), f32),
            pltpu.VMEM((per_core, packed_rows, width), f32),
            pltpu.VMEM((bits + 1, per_core, packed_rows, width), f32),
            *[pltpu.VMEM((2, plan.slot_rows[stage][1], width), f32) for stage in range(bits)],
            dma((2 + 2 * clips,)),
            dma((4 * per_core,)),
            dma((4 * per_core,)),
            dma((1,)),
            dma((1,)),
            dma((4,)),
            dma((2,)),
            dma((2,)),
            dma((2,)),
            dma((bits, 2, lanes)),
            dma((bits, 2, lanes)),
            dma((4, lanes)),
            dma((4, 2, lanes)),
            dma((bits, 2, lanes)),
            dma((bits, 2, lanes)),
            dma((bits + 1,)),
            dma((bits + 1,)),
            dma((2, 2)),
        ],
        compiler_params=pltpu.CompilerParams(
            collective_id=0, has_side_effects=True, vmem_limit_bytes=63 * 2**20
        ),
        cost_estimate=pl.CostEstimate(
            flops=24 * rows * width * hidden_width * 2, bytes_accessed=2**26, transcendentals=2**24
        ),
        name="blocks_step",
    )(
        inputs,
        grad_out,
        band_ids,
        conv_kernel,
        conv_bias,
        band_scale,
        band_shift,
        up_weight,
        up_bias,
        down_weight,
        down_bias,
        layer_scale,
    )
    outs = list(outs[:10])
    outs[5] = outs[5].reshape(up_weight.shape)
    outs[7] = outs[7].reshape(down_weight.shape)
    return tuple(outs)


def solution(mesh):
    in_specs = (
        P(None, "batch", None, None),
        P(None, "batch", None, None),
        P(None, "batch"),
        P("section", None, None),
        P("section", None),
        P("section", None, None),
        P("section", None, None),
        P("section", None, None),
        P("section", None),
        P("section", None, None),
        P("section", None),
        P("section", None),
    )
    out_specs = (
        P("section", None, "batch", None, None),
        P("section", None, None),
        P("section", None),
        P("section", None, None),
        P("section", None, None),
        P("section", None, None),
        P("section", None),
        P("section", None, None),
        P("section", None),
        P("section", None),
    )
    return jax.shard_map(body, mesh=mesh, in_specs=in_specs, out_specs=out_specs, check_vma=False)
```

```python
import functools

import jax
import jax.numpy as jnp
from jax import lax
from jax.experimental import pallas as pl
from jax.experimental.pallas import tpu as pltpu
from jax.sharding import PartitionSpec as P

norm_epsilon = 1e-06
f32 = jnp.float32
bf16 = jnp.bfloat16

knee = 1.0 / 0.325
tail = tuple(
    value * knee**power
    for power, value in enumerate((0.0023193, 0.10197519, 0.25681865, -0.17643491, 0.43540795, -0.12008618))
)

taps_row, conv_bias_row, scale_row, shift_row, up_bias_row, down_bias_row, gamma_row = 0, 7, 8, 12, 16, 19, 20
packed_rows = 24
pad = 8
chunk = 32


def gelu_and_slope(u):
    size = jnp.abs(u)
    exponential = jnp.exp2(u * (u * (-0.5 * 1.4426950408889634)))
    base = size + knee
    t = pl.reciprocal(base, approx=True)
    t = t * (2.0 - base * t)
    poly = tail[5] * t + tail[4]
    for k in range(3, -1, -1):
        poly = poly * t + tail[k]
    smooth = jnp.maximum(u, 0.0) - size * (exponential * poly)
    below = exponential * (poly - 0.3989422804014327 * size)
    return smooth, jnp.where(u < 0.0, below, 1.0 - below)


def fold(values):
    rows, columns = values.shape
    return jnp.sum(values.reshape(rows // 8, 8, columns), axis=0)


def dot_rows(left, right):
    return lax.dot_general(left, right, (((0,), (0,)), ((), ())), preferred_element_type=f32)


def dot_plain(left, right):
    return lax.dot_general(left, right, (((1,), (0,)), ((), ())), preferred_element_type=f32)


def dot_cols(left, right):
    return lax.dot_general(left, right, (((1,), (1,)), ((), ())), preferred_element_type=f32)


class Plan:
    def __init__(self, batch, rows):
        self.bits = batch.bit_length() - 1
        third = rows // 3
        order = list(range(self.bits))
        swapped = order[:]
        if self.bits > 1:
            swapped[0], swapped[1] = 1, 0
        late, later = order[:], order[:]
        if self.bits > 2:
            late = [2, 0, 1] + order[3:]
            later = [2, 1, 0] + order[3:]
        self.lanes = [
            (0, third, order),
            (third, third, swapped),
            (2 * third, third // 2, late),
            (2 * third + third // 2, third // 2, later),
        ]
        self.kept = []
        self.halves = []
        self.slot_rows = []
        for _, size, _ in self.lanes:
            kept, halves = [size], []
            for _ in range(self.bits):
                halves.append(kept[-1] // 2 >= 8)
                kept.append(kept[-1] // 2 if halves[-1] else kept[-1])
            self.kept.append(kept)
            self.halves.append(halves)
        for stage in range(self.bits):
            begin, starts = 0, []
            for lane in range(len(self.lanes)):
                starts.append(begin)
                begin += self.kept[lane][stage + 1]
            self.slot_rows.append((starts, begin))


def step_kernel(
    plan,
    inputs,
    grad_out,
    band_ids,
    conv_kernel,
    conv_bias,
    band_scale,
    band_shift,
    up_weight,
    up_bias,
    down_weight,
    down_bias,
    layer_scale,
    ends,
    up_out,
    down_out,
    small_out,
    spill,
    xs,
    normed,
    inv_std,
    adapted,
    hidden,
    slope,
    gb,
    g,
    gc,
    wup,
    wdn,
    packed,
    params,
    up_bias_row_of,
    upper_even,
    upper_odd,
    onehot,
    sums,
    up_sums,
    small,
    keep,
    outgo,
    income,
    small_sum,
    small_in,
    *rest,
):
    stage_in = rest[: plan.bits]
    (
        load_sem,
        wt_send,
        wt_recv,
        par_send,
        par_recv,
        ends_send,
        ends_recv,
        core_send,
        core_recv,
        rs_send,
        rs_recv,
        deliver_send,
        deliver_recv,
        ag_send,
        ag_recv,
        small_send,
        small_recv,
        spill_sem,
    ) = rest[plan.bits :]
    uppers = (upper_even, upper_odd)
    core = lax.axis_index("section")
    other = 1 - core
    batch = lax.axis_index("batch")
    clips, frames, width = g.shape
    rows = clips * frames
    layers = xs.shape[0] - 1
    per_core = layers // 2
    hidden_width = hidden.shape[2]
    tile = 2 * frames
    chunks = frames // chunk
    blocks = hidden_width // tile
    bits = plan.bits
    mesh_id = pl.DeviceIdType.MESH

    def bit_of(bit):
        return (batch // (1 << bit)) % 2

    def partner(bit):
        return batch + (1 - 2 * bit_of(bit)) * (1 << bit)

    def to_core(source, target, send, recv):
        return pltpu.make_async_remote_copy(source, target, send, recv, {"section": other}, mesh_id)

    def to_partner(source, target, send, recv, bit):
        return pltpu.make_async_remote_copy(source, target, send, recv, {"batch": partner(bit)}, mesh_id)

    own_blocks = pl.ds(per_core * core, per_core)
    own_up = pltpu.make_async_copy(up_weight, wup.at[own_blocks], load_sem.at[0])
    own_dn = pltpu.make_async_copy(down_weight, wdn.at[own_blocks], load_sem.at[1])
    own_up.start()
    own_dn.start()
    loads = []
    for source, target in ((inputs, adapted), (grad_out, gb)):
        for clip in range(clips):
            loads.append(
                pltpu.make_async_copy(
                    source.at[clip, core], target.at[pl.ds(clip * frames, frames)], load_sem.at[2 + len(loads)]
                )
            )
    for load in loads:
        load.start()

    for j in range(per_core):
        packed[j, taps_row : taps_row + 7] = conv_kernel[:, j]
        packed[j, conv_bias_row : conv_bias_row + 1] = conv_bias[j : j + 1]
        packed[j, scale_row : scale_row + 4] = band_scale[j]
        packed[j, shift_row : shift_row + 4] = band_shift[j]
        for q in range(3):
            row = up_bias_row + q
            packed[j, row : row + 1] = up_bias[j : j + 1, q * width : (q + 1) * width]
        packed[j, down_bias_row : down_bias_row + 1] = down_bias[j : j + 1]
        packed[j, gamma_row : gamma_row + 1] = layer_scale[j : j + 1]
        packed[j, gamma_row + 1 : packed_rows] = jnp.zeros((packed_rows - gamma_row - 1, width), f32)

    barrier = pltpu.get_barrier_semaphore()
    pl.semaphore_signal(barrier, inc=1, device_id={"section": other}, device_id_type=mesh_id)
    for bit in range(bits):
        pl.semaphore_signal(barrier, inc=1, device_id={"batch": partner(bit)}, device_id_type=mesh_id)
    pl.semaphore_wait(barrier, 1 + bits)

    par_copy = to_core(packed, params.at[own_blocks], par_send.at[0], par_recv.at[0])
    par_copy.start()
    params[own_blocks] = packed[...]

    stages = [
        xs.at[1, :, 0:frames],
        xs.at[2, :, 0:frames],
        xs.at[3, :, 0:frames],
        outgo.at[0],
        outgo.at[1],
        g,
        gc.at[:, 0:frames],
        xs.at[4, :, 0:frames],
    ]

    def weight_part(kind, layer, half, part):
        if kind == 0:
            return wup.at[
                layer,
                pl.ds(pl.multiple_of(half * (width // 2) + (part % 2) * frames, frames), frames),
                pl.ds(pl.multiple_of((part // 2) * width, width), width),
            ]
        return wdn.at[layer, pl.ds(pl.multiple_of(half * rows + part * frames, frames), frames), :]

    def weight_wait(k):
        return to_core(outgo.at[0], keep.at[k], wt_send.at[k], wt_recv.at[k])

    def send_weights(j):
        for kind in range(2):
            for half in range(2):
                k = 4 * j + 2 * kind + half

                def cast(part, carry, kind=kind, half=half, k=k):
                    stages[k][part] = weight_part(kind, per_core * core + j, half, part)[...].astype(f32)
                    return carry

                lax.fori_loop(0, clips, cast, 0)
                to_core(stages[k], keep.at[k], wt_send.at[k], wt_recv.at[k]).start()

    def take_weights(layer, kind):
        @pl.when(layer // per_core != core)
        def _():
            for half in range(2):
                k = 4 * (layer % per_core) + 2 * kind + half
                weight_wait(k).wait_recv()

                def cast(part, carry, half=half, k=k):
                    weight_part(kind, layer, half, part)[...] = keep[k, part].astype(bf16)
                    return carry

                lax.fori_loop(0, clips, cast, 0)

    own_up.wait()
    own_dn.wait()
    send_weights(0)

    for load in loads:
        load.wait()

    def load_x(clip, carry):
        xs[0, clip, 0:pad, :] = jnp.zeros((pad, width), f32)
        xs[0, clip, pad + frames : 2 * pad + frames, :] = jnp.zeros((pad, width), f32)
        xs[0, clip, pad : pad + frames, :] = adapted[
            pl.ds(pl.multiple_of(clip * frames, frames), frames), :
        ].astype(f32)
        for band in range(4):
            chosen = jnp.where(band_ids[core, clip] == band, 1.0, 0.0).astype(f32)
            onehot[clip, band : band + 1] = jnp.zeros((1, width), f32) + chosen
        return carry

    lax.fori_loop(0, clips, load_x, 0)
    par_copy.wait()
    for layer in range(layers):
        for block in range(blocks):
            row = up_bias_row + block // 2
            place = (block % 2) * tile
            up_bias_row_of[layer, block] = params[layer, row : row + 1, place : place + tile]

    def chosen_row(layer, clip, first):
        return jnp.sum(onehot[clip] * params[layer, first : first + 4], axis=0, keepdims=True)

    def norm_clip(layer, clip, save):
        table = params[layer]
        scale = chosen_row(layer, clip, scale_row)
        shift = chosen_row(layer, clip, shift_row)
        for j in range(chunks):
            window = xs[layer, clip, j * chunk : (j + 1) * chunk + 2 * pad, :]
            conv = window[pad : pad + chunk] * table[3:4] + table[conv_bias_row : conv_bias_row + 1]
            for k in (0, 1, 2, 4, 5, 6):
                conv = conv + window[pad - 3 + k : pad - 3 + k + chunk] * table[k : k + 1]
            centered = conv - jnp.mean(conv, axis=-1, keepdims=True)
            inv = lax.rsqrt(jnp.mean(centered * centered, axis=-1, keepdims=True) + norm_epsilon)
            value = centered * inv
            at = pl.ds(pl.multiple_of(clip * frames + j * chunk, chunk), chunk)
            if save:
                normed[at, :] = value
                inv_std[at, :] = inv
            adapted[at, :] = (value * scale + shift).astype(bf16)

    def saved_copy(layer, which, back):
        buffer = (hidden if which == 0 else slope).at[layer % 2]
        away = spill.at[layer % 2, which]
        source, target = (away, buffer) if back else (buffer, away)
        return pltpu.make_async_copy(source, target, spill_sem.at[layer % 2, which])

    def forward(layer, carry):
        slot = layer % 2

        def norm_body(clip, carry):
            norm_clip(layer, clip, False)
            return carry

        lax.fori_loop(0, clips, norm_body, 0)
        take_weights(layer, 0)

        @pl.when(layer >= 2)
        def _():
            for which in range(2):
                saved_copy(layer, which, False).wait()

        def up(block):
            columns = slice(block * tile, (block + 1) * tile)
            uppers[block % 2][...] = dot_plain(adapted[...], wup[layer, :, columns])

        def down(block):
            columns = slice(block * tile, (block + 1) * tile)
            value = dot_plain(hidden[slot, :, columns], wdn[layer, columns, :])
            normed[...] = value if block == 0 else normed[...] + value

        downs = {0: (), 1: (), 2: (), 3: (0, 1), 4: (2, 3), 5: (4,)}
        up(0)
        for block in range(blocks):
            columns = slice(block * tile, (block + 1) * tile)
            if block + 1 < blocks:
                up(block + 1)
            if block == blocks // 2:
                take_weights(layer, 1)
            for earlier in downs[block]:
                down(earlier)
            bias = up_bias_row_of[layer, block]
            for q in range(rows // chunk):
                at = slice(q * chunk, (q + 1) * chunk)
                smooth, steep = gelu_and_slope(uppers[block % 2][at, :] + bias)
                hidden[slot, at, columns] = smooth.astype(bf16)
                slope[slot, at, columns] = steep.astype(bf16)
        down(blocks - 1)

        @pl.when(layer < 2)
        def _():
            for which in range(2):
                saved_copy(layer, which, False).start()

        @pl.when(layer == 0)
        def _():
            for j in range(1, per_core):
                send_weights(j)

        for step in range(layers):

            @pl.when(layer == step)
            def _(step=step):
                for k in [step] if step < layers - 1 else range(layers - 1, 4 * per_core):
                    weight_wait(k).wait_send()

        def residual(clip, carry):
            bias = params[layer, down_bias_row : down_bias_row + 1]
            gamma = params[layer, gamma_row : gamma_row + 1]
            branch = normed[pl.ds(pl.multiple_of(clip * frames, frames), frames), :] + bias
            xs[layer + 1, clip, pad : pad + frames, :] = xs[layer, clip, pad : pad + frames, :] + gamma * branch
            return carry

        lax.fori_loop(0, clips, residual, 0)

        def zero_pads(clip, carry):
            xs[layer + 1, clip, 0:pad, :] = jnp.zeros((pad, width), f32)
            xs[layer + 1, clip, pad + frames : 2 * pad + frames, :] = jnp.zeros((pad, width), f32)
            return carry

        lax.fori_loop(0, clips, zero_pads, 0)
        return carry

    lax.fori_loop(0, layers, forward, 0)

    result = xs.at[layers, :, pad : pad + frames]
    result_remote = to_core(result, ends.at[0, :, 0], ends_send.at[0], ends_recv.at[0])
    result_local = pltpu.make_async_copy(result, ends.at[0, :, 1], ends_send.at[1])

    @pl.when(core == 0)
    def _():
        result_remote.start()

    @pl.when(core == 1)
    def _():
        result_local.start()

    def load_g(clip, carry):
        g[clip] = gb[pl.ds(pl.multiple_of(clip * frames, frames), frames), :].astype(f32)
        gc[clip, 0:pad, :] = jnp.zeros((pad, width), f32)
        gc[clip, pad + frames : 2 * pad + frames, :] = jnp.zeros((pad, width), f32)
        return carry

    lax.fori_loop(0, clips, load_g, 0)

    matrices = 2 * layers
    lane_count = len(plan.lanes)

    def core_copy(m, parity):
        return to_core(outgo.at[parity], income.at[parity], core_send.at[parity], core_recv.at[parity])

    keep_rows = keep.reshape(matrices, rows, width)

    def offset(lane, stage):
        start = 0
        for s in range(stage):
            if plan.halves[lane][s]:
                start = start + bit_of(plan.lanes[lane][2][s]) * plan.kept[lane][s + 1]
        return start

    def rs_copy(m, parity, lane, stage):
        begin, _, order = plan.lanes[lane]
        bit = order[stage]
        size = plan.kept[lane][stage + 1]
        at = begin + offset(lane, stage)
        if plan.halves[lane][stage]:
            at = at + (1 - bit_of(bit)) * size
        starts, _ = plan.slot_rows[stage]
        return to_partner(
            keep_rows.at[m, pl.ds(pl.multiple_of(at, 8), size)],
            stage_in[stage].at[parity, starts[lane] : starts[lane] + size],
            rs_send.at[stage, parity, lane],
            rs_recv.at[stage, parity, lane],
            bit,
        )

    def rs_add(m, parity, lane, stage):
        begin, _, _ = plan.lanes[lane]
        size = plan.kept[lane][stage + 1]
        at = begin + offset(lane, stage + 1)
        starts, _ = plan.slot_rows[stage]
        step = min(size, 2 * chunk)

        def body(i, carry):
            r = pl.multiple_of(at + i * step, 8)
            keep_rows[m, pl.ds(r, step), :] = (
                keep_rows[m, pl.ds(r, step), :]
                + stage_in[stage][parity, pl.ds(pl.multiple_of(starts[lane] + i * step, 8), step), :]
            )
            return carry

        lax.fori_loop(0, size // step, body, 0)

    def out_slice(kind, local, half, lane, at, size):
        begin, _, _ = plan.lanes[lane]
        third = rows // 3
        if kind == 0:
            return down_out.at[local, half, pl.ds(pl.multiple_of(begin + at, 8), size), :]
        column = (begin // third) * width
        return up_out.at[
            local, half, pl.ds(pl.multiple_of(begin % third + at, 8), size), column : column + width
        ]

    def deliver_copy(m, kind, local, lane, near):
        begin, _, _ = plan.lanes[lane]
        size = plan.kept[lane][bits]
        at = offset(lane, bits)
        source = keep_rows.at[m, pl.ds(pl.multiple_of(begin + at, 8), size)]
        target = out_slice(kind, local, core, lane, at, size)
        if near:
            return pltpu.make_async_copy(source, target, deliver_recv.at[m % 4, core, lane])
        return to_core(source, target, deliver_send.at[m % 4, lane], deliver_recv.at[m % 4, core, lane])

    def deliver_wait(m, kind, local, lane):
        size = plan.kept[lane][bits]
        at = offset(lane, bits)
        source = keep_rows.at[m, pl.ds(0, size)]
        near = pltpu.make_async_copy(
            source, out_slice(kind, local, core, lane, at, size), deliver_recv.at[m % 4, core, lane]
        )
        far = to_core(
            source,
            out_slice(kind, local, other, lane, at, size),
            deliver_send.at[m % 4, lane],
            deliver_recv.at[m % 4, other, lane],
        )
        return near, far

    def ag_copy(kind, local, parity, lane, stage):
        size = plan.kept[lane][stage + 1]
        at = offset(lane, stage + 1)
        place = out_slice(kind, local, slice(None), lane, at, size)
        return to_partner(
            place,
            place,
            ag_send.at[stage, parity, lane],
            ag_recv.at[stage, parity, lane],
            plan.lanes[lane][2][stage],
        )

    def tick(pair, phase):
        for s in range(2 * bits + 2, 0, -1):
            m = 2 * pair + phase + 1 - s
            parity = (phase + 1 - s) % 2
            kind = parity
            layer = layers - 1 - (m - kind) // 2
            owner = layer // per_core
            local = layer % per_core

            @pl.when((m >= 0) & (m < matrices))
            def _(s=s, m=m, parity=parity, kind=kind, owner=owner, local=local):
                if s == 1:
                    core_copy(m, parity).wait()

                    def body(clip, carry):
                        keep[m, clip] = keep[m, clip] + income[parity, clip]
                        return carry

                    lax.fori_loop(0, clips, body, 0)
                elif s <= bits + 1:
                    for lane in range(lane_count):
                        rs_copy(m, parity, lane, s - 2).wait()
                        rs_add(m, parity, lane, s - 2)
                if s <= bits:
                    for lane in range(lane_count):
                        rs_copy(m, parity, lane, s - 1).start()
                elif s == bits + 1:

                    @pl.when(owner == core)
                    def _():
                        for lane in range(lane_count):
                            deliver_copy(m, kind, local, lane, True).start()

                    @pl.when(owner != core)
                    def _():
                        for lane in range(lane_count):
                            deliver_copy(m, kind, local, lane, False).start()

                else:

                    @pl.when(owner == core)
                    def _():
                        if s == bits + 2:
                            for lane in range(lane_count):
                                near, far = deliver_wait(m, kind, local, lane)
                                near.wait()
                                far.wait_recv()
                        else:
                            stage = 2 * bits + 2 - s
                            for lane in range(lane_count):
                                if plan.halves[lane][stage]:
                                    ag_copy(kind, local, parity, lane, stage).wait()
                        if s < 2 * bits + 2:
                            stage = 2 * bits + 1 - s
                            for lane in range(lane_count):
                                if plan.halves[lane][stage]:
                                    ag_copy(kind, local, parity, lane, stage).start()

                    if s == bits + 2:

                        @pl.when(owner != core)
                        def _():
                            for lane in range(lane_count):
                                deliver_copy(m, kind, local, lane, False).wait_send()

    def store_block(m, phase, second, block, value):
        for q in range(2):
            piece = value[q * frames : (q + 1) * frames]
            if second == 0:
                outgo[phase, 2 * block + q] = piece
            else:
                keep[m, 2 * block + q] = piece

    def scale_clip(layer, clip):
        gamma = params[layer, gamma_row : gamma_row + 1]
        gamma_sum = bias_sum = jnp.zeros((8, width), f32)
        for j in range(chunks):
            here = g[clip, j * chunk : (j + 1) * chunk, :]
            at = slice(pad + j * chunk, pad + (j + 1) * chunk)
            gamma_sum = gamma_sum + fold(here * (xs[layer + 1, clip, at, :] - xs[layer, clip, at, :]))
            value = (gamma * here).astype(bf16)
            gb[pl.ds(pl.multiple_of(clip * frames + j * chunk, chunk), chunk), :] = value
            bias_sum = bias_sum + fold(value.astype(f32))
        sums[0] += gamma_sum
        sums[1] += bias_sum

    def norm_back(layer, clip):
        scale = chosen_row(layer, clip, scale_row)
        scale_sum = shift_sum = conv_sum = jnp.zeros((8, width), f32)
        for j in range(chunks):
            row = pl.ds(pl.multiple_of(clip * frames + j * chunk, chunk), chunk)
            at = slice(pad + j * chunk, pad + (j + 1) * chunk)
            ga = gc[clip, at, :]
            value = normed[row, :]
            scale_sum = scale_sum + fold(ga * value)
            shift_sum = shift_sum + fold(ga)
            dn = ga * scale
            first = jnp.mean(dn, axis=-1, keepdims=True)
            second = jnp.mean(dn * value, axis=-1, keepdims=True)
            result = inv_std[row, :] * (dn - first - value * second)
            gc[clip, at, :] = result
            conv_sum = conv_sum + fold(result)
        sums[9] += conv_sum
        choice = onehot[clip]
        small[layer, scale_row : scale_row + 4, :] += choice * jnp.sum(scale_sum, axis=0, keepdims=True)
        small[layer, shift_row : shift_row + 4, :] += choice * jnp.sum(shift_sum, axis=0, keepdims=True)

    def conv_back(layer, clip):
        table = params[layer]
        totals = [jnp.zeros((8, width), f32) for _ in range(7)]
        for j in range(chunks):
            around = slice(j * chunk, (j + 1) * chunk + 2 * pad)
            signal = xs[layer, clip, around, :]
            grads = gc[clip, around, :]
            here = grads[pad : pad + chunk]
            at = slice(j * chunk, (j + 1) * chunk)
            total = g[clip, at, :] + here * table[3:4]
            totals[3] = totals[3] + fold(signal[pad : pad + chunk] * here)
            for k in (0, 1, 2, 4, 5, 6):
                total = total + grads[pad + 3 - k : pad + 3 - k + chunk] * table[k : k + 1]
                totals[k] = totals[k] + fold(signal[pad - 3 + k : pad - 3 + k + chunk] * here)
            g[clip, at, :] = total
        for k in range(7):
            sums[2 + k] += totals[k]

    def backward(pair, carry):
        layer = layers - 1 - pair
        slot = layer % 2
        sums[...] = jnp.zeros(sums.shape, f32)
        small[layer] = jnp.zeros(small.shape[1:], f32)

        def scale_body(clip, carry):
            scale_clip(layer, clip)
            return carry

        lax.fori_loop(0, clips, scale_body, 0)

        @pl.when(layer < 2)
        def _():
            for which in range(2):
                saved_copy(layer, which, True).wait()

        for second in range(2):
            half = other if second == 0 else core

            def down_body(block, carry, second=second, half=half):
                at = pl.ds(pl.multiple_of(half * rows + block * tile, tile), tile)
                store_block(2 * pair, 0, second, block, dot_rows(hidden[slot, :, at], gb[...]))
                norm_clip(layer, block + 3 * second, True)
                return carry

            lax.fori_loop(0, clips // 2, down_body, 0)
            if second == 0:
                core_copy(2 * pair, 0).start()

        def up_grad(block, carry):
            columns = pl.ds(pl.multiple_of(block * tile, tile), tile)
            value = dot_cols(gb[...], wdn[layer, columns, :])
            total = jnp.zeros((8, tile), f32)
            for q in range(rows // chunk):
                at = slice(q * chunk, (q + 1) * chunk)
                piece = (value[at] * slope[slot, at, columns].astype(f32)).astype(bf16)
                slope[slot, at, columns] = piece
                total = total + fold(piece.astype(f32))
            up_sums[block] = total
            return carry

        lax.fori_loop(0, blocks, up_grad, 0)
        tick(pair, 0)

        for second in range(2):
            half = other if second == 0 else core
            at = pl.ds(pl.multiple_of(half * (width // 2), width // 2), width // 2)

            def up_body(block, carry, second=second, at=at):
                columns = pl.ds(pl.multiple_of(block * width, width), width)
                store_block(2 * pair + 1, 1, second, block, dot_rows(adapted[:, at], slope[slot, :, columns]))
                return carry

            lax.fori_loop(0, clips // 2, up_body, 0)
            if second == 0:
                core_copy(2 * pair + 1, 1).start()

        for block in range(width // tile):
            columns = slice(block * tile, (block + 1) * tile)
            value = dot_cols(slope[slot], wup[layer, columns, :])
            for clip in range(clips):
                gc[clip, pad : pad + frames, columns] = value[clip * frames : (clip + 1) * frames]

        tick(pair, 1)

        def norm_conv_back(clip, carry):
            norm_back(layer, clip)
            conv_back(layer, clip)
            return carry

        lax.fori_loop(0, clips, norm_conv_back, 0)

        @pl.when(layer >= 2)
        def _():
            for which in range(2):
                saved_copy(layer, which, True).start()

        gamma = params[layer, gamma_row : gamma_row + 1, :]
        small[layer, gamma_row : gamma_row + 1, :] = jnp.sum(sums[0], axis=0, keepdims=True) / gamma
        small[layer, down_bias_row : down_bias_row + 1, :] = jnp.sum(sums[1], axis=0, keepdims=True)
        for block in range(blocks):
            row = up_bias_row + block // 2
            place = (block % 2) * tile
            small[layer, row : row + 1, place : place + tile] = jnp.sum(up_sums[block], axis=0, keepdims=True)
        for k in range(7):
            small[layer, taps_row + k : taps_row + k + 1, :] = jnp.sum(sums[2 + k], axis=0, keepdims=True)
        small[layer, conv_bias_row : conv_bias_row + 1, :] = jnp.sum(sums[9], axis=0, keepdims=True)
        return carry

    lax.fori_loop(0, layers, backward, 0)

    grad_remote = to_core(g, ends.at[0, :, 1], ends_send.at[2], ends_recv.at[1])
    grad_local = pltpu.make_async_copy(g, ends.at[0, :, 0], ends_send.at[3])

    @pl.when(core == 0)
    def _():
        grad_local.start()

    @pl.when(core == 1)
    def _():
        grad_remote.start()

    small_core = to_core(
        small.at[pl.ds(per_core * other, per_core)], small_in.at[bits], small_send.at[bits], small_recv.at[bits]
    )
    small_core.start()

    def small_copy(bit):
        return to_partner(small_sum, small_in.at[bit], small_send.at[bit], small_recv.at[bit], bit)

    def drain(pair, carry):
        for phase in range(2):
            tick(pair, phase)
            for step in range(bits + 1):

                @pl.when(2 * pair + phase - matrices == step)
                def _(step=step):
                    if step == 0:
                        small_core.wait()
                        small_sum[...] = small[pl.ds(per_core * core, per_core)] + small_in[bits]
                    else:
                        small_copy(step - 1).wait()
                        small_sum[...] = small_sum[...] + small_in[step - 1]
                    if step < bits:
                        small_copy(step).start()

        return carry

    lax.fori_loop(layers, layers + bits + 1, drain, 0)
    small_out[...] = small_sum[...]

    @pl.when(core == 0)
    def _():
        grad_local.wait()
        result_remote.wait_send()
        grad_remote.wait_recv()

    @pl.when(core == 1)
    def _():
        result_local.wait()
        result_remote.wait_recv()
        grad_remote.wait_send()


def results_kernel(
    ends,
    up_grad,
    down_grad,
    small,
    ends_out,
    conv_kernel_out,
    conv_bias_out,
    band_scale_out,
    band_shift_out,
    up_out,
    up_bias_out,
    down_out,
    down_bias_out,
    layer_scale_out,
    sem,
):
    copies = []
    per_core, _, width = small.shape
    for j in range(per_core):
        for half in range(2):
            for source, target in ((up_grad, up_out), (down_grad, down_out)):
                copies.append(pltpu.make_async_copy(source.at[j, half], target.at[j, half], sem.at[len(copies)]))
    for clip in range(ends.shape[1]):
        copies.append(pltpu.make_async_copy(ends.at[0, clip], ends_out.at[0, clip], sem.at[len(copies)]))
    for copy in copies:
        copy.start()
    for j in range(per_core):
        conv_kernel_out[:, j] = small[j, taps_row : taps_row + 7]
        conv_bias_out[j : j + 1] = small[j, conv_bias_row : conv_bias_row + 1]
        band_scale_out[j] = small[j, scale_row : scale_row + 4]
        band_shift_out[j] = small[j, shift_row : shift_row + 4]
        for q in range(3):
            row = up_bias_row + q
            up_bias_out[j : j + 1, q * width : (q + 1) * width] = small[j, row : row + 1]
        down_bias_out[j : j + 1] = small[j, down_bias_row : down_bias_row + 1]
        layer_scale_out[j : j + 1] = small[j, gamma_row : gamma_row + 1]
    for copy in copies:
        copy.wait()


def body(
    inputs,
    grad_out,
    band_ids,
    conv_kernel,
    conv_bias,
    band_scale,
    band_shift,
    up_weight,
    up_bias,
    down_weight,
    down_bias,
    layer_scale,
):
    sections = lax.axis_size("section")
    batch = lax.axis_size("batch")
    clips, local_clips, frames, width = inputs.shape
    per_core, _, hidden_width = up_weight.shape
    layers = per_core * sections
    bands = band_scale.shape[1]
    rows = clips * frames
    assert sections == 2 and local_clips == 2 and batch & (batch - 1) == 0
    assert hidden_width == 3 * width and bands == 4 and layers == 4 and rows == 3 * width // 2
    plan = Plan(batch, rows)
    bits = plan.bits
    hbm = pl.BlockSpec(memory_space=pl.ANY)
    vmem = pl.BlockSpec(memory_space=pltpu.VMEM)
    smem = pl.BlockSpec(memory_space=pltpu.SMEM)
    padded = frames + 2 * pad
    dma = pltpu.SemaphoreType.DMA
    lanes = len(plan.lanes)
    tile = 2 * frames
    ends_shape = jax.ShapeDtypeStruct((1, clips, local_clips, frames, width), f32)
    up_shape = jax.ShapeDtypeStruct((per_core, 2, width // 2, hidden_width), f32)
    down_shape = jax.ShapeDtypeStruct((per_core, 2, hidden_width // 2, width), f32)
    small_shape = jax.ShapeDtypeStruct((per_core, packed_rows, width), f32)
    saved_shape = jax.ShapeDtypeStruct((2, 2, rows, hidden_width), bf16)
    conv_kernel = jnp.transpose(conv_kernel, (1, 0, 2))
    ends, up_grad, down_grad, small, _ = pl.pallas_call(
        functools.partial(step_kernel, plan),
        out_shape=[ends_shape, up_shape, down_shape, small_shape, saved_shape],
        in_specs=[hbm, hbm, smem, vmem, vmem, vmem, vmem, hbm, vmem, hbm, vmem, vmem],
        out_specs=[hbm, hbm, hbm, vmem, hbm],
        scratch_shapes=[
            pltpu.VMEM((layers + 1, clips, padded, width), f32),
            pltpu.VMEM((rows, width), f32),
            pltpu.VMEM((rows, 1), f32),
            pltpu.VMEM((rows, width), bf16),
            pltpu.VMEM((2, rows, hidden_width), bf16),
            pltpu.VMEM((2, rows, hidden_width), bf16),
            pltpu.VMEM((rows, width), bf16),
            pltpu.VMEM((clips, frames, width), f32),
            pltpu.VMEM((clips, padded, width), f32),
            pltpu.VMEM((layers, width, hidden_width), bf16),
            pltpu.VMEM((layers, hidden_width, width), bf16),
            pltpu.VMEM((per_core, packed_rows, width), f32),
            pltpu.VMEM((layers, packed_rows, width), f32),
            pltpu.VMEM((layers, hidden_width // tile, 1, tile), f32),
            pltpu.VMEM((rows, tile), f32),
            pltpu.VMEM((rows, tile), f32),
            pltpu.VMEM((clips, bands, width), f32),
            pltpu.VMEM((10, 8, width), f32),
            pltpu.VMEM((hidden_width // tile, 8, tile), f32),
            pltpu.VMEM((layers, packed_rows, width), f32),
            pltpu.VMEM((2 * layers, clips, frames, width), f32),
            pltpu.VMEM((2, clips, frames, width), f32),
            pltpu.VMEM((2, clips, frames, width), f32),
            pltpu.VMEM((per_core, packed_rows, width), f32),
            pltpu.VMEM((bits + 1, per_core, packed_rows, width), f32),
            *[pltpu.VMEM((2, plan.slot_rows[stage][1], width), f32) for stage in range(bits)],
            dma((2 + 2 * clips,)),
            dma((4 * per_core,)),
            dma((4 * per_core,)),
            dma((1,)),
            dma((1,)),
            dma((4,)),
            dma((2,)),
            dma((2,)),
            dma((2,)),
            dma((bits, 2, lanes)),
            dma((bits, 2, lanes)),
            dma((4, lanes)),
            dma((4, 2, lanes)),
            dma((bits, 2, lanes)),
            dma((bits, 2, lanes)),
            dma((bits + 1,)),
            dma((bits + 1,)),
            dma((2, 2)),
        ],
        compiler_params=pltpu.CompilerParams(
            collective_id=0, has_side_effects=True, vmem_limit_bytes=255 * 2**18
        ),
        cost_estimate=pl.CostEstimate(
            flops=24 * rows * width * hidden_width * 2, bytes_accessed=2**26, transcendentals=2**24
        ),
        name="blocks_step",
    )(
        inputs,
        grad_out,
        jnp.transpose(band_ids),
        conv_kernel,
        conv_bias,
        band_scale,
        band_shift,
        up_weight,
        up_bias,
        down_weight,
        down_bias,
        layer_scale,
    )

    def like(array):
        return jax.ShapeDtypeStruct(array.shape, f32)

    outs = pl.pallas_call(
        results_kernel,
        out_shape=[
            ends_shape,
            like(conv_kernel),
            like(conv_bias),
            like(band_scale),
            like(band_shift),
            up_shape,
            like(up_bias),
            down_shape,
            like(down_bias),
            like(layer_scale),
        ],
        in_specs=[hbm, hbm, hbm, vmem],
        out_specs=[hbm, vmem, vmem, vmem, vmem, hbm, vmem, hbm, vmem, vmem],
        scratch_shapes=[dma((4 * per_core + clips,))],
        cost_estimate=pl.CostEstimate(flops=0, bytes_accessed=2**25, transcendentals=0),
        name="results",
    )(ends, up_grad, down_grad, small)
    outs = list(outs)
    outs[1] = jnp.transpose(outs[1], (1, 0, 2))
    outs[5] = outs[5].reshape(up_weight.shape)
    outs[7] = outs[7].reshape(down_weight.shape)
    return tuple(outs)


def solution(mesh):
    in_specs = (
        P(None, "batch", None, None),
        P(None, "batch", None, None),
        P(None, "batch"),
        P("section", None, None),
        P("section", None),
        P("section", None, None),
        P("section", None, None),
        P("section", None, None),
        P("section", None),
        P("section", None, None),
        P("section", None),
        P("section", None),
    )
    out_specs = (
        P("section", None, "batch", None, None),
        P("section", None, None),
        P("section", None),
        P("section", None, None),
        P("section", None, None),
        P("section", None, None),
        P("section", None),
        P("section", None, None),
        P("section", None),
        P("section", None),
    )
    return jax.shard_map(body, mesh=mesh, in_specs=in_specs, out_specs=out_specs, check_vma=False)
```

```python
import functools

import jax
import jax.numpy as jnp
from jax import lax
from jax.experimental import pallas as pl
from jax.experimental.pallas import tpu as pltpu
from jax.sharding import PartitionSpec as P

norm_epsilon = 1e-06
f32 = jnp.float32
bf16 = jnp.bfloat16

knee = 1.0 / 0.325
tail = tuple(
    value * knee**power
    for power, value in enumerate((0.0023193, 0.10197519, 0.25681865, -0.17643491, 0.43540795, -0.12008618))
)

taps_row, conv_bias_row, scale_row, shift_row, up_bias_row, down_bias_row, gamma_row = 0, 7, 8, 12, 16, 19, 20
packed_rows = 24
pad = 8
chunk = 32


def gelu_and_slope(u):
    size = jnp.abs(u)
    exponential = jnp.exp2(u * (u * (-0.5 * 1.4426950408889634)))
    base = size + knee
    t = pl.reciprocal(base, approx=True)
    t = t * (2.0 - base * t)
    poly = tail[5] * t + tail[4]
    for k in range(3, -1, -1):
        poly = poly * t + tail[k]
    smooth = jnp.maximum(u, 0.0) - size * (exponential * poly)
    below = exponential * (poly - 0.3989422804014327 * size)
    return smooth, jnp.where(u < 0.0, below, 1.0 - below)


def fold(values):
    rows, columns = values.shape
    return jnp.sum(values.reshape(rows // 8, 8, columns), axis=0)


def dot_rows(left, right):
    return lax.dot_general(left, right, (((0,), (0,)), ((), ())), preferred_element_type=f32)


def dot_plain(left, right):
    return lax.dot_general(left, right, (((1,), (0,)), ((), ())), preferred_element_type=f32)


def dot_cols(left, right):
    return lax.dot_general(left, right, (((1,), (1,)), ((), ())), preferred_element_type=f32)


class Plan:
    def __init__(self, batch, rows):
        self.bits = batch.bit_length() - 1
        third = rows // 3
        order = list(range(self.bits))
        swapped = order[:]
        if self.bits > 1:
            swapped[0], swapped[1] = 1, 0
        late, later = order[:], order[:]
        if self.bits > 2:
            late = [2, 0, 1] + order[3:]
            later = [2, 1, 0] + order[3:]
        self.lanes = [
            (0, third, order),
            (third, third, swapped),
            (2 * third, third // 2, late),
            (2 * third + third // 2, third // 2, later),
        ]
        self.kept = []
        self.halves = []
        self.slot_rows = []
        for _, size, _ in self.lanes:
            kept, halves = [size], []
            for _ in range(self.bits):
                halves.append(kept[-1] // 2 >= 8)
                kept.append(kept[-1] // 2 if halves[-1] else kept[-1])
            self.kept.append(kept)
            self.halves.append(halves)
        for stage in range(self.bits):
            begin, starts = 0, []
            for lane in range(len(self.lanes)):
                starts.append(begin)
                begin += self.kept[lane][stage + 1]
            self.slot_rows.append((starts, begin))


def step_kernel(
    plan,
    inputs,
    grad_out,
    band_ids,
    conv_kernel,
    conv_bias,
    band_scale,
    band_shift,
    up_weight,
    up_bias,
    down_weight,
    down_bias,
    layer_scale,
    ends,
    up_out,
    down_out,
    small_out,
    spill,
    xs,
    normed,
    inv_std,
    adapted,
    hidden,
    slope,
    gb,
    g,
    gc,
    wup,
    wdn,
    packed,
    params,
    up_bias_row_of,
    upper_even,
    upper_odd,
    onehot,
    sums,
    up_sums,
    small,
    keep,
    outgo,
    income,
    small_sum,
    small_in,
    *rest,
):
    stage_in = rest[: plan.bits]
    (
        load_sem,
        wt_send,
        wt_recv,
        par_send,
        par_recv,
        ends_send,
        ends_recv,
        core_send,
        core_recv,
        rs_send,
        rs_recv,
        deliver_send,
        deliver_recv,
        ag_send,
        ag_recv,
        out_sem,
        credit,
        small_send,
        small_recv,
        spill_sem,
    ) = rest[plan.bits :]
    uppers = (upper_even, upper_odd)
    core = lax.axis_index("section")
    other = 1 - core
    batch = lax.axis_index("batch")
    clips, frames, width = g.shape
    rows = clips * frames
    layers = xs.shape[0] - 1
    per_core = layers // 2
    hidden_width = hidden.shape[2]
    tile = 2 * frames
    chunks = frames // chunk
    blocks = hidden_width // tile
    bits = plan.bits
    mesh_id = pl.DeviceIdType.MESH

    def bit_of(bit):
        return (batch // (1 << bit)) % 2

    def partner(bit):
        return batch + (1 - 2 * bit_of(bit)) * (1 << bit)

    def to_core(source, target, send, recv):
        return pltpu.make_async_remote_copy(source, target, send, recv, {"section": other}, mesh_id)

    def to_partner(source, target, send, recv, bit):
        return pltpu.make_async_remote_copy(source, target, send, recv, {"batch": partner(bit)}, mesh_id)

    own_blocks = pl.ds(per_core * core, per_core)
    own_up = pltpu.make_async_copy(up_weight, wup.at[own_blocks], load_sem.at[0])
    own_dn = pltpu.make_async_copy(down_weight, wdn.at[own_blocks], load_sem.at[1])
    own_up.start()
    own_dn.start()
    loads = []
    for source, target in ((inputs, adapted), (grad_out, gb)):
        for clip in range(clips):
            loads.append(
                pltpu.make_async_copy(
                    source.at[clip, core], target.at[pl.ds(clip * frames, frames)], load_sem.at[2 + len(loads)]
                )
            )
    for load in loads:
        load.start()

    for j in range(per_core):
        packed[j, taps_row : taps_row + 7] = conv_kernel[:, j]
        packed[j, conv_bias_row : conv_bias_row + 1] = conv_bias[j : j + 1]
        packed[j, scale_row : scale_row + 4] = band_scale[j]
        packed[j, shift_row : shift_row + 4] = band_shift[j]
        for q in range(3):
            row = up_bias_row + q
            packed[j, row : row + 1] = up_bias[j : j + 1, q * width : (q + 1) * width]
        packed[j, down_bias_row : down_bias_row + 1] = down_bias[j : j + 1]
        packed[j, gamma_row : gamma_row + 1] = layer_scale[j : j + 1]
        packed[j, gamma_row + 1 : packed_rows] = jnp.zeros((packed_rows - gamma_row - 1, width), f32)

    barrier = pltpu.get_barrier_semaphore()
    pl.semaphore_signal(barrier, inc=1, device_id={"section": other}, device_id_type=mesh_id)
    for bit in range(bits):
        pl.semaphore_signal(barrier, inc=1, device_id={"batch": partner(bit)}, device_id_type=mesh_id)
    pl.semaphore_wait(barrier, 1 + bits)

    par_copy = to_core(packed, params.at[own_blocks], par_send.at[0], par_recv.at[0])
    par_copy.start()
    params[own_blocks] = packed[...]

    stages = [
        xs.at[1, :, 0:frames],
        xs.at[2, :, 0:frames],
        xs.at[3, :, 0:frames],
        outgo.at[0],
        outgo.at[1],
        g,
        gc.at[:, 0:frames],
        xs.at[4, :, 0:frames],
    ]

    def weight_part(kind, layer, half, part):
        if kind == 0:
            return wup.at[
                layer,
                pl.ds(pl.multiple_of(half * (width // 2) + (part % 2) * frames, frames), frames),
                pl.ds(pl.multiple_of((part // 2) * width, width), width),
            ]
        return wdn.at[layer, pl.ds(pl.multiple_of(half * rows + part * frames, frames), frames), :]

    def weight_wait(k):
        return to_core(outgo.at[0], keep.at[k], wt_send.at[k], wt_recv.at[k])

    def send_weights(j):
        for kind in range(2):
            for half in range(2):
                k = 4 * j + 2 * kind + half

                def cast(part, carry, kind=kind, half=half, k=k):
                    stages[k][part] = weight_part(kind, per_core * core + j, half, part)[...].astype(f32)
                    return carry

                lax.fori_loop(0, clips, cast, 0)
                to_core(stages[k], keep.at[k], wt_send.at[k], wt_recv.at[k]).start()

    def take_weights(layer, kind):
        @pl.when(layer // per_core != core)
        def _():
            for half in range(2):
                k = 4 * (layer % per_core) + 2 * kind + half
                weight_wait(k).wait_recv()

                def cast(part, carry, half=half, k=k):
                    weight_part(kind, layer, half, part)[...] = keep[k, part].astype(bf16)
                    return carry

                lax.fori_loop(0, clips, cast, 0)

    own_up.wait()
    own_dn.wait()
    send_weights(0)

    for load in loads:
        load.wait()

    def load_x(clip, carry):
        xs[0, clip, 0:pad, :] = jnp.zeros((pad, width), f32)
        xs[0, clip, pad + frames : 2 * pad + frames, :] = jnp.zeros((pad, width), f32)
        xs[0, clip, pad : pad + frames, :] = adapted[
            pl.ds(pl.multiple_of(clip * frames, frames), frames), :
        ].astype(f32)
        for band in range(4):
            chosen = jnp.where(band_ids[core, clip] == band, 1.0, 0.0).astype(f32)
            onehot[clip, band : band + 1] = jnp.zeros((1, width), f32) + chosen
        return carry

    lax.fori_loop(0, clips, load_x, 0)
    par_copy.wait()
    for layer in range(layers):
        for block in range(blocks):
            row = up_bias_row + block // 2
            place = (block % 2) * tile
            up_bias_row_of[layer, block] = params[layer, row : row + 1, place : place + tile]

    def chosen_row(layer, clip, first):
        return jnp.sum(onehot[clip] * params[layer, first : first + 4], axis=0, keepdims=True)

    def norm_clip(layer, clip, save):
        table = params[layer]
        scale = chosen_row(layer, clip, scale_row)
        shift = chosen_row(layer, clip, shift_row)
        for j in range(chunks):
            window = xs[layer, clip, j * chunk : (j + 1) * chunk + 2 * pad, :]
            conv = window[pad : pad + chunk] * table[3:4] + table[conv_bias_row : conv_bias_row + 1]
            for k in (0, 1, 2, 4, 5, 6):
                conv = conv + window[pad - 3 + k : pad - 3 + k + chunk] * table[k : k + 1]
            centered = conv - jnp.mean(conv, axis=-1, keepdims=True)
            inv = lax.rsqrt(jnp.mean(centered * centered, axis=-1, keepdims=True) + norm_epsilon)
            value = centered * inv
            at = pl.ds(pl.multiple_of(clip * frames + j * chunk, chunk), chunk)
            if save:
                normed[at, :] = value
                inv_std[at, :] = inv
            adapted[at, :] = (value * scale + shift).astype(bf16)

    def saved_copy(layer, which, back):
        buffer = (hidden if which == 0 else slope).at[layer % 2]
        away = spill.at[layer % 2, which]
        source, target = (away, buffer) if back else (buffer, away)
        return pltpu.make_async_copy(source, target, spill_sem.at[layer % 2, which])

    def forward(layer, carry):
        slot = layer % 2

        def norm_body(clip, carry):
            norm_clip(layer, clip, False)
            return carry

        lax.fori_loop(0, clips, norm_body, 0)
        take_weights(layer, 0)

        @pl.when(layer >= 2)
        def _():
            for which in range(2):
                saved_copy(layer, which, False).wait()

        def up(block):
            columns = slice(block * tile, (block + 1) * tile)
            uppers[block % 2][...] = dot_plain(adapted[...], wup[layer, :, columns])

        def down(block):
            columns = slice(block * tile, (block + 1) * tile)
            value = dot_plain(hidden[slot, :, columns], wdn[layer, columns, :])
            normed[...] = value if block == 0 else normed[...] + value

        downs = {0: (), 1: (), 2: (), 3: (0, 1), 4: (2, 3), 5: (4,)}
        up(0)
        for block in range(blocks):
            columns = slice(block * tile, (block + 1) * tile)
            if block + 1 < blocks:
                up(block + 1)
            if block == blocks // 2:
                take_weights(layer, 1)
            for earlier in downs[block]:
                down(earlier)
            bias = up_bias_row_of[layer, block]
            for q in range(rows // chunk):
                at = slice(q * chunk, (q + 1) * chunk)
                smooth, steep = gelu_and_slope(uppers[block % 2][at, :] + bias)
                hidden[slot, at, columns] = smooth.astype(bf16)
                slope[slot, at, columns] = steep.astype(bf16)
        down(blocks - 1)

        @pl.when(layer < 2)
        def _():
            for which in range(2):
                saved_copy(layer, which, False).start()

        @pl.when(layer == 0)
        def _():
            for j in range(1, per_core):
                send_weights(j)

        for step in range(layers):

            @pl.when(layer == step)
            def _(step=step):
                for k in [step] if step < layers - 1 else range(layers - 1, 4 * per_core):
                    weight_wait(k).wait_send()

        def residual(clip, carry):
            bias = params[layer, down_bias_row : down_bias_row + 1]
            gamma = params[layer, gamma_row : gamma_row + 1]
            branch = normed[pl.ds(pl.multiple_of(clip * frames, frames), frames), :] + bias
            xs[layer + 1, clip, pad : pad + frames, :] = xs[layer, clip, pad : pad + frames, :] + gamma * branch
            return carry

        lax.fori_loop(0, clips, residual, 0)

        def zero_pads(clip, carry):
            xs[layer + 1, clip, 0:pad, :] = jnp.zeros((pad, width), f32)
            xs[layer + 1, clip, pad + frames : 2 * pad + frames, :] = jnp.zeros((pad, width), f32)
            return carry

        lax.fori_loop(0, clips, zero_pads, 0)
        return carry

    lax.fori_loop(0, layers, forward, 0)

    result = xs.at[layers, :, pad : pad + frames]
    result_remote = to_core(result, ends.at[0, :, 0], ends_send.at[0], ends_recv.at[0])
    result_local = pltpu.make_async_copy(result, ends.at[0, :, 1], ends_send.at[1])

    @pl.when(core == 0)
    def _():
        result_remote.start()

    @pl.when(core == 1)
    def _():
        result_local.start()

    def load_g(clip, carry):
        g[clip] = gb[pl.ds(pl.multiple_of(clip * frames, frames), frames), :].astype(f32)
        gc[clip, 0:pad, :] = jnp.zeros((pad, width), f32)
        gc[clip, pad + frames : 2 * pad + frames, :] = jnp.zeros((pad, width), f32)
        return carry

    lax.fori_loop(0, clips, load_g, 0)

    matrices = 2 * layers
    lane_count = len(plan.lanes)

    def core_copy(m, parity):
        return to_core(outgo.at[parity], income.at[parity], core_send.at[parity], core_recv.at[parity])

    keep_rows = keep.reshape(matrices, rows, width)

    def offset(lane, stage):
        start = 0
        for s in range(stage):
            if plan.halves[lane][s]:
                start = start + bit_of(plan.lanes[lane][2][s]) * plan.kept[lane][s + 1]
        return start

    def rs_copy(m, parity, lane, stage):
        begin, _, order = plan.lanes[lane]
        bit = order[stage]
        size = plan.kept[lane][stage + 1]
        at = begin + offset(lane, stage)
        if plan.halves[lane][stage]:
            at = at + (1 - bit_of(bit)) * size
        starts, _ = plan.slot_rows[stage]
        return to_partner(
            keep_rows.at[m, pl.ds(pl.multiple_of(at, 8), size)],
            stage_in[stage].at[parity, starts[lane] : starts[lane] + size],
            rs_send.at[stage, parity, lane],
            rs_recv.at[stage, parity, lane],
            bit,
        )

    def rs_add(m, parity, lane, stage):
        begin, _, _ = plan.lanes[lane]
        size = plan.kept[lane][stage + 1]
        at = begin + offset(lane, stage + 1)
        starts, _ = plan.slot_rows[stage]
        step = min(size, 2 * chunk)

        def body(i, carry):
            r = pl.multiple_of(at + i * step, 8)
            keep_rows[m, pl.ds(r, step), :] = (
                keep_rows[m, pl.ds(r, step), :]
                + stage_in[stage][parity, pl.ds(pl.multiple_of(starts[lane] + i * step, 8), step), :]
            )
            return carry

        lax.fori_loop(0, size // step, body, 0)

    half_way = matrices // 2
    xs_rows = xs.reshape(layers + 1, clips * (frames + 2 * pad), width)

    def rows_of(m, owner, own, lane, at, size):
        span = pl.ds(pl.multiple_of(plan.lanes[lane][0] + at, 8), size)
        if own:
            return keep_rows.at[m, span]
        return xs_rows.at[layers - m, span] if owner == 1 else keep_rows.at[m - half_way, span]

    def deliver_copy(m, owner, lane):
        size = plan.kept[lane][bits]
        at = offset(lane, bits)
        return to_core(
            rows_of(m, owner, True, lane, at, size),
            rows_of(m, owner, False, lane, at, size),
            deliver_send.at[m % half_way, lane],
            deliver_recv.at[m % half_way, lane],
        )

    def ag_copy(m, owner, own, parity, lane, stage):
        size = plan.kept[lane][stage + 1]
        place = rows_of(m, owner, own, lane, offset(lane, stage + 1), size)
        return to_partner(
            place,
            place,
            ag_send.at[stage, parity, own, lane],
            ag_recv.at[stage, parity, own, lane],
            plan.lanes[lane][2][stage],
        )

    def out_copies(m, kind, local, owner):
        copies = []
        third = rows // 3
        for own in range(2):
            half = owner if own else 1 - owner
            if own:
                source = keep_rows.at[m]
            else:
                source = xs_rows.at[layers - m] if owner == 1 else keep_rows.at[m - half_way]
            sem = out_sem.at[m % half_way, own]
            if kind == 0:
                copies.append(pltpu.make_async_copy(source.at[0:rows], down_out.at[local, half], sem.at[0]))
                continue
            for part in range(3):
                columns = slice(part * width, (part + 1) * width)
                copies.append(
                    pltpu.make_async_copy(
                        source.at[part * third : (part + 1) * third],
                        up_out.at[local, half, :, columns],
                        sem.at[part],
                    )
                )
        return copies

    def owner_of(m):
        return 1 - m // half_way

    def owned_by(owner, m):
        return m < half_way if owner == 1 else m >= half_way

    def tick(pair, phase):
        for s in range(2 * bits + 3, 0, -1):
            m = 2 * pair + phase + 1 - s
            parity = (phase + 1 - s) % 2
            kind = parity
            local = (layers - 1 - (m - kind) // 2) % per_core
            valid = (m >= 0) & (m < matrices)

            if s <= bits + 1:

                @pl.when(valid)
                def _(s=s, m=m, parity=parity):
                    if s == 1:
                        core_copy(m, parity).wait()

                        def body(clip, carry):
                            keep[m, clip] = keep[m, clip] + income[parity, clip]
                            return carry

                        lax.fori_loop(0, clips, body, 0)
                    else:
                        for lane in range(lane_count):
                            rs_copy(m, parity, lane, s - 2).wait()
                            if plan.halves[lane][s - 2]:
                                @pl.when(owner_of(m) == core)
                                def _(lane=lane):
                                    pl.semaphore_signal(
                                        credit.at[s - 2, lane],
                                        inc=1,
                                        device_id={"batch": partner(plan.lanes[lane][2][s - 2])},
                                        device_id_type=mesh_id,
                                    )

                            rs_add(m, parity, lane, s - 2)
                    if s <= bits:
                        for lane in range(lane_count):
                            rs_copy(m, parity, lane, s - 1).start()

            for owner in range(2):
                if s == bits + 1:

                    @pl.when(valid & owned_by(owner, m) & (core == 1 - owner))
                    def _(m=m, owner=owner):
                        for lane in range(lane_count):
                            deliver_copy(m, owner, lane).start()

                if s > bits + 1:

                    @pl.when(valid & owned_by(owner, m) & (core == owner))
                    def _(s=s, m=m, parity=parity, kind=kind, local=local, owner=owner):
                        if s == bits + 2:
                            for lane in range(lane_count):
                                deliver_copy(m, owner, lane).wait_recv()
                        elif s <= 2 * bits + 2:
                            stage = 2 * bits + 2 - s
                            for lane in range(lane_count):
                                if plan.halves[lane][stage]:
                                    for own in range(2):
                                        ag_copy(m, owner, own, parity, lane, stage).wait()
                        if s <= 2 * bits + 1:
                            stage = 2 * bits + 1 - s
                            for lane in range(lane_count):
                                if plan.halves[lane][stage]:
                                    pl.semaphore_wait(credit.at[stage, lane], 1)
                                    for own in range(2):
                                        ag_copy(m, owner, own, parity, lane, stage).start()
                        elif s == 2 * bits + 2:
                            for copy in out_copies(m, kind, local, owner):
                                copy.start()
                        else:
                            for copy in out_copies(m, kind, local, owner):
                                copy.wait()

        m = 2 * pair + phase - bits
        for owner in range(2):

            @pl.when((m >= 0) & (m < matrices) & owned_by(owner, m) & (core == 1 - owner))
            def _(m=m, owner=owner):
                for lane in range(lane_count):
                    deliver_copy(m, owner, lane).wait_send()

    def store_block(m, phase, second, block, value):
        for q in range(2):
            piece = value[q * frames : (q + 1) * frames]
            if second == 0:
                outgo[phase, 2 * block + q] = piece
            else:
                keep[m, 2 * block + q] = piece

    def scale_clip(layer, clip):
        gamma = params[layer, gamma_row : gamma_row + 1]
        gamma_sum = bias_sum = jnp.zeros((8, width), f32)
        for j in range(chunks):
            here = g[clip, j * chunk : (j + 1) * chunk, :]
            at = slice(pad + j * chunk, pad + (j + 1) * chunk)
            gamma_sum = gamma_sum + fold(here * (xs[layer + 1, clip, at, :] - xs[layer, clip, at, :]))
            value = (gamma * here).astype(bf16)
            gb[pl.ds(pl.multiple_of(clip * frames + j * chunk, chunk), chunk), :] = value
            bias_sum = bias_sum + fold(value.astype(f32))
        sums[0] += gamma_sum
        sums[1] += bias_sum

    def norm_back(layer, clip):
        scale = chosen_row(layer, clip, scale_row)
        scale_sum = shift_sum = conv_sum = jnp.zeros((8, width), f32)
        for j in range(chunks):
            row = pl.ds(pl.multiple_of(clip * frames + j * chunk, chunk), chunk)
            at = slice(pad + j * chunk, pad + (j + 1) * chunk)
            ga = gc[clip, at, :]
            value = normed[row, :]
            scale_sum = scale_sum + fold(ga * value)
            shift_sum = shift_sum + fold(ga)
            dn = ga * scale
            first = jnp.mean(dn, axis=-1, keepdims=True)
            second = jnp.mean(dn * value, axis=-1, keepdims=True)
            result = inv_std[row, :] * (dn - first - value * second)
            gc[clip, at, :] = result
            conv_sum = conv_sum + fold(result)
        sums[9] += conv_sum
        choice = onehot[clip]
        small[layer, scale_row : scale_row + 4, :] += choice * jnp.sum(scale_sum, axis=0, keepdims=True)
        small[layer, shift_row : shift_row + 4, :] += choice * jnp.sum(shift_sum, axis=0, keepdims=True)

    def conv_back(layer, clip):
        table = params[layer]
        totals = [jnp.zeros((8, width), f32) for _ in range(7)]
        for j in range(chunks):
            around = slice(j * chunk, (j + 1) * chunk + 2 * pad)
            signal = xs[layer, clip, around, :]
            grads = gc[clip, around, :]
            here = grads[pad : pad + chunk]
            at = slice(j * chunk, (j + 1) * chunk)
            total = g[clip, at, :] + here * table[3:4]
            totals[3] = totals[3] + fold(signal[pad : pad + chunk] * here)
            for k in (0, 1, 2, 4, 5, 6):
                total = total + grads[pad + 3 - k : pad + 3 - k + chunk] * table[k : k + 1]
                totals[k] = totals[k] + fold(signal[pad - 3 + k : pad - 3 + k + chunk] * here)
            g[clip, at, :] = total
        for k in range(7):
            sums[2 + k] += totals[k]

    def backward(pair, carry):
        layer = layers - 1 - pair
        slot = layer % 2

        @pl.when((pair == 1) & (core == 0))
        def _():
            result_remote.wait_send()

        @pl.when((pair == 1) & (core == 1))
        def _():
            result_local.wait()

        sums[...] = jnp.zeros(sums.shape, f32)
        small[layer] = jnp.zeros(small.shape[1:], f32)

        def scale_body(clip, carry):
            scale_clip(layer, clip)
            return carry

        lax.fori_loop(0, clips, scale_body, 0)

        @pl.when(layer < 2)
        def _():
            for which in range(2):
                saved_copy(layer, which, True).wait()

        for second in range(2):
            half = other if second == 0 else core

            def down_body(block, carry, second=second, half=half):
                at = pl.ds(pl.multiple_of(half * rows + block * tile, tile), tile)
                store_block(2 * pair, 0, second, block, dot_rows(hidden[slot, :, at], gb[...]))
                norm_clip(layer, block + 3 * second, True)
                return carry

            lax.fori_loop(0, clips // 2, down_body, 0)
            if second == 0:
                core_copy(2 * pair, 0).start()

        def up_grad(block, carry):
            columns = pl.ds(pl.multiple_of(block * tile, tile), tile)
            value = dot_cols(gb[...], wdn[layer, columns, :])
            total = jnp.zeros((8, tile), f32)
            for q in range(rows // chunk):
                at = slice(q * chunk, (q + 1) * chunk)
                piece = (value[at] * slope[slot, at, columns].astype(f32)).astype(bf16)
                slope[slot, at, columns] = piece
                total = total + fold(piece.astype(f32))
            up_sums[block] = total
            return carry

        lax.fori_loop(0, blocks, up_grad, 0)
        tick(pair, 0)

        for second in range(2):
            half = other if second == 0 else core
            at = pl.ds(pl.multiple_of(half * (width // 2), width // 2), width // 2)

            def up_body(block, carry, second=second, at=at):
                columns = pl.ds(pl.multiple_of(block * width, width), width)
                store_block(2 * pair + 1, 1, second, block, dot_rows(adapted[:, at], slope[slot, :, columns]))
                return carry

            lax.fori_loop(0, clips // 2, up_body, 0)
            if second == 0:
                core_copy(2 * pair + 1, 1).start()

        for block in range(width // tile):
            columns = slice(block * tile, (block + 1) * tile)
            value = dot_cols(slope[slot], wup[layer, columns, :])
            for clip in range(clips):
                gc[clip, pad : pad + frames, columns] = value[clip * frames : (clip + 1) * frames]

        tick(pair, 1)

        def norm_conv_back(clip, carry):
            norm_back(layer, clip)
            conv_back(layer, clip)
            return carry

        lax.fori_loop(0, clips, norm_conv_back, 0)

        @pl.when(layer >= 2)
        def _():
            for which in range(2):
                saved_copy(layer, which, True).start()

        gamma = params[layer, gamma_row : gamma_row + 1, :]
        small[layer, gamma_row : gamma_row + 1, :] = jnp.sum(sums[0], axis=0, keepdims=True) / gamma
        small[layer, down_bias_row : down_bias_row + 1, :] = jnp.sum(sums[1], axis=0, keepdims=True)
        for block in range(blocks):
            row = up_bias_row + block // 2
            place = (block % 2) * tile
            small[layer, row : row + 1, place : place + tile] = jnp.sum(up_sums[block], axis=0, keepdims=True)
        for k in range(7):
            small[layer, taps_row + k : taps_row + k + 1, :] = jnp.sum(sums[2 + k], axis=0, keepdims=True)
        small[layer, conv_bias_row : conv_bias_row + 1, :] = jnp.sum(sums[9], axis=0, keepdims=True)
        return carry

    lax.fori_loop(0, layers, backward, 0)

    grad_remote = to_core(g, ends.at[0, :, 1], ends_send.at[2], ends_recv.at[1])
    grad_local = pltpu.make_async_copy(g, ends.at[0, :, 0], ends_send.at[3])

    @pl.when(core == 0)
    def _():
        grad_local.start()

    @pl.when(core == 1)
    def _():
        grad_remote.start()

    small_core = to_core(
        small.at[pl.ds(per_core * other, per_core)], small_in.at[bits], small_send.at[bits], small_recv.at[bits]
    )
    small_core.start()

    def small_copy(bit):
        return to_partner(small_sum, small_in.at[bit], small_send.at[bit], small_recv.at[bit], bit)

    def drain(pair, carry):
        for phase in range(2):
            tick(pair, phase)
            for step in range(bits + 1):

                @pl.when(2 * pair + phase - matrices == step)
                def _(step=step):
                    if step == 0:
                        small_core.wait()
                        small_sum[...] = small[pl.ds(per_core * core, per_core)] + small_in[bits]
                    else:
                        small_copy(step - 1).wait()
                        small_sum[...] = small_sum[...] + small_in[step - 1]
                    if step < bits:
                        small_copy(step).start()

        return carry

    lax.fori_loop(layers, layers + bits + 1, drain, 0)
    small_out[...] = small_sum[...]

    @pl.when(core == 0)
    def _():
        grad_local.wait()
        grad_remote.wait_recv()

    @pl.when(core == 1)
    def _():
        result_remote.wait_recv()
        grad_remote.wait_send()


def results_kernel(
    ends,
    up_grad,
    down_grad,
    small,
    ends_out,
    conv_kernel_out,
    conv_bias_out,
    band_scale_out,
    band_shift_out,
    up_out,
    up_bias_out,
    down_out,
    down_bias_out,
    layer_scale_out,
    ends_stage,
    up_stage,
    down_stage,
    in_sem,
    out_sem,
):
    copies = []
    per_core, _, width = small.shape
    for clip in range(ends.shape[1]):
        copies.append((ends.at[0, clip], ends_stage.at[clip], ends_out.at[0, clip]))
    for j in range(per_core):
        for half in range(2):
            copies.append((up_grad.at[j, half], up_stage.at[j, half], up_out.at[j, half]))
            copies.append((down_grad.at[j, half], down_stage.at[j, half], down_out.at[j, half]))
    loads = [pltpu.make_async_copy(a, b, in_sem.at[i]) for i, (a, b, _) in enumerate(copies)]
    stores = [pltpu.make_async_copy(b, c, out_sem.at[i]) for i, (_, b, c) in enumerate(copies)]
    for load in loads:
        load.start()
    for load, store in zip(loads, stores):
        load.wait()
        store.start()
    for j in range(per_core):
        conv_kernel_out[:, j] = small[j, taps_row : taps_row + 7]
        conv_bias_out[j : j + 1] = small[j, conv_bias_row : conv_bias_row + 1]
        band_scale_out[j] = small[j, scale_row : scale_row + 4]
        band_shift_out[j] = small[j, shift_row : shift_row + 4]
        for q in range(3):
            row = up_bias_row + q
            up_bias_out[j : j + 1, q * width : (q + 1) * width] = small[j, row : row + 1]
        down_bias_out[j : j + 1] = small[j, down_bias_row : down_bias_row + 1]
        layer_scale_out[j : j + 1] = small[j, gamma_row : gamma_row + 1]
    for store in stores:
        store.wait()


def body(
    inputs,
    grad_out,
    band_ids,
    conv_kernel,
    conv_bias,
    band_scale,
    band_shift,
    up_weight,
    up_bias,
    down_weight,
    down_bias,
    layer_scale,
):
    sections = lax.axis_size("section")
    batch = lax.axis_size("batch")
    clips, local_clips, frames, width = inputs.shape
    per_core, _, hidden_width = up_weight.shape
    layers = per_core * sections
    bands = band_scale.shape[1]
    rows = clips * frames
    assert sections == 2 and local_clips == 2 and batch & (batch - 1) == 0
    assert hidden_width == 3 * width and bands == 4 and layers == 4 and rows == 3 * width // 2
    plan = Plan(batch, rows)
    bits = plan.bits
    hbm = pl.BlockSpec(memory_space=pl.ANY)
    vmem = pl.BlockSpec(memory_space=pltpu.VMEM)
    smem = pl.BlockSpec(memory_space=pltpu.SMEM)
    padded = frames + 2 * pad
    dma = pltpu.SemaphoreType.DMA
    lanes = len(plan.lanes)
    tile = 2 * frames
    ends_shape = jax.ShapeDtypeStruct((1, clips, local_clips, frames, width), f32)
    up_shape = jax.ShapeDtypeStruct((per_core, 2, width // 2, hidden_width), f32)
    down_shape = jax.ShapeDtypeStruct((per_core, 2, hidden_width // 2, width), f32)
    small_shape = jax.ShapeDtypeStruct((per_core, packed_rows, width), f32)
    saved_shape = jax.ShapeDtypeStruct((2, 2, rows, hidden_width), bf16)
    conv_kernel = jnp.transpose(conv_kernel, (1, 0, 2))
    ends, up_grad, down_grad, small, _ = pl.pallas_call(
        functools.partial(step_kernel, plan),
        out_shape=[ends_shape, up_shape, down_shape, small_shape, saved_shape],
        in_specs=[hbm, hbm, smem, vmem, vmem, vmem, vmem, hbm, vmem, hbm, vmem, vmem],
        out_specs=[hbm, hbm, hbm, vmem, hbm],
        scratch_shapes=[
            pltpu.VMEM((layers + 1, clips, padded, width), f32),
            pltpu.VMEM((rows, width), f32),
            pltpu.VMEM((rows, 1), f32),
            pltpu.VMEM((rows, width), bf16),
            pltpu.VMEM((2, rows, hidden_width), bf16),
            pltpu.VMEM((2, rows, hidden_width), bf16),
            pltpu.VMEM((rows, width), bf16),
            pltpu.VMEM((clips, frames, width), f32),
            pltpu.VMEM((clips, padded, width), f32),
            pltpu.VMEM((layers, width, hidden_width), bf16),
            pltpu.VMEM((layers, hidden_width, width), bf16),
            pltpu.VMEM((per_core, packed_rows, width), f32),
            pltpu.VMEM((layers, packed_rows, width), f32),
            pltpu.VMEM((layers, hidden_width // tile, 1, tile), f32),
            pltpu.VMEM((rows, tile), f32),
            pltpu.VMEM((rows, tile), f32),
            pltpu.VMEM((clips, bands, width), f32),
            pltpu.VMEM((10, 8, width), f32),
            pltpu.VMEM((hidden_width // tile, 8, tile), f32),
            pltpu.VMEM((layers, packed_rows, width), f32),
            pltpu.VMEM((2 * layers, clips, frames, width), f32),
            pltpu.VMEM((2, clips, frames, width), f32),
            pltpu.VMEM((2, clips, frames, width), f32),
            pltpu.VMEM((per_core, packed_rows, width), f32),
            pltpu.VMEM((bits + 1, per_core, packed_rows, width), f32),
            *[pltpu.VMEM((2, plan.slot_rows[stage][1], width), f32) for stage in range(bits)],
            dma((2 + 2 * clips,)),
            dma((4 * per_core,)),
            dma((4 * per_core,)),
            dma((1,)),
            dma((1,)),
            dma((4,)),
            dma((2,)),
            dma((2,)),
            dma((2,)),
            dma((bits, 2, lanes)),
            dma((bits, 2, lanes)),
            dma((layers, lanes)),
            dma((layers, lanes)),
            dma((bits, 2, 2, lanes)),
            dma((bits, 2, 2, lanes)),
            dma((layers, 2, 3)),
            pltpu.SemaphoreType.REGULAR((bits, lanes)),
            dma((bits + 1,)),
            dma((bits + 1,)),
            dma((2, 2)),
        ],
        compiler_params=pltpu.CompilerParams(
            collective_id=0, has_side_effects=True, vmem_limit_bytes=255 * 2**18
        ),
        cost_estimate=pl.CostEstimate(
            flops=24 * rows * width * hidden_width * 2, bytes_accessed=2**26, transcendentals=2**24
        ),
        name="blocks_step",
    )(
        inputs,
        grad_out,
        jnp.transpose(band_ids),
        conv_kernel,
        conv_bias,
        band_scale,
        band_shift,
        up_weight,
        up_bias,
        down_weight,
        down_bias,
        layer_scale,
    )

    def like(array):
        return jax.ShapeDtypeStruct(array.shape, f32)

    outs = pl.pallas_call(
        results_kernel,
        out_shape=[
            ends_shape,
            like(conv_kernel),
            like(conv_bias),
            like(band_scale),
            like(band_shift),
            up_shape,
            like(up_bias),
            down_shape,
            like(down_bias),
            like(layer_scale),
        ],
        in_specs=[hbm, hbm, hbm, vmem],
        out_specs=[hbm, vmem, vmem, vmem, vmem, hbm, vmem, hbm, vmem, vmem],
        scratch_shapes=[
            pltpu.VMEM(ends_shape.shape[1:], f32),
            pltpu.VMEM(up_shape.shape, f32),
            pltpu.VMEM(down_shape.shape, f32),
            dma((4 * per_core + clips,)),
            dma((4 * per_core + clips,)),
        ],
        compiler_params=pltpu.CompilerParams(vmem_limit_bytes=2**25),
        cost_estimate=pl.CostEstimate(flops=0, bytes_accessed=2**25, transcendentals=0),
        name="results",
    )(ends, up_grad, down_grad, small)
    outs = list(outs)
    outs[1] = jnp.transpose(outs[1], (1, 0, 2))
    outs[5] = outs[5].reshape(up_weight.shape)
    outs[7] = outs[7].reshape(down_weight.shape)
    return tuple(outs)


def solution(mesh):
    in_specs = (
        P(None, "batch", None, None),
        P(None, "batch", None, None),
        P(None, "batch"),
        P("section", None, None),
        P("section", None),
        P("section", None, None),
        P("section", None, None),
        P("section", None, None),
        P("section", None),
        P("section", None, None),
        P("section", None),
        P("section", None),
    )
    out_specs = (
        P("section", None, "batch", None, None),
        P("section", None, None),
        P("section", None),
        P("section", None, None),
        P("section", None, None),
        P("section", None, None),
        P("section", None),
        P("section", None, None),
        P("section", None),
        P("section", None),
    )
    return jax.shard_map(body, mesh=mesh, in_specs=in_specs, out_specs=out_specs, check_vma=False)
```

```python
import functools

import jax
import jax.numpy as jnp
from jax import lax
from jax.experimental import pallas as pl
from jax.experimental.pallas import tpu as pltpu
from jax.sharding import PartitionSpec as P

norm_epsilon = 1e-06
f32 = jnp.float32
bf16 = jnp.bfloat16

knee = 1.0 / 0.325
tail = tuple(
    value * knee**power
    for power, value in enumerate((0.0023193, 0.10197519, 0.25681865, -0.17643491, 0.43540795, -0.12008618))
)

taps_row, conv_bias_row, scale_row, shift_row, up_bias_row, down_bias_row, gamma_row = 0, 7, 8, 12, 16, 19, 20
packed_rows = 24
pad = 8
chunk = 32


def gelu_and_slope(u):
    size = jnp.abs(u)
    exponential = jnp.exp2(u * (u * (-0.5 * 1.4426950408889634)))
    base = size + knee
    t = pl.reciprocal(base, approx=True)
    t = t * (2.0 - base * t)
    poly = tail[5] * t + tail[4]
    for k in range(3, -1, -1):
        poly = poly * t + tail[k]
    smooth = jnp.maximum(u, 0.0) - size * (exponential * poly)
    below = exponential * (poly - 0.3989422804014327 * size)
    return smooth, jnp.where(u < 0.0, below, 1.0 - below)


def fold(values):
    rows, columns = values.shape
    return jnp.sum(values.reshape(rows // 8, 8, columns), axis=0)


def dot_rows(left, right):
    return lax.dot_general(left, right, (((0,), (0,)), ((), ())), preferred_element_type=f32)


def dot_plain(left, right):
    return lax.dot_general(left, right, (((1,), (0,)), ((), ())), preferred_element_type=f32)


def dot_cols(left, right):
    return lax.dot_general(left, right, (((1,), (1,)), ((), ())), preferred_element_type=f32)


class Plan:
    def __init__(self, batch, rows):
        self.bits = batch.bit_length() - 1
        order = [(bit, bit) for bit in range(self.bits)]
        if self.bits > 1:
            order[:2] = [(0, 1), (1, 0)]
        late = order[:]
        if self.bits > 2:
            late = [order[2]] + order[:2] + order[3:]
        third = rows // 3
        self.lanes = [(0, 2 * third, order), (2 * third, third, late)]
        self.kept = []
        self.halves = []
        self.slot_rows = []
        for _, size, _ in self.lanes:
            kept, halves = [size], []
            for _ in range(self.bits):
                halves.append(kept[-1] // 2 >= 8)
                kept.append(kept[-1] // 2 if halves[-1] else kept[-1])
            self.kept.append(kept)
            self.halves.append(halves)
        for stage in range(self.bits):
            begin, starts = 0, []
            for lane in range(len(self.lanes)):
                starts.append(begin)
                begin += self.kept[lane][stage + 1]
            self.slot_rows.append((starts, begin))


def step_kernel(
    plan,
    inputs,
    grad_out,
    band_ids,
    conv_kernel,
    conv_bias,
    band_scale,
    band_shift,
    up_weight,
    up_bias,
    down_weight,
    down_bias,
    layer_scale,
    ends,
    up_out,
    down_out,
    small_out,
    spill,
    xs,
    normed,
    inv_std,
    adapted,
    hidden,
    slope,
    gb,
    g,
    gc,
    wup,
    wdn,
    packed,
    params,
    up_bias_row_of,
    upper_even,
    upper_odd,
    onehot,
    sums,
    up_sums,
    small,
    keep,
    outgo,
    income,
    small_sum,
    small_in,
    *rest,
):
    stage_in = rest[: plan.bits]
    (
        load_sem,
        wt_send,
        wt_recv,
        par_send,
        par_recv,
        ends_send,
        ends_recv,
        core_send,
        core_recv,
        rs_send,
        rs_recv,
        deliver_send,
        deliver_recv,
        ag_send,
        ag_recv,
        out_sem,
        credit,
        small_send,
        small_recv,
        spill_sem,
    ) = rest[plan.bits :]
    uppers = (upper_even, upper_odd)
    core = lax.axis_index("section")
    other = 1 - core
    batch = lax.axis_index("batch")
    clips, frames, width = g.shape
    rows = clips * frames
    layers = xs.shape[0] - 1
    per_core = layers // 2
    hidden_width = hidden.shape[2]
    tile = 2 * frames
    chunks = frames // chunk
    blocks = hidden_width // tile
    bits = plan.bits
    mesh_id = pl.DeviceIdType.MESH

    def bit_of(bit):
        return (batch // (1 << bit)) % 2

    def partner(bit):
        return batch + (1 - 2 * bit_of(bit)) * (1 << bit)

    def choose(pair, side, value):
        first, second = pair
        if first == second:
            return value(first)
        if isinstance(side, int):
            return value(pair[side])
        return (1 - side) * value(first) + side * value(second)

    def to_core(source, target, send, recv):
        return pltpu.make_async_remote_copy(source, target, send, recv, {"section": other}, mesh_id)

    def to_batch(source, target, send, recv, device):
        return pltpu.make_async_remote_copy(source, target, send, recv, {"batch": device}, mesh_id)

    own_blocks = pl.ds(per_core * core, per_core)
    own_up = pltpu.make_async_copy(up_weight, wup.at[own_blocks], load_sem.at[0])
    own_dn = pltpu.make_async_copy(down_weight, wdn.at[own_blocks], load_sem.at[1])
    own_up.start()
    own_dn.start()
    loads = []
    for source, target in ((inputs, adapted), (grad_out, gb)):
        for clip in range(clips):
            loads.append(
                pltpu.make_async_copy(
                    source.at[clip, core], target.at[pl.ds(clip * frames, frames)], load_sem.at[2 + len(loads)]
                )
            )
    for load in loads:
        load.start()

    for j in range(per_core):
        packed[j, taps_row : taps_row + 7] = conv_kernel[:, j]
        packed[j, conv_bias_row : conv_bias_row + 1] = conv_bias[j : j + 1]
        packed[j, scale_row : scale_row + 4] = band_scale[j]
        packed[j, shift_row : shift_row + 4] = band_shift[j]
        for q in range(3):
            row = up_bias_row + q
            packed[j, row : row + 1] = up_bias[j : j + 1, q * width : (q + 1) * width]
        packed[j, down_bias_row : down_bias_row + 1] = down_bias[j : j + 1]
        packed[j, gamma_row : gamma_row + 1] = layer_scale[j : j + 1]
        packed[j, gamma_row + 1 : packed_rows] = jnp.zeros((packed_rows - gamma_row - 1, width), f32)

    barrier = pltpu.get_barrier_semaphore()
    pl.semaphore_signal(barrier, inc=1, device_id={"section": other}, device_id_type=mesh_id)
    for bit in range(bits):
        pl.semaphore_signal(barrier, inc=1, device_id={"batch": partner(bit)}, device_id_type=mesh_id)
    pl.semaphore_wait(barrier, 1 + bits)

    par_copy = to_core(packed, params.at[own_blocks], par_send.at[0], par_recv.at[0])
    par_copy.start()
    params[own_blocks] = packed[...]

    stages = [
        xs.at[1, :, 0:frames],
        xs.at[2, :, 0:frames],
        xs.at[3, :, 0:frames],
        outgo.at[0],
        outgo.at[1],
        g,
        gc.at[:, 0:frames],
        xs.at[4, :, 0:frames],
    ]

    def weight_part(kind, layer, half, part):
        if kind == 0:
            return wup.at[
                layer,
                pl.ds(pl.multiple_of(half * (width // 2) + (part % 2) * frames, frames), frames),
                pl.ds(pl.multiple_of((part // 2) * width, width), width),
            ]
        return wdn.at[layer, pl.ds(pl.multiple_of(half * rows + part * frames, frames), frames), :]

    def weight_wait(k):
        return to_core(outgo.at[0], keep.at[k], wt_send.at[k], wt_recv.at[k])

    def send_weights(j):
        for kind in range(2):
            for half in range(2):
                k = 4 * j + 2 * kind + half

                def cast(part, carry, kind=kind, half=half, k=k):
                    stages[k][part] = weight_part(kind, per_core * core + j, half, part)[...].astype(f32)
                    return carry

                lax.fori_loop(0, clips, cast, 0)
                to_core(stages[k], keep.at[k], wt_send.at[k], wt_recv.at[k]).start()

    def take_weights(layer, kind):
        @pl.when(layer // per_core != core)
        def _():
            for half in range(2):
                k = 4 * (layer % per_core) + 2 * kind + half
                weight_wait(k).wait_recv()

                def cast(part, carry, half=half, k=k):
                    weight_part(kind, layer, half, part)[...] = keep[k, part].astype(bf16)
                    return carry

                lax.fori_loop(0, clips, cast, 0)

    own_up.wait()
    own_dn.wait()
    for j in range(per_core):
        send_weights(j)

    for load in loads:
        load.wait()

    def load_x(clip, carry):
        xs[0, clip, 0:pad, :] = jnp.zeros((pad, width), f32)
        xs[0, clip, pad + frames : 2 * pad + frames, :] = jnp.zeros((pad, width), f32)
        xs[0, clip, pad : pad + frames, :] = adapted[
            pl.ds(pl.multiple_of(clip * frames, frames), frames), :
        ].astype(f32)
        for band in range(4):
            chosen = jnp.where(band_ids[core, clip] == band, 1.0, 0.0).astype(f32)
            onehot[clip, band : band + 1] = jnp.zeros((1, width), f32) + chosen
        return carry

    lax.fori_loop(0, clips, load_x, 0)
    par_copy.wait()
    for layer in range(layers):
        for block in range(blocks):
            row = up_bias_row + block // 2
            place = (block % 2) * tile
            up_bias_row_of[layer, block] = params[layer, row : row + 1, place : place + tile]

    def chosen_row(layer, clip, first):
        return jnp.sum(onehot[clip] * params[layer, first : first + 4], axis=0, keepdims=True)

    def norm_clip(layer, clip, save):
        table = params[layer]
        scale = chosen_row(layer, clip, scale_row)
        shift = chosen_row(layer, clip, shift_row)
        for j in range(chunks):
            window = xs[layer, clip, j * chunk : (j + 1) * chunk + 2 * pad, :]
            conv = window[pad : pad + chunk] * table[3:4] + table[conv_bias_row : conv_bias_row + 1]
            for k in (0, 1, 2, 4, 5, 6):
                conv = conv + window[pad - 3 + k : pad - 3 + k + chunk] * table[k : k + 1]
            centered = conv - jnp.mean(conv, axis=-1, keepdims=True)
            inv = lax.rsqrt(jnp.mean(centered * centered, axis=-1, keepdims=True) + norm_epsilon)
            value = centered * inv
            at = pl.ds(pl.multiple_of(clip * frames + j * chunk, chunk), chunk)
            if save:
                normed[at, :] = value
                inv_std[at, :] = inv
            adapted[at, :] = (value * scale + shift).astype(bf16)

    def saved_copy(layer, which, back):
        buffer = (hidden if which == 0 else slope).at[layer % 2]
        away = spill.at[layer % 2, which]
        source, target = (away, buffer) if back else (buffer, away)
        return pltpu.make_async_copy(source, target, spill_sem.at[layer % 2, which])

    def forward(layer, carry):
        slot = layer % 2

        def norm_body(clip, carry):
            norm_clip(layer, clip, False)
            return carry

        lax.fori_loop(0, clips, norm_body, 0)
        take_weights(layer, 0)

        @pl.when(layer >= 2)
        def _():
            for which in range(2):
                saved_copy(layer, which, False).wait()

        def up(block):
            columns = slice(block * tile, (block + 1) * tile)
            uppers[block % 2][...] = dot_plain(adapted[...], wup[layer, :, columns])

        def down(block):
            columns = slice(block * tile, (block + 1) * tile)
            value = dot_plain(hidden[slot, :, columns], wdn[layer, columns, :])
            normed[...] = value if block == 0 else normed[...] + value

        downs = {0: (), 1: (), 2: (), 3: (0, 1), 4: (2, 3), 5: (4,)}
        up(0)
        for block in range(blocks):
            columns = slice(block * tile, (block + 1) * tile)
            if block + 1 < blocks:
                up(block + 1)
            if block == blocks // 2:
                take_weights(layer, 1)
            for earlier in downs[block]:
                down(earlier)
            bias = up_bias_row_of[layer, block]
            for q in range(rows // chunk):
                at = slice(q * chunk, (q + 1) * chunk)
                smooth, steep = gelu_and_slope(uppers[block % 2][at, :] + bias)
                hidden[slot, at, columns] = smooth.astype(bf16)
                slope[slot, at, columns] = steep.astype(bf16)
        down(blocks - 1)

        @pl.when(layer < 2)
        def _():
            for which in range(2):
                saved_copy(layer, which, False).start()

        for step in range(layers):

            @pl.when(layer == step)
            def _(step=step):
                for k in [step] if step < layers - 1 else range(layers - 1, 4 * per_core):
                    weight_wait(k).wait_send()

        def residual(clip, carry):
            bias = params[layer, down_bias_row : down_bias_row + 1]
            gamma = params[layer, gamma_row : gamma_row + 1]
            branch = normed[pl.ds(pl.multiple_of(clip * frames, frames), frames), :] + bias
            xs[layer + 1, clip, pad : pad + frames, :] = xs[layer, clip, pad : pad + frames, :] + gamma * branch
            return carry

        lax.fori_loop(0, clips, residual, 0)

        def zero_pads(clip, carry):
            xs[layer + 1, clip, 0:pad, :] = jnp.zeros((pad, width), f32)
            xs[layer + 1, clip, pad + frames : 2 * pad + frames, :] = jnp.zeros((pad, width), f32)
            return carry

        lax.fori_loop(0, clips, zero_pads, 0)
        return carry

    lax.fori_loop(0, layers, forward, 0)

    result = xs.at[layers, :, pad : pad + frames]
    result_remote = to_core(result, ends.at[0, :, 0], ends_send.at[0], ends_recv.at[0])
    result_local = pltpu.make_async_copy(result, ends.at[0, :, 1], ends_send.at[1])

    @pl.when(core == 0)
    def _():
        result_remote.start()

    @pl.when(core == 1)
    def _():
        result_local.start()

    def load_g(clip, carry):
        g[clip] = gb[pl.ds(pl.multiple_of(clip * frames, frames), frames), :].astype(f32)
        gc[clip, 0:pad, :] = jnp.zeros((pad, width), f32)
        gc[clip, pad + frames : 2 * pad + frames, :] = jnp.zeros((pad, width), f32)
        return carry

    lax.fori_loop(0, clips, load_g, 0)

    matrices = 2 * layers
    lane_count = len(plan.lanes)

    def core_copy(m, parity):
        return to_core(outgo.at[parity], income.at[parity], core_send.at[parity], core_recv.at[parity])

    keep_rows = keep.reshape(matrices, rows, width)

    def offset(lane, stage, side):
        start = 0
        for s in range(stage):
            if plan.halves[lane][s]:
                start = start + choose(plan.lanes[lane][2][s], side, bit_of) * plan.kept[lane][s + 1]
        return start

    def rs_copy(m, parity, lane, stage):
        begin, _, order = plan.lanes[lane]
        size = plan.kept[lane][stage + 1]
        at = begin + offset(lane, stage, core)
        if plan.halves[lane][stage]:
            at = at + (1 - choose(order[stage], core, bit_of)) * size
        starts, _ = plan.slot_rows[stage]
        return to_batch(
            keep_rows.at[m, pl.ds(pl.multiple_of(at, 8), size)],
            stage_in[stage].at[parity, starts[lane] : starts[lane] + size],
            rs_send.at[stage, parity, lane],
            rs_recv.at[stage, parity, lane],
            choose(order[stage], core, partner),
        )

    def rs_add(m, parity, lane, stage):
        begin, _, _ = plan.lanes[lane]
        size = plan.kept[lane][stage + 1]
        at = begin + offset(lane, stage + 1, core)
        starts, _ = plan.slot_rows[stage]
        step = min(size, 2 * chunk)

        def body(i, carry):
            r = pl.multiple_of(at + i * step, 8)
            keep_rows[m, pl.ds(r, step), :] = (
                keep_rows[m, pl.ds(r, step), :]
                + stage_in[stage][parity, pl.ds(pl.multiple_of(starts[lane] + i * step, 8), step), :]
            )
            return carry

        lax.fori_loop(0, size // step, body, 0)

    half_way = matrices // 2
    xs_rows = xs.reshape(layers + 1, clips * (frames + 2 * pad), width)

    def rows_of(m, owner, own, lane, at, size):
        span = pl.ds(pl.multiple_of(plan.lanes[lane][0] + at, 8), size)
        if own:
            return keep_rows.at[m, span]
        return xs_rows.at[layers - m, span] if owner == 1 else keep_rows.at[m - half_way, span]

    def deliver_copy(m, owner, lane):
        size = plan.kept[lane][bits]
        at = offset(lane, bits, 1 - owner)
        return to_core(
            rows_of(m, owner, True, lane, at, size),
            rows_of(m, owner, False, lane, at, size),
            deliver_send.at[m % half_way, lane],
            deliver_recv.at[m % half_way, lane],
        )

    def ag_copy(m, owner, own, parity, lane, stage):
        size = plan.kept[lane][stage + 1]
        side = owner if own else 1 - owner
        place = rows_of(m, owner, own, lane, offset(lane, stage + 1, side), size)
        return to_batch(
            place,
            place,
            ag_send.at[stage, parity, own, lane],
            ag_recv.at[stage, parity, own, lane],
            choose(plan.lanes[lane][2][stage], side, partner),
        )

    def out_copies(m, kind, local, owner):
        copies = []
        third = rows // 3
        for own in range(2):
            half = owner if own else 1 - owner
            if own:
                source = keep_rows.at[m]
            else:
                source = xs_rows.at[layers - m] if owner == 1 else keep_rows.at[m - half_way]
            sem = out_sem.at[m % half_way, own]
            if kind == 0:
                copies.append(pltpu.make_async_copy(source.at[0:rows], down_out.at[local, half], sem.at[0]))
                continue
            for part in range(3):
                columns = slice(part * width, (part + 1) * width)
                copies.append(
                    pltpu.make_async_copy(
                        source.at[part * third : (part + 1) * third],
                        up_out.at[local, half, :, columns],
                        sem.at[part],
                    )
                )
        return copies

    def owner_of(m):
        return 1 - m // half_way

    def owned_by(owner, m):
        return m < half_way if owner == 1 else m >= half_way

    def tick(pair, phase):
        for s in range(2 * bits + 3, 0, -1):
            m = 2 * pair + phase + 1 - s
            parity = (phase + 1 - s) % 2
            kind = parity
            local = (layers - 1 - (m - kind) // 2) % per_core
            valid = (m >= 0) & (m < matrices)

            if s <= bits + 1:

                @pl.when(valid)
                def _(s=s, m=m, parity=parity):
                    if s == 1:
                        core_copy(m, parity).wait()

                        def body(clip, carry):
                            keep[m, clip] = keep[m, clip] + income[parity, clip]
                            return carry

                        lax.fori_loop(0, clips, body, 0)
                    else:
                        for lane in range(lane_count):
                            rs_copy(m, parity, lane, s - 2).wait()
                            if plan.halves[lane][s - 2]:
                                @pl.when(owner_of(m) == core)
                                def _(lane=lane):
                                    pl.semaphore_signal(
                                        credit.at[s - 2, lane],
                                        inc=1,
                                        device_id={"batch": choose(plan.lanes[lane][2][s - 2], core, partner)},
                                        device_id_type=mesh_id,
                                    )

                            rs_add(m, parity, lane, s - 2)
                    if s <= bits:
                        for lane in range(lane_count):
                            rs_copy(m, parity, lane, s - 1).start()

            for owner in range(2):
                if s == bits + 1:

                    @pl.when(valid & owned_by(owner, m) & (core == 1 - owner))
                    def _(m=m, owner=owner):
                        for lane in range(lane_count):
                            deliver_copy(m, owner, lane).start()

                if s > bits + 1:

                    @pl.when(valid & owned_by(owner, m) & (core == owner))
                    def _(s=s, m=m, parity=parity, kind=kind, local=local, owner=owner):
                        if s == bits + 2:
                            for lane in range(lane_count):
                                deliver_copy(m, owner, lane).wait_recv()
                        elif s <= 2 * bits + 2:
                            stage = 2 * bits + 2 - s
                            for lane in range(lane_count):
                                if plan.halves[lane][stage]:
                                    for own in range(2):
                                        ag_copy(m, owner, own, parity, lane, stage).wait()
                        if s <= 2 * bits + 1:
                            stage = 2 * bits + 1 - s
                            for lane in range(lane_count):
                                if plan.halves[lane][stage]:
                                    pl.semaphore_wait(credit.at[stage, lane], 1)
                                    for own in range(2):
                                        ag_copy(m, owner, own, parity, lane, stage).start()
                        elif s == 2 * bits + 2:
                            for copy in out_copies(m, kind, local, owner):
                                copy.start()
                        else:
                            for copy in out_copies(m, kind, local, owner):
                                copy.wait()

        m = 2 * pair + phase - bits
        for owner in range(2):

            @pl.when((m >= 0) & (m < matrices) & owned_by(owner, m) & (core == 1 - owner))
            def _(m=m, owner=owner):
                for lane in range(lane_count):
                    deliver_copy(m, owner, lane).wait_send()

    def store_block(m, phase, second, block, value):
        for q in range(2):
            piece = value[q * frames : (q + 1) * frames]
            if second == 0:
                outgo[phase, 2 * block + q] = piece
            else:
                keep[m, 2 * block + q] = piece

    def scale_clip(layer, clip):
        gamma = params[layer, gamma_row : gamma_row + 1]
        gamma_sum = bias_sum = jnp.zeros((8, width), f32)
        for j in range(chunks):
            here = g[clip, j * chunk : (j + 1) * chunk, :]
            at = slice(pad + j * chunk, pad + (j + 1) * chunk)
            gamma_sum = gamma_sum + fold(here * (xs[layer + 1, clip, at, :] - xs[layer, clip, at, :]))
            value = (gamma * here).astype(bf16)
            gb[pl.ds(pl.multiple_of(clip * frames + j * chunk, chunk), chunk), :] = value
            bias_sum = bias_sum + fold(value.astype(f32))
        sums[0] += gamma_sum
        sums[1] += bias_sum

    def norm_back(layer, clip):
        scale = chosen_row(layer, clip, scale_row)
        scale_sum = shift_sum = conv_sum = jnp.zeros((8, width), f32)
        for j in range(chunks):
            row = pl.ds(pl.multiple_of(clip * frames + j * chunk, chunk), chunk)
            at = slice(pad + j * chunk, pad + (j + 1) * chunk)
            ga = gc[clip, at, :]
            value = normed[row, :]
            scale_sum = scale_sum + fold(ga * value)
            shift_sum = shift_sum + fold(ga)
            dn = ga * scale
            first = jnp.mean(dn, axis=-1, keepdims=True)
            second = jnp.mean(dn * value, axis=-1, keepdims=True)
            result = inv_std[row, :] * (dn - first - value * second)
            gc[clip, at, :] = result
            conv_sum = conv_sum + fold(result)
        sums[9] += conv_sum
        choice = onehot[clip]
        small[layer, scale_row : scale_row + 4, :] += choice * jnp.sum(scale_sum, axis=0, keepdims=True)
        small[layer, shift_row : shift_row + 4, :] += choice * jnp.sum(shift_sum, axis=0, keepdims=True)

    def conv_back(layer, clip):
        table = params[layer]
        totals = [jnp.zeros((8, width), f32) for _ in range(7)]
        for j in range(chunks):
            around = slice(j * chunk, (j + 1) * chunk + 2 * pad)
            signal = xs[layer, clip, around, :]
            grads = gc[clip, around, :]
            here = grads[pad : pad + chunk]
            at = slice(j * chunk, (j + 1) * chunk)
            total = g[clip, at, :] + here * table[3:4]
            totals[3] = totals[3] + fold(signal[pad : pad + chunk] * here)
            for k in (0, 1, 2, 4, 5, 6):
                total = total + grads[pad + 3 - k : pad + 3 - k + chunk] * table[k : k + 1]
                totals[k] = totals[k] + fold(signal[pad - 3 + k : pad - 3 + k + chunk] * here)
            g[clip, at, :] = total
        for k in range(7):
            sums[2 + k] += totals[k]

    def backward(pair, carry):
        layer = layers - 1 - pair
        slot = layer % 2

        @pl.when((pair == 1) & (core == 0))
        def _():
            result_remote.wait_send()

        @pl.when((pair == 1) & (core == 1))
        def _():
            result_local.wait()

        sums[...] = jnp.zeros(sums.shape, f32)
        small[layer] = jnp.zeros(small.shape[1:], f32)

        def scale_body(clip, carry):
            scale_clip(layer, clip)
            return carry

        lax.fori_loop(0, clips, scale_body, 0)

        @pl.when(layer < 2)
        def _():
            for which in range(2):
                saved_copy(layer, which, True).wait()

        for second in range(2):
            half = other if second == 0 else core

            def down_body(block, carry, second=second, half=half):
                at = pl.ds(pl.multiple_of(half * rows + block * tile, tile), tile)
                store_block(2 * pair, 0, second, block, dot_rows(hidden[slot, :, at], gb[...]))
                norm_clip(layer, block + 3 * second, True)
                return carry

            lax.fori_loop(0, clips // 2, down_body, 0)
            if second == 0:
                core_copy(2 * pair, 0).start()

        def up_grad(block, carry):
            columns = pl.ds(pl.multiple_of(block * tile, tile), tile)
            value = dot_cols(gb[...], wdn[layer, columns, :])
            total = jnp.zeros((8, tile), f32)
            for q in range(rows // chunk):
                at = slice(q * chunk, (q + 1) * chunk)
                piece = (value[at] * slope[slot, at, columns].astype(f32)).astype(bf16)
                slope[slot, at, columns] = piece
                total = total + fold(piece.astype(f32))
            up_sums[block] = total
            return carry

        lax.fori_loop(0, blocks, up_grad, 0)
        tick(pair, 0)

        for second in range(2):
            half = other if second == 0 else core
            at = pl.ds(pl.multiple_of(half * (width // 2), width // 2), width // 2)

            def up_body(block, carry, second=second, at=at):
                columns = pl.ds(pl.multiple_of(block * width, width), width)
                store_block(2 * pair + 1, 1, second, block, dot_rows(adapted[:, at], slope[slot, :, columns]))
                return carry

            lax.fori_loop(0, clips // 2, up_body, 0)
            if second == 0:
                core_copy(2 * pair + 1, 1).start()

        for block in range(width // tile):
            columns = slice(block * tile, (block + 1) * tile)
            value = dot_cols(slope[slot], wup[layer, columns, :])
            for clip in range(clips):
                gc[clip, pad : pad + frames, columns] = value[clip * frames : (clip + 1) * frames]

        tick(pair, 1)

        def norm_conv_back(clip, carry):
            norm_back(layer, clip)
            conv_back(layer, clip)
            return carry

        lax.fori_loop(0, clips, norm_conv_back, 0)

        @pl.when(layer >= 2)
        def _():
            for which in range(2):
                saved_copy(layer, which, True).start()

        gamma = params[layer, gamma_row : gamma_row + 1, :]
        small[layer, gamma_row : gamma_row + 1, :] = jnp.sum(sums[0], axis=0, keepdims=True) / gamma
        small[layer, down_bias_row : down_bias_row + 1, :] = jnp.sum(sums[1], axis=0, keepdims=True)
        for block in range(blocks):
            row = up_bias_row + block // 2
            place = (block % 2) * tile
            small[layer, row : row + 1, place : place + tile] = jnp.sum(up_sums[block], axis=0, keepdims=True)
        for k in range(7):
            small[layer, taps_row + k : taps_row + k + 1, :] = jnp.sum(sums[2 + k], axis=0, keepdims=True)
        small[layer, conv_bias_row : conv_bias_row + 1, :] = jnp.sum(sums[9], axis=0, keepdims=True)
        return carry

    lax.fori_loop(0, layers, backward, 0)

    grad_remote = to_core(g, ends.at[0, :, 1], ends_send.at[2], ends_recv.at[1])
    grad_local = pltpu.make_async_copy(g, ends.at[0, :, 0], ends_send.at[3])

    @pl.when(core == 0)
    def _():
        grad_local.start()

    @pl.when(core == 1)
    def _():
        grad_remote.start()

    small_core = to_core(
        small.at[pl.ds(per_core * other, per_core)], small_in.at[bits], small_send.at[bits], small_recv.at[bits]
    )
    small_core.start()

    def small_copy(bit):
        return to_batch(small_sum, small_in.at[bit], small_send.at[bit], small_recv.at[bit], partner(bit))

    def drain(pair, carry):
        for phase in range(2):
            tick(pair, phase)
            for step in range(bits + 1):

                @pl.when(2 * pair + phase - matrices == step)
                def _(step=step):
                    if step == 0:
                        small_core.wait()
                        small_sum[...] = small[pl.ds(per_core * core, per_core)] + small_in[bits]
                    else:
                        small_copy(step - 1).wait()
                        small_sum[...] = small_sum[...] + small_in[step - 1]
                    if step < bits:
                        small_copy(step).start()

        return carry

    lax.fori_loop(layers, layers + bits + 1, drain, 0)
    small_out[...] = small_sum[...]

    @pl.when(core == 0)
    def _():
        grad_local.wait()
        grad_remote.wait_recv()

    @pl.when(core == 1)
    def _():
        result_remote.wait_recv()
        grad_remote.wait_send()


def results_kernel(
    ends,
    up_grad,
    down_grad,
    small,
    ends_out,
    conv_kernel_out,
    conv_bias_out,
    band_scale_out,
    band_shift_out,
    up_out,
    up_bias_out,
    down_out,
    down_bias_out,
    layer_scale_out,
    ends_stage,
    up_stage,
    down_stage,
    in_sem,
    out_sem,
):
    copies = []
    per_core, _, width = small.shape
    for clip in range(ends.shape[1]):
        copies.append((ends.at[0, clip], ends_stage.at[clip], ends_out.at[0, clip]))
    for j in range(per_core):
        for half in range(2):
            copies.append((up_grad.at[j, half], up_stage.at[j, half], up_out.at[j, half]))
            copies.append((down_grad.at[j, half], down_stage.at[j, half], down_out.at[j, half]))
    loads = [pltpu.make_async_copy(a, b, in_sem.at[i]) for i, (a, b, _) in enumerate(copies)]
    stores = [pltpu.make_async_copy(b, c, out_sem.at[i]) for i, (_, b, c) in enumerate(copies)]
    for load in loads:
        load.start()
    for load, store in zip(loads, stores):
        load.wait()
        store.start()
    for j in range(per_core):
        conv_kernel_out[:, j] = small[j, taps_row : taps_row + 7]
        conv_bias_out[j : j + 1] = small[j, conv_bias_row : conv_bias_row + 1]
        band_scale_out[j] = small[j, scale_row : scale_row + 4]
        band_shift_out[j] = small[j, shift_row : shift_row + 4]
        for q in range(3):
            row = up_bias_row + q
            up_bias_out[j : j + 1, q * width : (q + 1) * width] = small[j, row : row + 1]
        down_bias_out[j : j + 1] = small[j, down_bias_row : down_bias_row + 1]
        layer_scale_out[j : j + 1] = small[j, gamma_row : gamma_row + 1]
    for store in stores:
        store.wait()


def body(
    inputs,
    grad_out,
    band_ids,
    conv_kernel,
    conv_bias,
    band_scale,
    band_shift,
    up_weight,
    up_bias,
    down_weight,
    down_bias,
    layer_scale,
):
    sections = lax.axis_size("section")
    batch = lax.axis_size("batch")
    clips, local_clips, frames, width = inputs.shape
    per_core, _, hidden_width = up_weight.shape
    layers = per_core * sections
    bands = band_scale.shape[1]
    rows = clips * frames
    assert sections == 2 and local_clips == 2 and batch & (batch - 1) == 0
    assert hidden_width == 3 * width and bands == 4 and layers == 4 and rows == 3 * width // 2
    plan = Plan(batch, rows)
    bits = plan.bits
    hbm = pl.BlockSpec(memory_space=pl.ANY)
    vmem = pl.BlockSpec(memory_space=pltpu.VMEM)
    smem = pl.BlockSpec(memory_space=pltpu.SMEM)
    padded = frames + 2 * pad
    dma = pltpu.SemaphoreType.DMA
    lanes = len(plan.lanes)
    tile = 2 * frames
    ends_shape = jax.ShapeDtypeStruct((1, clips, local_clips, frames, width), f32)
    up_shape = jax.ShapeDtypeStruct((per_core, 2, width // 2, hidden_width), f32)
    down_shape = jax.ShapeDtypeStruct((per_core, 2, hidden_width // 2, width), f32)
    small_shape = jax.ShapeDtypeStruct((per_core, packed_rows, width), f32)
    saved_shape = jax.ShapeDtypeStruct((2, 2, rows, hidden_width), bf16)
    conv_kernel = jnp.transpose(conv_kernel, (1, 0, 2))
    ends, up_grad, down_grad, small, _ = pl.pallas_call(
        functools.partial(step_kernel, plan),
        out_shape=[ends_shape, up_shape, down_shape, small_shape, saved_shape],
        in_specs=[hbm, hbm, smem, vmem, vmem, vmem, vmem, hbm, vmem, hbm, vmem, vmem],
        out_specs=[hbm, hbm, hbm, vmem, hbm],
        scratch_shapes=[
            pltpu.VMEM((layers + 1, clips, padded, width), f32),
            pltpu.VMEM((rows, width), f32),
            pltpu.VMEM((rows, 1), f32),
            pltpu.VMEM((rows, width), bf16),
            pltpu.VMEM((2, rows, hidden_width), bf16),
            pltpu.VMEM((2, rows, hidden_width), bf16),
            pltpu.VMEM((rows, width), bf16),
            pltpu.VMEM((clips, frames, width), f32),
            pltpu.VMEM((clips, padded, width), f32),
            pltpu.VMEM((layers, width, hidden_width), bf16),
            pltpu.VMEM((layers, hidden_width, width), bf16),
            pltpu.VMEM((per_core, packed_rows, width), f32),
            pltpu.VMEM((layers, packed_rows, width), f32),
            pltpu.VMEM((layers, hidden_width // tile, 1, tile), f32),
            pltpu.VMEM((rows, tile), f32),
            pltpu.VMEM((rows, tile), f32),
            pltpu.VMEM((clips, bands, width), f32),
            pltpu.VMEM((10, 8, width), f32),
            pltpu.VMEM((hidden_width // tile, 8, tile), f32),
            pltpu.VMEM((layers, packed_rows, width), f32),
            pltpu.VMEM((2 * layers, clips, frames, width), f32),
            pltpu.VMEM((2, clips, frames, width), f32),
            pltpu.VMEM((2, clips, frames, width), f32),
            pltpu.VMEM((per_core, packed_rows, width), f32),
            pltpu.VMEM((bits + 1, per_core, packed_rows, width), f32),
            *[pltpu.VMEM((2, plan.slot_rows[stage][1], width), f32) for stage in range(bits)],
            dma((2 + 2 * clips,)),
            dma((4 * per_core,)),
            dma((4 * per_core,)),
            dma((1,)),
            dma((1,)),
            dma((4,)),
            dma((2,)),
            dma((2,)),
            dma((2,)),
            dma((bits, 2, lanes)),
            dma((bits, 2, lanes)),
            dma((layers, lanes)),
            dma((layers, lanes)),
            dma((bits, 2, 2, lanes)),
            dma((bits, 2, 2, lanes)),
            dma((layers, 2, 3)),
            pltpu.SemaphoreType.REGULAR((bits, lanes)),
            dma((bits + 1,)),
            dma((bits + 1,)),
            dma((2, 2)),
        ],
        compiler_params=pltpu.CompilerParams(
            collective_id=0, has_side_effects=True, vmem_limit_bytes=255 * 2**18
        ),
        cost_estimate=pl.CostEstimate(
            flops=24 * rows * width * hidden_width * 2, bytes_accessed=2**26, transcendentals=2**24
        ),
        name="blocks_step",
    )(
        inputs,
        grad_out,
        jnp.transpose(band_ids),
        conv_kernel,
        conv_bias,
        band_scale,
        band_shift,
        up_weight,
        up_bias,
        down_weight,
        down_bias,
        layer_scale,
    )

    def like(array):
        return jax.ShapeDtypeStruct(array.shape, f32)

    outs = pl.pallas_call(
        results_kernel,
        out_shape=[
            ends_shape,
            like(conv_kernel),
            like(conv_bias),
            like(band_scale),
            like(band_shift),
            up_shape,
            like(up_bias),
            down_shape,
            like(down_bias),
            like(layer_scale),
        ],
        in_specs=[hbm, hbm, hbm, vmem],
        out_specs=[hbm, vmem, vmem, vmem, vmem, hbm, vmem, hbm, vmem, vmem],
        scratch_shapes=[
            pltpu.VMEM(ends_shape.shape[1:], f32),
            pltpu.VMEM(up_shape.shape, f32),
            pltpu.VMEM(down_shape.shape, f32),
            dma((4 * per_core + clips,)),
            dma((4 * per_core + clips,)),
        ],
        compiler_params=pltpu.CompilerParams(vmem_limit_bytes=255 * 2**18),
        cost_estimate=pl.CostEstimate(flops=0, bytes_accessed=2**25, transcendentals=0),
        name="results",
    )(ends, up_grad, down_grad, small)
    outs = list(outs)
    outs[1] = jnp.transpose(outs[1], (1, 0, 2))
    outs[5] = outs[5].reshape(up_weight.shape)
    outs[7] = outs[7].reshape(down_weight.shape)
    return tuple(outs)


def solution(mesh):
    in_specs = (
        P(None, "batch", None, None),
        P(None, "batch", None, None),
        P(None, "batch"),
        P("section", None, None),
        P("section", None),
        P("section", None, None),
        P("section", None, None),
        P("section", None, None),
        P("section", None),
        P("section", None, None),
        P("section", None),
        P("section", None),
    )
    out_specs = (
        P("section", None, "batch", None, None),
        P("section", None, None),
        P("section", None),
        P("section", None, None),
        P("section", None, None),
        P("section", None, None),
        P("section", None),
        P("section", None, None),
        P("section", None),
        P("section", None),
    )
    return jax.shard_map(body, mesh=mesh, in_specs=in_specs, out_specs=out_specs, check_vma=False)
```

```python
import functools

import jax
import jax.numpy as jnp
from jax import lax
from jax.experimental import pallas as pl
from jax.experimental.pallas import tpu as pltpu
from jax.sharding import PartitionSpec as P

norm_epsilon = 1e-06
f32 = jnp.float32
bf16 = jnp.bfloat16

knee = 1.0 / 0.325
tail = tuple(
    value * knee**power
    for power, value in enumerate((0.0023193, 0.10197519, 0.25681865, -0.17643491, 0.43540795, -0.12008618))
)

taps_row, conv_bias_row, scale_row, shift_row, up_bias_row, down_bias_row, gamma_row = 0, 7, 8, 12, 16, 19, 20
packed_rows = 24
pad = 8
chunk = 32


def gelu_and_slope(u):
    size = jnp.abs(u)
    exponential = jnp.exp2(u * (u * (-0.5 * 1.4426950408889634)))
    base = size + knee
    t = pl.reciprocal(base, approx=True)
    t = t * (2.0 - base * t)
    poly = tail[5] * t + tail[4]
    for k in range(3, -1, -1):
        poly = poly * t + tail[k]
    smooth = jnp.maximum(u, 0.0) - size * (exponential * poly)
    below = exponential * (poly - 0.3989422804014327 * size)
    return smooth, jnp.where(u < 0.0, below, 1.0 - below)


def fold(values):
    rows, columns = values.shape
    return jnp.sum(values.reshape(rows // 8, 8, columns), axis=0)


def dot_rows(left, right):
    return lax.dot_general(left, right, (((0,), (0,)), ((), ())), preferred_element_type=f32)


def dot_plain(left, right):
    return lax.dot_general(left, right, (((1,), (0,)), ((), ())), preferred_element_type=f32)


def dot_cols(left, right):
    return lax.dot_general(left, right, (((1,), (1,)), ((), ())), preferred_element_type=f32)


class Plan:
    def __init__(self, batch, rows):
        self.bits = batch.bit_length() - 1
        order = [(bit, bit) for bit in range(self.bits)]
        if self.bits > 1:
            order[:2] = [(0, 1), (1, 0)]
        late = order[:]
        if self.bits > 2:
            late = [order[2]] + order[:2] + order[3:]
        third = rows // 3
        self.lanes = [(0, 2 * third, order), (2 * third, third, late)]
        self.kept = []
        self.halves = []
        self.slot_rows = []
        for _, size, _ in self.lanes:
            kept, halves = [size], []
            for _ in range(self.bits):
                halves.append(kept[-1] // 2 >= 8)
                kept.append(kept[-1] // 2 if halves[-1] else kept[-1])
            self.kept.append(kept)
            self.halves.append(halves)
        for stage in range(self.bits):
            begin, starts = 0, []
            for lane in range(len(self.lanes)):
                starts.append(begin)
                begin += self.kept[lane][stage + 1]
            self.slot_rows.append((starts, begin))


def step_kernel(
    plan,
    inputs,
    grad_out,
    band_ids,
    conv_kernel,
    conv_bias,
    band_scale,
    band_shift,
    up_weight,
    up_bias,
    down_weight,
    down_bias,
    layer_scale,
    ends,
    up_out,
    down_out,
    small_out,
    spill,
    normed_spill,
    inv_spill,
    adapted_spill,
    xs,
    normed,
    inv_std,
    adapted,
    hidden,
    slope,
    gb,
    g,
    gc,
    wup,
    wdn,
    packed,
    params,
    up_bias_row_of,
    upper_even,
    upper_odd,
    onehot,
    sums,
    up_sums,
    small,
    keep,
    outgo,
    income,
    small_sum,
    small_in,
    *rest,
):
    stage_in = rest[: plan.bits]
    (
        load_sem,
        wt_send,
        wt_recv,
        par_send,
        par_recv,
        ends_send,
        ends_recv,
        core_send,
        core_recv,
        rs_send,
        rs_recv,
        deliver_send,
        deliver_recv,
        ag_send,
        ag_recv,
        out_sem,
        credit,
        small_send,
        small_recv,
        spill_sem,
        norm_sem,
    ) = rest[plan.bits :]
    uppers = (upper_even, upper_odd)
    core = lax.axis_index("section")
    other = 1 - core
    batch = lax.axis_index("batch")
    clips, frames, width = g.shape
    rows = clips * frames
    layers = xs.shape[0] - 1
    per_core = layers // 2
    hidden_width = hidden.shape[2]
    tile = 2 * frames
    chunks = frames // chunk
    blocks = hidden_width // tile
    bits = plan.bits
    mesh_id = pl.DeviceIdType.MESH

    def bit_of(bit):
        return (batch // (1 << bit)) % 2

    def partner(bit):
        return batch + (1 - 2 * bit_of(bit)) * (1 << bit)

    def choose(pair, side, value):
        first, second = pair
        if first == second:
            return value(first)
        if isinstance(side, int):
            return value(pair[side])
        return (1 - side) * value(first) + side * value(second)

    def to_core(source, target, send, recv):
        return pltpu.make_async_remote_copy(source, target, send, recv, {"section": other}, mesh_id)

    def to_batch(source, target, send, recv, device):
        return pltpu.make_async_remote_copy(source, target, send, recv, {"batch": device}, mesh_id)

    own_blocks = pl.ds(per_core * core, per_core)
    own_up = pltpu.make_async_copy(up_weight, wup.at[own_blocks], load_sem.at[0])
    own_dn = pltpu.make_async_copy(down_weight, wdn.at[own_blocks], load_sem.at[1])
    own_up.start()
    own_dn.start()
    loads = []
    for source, target in ((inputs, adapted), (grad_out, gb)):
        for clip in range(clips):
            loads.append(
                pltpu.make_async_copy(
                    source.at[clip, core], target.at[pl.ds(clip * frames, frames)], load_sem.at[2 + len(loads)]
                )
            )
    for load in loads:
        load.start()

    for j in range(per_core):
        packed[j, taps_row : taps_row + 7] = conv_kernel[:, j]
        packed[j, conv_bias_row : conv_bias_row + 1] = conv_bias[j : j + 1]
        packed[j, scale_row : scale_row + 4] = band_scale[j]
        packed[j, shift_row : shift_row + 4] = band_shift[j]
        for q in range(3):
            row = up_bias_row + q
            packed[j, row : row + 1] = up_bias[j : j + 1, q * width : (q + 1) * width]
        packed[j, down_bias_row : down_bias_row + 1] = down_bias[j : j + 1]
        packed[j, gamma_row : gamma_row + 1] = layer_scale[j : j + 1]
        packed[j, gamma_row + 1 : packed_rows] = jnp.zeros((packed_rows - gamma_row - 1, width), f32)

    barrier = pltpu.get_barrier_semaphore()
    pl.semaphore_signal(barrier, inc=1, device_id={"section": other}, device_id_type=mesh_id)
    for bit in range(bits):
        pl.semaphore_signal(barrier, inc=1, device_id={"batch": partner(bit)}, device_id_type=mesh_id)
    pl.semaphore_wait(barrier, 1 + bits)

    par_copy = to_core(packed, params.at[own_blocks], par_send.at[0], par_recv.at[0])
    par_copy.start()
    params[own_blocks] = packed[...]

    stages = [
        xs.at[1, :, 0:frames],
        xs.at[2, :, 0:frames],
        xs.at[3, :, 0:frames],
        outgo.at[0],
        outgo.at[1],
        xs.at[4, :, 0:frames],
        gc.at[:, 0:frames],
        outgo.at[0],
    ]

    def weight_part(kind, layer, half, part):
        if kind == 0:
            return wup.at[
                layer,
                pl.ds(pl.multiple_of(half * (width // 2) + (part % 2) * frames, frames), frames),
                pl.ds(pl.multiple_of((part // 2) * width, width), width),
            ]
        return wdn.at[layer, pl.ds(pl.multiple_of(half * rows + part * frames, frames), frames), :]

    def weight_wait(k):
        return to_core(outgo.at[0], keep.at[k], wt_send.at[k], wt_recv.at[k])

    def send_weights(k):
        j, kind, half = k // 4, k // 2 % 2, k % 2

        def cast(part, carry):
            stages[k][part] = weight_part(kind, per_core * core + j, half, part)[...].astype(f32)
            return carry

        lax.fori_loop(0, clips, cast, 0)
        to_core(stages[k], keep.at[k], wt_send.at[k], wt_recv.at[k]).start()

    def take_weights(layer, kind):
        @pl.when(layer // per_core != core)
        def _():
            for half in range(2):
                k = 4 * (layer % per_core) + 2 * kind + half
                weight_wait(k).wait_recv()

                def cast(part, carry, half=half, k=k):
                    weight_part(kind, layer, half, part)[...] = keep[k, part].astype(bf16)
                    return carry

                lax.fori_loop(0, clips, cast, 0)

    own_up.wait()
    own_dn.wait()
    for k in range(4 * per_core - 1):
        send_weights(k)

    for load in loads:
        load.wait()

    def load_x(clip, carry):
        xs[0, clip, 0:pad, :] = jnp.zeros((pad, width), f32)
        xs[0, clip, pad + frames : 2 * pad + frames, :] = jnp.zeros((pad, width), f32)
        xs[0, clip, pad : pad + frames, :] = adapted[
            pl.ds(pl.multiple_of(clip * frames, frames), frames), :
        ].astype(f32)
        for band in range(4):
            chosen = jnp.where(band_ids[core, clip] == band, 1.0, 0.0).astype(f32)
            onehot[clip, band : band + 1] = jnp.zeros((1, width), f32) + chosen
        return carry

    lax.fori_loop(0, clips, load_x, 0)
    par_copy.wait()
    for layer in range(layers):
        for block in range(blocks):
            row = up_bias_row + block // 2
            place = (block % 2) * tile
            up_bias_row_of[layer, block] = params[layer, row : row + 1, place : place + tile]

    def chosen_row(layer, clip, first):
        return jnp.sum(onehot[clip] * params[layer, first : first + 4], axis=0, keepdims=True)

    def norm_clip(layer, clip):
        table = params[layer]
        scale = chosen_row(layer, clip, scale_row)
        shift = chosen_row(layer, clip, shift_row)
        for j in range(chunks):
            window = xs[layer, clip, j * chunk : (j + 1) * chunk + 2 * pad, :]
            conv = window[pad : pad + chunk] * table[3:4] + table[conv_bias_row : conv_bias_row + 1]
            for k in (0, 1, 2, 4, 5, 6):
                conv = conv + window[pad - 3 + k : pad - 3 + k + chunk] * table[k : k + 1]
            centered = conv - jnp.mean(conv, axis=-1, keepdims=True)
            inv = lax.rsqrt(jnp.mean(centered * centered, axis=-1, keepdims=True) + norm_epsilon)
            value = centered * inv
            at = pl.ds(pl.multiple_of(clip * frames + j * chunk, chunk), chunk)
            normed[at, :] = value
            inv_std[at, :] = inv
            adapted[at, :] = (value * scale + shift).astype(bf16)

    def saved_copy(layer, which, back):
        buffer = (hidden if which == 0 else slope).at[layer % 2]
        away = spill.at[layer % 2, which]
        source, target = (away, buffer) if back else (buffer, away)
        return pltpu.make_async_copy(source, target, spill_sem.at[layer % 2, which])

    def norm_copies(layer, back):
        copies = []
        for i, (near, away) in enumerate(((normed, normed_spill), (inv_std, inv_spill), (adapted, adapted_spill))):
            source, target = (away.at[layer], near) if back else (near, away.at[layer])
            copies.append(pltpu.make_async_copy(source, target, norm_sem.at[i]))
        return copies

    branch_sum = g.reshape(rows, width)

    def forward(layer, carry):
        slot = layer % 2

        @pl.when(layer > 0)
        def _():
            for copy in norm_copies(layer - 1, False):
                copy.wait()

        def norm_body(clip, carry):
            norm_clip(layer, clip)
            return carry

        lax.fori_loop(0, clips, norm_body, 0)

        @pl.when(layer < layers - 1)
        def _():
            for copy in norm_copies(layer, False):
                copy.start()

        take_weights(layer, 0)

        @pl.when(layer >= 2)
        def _():
            for which in range(2):
                saved_copy(layer, which, False).wait()

        def up(block):
            columns = slice(block * tile, (block + 1) * tile)
            uppers[block % 2][...] = dot_plain(adapted[...], wup[layer, :, columns])

        def down(block):
            columns = slice(block * tile, (block + 1) * tile)
            value = dot_plain(hidden[slot, :, columns], wdn[layer, columns, :])
            branch_sum[...] = value if block == 0 else branch_sum[...] + value

        downs = {0: (), 1: (), 2: (), 3: (0, 1), 4: (2, 3), 5: (4,)}
        up(0)
        for block in range(blocks):
            columns = slice(block * tile, (block + 1) * tile)
            if block + 1 < blocks:
                up(block + 1)
            if block == blocks // 2:
                take_weights(layer, 1)
            for earlier in downs[block]:
                down(earlier)
            bias = up_bias_row_of[layer, block]
            for q in range(rows // chunk):
                at = slice(q * chunk, (q + 1) * chunk)
                smooth, steep = gelu_and_slope(uppers[block % 2][at, :] + bias)
                hidden[slot, at, columns] = smooth.astype(bf16)
                slope[slot, at, columns] = steep.astype(bf16)
        down(blocks - 1)

        @pl.when(layer < 2)
        def _():
            for which in range(2):
                saved_copy(layer, which, False).start()

        for step in range(layers):

            @pl.when(layer == step)
            def _(step=step):
                for k in [step] if step < layers - 1 else range(layers, 4 * per_core):
                    weight_wait(k).wait_send()
                if step == 0:
                    weight_wait(layers - 1).wait_send()
                    send_weights(4 * per_core - 1)

        def residual(clip, carry):
            bias = params[layer, down_bias_row : down_bias_row + 1]
            gamma = params[layer, gamma_row : gamma_row + 1]
            branch = g[clip] + bias
            xs[layer + 1, clip, pad : pad + frames, :] = xs[layer, clip, pad : pad + frames, :] + gamma * branch
            return carry

        lax.fori_loop(0, clips, residual, 0)

        def zero_pads(clip, carry):
            xs[layer + 1, clip, 0:pad, :] = jnp.zeros((pad, width), f32)
            xs[layer + 1, clip, pad + frames : 2 * pad + frames, :] = jnp.zeros((pad, width), f32)
            return carry

        lax.fori_loop(0, clips, zero_pads, 0)
        return carry

    lax.fori_loop(0, layers, forward, 0)

    result = xs.at[layers, :, pad : pad + frames]
    result_remote = to_core(result, ends.at[0, :, 0], ends_send.at[0], ends_recv.at[0])
    result_local = pltpu.make_async_copy(result, ends.at[0, :, 1], ends_send.at[1])

    @pl.when(core == 0)
    def _():
        result_remote.start()

    @pl.when(core == 1)
    def _():
        result_local.start()

    def load_g(clip, carry):
        g[clip] = gb[pl.ds(pl.multiple_of(clip * frames, frames), frames), :].astype(f32)
        gc[clip, 0:pad, :] = jnp.zeros((pad, width), f32)
        gc[clip, pad + frames : 2 * pad + frames, :] = jnp.zeros((pad, width), f32)
        return carry

    lax.fori_loop(0, clips, load_g, 0)

    matrices = 2 * layers
    lane_count = len(plan.lanes)

    def core_copy(m, parity):
        return to_core(outgo.at[parity], income.at[parity], core_send.at[parity], core_recv.at[parity])

    keep_rows = keep.reshape(matrices, rows, width)

    def offset(lane, stage, side):
        start = 0
        for s in range(stage):
            if plan.halves[lane][s]:
                start = start + choose(plan.lanes[lane][2][s], side, bit_of) * plan.kept[lane][s + 1]
        return start

    def rs_copy(m, parity, lane, stage):
        begin, _, order = plan.lanes[lane]
        size = plan.kept[lane][stage + 1]
        at = begin + offset(lane, stage, core)
        if plan.halves[lane][stage]:
            at = at + (1 - choose(order[stage], core, bit_of)) * size
        starts, _ = plan.slot_rows[stage]
        return to_batch(
            keep_rows.at[m, pl.ds(pl.multiple_of(at, 8), size)],
            stage_in[stage].at[parity, starts[lane] : starts[lane] + size],
            rs_send.at[stage, parity, lane],
            rs_recv.at[stage, parity, lane],
            choose(order[stage], core, partner),
        )

    def rs_add(m, parity, lane, stage):
        begin, _, _ = plan.lanes[lane]
        size = plan.kept[lane][stage + 1]
        at = begin + offset(lane, stage + 1, core)
        starts, _ = plan.slot_rows[stage]
        step = min(size, 2 * chunk)

        def body(i, carry):
            r = pl.multiple_of(at + i * step, 8)
            keep_rows[m, pl.ds(r, step), :] = (
                keep_rows[m, pl.ds(r, step), :]
                + stage_in[stage][parity, pl.ds(pl.multiple_of(starts[lane] + i * step, 8), step), :]
            )
            return carry

        lax.fori_loop(0, size // step, body, 0)

    half_way = matrices // 2
    xs_rows = xs.reshape(layers + 1, clips * (frames + 2 * pad), width)

    def rows_of(m, owner, own, lane, at, size):
        span = pl.ds(pl.multiple_of(plan.lanes[lane][0] + at, 8), size)
        if own:
            return keep_rows.at[m, span]
        return xs_rows.at[layers - m, span] if owner == 1 else keep_rows.at[m - half_way, span]

    def deliver_copy(m, owner, lane):
        size = plan.kept[lane][bits]
        at = offset(lane, bits, 1 - owner)
        return to_core(
            rows_of(m, owner, True, lane, at, size),
            rows_of(m, owner, False, lane, at, size),
            deliver_send.at[m % half_way, lane],
            deliver_recv.at[m % half_way, lane],
        )

    def ag_copy(m, owner, own, parity, lane, stage):
        size = plan.kept[lane][stage + 1]
        side = owner if own else 1 - owner
        place = rows_of(m, owner, own, lane, offset(lane, stage + 1, side), size)
        return to_batch(
            place,
            place,
            ag_send.at[stage, parity, own, lane],
            ag_recv.at[stage, parity, own, lane],
            choose(plan.lanes[lane][2][stage], side, partner),
        )

    def out_copies(m, kind, local, owner):
        copies = []
        third = rows // 3
        for own in range(2):
            half = owner if own else 1 - owner
            if own:
                source = keep_rows.at[m]
            else:
                source = xs_rows.at[layers - m] if owner == 1 else keep_rows.at[m - half_way]
            sem = out_sem.at[m % half_way, own]
            if kind == 0:
                copies.append(pltpu.make_async_copy(source.at[0:rows], down_out.at[local, half], sem.at[0]))
                continue
            for part in range(3):
                columns = slice(part * width, (part + 1) * width)
                copies.append(
                    pltpu.make_async_copy(
                        source.at[part * third : (part + 1) * third],
                        up_out.at[local, half, :, columns],
                        sem.at[part],
                    )
                )
        return copies

    def owner_of(m):
        return 1 - m // half_way

    def owned_by(owner, m):
        return m < half_way if owner == 1 else m >= half_way

    def tick(pair, phase):
        for s in range(2 * bits + 3, 0, -1):
            m = 2 * pair + phase + 1 - s
            parity = (phase + 1 - s) % 2
            kind = parity
            local = (layers - 1 - (m - kind) // 2) % per_core
            valid = (m >= 0) & (m < matrices)

            if s <= bits + 1:

                @pl.when(valid)
                def _(s=s, m=m, parity=parity):
                    if s == 1:
                        core_copy(m, parity).wait()

                        def body(clip, carry):
                            keep[m, clip] = keep[m, clip] + income[parity, clip]
                            return carry

                        lax.fori_loop(0, clips, body, 0)
                    else:
                        for lane in range(lane_count):
                            rs_copy(m, parity, lane, s - 2).wait()
                            if plan.halves[lane][s - 2]:
                                @pl.when(owner_of(m) == core)
                                def _(lane=lane):
                                    pl.semaphore_signal(
                                        credit.at[s - 2, lane],
                                        inc=1,
                                        device_id={"batch": choose(plan.lanes[lane][2][s - 2], core, partner)},
                                        device_id_type=mesh_id,
                                    )

                            rs_add(m, parity, lane, s - 2)
                    if s <= bits:
                        for lane in range(lane_count):
                            rs_copy(m, parity, lane, s - 1).start()

            for owner in range(2):
                if s == bits + 1:

                    @pl.when(valid & owned_by(owner, m) & (core == 1 - owner))
                    def _(m=m, owner=owner):
                        for lane in range(lane_count):
                            deliver_copy(m, owner, lane).start()

                if s > bits + 1:

                    @pl.when(valid & owned_by(owner, m) & (core == owner))
                    def _(s=s, m=m, parity=parity, kind=kind, local=local, owner=owner):
                        if s == bits + 2:
                            for lane in range(lane_count):
                                deliver_copy(m, owner, lane).wait_recv()
                        elif s <= 2 * bits + 2:
                            stage = 2 * bits + 2 - s
                            for lane in range(lane_count):
                                if plan.halves[lane][stage]:
                                    for own in range(2):
                                        ag_copy(m, owner, own, parity, lane, stage).wait()
                        if s <= 2 * bits + 1:
                            stage = 2 * bits + 1 - s
                            for lane in range(lane_count):
                                if plan.halves[lane][stage]:
                                    pl.semaphore_wait(credit.at[stage, lane], 1)
                                    for own in range(2):
                                        ag_copy(m, owner, own, parity, lane, stage).start()
                        elif s == 2 * bits + 2:
                            for copy in out_copies(m, kind, local, owner):
                                copy.start()
                        else:
                            for copy in out_copies(m, kind, local, owner):
                                copy.wait()

        m = 2 * pair + phase - bits
        for owner in range(2):

            @pl.when((m >= 0) & (m < matrices) & owned_by(owner, m) & (core == 1 - owner))
            def _(m=m, owner=owner):
                for lane in range(lane_count):
                    deliver_copy(m, owner, lane).wait_send()

    def store_block(m, phase, second, block, value):
        for q in range(2):
            piece = value[q * frames : (q + 1) * frames]
            if second == 0:
                outgo[phase, 2 * block + q] = piece
            else:
                keep[m, 2 * block + q] = piece

    def scale_clip(layer, clip):
        gamma = params[layer, gamma_row : gamma_row + 1]
        gamma_sum = bias_sum = jnp.zeros((8, width), f32)
        for j in range(chunks):
            here = g[clip, j * chunk : (j + 1) * chunk, :]
            at = slice(pad + j * chunk, pad + (j + 1) * chunk)
            gamma_sum = gamma_sum + fold(here * (xs[layer + 1, clip, at, :] - xs[layer, clip, at, :]))
            value = (gamma * here).astype(bf16)
            gb[pl.ds(pl.multiple_of(clip * frames + j * chunk, chunk), chunk), :] = value
            bias_sum = bias_sum + fold(value.astype(f32))
        sums[0] += gamma_sum
        sums[1] += bias_sum

    def norm_back(layer, clip):
        scale = chosen_row(layer, clip, scale_row)
        scale_sum = shift_sum = conv_sum = jnp.zeros((8, width), f32)
        for j in range(chunks):
            row = pl.ds(pl.multiple_of(clip * frames + j * chunk, chunk), chunk)
            at = slice(pad + j * chunk, pad + (j + 1) * chunk)
            ga = gc[clip, at, :]
            value = normed[row, :]
            scale_sum = scale_sum + fold(ga * value)
            shift_sum = shift_sum + fold(ga)
            dn = ga * scale
            first = jnp.mean(dn, axis=-1, keepdims=True)
            second = jnp.mean(dn * value, axis=-1, keepdims=True)
            result = inv_std[row, :] * (dn - first - value * second)
            gc[clip, at, :] = result
            conv_sum = conv_sum + fold(result)
        sums[9] += conv_sum
        choice = onehot[clip]
        small[layer, scale_row : scale_row + 4, :] += choice * jnp.sum(scale_sum, axis=0, keepdims=True)
        small[layer, shift_row : shift_row + 4, :] += choice * jnp.sum(shift_sum, axis=0, keepdims=True)

    def conv_back(layer, clip):
        table = params[layer]
        totals = [jnp.zeros((8, width), f32) for _ in range(7)]
        for j in range(chunks):
            grads = gc[clip, j * chunk : (j + 1) * chunk + 2 * pad, :]
            signal = xs[layer, clip, pad + j * chunk : pad + (j + 1) * chunk, :]
            at = slice(j * chunk, (j + 1) * chunk)
            total = g[clip, at, :]
            for k in (3, 0, 1, 2, 4, 5, 6):
                shifted = grads[pad + 3 - k : pad + 3 - k + chunk]
                total = total + shifted * table[k : k + 1]
                totals[k] = totals[k] + fold(signal * shifted)
            g[clip, at, :] = total
        for k in range(7):
            sums[2 + k] += totals[k]

    def backward(pair, carry):
        layer = layers - 1 - pair
        slot = layer % 2

        @pl.when((pair == 1) & (core == 0))
        def _():
            result_remote.wait_send()

        @pl.when((pair == 1) & (core == 1))
        def _():
            result_local.wait()

        sums[...] = jnp.zeros(sums.shape, f32)
        small[layer] = jnp.zeros(small.shape[1:], f32)

        def scale_body(clip, carry):
            scale_clip(layer, clip)
            return carry

        lax.fori_loop(0, clips, scale_body, 0)

        @pl.when(layer < 2)
        def _():
            for which in range(2):
                saved_copy(layer, which, True).wait()

        def up_grad(block):
            columns = pl.ds(pl.multiple_of(block * tile, tile), tile)
            value = dot_cols(gb[...], wdn[layer, columns, :])
            total = jnp.zeros((8, tile), f32)
            for q in range(rows // chunk):
                at = slice(q * chunk, (q + 1) * chunk)
                piece = (value[at] * slope[slot, at, columns].astype(f32)).astype(bf16)
                slope[slot, at, columns] = piece
                total = total + fold(piece.astype(f32))
            up_sums[block] = total

        for second in range(2):
            half = other if second == 0 else core

            def down_body(block, carry, second=second, half=half):
                at = pl.ds(pl.multiple_of(half * rows + block * tile, tile), tile)
                store_block(2 * pair, 0, second, block, dot_rows(hidden[slot, :, at], gb[...]))
                up_grad(block + 3 * second)
                return carry

            lax.fori_loop(0, clips // 2, down_body, 0)
            if second == 0:
                core_copy(2 * pair, 0).start()

        @pl.when(pair > 0)
        def _():
            for copy in norm_copies(layer, True):
                copy.wait()

        tick(pair, 0)

        def up_weight_grad(second, block):
            half = other if second == 0 else core
            at = pl.ds(pl.multiple_of(half * (width // 2), width // 2), width // 2)
            columns = pl.ds(pl.multiple_of(block * width, width), width)
            store_block(2 * pair + 1, 1, second, block, dot_rows(adapted[:, at], slope[slot, :, columns]))

        def adapted_grad(i):
            r = pl.multiple_of(i * tile, tile)
            value = dot_cols(slope[slot, pl.ds(r, tile), :], wup[layer])
            for q in range(2):
                gc[2 * i + q, pad : pad + frames, :] = value[q * frames : (q + 1) * frames]

        def norm_conv_back(i):
            for q in range(2):
                norm_back(layer, 2 * i + q)
                conv_back(layer, 2 * i + q)

        adapted_grad(0)
        up_weight_grad(0, 0)

        def tile_body(i, carry):
            adapted_grad(i + 1)
            up_weight_grad(0, i + 1)
            norm_conv_back(i)
            return carry

        lax.fori_loop(0, rows // tile - 1, tile_body, 0)
        core_copy(2 * pair + 1, 1).start()
        for block in range(3):
            up_weight_grad(1, block)
        norm_conv_back(rows // tile - 1)

        @pl.when(layer > 0)
        def _():
            for copy in norm_copies(layer - 1, True):
                copy.start()

        @pl.when(layer >= 2)
        def _():
            for which in range(2):
                saved_copy(layer, which, True).start()

        gamma = params[layer, gamma_row : gamma_row + 1, :]
        small[layer, gamma_row : gamma_row + 1, :] = jnp.sum(sums[0], axis=0, keepdims=True) / gamma
        small[layer, down_bias_row : down_bias_row + 1, :] = jnp.sum(sums[1], axis=0, keepdims=True)
        for block in range(blocks):
            row = up_bias_row + block // 2
            place = (block % 2) * tile
            small[layer, row : row + 1, place : place + tile] = jnp.sum(up_sums[block], axis=0, keepdims=True)
        for k in range(7):
            small[layer, taps_row + k : taps_row + k + 1, :] = jnp.sum(sums[2 + k], axis=0, keepdims=True)
        small[layer, conv_bias_row : conv_bias_row + 1, :] = jnp.sum(sums[9], axis=0, keepdims=True)
        tick(pair, 1)
        return carry

    lax.fori_loop(0, layers, backward, 0)

    grad_remote = to_core(g, ends.at[0, :, 1], ends_send.at[2], ends_recv.at[1])
    grad_local = pltpu.make_async_copy(g, ends.at[0, :, 0], ends_send.at[3])

    @pl.when(core == 0)
    def _():
        grad_local.start()

    @pl.when(core == 1)
    def _():
        grad_remote.start()

    small_core = to_core(
        small.at[pl.ds(per_core * other, per_core)], small_in.at[bits], small_send.at[bits], small_recv.at[bits]
    )
    small_core.start()

    def small_copy(bit):
        return to_batch(small_sum, small_in.at[bit], small_send.at[bit], small_recv.at[bit], partner(bit))

    def drain(pair, carry):
        for phase in range(2):
            tick(pair, phase)
            for step in range(bits + 1):

                @pl.when(2 * pair + phase - matrices == step)
                def _(step=step):
                    if step == 0:
                        small_core.wait()
                        small_sum[...] = small[pl.ds(per_core * core, per_core)] + small_in[bits]
                    else:
                        small_copy(step - 1).wait()
                        small_sum[...] = small_sum[...] + small_in[step - 1]
                    if step < bits:
                        small_copy(step).start()

        return carry

    lax.fori_loop(layers, layers + bits + 1, drain, 0)
    small_out[...] = small_sum[...]

    @pl.when(core == 0)
    def _():
        grad_local.wait()
        grad_remote.wait_recv()

    @pl.when(core == 1)
    def _():
        result_remote.wait_recv()
        grad_remote.wait_send()


def results_kernel(
    ends,
    up_grad,
    down_grad,
    small,
    ends_out,
    conv_kernel_out,
    conv_bias_out,
    band_scale_out,
    band_shift_out,
    up_out,
    up_bias_out,
    down_out,
    down_bias_out,
    layer_scale_out,
    ends_stage,
    up_stage,
    down_stage,
    in_sem,
    out_sem,
):
    copies = []
    per_core, _, width = small.shape
    for clip in range(ends.shape[1]):
        copies.append((ends.at[0, clip], ends_stage.at[clip], ends_out.at[0, clip]))
    for j in range(per_core):
        for half in range(2):
            for source, stage, target in ((up_grad, up_stage, up_out), (down_grad, down_stage, down_out)):
                size = source.shape[2] // 2
                for part in range(2):
                    at = (j, half, slice(part * size, (part + 1) * size))
                    copies.append((source.at[at], stage.at[at], target.at[at]))
    loads = [pltpu.make_async_copy(a, b, in_sem.at[i]) for i, (a, b, _) in enumerate(copies)]
    stores = [pltpu.make_async_copy(b, c, out_sem.at[i]) for i, (_, b, c) in enumerate(copies)]
    ahead = 6
    for load in loads[:ahead]:
        load.start()
    for i, (load, store) in enumerate(zip(loads, stores)):
        load.wait()
        store.start()
        if i + ahead < len(loads):
            loads[i + ahead].start()
    for j in range(per_core):
        conv_kernel_out[:, j] = small[j, taps_row : taps_row + 7]
        conv_bias_out[j : j + 1] = small[j, conv_bias_row : conv_bias_row + 1]
        band_scale_out[j] = small[j, scale_row : scale_row + 4]
        band_shift_out[j] = small[j, shift_row : shift_row + 4]
        for q in range(3):
            row = up_bias_row + q
            up_bias_out[j : j + 1, q * width : (q + 1) * width] = small[j, row : row + 1]
        down_bias_out[j : j + 1] = small[j, down_bias_row : down_bias_row + 1]
        layer_scale_out[j : j + 1] = small[j, gamma_row : gamma_row + 1]
    for store in stores:
        store.wait()


def body(
    inputs,
    grad_out,
    band_ids,
    conv_kernel,
    conv_bias,
    band_scale,
    band_shift,
    up_weight,
    up_bias,
    down_weight,
    down_bias,
    layer_scale,
):
    sections = lax.axis_size("section")
    batch = lax.axis_size("batch")
    clips, local_clips, frames, width = inputs.shape
    per_core, _, hidden_width = up_weight.shape
    layers = per_core * sections
    bands = band_scale.shape[1]
    rows = clips * frames
    assert sections == 2 and local_clips == 2 and batch & (batch - 1) == 0
    assert hidden_width == 3 * width and bands == 4 and layers == 4 and rows == 3 * width // 2
    plan = Plan(batch, rows)
    bits = plan.bits
    hbm = pl.BlockSpec(memory_space=pl.ANY)
    vmem = pl.BlockSpec(memory_space=pltpu.VMEM)
    smem = pl.BlockSpec(memory_space=pltpu.SMEM)
    padded = frames + 2 * pad
    dma = pltpu.SemaphoreType.DMA
    lanes = len(plan.lanes)
    tile = 2 * frames
    ends_shape = jax.ShapeDtypeStruct((1, clips, local_clips, frames, width), f32)
    up_shape = jax.ShapeDtypeStruct((per_core, 2, width // 2, hidden_width), f32)
    down_shape = jax.ShapeDtypeStruct((per_core, 2, hidden_width // 2, width), f32)
    small_shape = jax.ShapeDtypeStruct((per_core, packed_rows, width), f32)
    conv_kernel = jnp.transpose(conv_kernel, (1, 0, 2))
    ends, up_grad, down_grad, small, *_ = pl.pallas_call(
        functools.partial(step_kernel, plan),
        out_shape=[
            ends_shape,
            up_shape,
            down_shape,
            small_shape,
            jax.ShapeDtypeStruct((2, 2, rows, hidden_width), bf16),
            jax.ShapeDtypeStruct((layers - 1, rows, width), f32),
            jax.ShapeDtypeStruct((layers - 1, rows, 1), f32),
            jax.ShapeDtypeStruct((layers - 1, rows, width), bf16),
        ],
        in_specs=[hbm, hbm, smem, vmem, vmem, vmem, vmem, hbm, vmem, hbm, vmem, vmem],
        out_specs=[hbm, hbm, hbm, vmem, hbm, hbm, hbm, hbm],
        scratch_shapes=[
            pltpu.VMEM((layers + 1, clips, padded, width), f32),
            pltpu.VMEM((rows, width), f32),
            pltpu.VMEM((rows, 1), f32),
            pltpu.VMEM((rows, width), bf16),
            pltpu.VMEM((2, rows, hidden_width), bf16),
            pltpu.VMEM((2, rows, hidden_width), bf16),
            pltpu.VMEM((rows, width), bf16),
            pltpu.VMEM((clips, frames, width), f32),
            pltpu.VMEM((clips, padded, width), f32),
            pltpu.VMEM((layers, width, hidden_width), bf16),
            pltpu.VMEM((layers, hidden_width, width), bf16),
            pltpu.VMEM((per_core, packed_rows, width), f32),
            pltpu.VMEM((layers, packed_rows, width), f32),
            pltpu.VMEM((layers, hidden_width // tile, 1, tile), f32),
            pltpu.VMEM((rows, tile), f32),
            pltpu.VMEM((rows, tile), f32),
            pltpu.VMEM((clips, bands, width), f32),
            pltpu.VMEM((10, 8, width), f32),
            pltpu.VMEM((hidden_width // tile, 8, tile), f32),
            pltpu.VMEM((layers, packed_rows, width), f32),
            pltpu.VMEM((2 * layers, clips, frames, width), f32),
            pltpu.VMEM((2, clips, frames, width), f32),
            pltpu.VMEM((2, clips, frames, width), f32),
            pltpu.VMEM((per_core, packed_rows, width), f32),
            pltpu.VMEM((bits + 1, per_core, packed_rows, width), f32),
            *[pltpu.VMEM((2, plan.slot_rows[stage][1], width), f32) for stage in range(bits)],
            dma((2 + 2 * clips,)),
            dma((4 * per_core,)),
            dma((4 * per_core,)),
            dma((1,)),
            dma((1,)),
            dma((4,)),
            dma((2,)),
            dma((2,)),
            dma((2,)),
            dma((bits, 2, lanes)),
            dma((bits, 2, lanes)),
            dma((layers, lanes)),
            dma((layers, lanes)),
            dma((bits, 2, 2, lanes)),
            dma((bits, 2, 2, lanes)),
            dma((layers, 2, 3)),
            pltpu.SemaphoreType.REGULAR((bits, lanes)),
            dma((bits + 1,)),
            dma((bits + 1,)),
            dma((2, 2)),
            dma((3,)),
        ],
        compiler_params=pltpu.CompilerParams(
            collective_id=0, has_side_effects=True, vmem_limit_bytes=255 * 2**18
        ),
        cost_estimate=pl.CostEstimate(
            flops=24 * rows * width * hidden_width * 2, bytes_accessed=2**26, transcendentals=2**24
        ),
        name="blocks_step",
    )(
        inputs,
        grad_out,
        jnp.transpose(band_ids),
        conv_kernel,
        conv_bias,
        band_scale,
        band_shift,
        up_weight,
        up_bias,
        down_weight,
        down_bias,
        layer_scale,
    )

    def like(array):
        return jax.ShapeDtypeStruct(array.shape, f32)

    outs = pl.pallas_call(
        results_kernel,
        out_shape=[
            ends_shape,
            like(conv_kernel),
            like(conv_bias),
            like(band_scale),
            like(band_shift),
            up_shape,
            like(up_bias),
            down_shape,
            like(down_bias),
            like(layer_scale),
        ],
        in_specs=[hbm, hbm, hbm, vmem],
        out_specs=[hbm, vmem, vmem, vmem, vmem, hbm, vmem, hbm, vmem, vmem],
        scratch_shapes=[
            pltpu.VMEM(ends_shape.shape[1:], f32),
            pltpu.VMEM(up_shape.shape, f32),
            pltpu.VMEM(down_shape.shape, f32),
            dma((8 * per_core + clips,)),
            dma((8 * per_core + clips,)),
        ],
        compiler_params=pltpu.CompilerParams(vmem_limit_bytes=255 * 2**18),
        cost_estimate=pl.CostEstimate(flops=0, bytes_accessed=2**25, transcendentals=0),
        name="results",
    )(ends, up_grad, down_grad, small)
    outs = list(outs)
    outs[1] = jnp.transpose(outs[1], (1, 0, 2))
    outs[5] = outs[5].reshape(up_weight.shape)
    outs[7] = outs[7].reshape(down_weight.shape)
    return tuple(outs)


def solution(mesh):
    in_specs = (
        P(None, "batch", None, None),
        P(None, "batch", None, None),
        P(None, "batch"),
        P("section", None, None),
        P("section", None),
        P("section", None, None),
        P("section", None, None),
        P("section", None, None),
        P("section", None),
        P("section", None, None),
        P("section", None),
        P("section", None),
    )
    out_specs = (
        P("section", None, "batch", None, None),
        P("section", None, None),
        P("section", None),
        P("section", None, None),
        P("section", None, None),
        P("section", None, None),
        P("section", None),
        P("section", None, None),
        P("section", None),
        P("section", None),
    )
    return jax.shard_map(body, mesh=mesh, in_specs=in_specs, out_specs=out_specs, check_vma=False)
```

```python
import functools

import jax
import jax.numpy as jnp
from jax import lax
from jax.experimental import pallas as pl
from jax.experimental.pallas import tpu as pltpu
from jax.sharding import PartitionSpec as P

norm_epsilon = 1e-06
f32 = jnp.float32
bf16 = jnp.bfloat16

knee = 1.0 / 0.325
tail = tuple(
    value * knee**power
    for power, value in enumerate((0.0023193, 0.10197519, 0.25681865, -0.17643491, 0.43540795, -0.12008618))
)

taps_row, conv_bias_row, scale_row, shift_row, up_bias_row, down_bias_row, gamma_row = 0, 7, 8, 12, 16, 19, 20
packed_rows = 24
pad = 8
chunk = 32


def gelu_and_slope(u):
    size = jnp.abs(u)
    exponential = jnp.exp2(u * (u * (-0.5 * 1.4426950408889634)))
    base = size + knee
    t = pl.reciprocal(base, approx=True)
    t = t * (2.0 - base * t)
    poly = tail[5] * t + tail[4]
    for k in range(3, -1, -1):
        poly = poly * t + tail[k]
    smooth = jnp.maximum(u, 0.0) - size * (exponential * poly)
    below = exponential * (poly - 0.3989422804014327 * size)
    return smooth, jnp.where(u < 0.0, below, 1.0 - below)


def fold(values):
    rows, columns = values.shape
    return jnp.sum(values.reshape(rows // 8, 8, columns), axis=0)


def dot_rows(left, right):
    return lax.dot_general(left, right, (((0,), (0,)), ((), ())), preferred_element_type=f32)


def dot_plain(left, right):
    return lax.dot_general(left, right, (((1,), (0,)), ((), ())), preferred_element_type=f32)


def dot_cols(left, right):
    return lax.dot_general(left, right, (((1,), (1,)), ((), ())), preferred_element_type=f32)


class Plan:
    def __init__(self, batch, rows):
        self.bits = batch.bit_length() - 1
        order = [(bit, bit) for bit in range(self.bits)]
        if self.bits > 1:
            order[:2] = [(0, 1), (1, 0)]
        late = order[:]
        if self.bits > 2:
            late = [order[2]] + order[:2] + order[3:]
        third = rows // 3
        self.lanes = [(0, 2 * third, order), (2 * third, third, late)]
        self.kept = []
        self.halves = []
        self.slot_rows = []
        for _, size, _ in self.lanes:
            kept, halves = [size], []
            for _ in range(self.bits):
                halves.append(kept[-1] // 2 >= 8)
                kept.append(kept[-1] // 2 if halves[-1] else kept[-1])
            self.kept.append(kept)
            self.halves.append(halves)
        for stage in range(self.bits):
            begin, starts = 0, []
            for lane in range(len(self.lanes)):
                starts.append(begin)
                begin += self.kept[lane][stage + 1]
            self.slot_rows.append((starts, begin))


def step_kernel(
    plan,
    inputs,
    grad_out,
    band_ids,
    conv_kernel,
    conv_bias,
    band_scale,
    band_shift,
    up_weight,
    up_bias,
    down_weight,
    down_bias,
    layer_scale,
    ends,
    up_out,
    down_out,
    small_out,
    spill,
    normed_spill,
    inv_spill,
    adapted_spill,
    xs,
    normed,
    inv_std,
    adapted,
    hidden,
    slope,
    gb,
    g,
    gc,
    wup,
    wdn,
    packed,
    params,
    up_bias_row_of,
    upper_even,
    upper_odd,
    onehot,
    sums,
    up_sums,
    small,
    keep,
    outgo,
    income,
    small_sum,
    small_in,
    *rest,
):
    stage_in = rest[: plan.bits]
    (
        load_sem,
        wt_send,
        wt_recv,
        par_send,
        par_recv,
        ends_send,
        ends_recv,
        core_send,
        core_recv,
        rs_send,
        rs_recv,
        deliver_send,
        deliver_recv,
        ag_send,
        ag_recv,
        out_sem,
        credit,
        small_send,
        small_recv,
        spill_sem,
        norm_sem,
    ) = rest[plan.bits :]
    uppers = (upper_even, upper_odd)
    core = lax.axis_index("section")
    other = 1 - core
    batch = lax.axis_index("batch")
    clips, frames, width = g.shape
    rows = clips * frames
    layers = xs.shape[0] - 1
    per_core = layers // 2
    hidden_width = hidden.shape[2]
    tile = 2 * frames
    chunks = frames // chunk
    blocks = hidden_width // tile
    bits = plan.bits
    mesh_id = pl.DeviceIdType.MESH

    def bit_of(bit):
        return (batch // (1 << bit)) % 2

    def partner(bit):
        return batch + (1 - 2 * bit_of(bit)) * (1 << bit)

    def choose(pair, side, value):
        first, second = pair
        if first == second:
            return value(first)
        if isinstance(side, int):
            return value(pair[side])
        return (1 - side) * value(first) + side * value(second)

    def to_core(source, target, send, recv):
        return pltpu.make_async_remote_copy(source, target, send, recv, {"section": other}, mesh_id)

    def to_batch(source, target, send, recv, device):
        return pltpu.make_async_remote_copy(source, target, send, recv, {"batch": device}, mesh_id)

    own_blocks = pl.ds(per_core * core, per_core)
    own_up = pltpu.make_async_copy(up_weight, wup.at[own_blocks], load_sem.at[0])
    own_dn = pltpu.make_async_copy(down_weight, wdn.at[own_blocks], load_sem.at[1])
    own_up.start()
    own_dn.start()
    loads = []
    for source, target in ((inputs, adapted), (grad_out, gb)):
        for clip in range(clips):
            loads.append(
                pltpu.make_async_copy(
                    source.at[clip, core], target.at[pl.ds(clip * frames, frames)], load_sem.at[2 + len(loads)]
                )
            )
    for load in loads:
        load.start()

    for j in range(per_core):
        packed[j, taps_row : taps_row + 7] = conv_kernel[:, j]
        packed[j, conv_bias_row : conv_bias_row + 1] = conv_bias[j : j + 1]
        packed[j, scale_row : scale_row + 4] = band_scale[j]
        packed[j, shift_row : shift_row + 4] = band_shift[j]
        for q in range(3):
            row = up_bias_row + q
            packed[j, row : row + 1] = up_bias[j : j + 1, q * width : (q + 1) * width]
        packed[j, down_bias_row : down_bias_row + 1] = down_bias[j : j + 1]
        packed[j, gamma_row : gamma_row + 1] = layer_scale[j : j + 1]
        packed[j, gamma_row + 1 : packed_rows] = jnp.zeros((packed_rows - gamma_row - 1, width), f32)

    barrier = pltpu.get_barrier_semaphore()
    pl.semaphore_signal(barrier, inc=1, device_id={"section": other}, device_id_type=mesh_id)
    for bit in range(bits):
        pl.semaphore_signal(barrier, inc=1, device_id={"batch": partner(bit)}, device_id_type=mesh_id)
    for bit in range(min(bits, 3)):
        pl.semaphore_signal(
            barrier, inc=1, device_id={"section": other, "batch": partner(bit)}, device_id_type=mesh_id
        )

    for load in loads[:clips]:
        load.wait()

    def load_x(clip, carry):
        xs[0, clip, 0:pad, :] = jnp.zeros((pad, width), f32)
        xs[0, clip, pad + frames : 2 * pad + frames, :] = jnp.zeros((pad, width), f32)
        xs[0, clip, pad : pad + frames, :] = adapted[
            pl.ds(pl.multiple_of(clip * frames, frames), frames), :
        ].astype(f32)
        for band in range(4):
            chosen = jnp.where(band_ids[core, clip] == band, 1.0, 0.0).astype(f32)
            onehot[clip, band : band + 1] = jnp.zeros((1, width), f32) + chosen
        return carry

    lax.fori_loop(0, clips, load_x, 0)
    pl.semaphore_wait(barrier, 1 + bits + min(bits, 3))

    par_copy = to_core(packed, params.at[own_blocks], par_send.at[0], par_recv.at[0])
    par_copy.start()
    params[own_blocks] = packed[...]

    stages = [
        xs.at[1, :, 0:frames],
        xs.at[2, :, 0:frames],
        xs.at[3, :, 0:frames],
        outgo.at[0],
        outgo.at[1],
        xs.at[4, :, 0:frames],
        gc.at[:, 0:frames],
        outgo.at[0],
    ]

    def weight_part(kind, layer, half, part):
        if kind == 0:
            return wup.at[
                layer,
                pl.ds(pl.multiple_of(half * (width // 2) + (part % 2) * frames, frames), frames),
                pl.ds(pl.multiple_of((part // 2) * width, width), width),
            ]
        return wdn.at[layer, pl.ds(pl.multiple_of(half * rows + part * frames, frames), frames), :]

    routes = min(bits, 3)

    def weight_copies(stage, k, route):
        last = clips - 1
        near = to_core(stage.at[0:last], keep.at[k, 0:last], wt_send.at[k, 0], wt_recv.at[k, 0])
        far = pltpu.make_async_remote_copy(
            stage.at[last],
            keep.at[k, last],
            wt_send.at[k, 1],
            wt_recv.at[k, 1],
            {"section": other, "batch": partner(route)},
            mesh_id,
        )
        return near, far

    def weight_wait(k, sent):
        for copy in weight_copies(outgo.at[0], k, 0):
            if sent:
                copy.wait_send()
            else:
                copy.wait_recv()

    def send_weights(k):
        j, kind, half = k // 4, k // 2 % 2, k % 2

        def cast(part, carry):
            stages[k][part] = weight_part(kind, per_core * core + j, half, part)[...].astype(f32)
            return carry

        lax.fori_loop(0, clips, cast, 0)
        for copy in weight_copies(stages[k], k, k % routes):
            copy.start()

    def take_weights(layer, kind):
        @pl.when(layer // per_core != core)
        def _():
            for half in range(2):
                k = 4 * (layer % per_core) + 2 * kind + half
                weight_wait(k, False)

                def cast(part, carry, half=half, k=k):
                    weight_part(kind, layer, half, part)[...] = keep[k, part].astype(bf16)
                    return carry

                lax.fori_loop(0, clips, cast, 0)

    own_up.wait()
    for k in range(2):
        send_weights(k)
    own_dn.wait()
    for k in range(2, 4):
        send_weights(k)
    par_copy.wait()
    for layer in range(layers):
        for block in range(blocks):
            row = up_bias_row + block // 2
            place = (block % 2) * tile
            up_bias_row_of[layer, block] = params[layer, row : row + 1, place : place + tile]

    def chosen_row(layer, clip, first):
        return jnp.sum(onehot[clip] * params[layer, first : first + 4], axis=0, keepdims=True)

    def norm_clip(layer, clip):
        table = params[layer]
        scale = chosen_row(layer, clip, scale_row)
        shift = chosen_row(layer, clip, shift_row)
        for j in range(chunks):
            window = xs[layer, clip, j * chunk : (j + 1) * chunk + 2 * pad, :]
            conv = window[pad : pad + chunk] * table[3:4] + table[conv_bias_row : conv_bias_row + 1]
            for k in (0, 1, 2, 4, 5, 6):
                conv = conv + window[pad - 3 + k : pad - 3 + k + chunk] * table[k : k + 1]
            centered = conv - jnp.mean(conv, axis=-1, keepdims=True)
            inv = lax.rsqrt(jnp.mean(centered * centered, axis=-1, keepdims=True) + norm_epsilon)
            value = centered * inv
            at = pl.ds(pl.multiple_of(clip * frames + j * chunk, chunk), chunk)
            normed[at, :] = value
            inv_std[at, :] = inv
            adapted[at, :] = (value * scale + shift).astype(bf16)

    def saved_copy(layer, which, back):
        buffer = (hidden if which == 0 else slope).at[layer % 2]
        away = spill.at[layer % 2, which]
        source, target = (away, buffer) if back else (buffer, away)
        return pltpu.make_async_copy(source, target, spill_sem.at[layer % 2, which])

    def norm_copies(layer, back):
        copies = []
        for i, (near, away) in enumerate(((normed, normed_spill), (inv_std, inv_spill), (adapted, adapted_spill))):
            source, target = (away.at[layer], near) if back else (near, away.at[layer])
            copies.append(pltpu.make_async_copy(source, target, norm_sem.at[i]))
        return copies

    branch_sum = g.reshape(rows, width)

    def forward(layer, carry):
        slot = layer % 2

        @pl.when(layer > 0)
        def _():
            for copy in norm_copies(layer - 1, False):
                copy.wait()

        def norm_body(clip, carry):
            norm_clip(layer, clip)
            return carry

        lax.fori_loop(0, clips, norm_body, 0)

        @pl.when(layer == 0)
        def _():
            for k in range(4, 4 * per_core - 1):
                send_weights(k)

        @pl.when(layer < layers - 1)
        def _():
            for copy in norm_copies(layer, False):
                copy.start()

        take_weights(layer, 0)

        @pl.when(layer >= 2)
        def _():
            for which in range(2):
                saved_copy(layer, which, False).wait()

        def up(block):
            columns = slice(block * tile, (block + 1) * tile)
            uppers[block % 2][...] = dot_plain(adapted[...], wup[layer, :, columns])

        def down(block):
            columns = slice(block * tile, (block + 1) * tile)
            value = dot_plain(hidden[slot, :, columns], wdn[layer, columns, :])
            branch_sum[...] = value if block == 0 else branch_sum[...] + value

        downs = {0: (), 1: (), 2: (), 3: (0, 1), 4: (2, 3), 5: (4,)}
        up(0)
        for block in range(blocks):
            columns = slice(block * tile, (block + 1) * tile)
            if block + 1 < blocks:
                up(block + 1)
            if block == blocks // 2:
                take_weights(layer, 1)
            for earlier in downs[block]:
                down(earlier)
            bias = up_bias_row_of[layer, block]
            for q in range(rows // chunk):
                at = slice(q * chunk, (q + 1) * chunk)
                smooth, steep = gelu_and_slope(uppers[block % 2][at, :] + bias)
                hidden[slot, at, columns] = smooth.astype(bf16)
                slope[slot, at, columns] = steep.astype(bf16)
        down(blocks - 1)

        @pl.when(layer < 2)
        def _():
            for which in range(2):
                saved_copy(layer, which, False).start()

        for step in range(layers):

            @pl.when(layer == step)
            def _(step=step):
                for k in [step] if step < layers - 1 else range(layers, 4 * per_core):
                    weight_wait(k, True)
                if step == 0:
                    weight_wait(layers - 1, True)
                    send_weights(4 * per_core - 1)

        def residual(clip, carry):
            bias = params[layer, down_bias_row : down_bias_row + 1]
            gamma = params[layer, gamma_row : gamma_row + 1]
            branch = g[clip] + bias
            xs[layer + 1, clip, pad : pad + frames, :] = xs[layer, clip, pad : pad + frames, :] + gamma * branch
            return carry

        lax.fori_loop(0, clips, residual, 0)

        def zero_pads(clip, carry):
            xs[layer + 1, clip, 0:pad, :] = jnp.zeros((pad, width), f32)
            xs[layer + 1, clip, pad + frames : 2 * pad + frames, :] = jnp.zeros((pad, width), f32)
            return carry

        lax.fori_loop(0, clips, zero_pads, 0)
        return carry

    lax.fori_loop(0, layers, forward, 0)

    result = xs.at[layers, :, pad : pad + frames]
    result_remote = to_core(result, ends.at[0, :, 0], ends_send.at[0], ends_recv.at[0])
    result_local = pltpu.make_async_copy(result, ends.at[0, :, 1], ends_send.at[1])

    @pl.when(core == 0)
    def _():
        result_remote.start()

    @pl.when(core == 1)
    def _():
        result_local.start()

    for load in loads[clips:]:
        load.wait()

    def load_g(clip, carry):
        g[clip] = gb[pl.ds(pl.multiple_of(clip * frames, frames), frames), :].astype(f32)
        gc[clip, 0:pad, :] = jnp.zeros((pad, width), f32)
        gc[clip, pad + frames : 2 * pad + frames, :] = jnp.zeros((pad, width), f32)
        return carry

    lax.fori_loop(0, clips, load_g, 0)

    matrices = 2 * layers
    lane_count = len(plan.lanes)

    def core_copy(m, parity):
        return to_core(outgo.at[parity], income.at[parity], core_send.at[parity], core_recv.at[parity])

    keep_rows = keep.reshape(matrices, rows, width)

    def offset(lane, stage, side):
        start = 0
        for s in range(stage):
            if plan.halves[lane][s]:
                start = start + choose(plan.lanes[lane][2][s], side, bit_of) * plan.kept[lane][s + 1]
        return start

    def rs_copy(m, parity, lane, stage):
        begin, _, order = plan.lanes[lane]
        size = plan.kept[lane][stage + 1]
        at = begin + offset(lane, stage, core)
        if plan.halves[lane][stage]:
            at = at + (1 - choose(order[stage], core, bit_of)) * size
        starts, _ = plan.slot_rows[stage]
        return to_batch(
            keep_rows.at[m, pl.ds(pl.multiple_of(at, 8), size)],
            stage_in[stage].at[parity, starts[lane] : starts[lane] + size],
            rs_send.at[stage, parity, lane],
            rs_recv.at[stage, parity, lane],
            choose(order[stage], core, partner),
        )

    def rs_add(m, parity, lane, stage):
        begin, _, _ = plan.lanes[lane]
        size = plan.kept[lane][stage + 1]
        at = begin + offset(lane, stage + 1, core)
        starts, _ = plan.slot_rows[stage]
        step = min(size, 2 * chunk)

        def body(i, carry):
            r = pl.multiple_of(at + i * step, 8)
            keep_rows[m, pl.ds(r, step), :] = (
                keep_rows[m, pl.ds(r, step), :]
                + stage_in[stage][parity, pl.ds(pl.multiple_of(starts[lane] + i * step, 8), step), :]
            )
            return carry

        lax.fori_loop(0, size // step, body, 0)

    half_way = matrices // 2
    xs_rows = xs.reshape(layers + 1, clips * (frames + 2 * pad), width)

    def rows_of(m, owner, own, lane, at, size):
        span = pl.ds(pl.multiple_of(plan.lanes[lane][0] + at, 8), size)
        if own:
            return keep_rows.at[m, span]
        return xs_rows.at[layers - m, span] if owner == 1 else keep_rows.at[m - half_way, span]

    def deliver_copy(m, owner, lane):
        size = plan.kept[lane][bits]
        at = offset(lane, bits, 1 - owner)
        return to_core(
            rows_of(m, owner, True, lane, at, size),
            rows_of(m, owner, False, lane, at, size),
            deliver_send.at[m % half_way, lane],
            deliver_recv.at[m % half_way, lane],
        )

    def ag_copy(m, owner, own, parity, lane, stage):
        size = plan.kept[lane][stage + 1]
        side = owner if own else 1 - owner
        place = rows_of(m, owner, own, lane, offset(lane, stage + 1, side), size)
        return to_batch(
            place,
            place,
            ag_send.at[stage, parity, own, lane],
            ag_recv.at[stage, parity, own, lane],
            choose(plan.lanes[lane][2][stage], side, partner),
        )

    def out_copies(m, kind, local, owner):
        copies = []
        third = rows // 3
        for own in range(2):
            half = owner if own else 1 - owner
            if own:
                source = keep_rows.at[m]
            else:
                source = xs_rows.at[layers - m] if owner == 1 else keep_rows.at[m - half_way]
            sem = out_sem.at[m % half_way, own]
            if kind == 0:
                copies.append(pltpu.make_async_copy(source.at[0:rows], down_out.at[local, half], sem.at[0]))
                continue
            for part in range(3):
                columns = slice(part * width, (part + 1) * width)
                copies.append(
                    pltpu.make_async_copy(
                        source.at[part * third : (part + 1) * third],
                        up_out.at[local, half, :, columns],
                        sem.at[part],
                    )
                )
        return copies

    def owner_of(m):
        return 1 - m // half_way

    def owned_by(owner, m):
        return m < half_way if owner == 1 else m >= half_way

    def tick(pair, phase):
        for s in range(2 * bits + 3, 0, -1):
            m = 2 * pair + phase + 1 - s
            parity = (phase + 1 - s) % 2
            kind = parity
            local = (layers - 1 - (m - kind) // 2) % per_core
            valid = (m >= 0) & (m < matrices)

            if s <= bits + 1:

                @pl.when(valid)
                def _(s=s, m=m, parity=parity):
                    if s == 1:
                        core_copy(m, parity).wait()

                        def body(clip, carry):
                            keep[m, clip] = keep[m, clip] + income[parity, clip]
                            return carry

                        lax.fori_loop(0, clips, body, 0)
                    else:
                        for lane in range(lane_count):
                            rs_copy(m, parity, lane, s - 2).wait()
                            if plan.halves[lane][s - 2]:
                                @pl.when(owner_of(m) == core)
                                def _(lane=lane):
                                    pl.semaphore_signal(
                                        credit.at[s - 2, lane],
                                        inc=1,
                                        device_id={"batch": choose(plan.lanes[lane][2][s - 2], core, partner)},
                                        device_id_type=mesh_id,
                                    )

                            rs_add(m, parity, lane, s - 2)
                    if s <= bits:
                        for lane in range(lane_count):
                            rs_copy(m, parity, lane, s - 1).start()

            for owner in range(2):
                if s == bits + 1:

                    @pl.when(valid & owned_by(owner, m) & (core == 1 - owner))
                    def _(m=m, owner=owner):
                        for lane in range(lane_count):
                            deliver_copy(m, owner, lane).start()

                if s > bits + 1:

                    @pl.when(valid & owned_by(owner, m) & (core == owner))
                    def _(s=s, m=m, parity=parity, kind=kind, local=local, owner=owner):
                        if s == bits + 2:
                            for lane in range(lane_count):
                                deliver_copy(m, owner, lane).wait_recv()
                        elif s <= 2 * bits + 2:
                            stage = 2 * bits + 2 - s
                            for lane in range(lane_count):
                                if plan.halves[lane][stage]:
                                    for own in range(2):
                                        ag_copy(m, owner, own, parity, lane, stage).wait()
                        if s <= 2 * bits + 1:
                            stage = 2 * bits + 1 - s
                            for lane in range(lane_count):
                                if plan.halves[lane][stage]:
                                    pl.semaphore_wait(credit.at[stage, lane], 1)
                                    for own in range(2):
                                        ag_copy(m, owner, own, parity, lane, stage).start()
                        elif s == 2 * bits + 2:
                            for copy in out_copies(m, kind, local, owner):
                                copy.start()
                        else:
                            for copy in out_copies(m, kind, local, owner):
                                copy.wait()

        m = 2 * pair + phase - bits
        for owner in range(2):

            @pl.when((m >= 0) & (m < matrices) & owned_by(owner, m) & (core == 1 - owner))
            def _(m=m, owner=owner):
                for lane in range(lane_count):
                    deliver_copy(m, owner, lane).wait_send()

    def store_block(m, phase, second, block, value):
        for q in range(2):
            piece = value[q * frames : (q + 1) * frames]
            if second == 0:
                outgo[phase, 2 * block + q] = piece
            else:
                keep[m, 2 * block + q] = piece

    def scale_clip(layer, clip):
        gamma = params[layer, gamma_row : gamma_row + 1]
        gamma_sum = bias_sum = jnp.zeros((8, width), f32)
        for j in range(chunks):
            here = g[clip, j * chunk : (j + 1) * chunk, :]
            at = slice(pad + j * chunk, pad + (j + 1) * chunk)
            gamma_sum = gamma_sum + fold(here * (xs[layer + 1, clip, at, :] - xs[layer, clip, at, :]))
            value = (gamma * here).astype(bf16)
            gb[pl.ds(pl.multiple_of(clip * frames + j * chunk, chunk), chunk), :] = value
            bias_sum = bias_sum + fold(value.astype(f32))
        sums[0] += gamma_sum
        sums[1] += bias_sum

    def norm_back(layer, clip):
        scale = chosen_row(layer, clip, scale_row)
        scale_sum = shift_sum = conv_sum = jnp.zeros((8, width), f32)
        for j in range(chunks):
            row = pl.ds(pl.multiple_of(clip * frames + j * chunk, chunk), chunk)
            at = slice(pad + j * chunk, pad + (j + 1) * chunk)
            ga = gc[clip, at, :]
            value = normed[row, :]
            scale_sum = scale_sum + fold(ga * value)
            shift_sum = shift_sum + fold(ga)
            dn = ga * scale
            first = jnp.mean(dn, axis=-1, keepdims=True)
            second = jnp.mean(dn * value, axis=-1, keepdims=True)
            result = inv_std[row, :] * (dn - first - value * second)
            gc[clip, at, :] = result
            conv_sum = conv_sum + fold(result)
        sums[9] += conv_sum
        choice = onehot[clip]
        small[layer, scale_row : scale_row + 4, :] += choice * jnp.sum(scale_sum, axis=0, keepdims=True)
        small[layer, shift_row : shift_row + 4, :] += choice * jnp.sum(shift_sum, axis=0, keepdims=True)

    def conv_back(layer, clip):
        table = params[layer]
        totals = [jnp.zeros((8, width), f32) for _ in range(7)]
        for j in range(chunks):
            grads = gc[clip, j * chunk : (j + 1) * chunk + 2 * pad, :]
            signal = xs[layer, clip, pad + j * chunk : pad + (j + 1) * chunk, :]
            at = slice(j * chunk, (j + 1) * chunk)
            total = g[clip, at, :]
            for k in (3, 0, 1, 2, 4, 5, 6):
                shifted = grads[pad + 3 - k : pad + 3 - k + chunk]
                total = total + shifted * table[k : k + 1]
                totals[k] = totals[k] + fold(signal * shifted)
            g[clip, at, :] = total
        for k in range(7):
            sums[2 + k] += totals[k]

    def backward(pair, carry):
        layer = layers - 1 - pair
        slot = layer % 2

        @pl.when((pair == 1) & (core == 0))
        def _():
            result_remote.wait_send()

        @pl.when((pair == 1) & (core == 1))
        def _():
            result_local.wait()

        sums[...] = jnp.zeros(sums.shape, f32)
        small[layer] = jnp.zeros(small.shape[1:], f32)

        def scale_body(clip, carry):
            scale_clip(layer, clip)
            return carry

        lax.fori_loop(0, clips, scale_body, 0)

        @pl.when(layer < 2)
        def _():
            for which in range(2):
                saved_copy(layer, which, True).wait()

        def up_grad(block):
            columns = pl.ds(pl.multiple_of(block * tile, tile), tile)
            value = dot_cols(gb[...], wdn[layer, columns, :])
            total = jnp.zeros((8, tile), f32)
            for q in range(rows // chunk):
                at = slice(q * chunk, (q + 1) * chunk)
                piece = (value[at] * slope[slot, at, columns].astype(f32)).astype(bf16)
                slope[slot, at, columns] = piece
                total = total + fold(piece.astype(f32))
            up_sums[block] = total

        for second in range(2):
            half = other if second == 0 else core

            def down_body(block, carry, second=second, half=half):
                at = pl.ds(pl.multiple_of(half * rows + block * tile, tile), tile)
                store_block(2 * pair, 0, second, block, dot_rows(hidden[slot, :, at], gb[...]))
                up_grad(block + 3 * second)
                return carry

            lax.fori_loop(0, clips // 2, down_body, 0)
            if second == 0:
                core_copy(2 * pair, 0).start()

        @pl.when(pair > 0)
        def _():
            for copy in norm_copies(layer, True):
                copy.wait()

        tick(pair, 0)

        def up_weight_grad(second, block):
            half = other if second == 0 else core
            at = pl.ds(pl.multiple_of(half * (width // 2), width // 2), width // 2)
            columns = pl.ds(pl.multiple_of(block * width, width), width)
            store_block(2 * pair + 1, 1, second, block, dot_rows(adapted[:, at], slope[slot, :, columns]))

        def adapted_grad(i):
            r = pl.multiple_of(i * tile, tile)
            value = dot_cols(slope[slot, pl.ds(r, tile), :], wup[layer])
            for q in range(2):
                gc[2 * i + q, pad : pad + frames, :] = value[q * frames : (q + 1) * frames]

        def norm_conv_back(i):
            for q in range(2):
                norm_back(layer, 2 * i + q)
                conv_back(layer, 2 * i + q)

        adapted_grad(0)
        up_weight_grad(0, 0)

        def tile_body(i, carry):
            adapted_grad(i + 1)
            up_weight_grad(0, i + 1)
            norm_conv_back(i)
            return carry

        lax.fori_loop(0, rows // tile - 1, tile_body, 0)
        core_copy(2 * pair + 1, 1).start()
        for block in range(3):
            up_weight_grad(1, block)
        norm_conv_back(rows // tile - 1)

        @pl.when(layer > 0)
        def _():
            for copy in norm_copies(layer - 1, True):
                copy.start()

        @pl.when(layer >= 2)
        def _():
            for which in range(2):
                saved_copy(layer, which, True).start()

        gamma = params[layer, gamma_row : gamma_row + 1, :]
        small[layer, gamma_row : gamma_row + 1, :] = jnp.sum(sums[0], axis=0, keepdims=True) / gamma
        small[layer, down_bias_row : down_bias_row + 1, :] = jnp.sum(sums[1], axis=0, keepdims=True)
        for block in range(blocks):
            row = up_bias_row + block // 2
            place = (block % 2) * tile
            small[layer, row : row + 1, place : place + tile] = jnp.sum(up_sums[block], axis=0, keepdims=True)
        for k in range(7):
            small[layer, taps_row + k : taps_row + k + 1, :] = jnp.sum(sums[2 + k], axis=0, keepdims=True)
        small[layer, conv_bias_row : conv_bias_row + 1, :] = jnp.sum(sums[9], axis=0, keepdims=True)
        tick(pair, 1)
        return carry

    lax.fori_loop(0, layers, backward, 0)

    grad_remote = to_core(g, ends.at[0, :, 1], ends_send.at[2], ends_recv.at[1])
    grad_local = pltpu.make_async_copy(g, ends.at[0, :, 0], ends_send.at[3])

    @pl.when(core == 0)
    def _():
        grad_local.start()

    @pl.when(core == 1)
    def _():
        grad_remote.start()

    small_core = to_core(
        small.at[pl.ds(per_core * other, per_core)], small_in.at[bits], small_send.at[bits], small_recv.at[bits]
    )
    small_core.start()

    def small_copy(bit):
        return to_batch(small_sum, small_in.at[bit], small_send.at[bit], small_recv.at[bit], partner(bit))

    def drain(pair, carry):
        for phase in range(2):
            tick(pair, phase)
            for step in range(bits + 1):

                @pl.when(2 * pair + phase - matrices == step)
                def _(step=step):
                    if step == 0:
                        small_core.wait()
                        small_sum[...] = small[pl.ds(per_core * core, per_core)] + small_in[bits]
                    else:
                        small_copy(step - 1).wait()
                        small_sum[...] = small_sum[...] + small_in[step - 1]
                    if step < bits:
                        small_copy(step).start()

        return carry

    lax.fori_loop(layers, layers + bits + 1, drain, 0)
    small_out[...] = small_sum[...]

    @pl.when(core == 0)
    def _():
        grad_local.wait()
        grad_remote.wait_recv()

    @pl.when(core == 1)
    def _():
        result_remote.wait_recv()
        grad_remote.wait_send()


def results_kernel(
    ends,
    up_grad,
    down_grad,
    small,
    ends_out,
    conv_kernel_out,
    conv_bias_out,
    band_scale_out,
    band_shift_out,
    up_out,
    up_bias_out,
    down_out,
    down_bias_out,
    layer_scale_out,
    ends_stage,
    up_stage,
    down_stage,
    in_sem,
    out_sem,
):
    copies = []
    per_core, _, width = small.shape
    for clip in range(ends.shape[1]):
        copies.append((ends.at[0, clip], ends_stage.at[clip], ends_out.at[0, clip]))
    for j in range(per_core):
        for half in range(2):
            for source, stage, target in ((up_grad, up_stage, up_out), (down_grad, down_stage, down_out)):
                size = source.shape[2] // 2
                for part in range(2):
                    at = (j, half, slice(part * size, (part + 1) * size))
                    copies.append((source.at[at], stage.at[at], target.at[at]))
    loads = [pltpu.make_async_copy(a, b, in_sem.at[i]) for i, (a, b, _) in enumerate(copies)]
    stores = [pltpu.make_async_copy(b, c, out_sem.at[i]) for i, (_, b, c) in enumerate(copies)]
    ahead = 6
    for load in loads[:ahead]:
        load.start()
    for i, (load, store) in enumerate(zip(loads, stores)):
        load.wait()
        store.start()
        if i + ahead < len(loads):
            loads[i + ahead].start()
    for j in range(per_core):
        conv_kernel_out[:, j] = small[j, taps_row : taps_row + 7]
        conv_bias_out[j : j + 1] = small[j, conv_bias_row : conv_bias_row + 1]
        band_scale_out[j] = small[j, scale_row : scale_row + 4]
        band_shift_out[j] = small[j, shift_row : shift_row + 4]
        for q in range(3):
            row = up_bias_row + q
            up_bias_out[j : j + 1, q * width : (q + 1) * width] = small[j, row : row + 1]
        down_bias_out[j : j + 1] = small[j, down_bias_row : down_bias_row + 1]
        layer_scale_out[j : j + 1] = small[j, gamma_row : gamma_row + 1]
    for store in stores:
        store.wait()


def body(
    inputs,
    grad_out,
    band_ids,
    conv_kernel,
    conv_bias,
    band_scale,
    band_shift,
    up_weight,
    up_bias,
    down_weight,
    down_bias,
    layer_scale,
):
    sections = lax.axis_size("section")
    batch = lax.axis_size("batch")
    clips, local_clips, frames, width = inputs.shape
    per_core, _, hidden_width = up_weight.shape
    layers = per_core * sections
    bands = band_scale.shape[1]
    rows = clips * frames
    assert sections == 2 and local_clips == 2 and batch & (batch - 1) == 0
    assert hidden_width == 3 * width and bands == 4 and layers == 4 and rows == 3 * width // 2
    plan = Plan(batch, rows)
    bits = plan.bits
    hbm = pl.BlockSpec(memory_space=pl.ANY)
    vmem = pl.BlockSpec(memory_space=pltpu.VMEM)
    smem = pl.BlockSpec(memory_space=pltpu.SMEM)
    padded = frames + 2 * pad
    dma = pltpu.SemaphoreType.DMA
    lanes = len(plan.lanes)
    tile = 2 * frames
    ends_shape = jax.ShapeDtypeStruct((1, clips, local_clips, frames, width), f32)
    up_shape = jax.ShapeDtypeStruct((per_core, 2, width // 2, hidden_width), f32)
    down_shape = jax.ShapeDtypeStruct((per_core, 2, hidden_width // 2, width), f32)
    small_shape = jax.ShapeDtypeStruct((per_core, packed_rows, width), f32)
    conv_kernel = jnp.transpose(conv_kernel, (1, 0, 2))
    ends, up_grad, down_grad, small, *_ = pl.pallas_call(
        functools.partial(step_kernel, plan),
        out_shape=[
            ends_shape,
            up_shape,
            down_shape,
            small_shape,
            jax.ShapeDtypeStruct((2, 2, rows, hidden_width), bf16),
            jax.ShapeDtypeStruct((layers - 1, rows, width), f32),
            jax.ShapeDtypeStruct((layers - 1, rows, 1), f32),
            jax.ShapeDtypeStruct((layers - 1, rows, width), bf16),
        ],
        in_specs=[hbm, hbm, smem, vmem, vmem, vmem, vmem, hbm, vmem, hbm, vmem, vmem],
        out_specs=[hbm, hbm, hbm, vmem, hbm, hbm, hbm, hbm],
        scratch_shapes=[
            pltpu.VMEM((layers + 1, clips, padded, width), f32),
            pltpu.VMEM((rows, width), f32),
            pltpu.VMEM((rows, 1), f32),
            pltpu.VMEM((rows, width), bf16),
            pltpu.VMEM((2, rows, hidden_width), bf16),
            pltpu.VMEM((2, rows, hidden_width), bf16),
            pltpu.VMEM((rows, width), bf16),
            pltpu.VMEM((clips, frames, width), f32),
            pltpu.VMEM((clips, padded, width), f32),
            pltpu.VMEM((layers, width, hidden_width), bf16),
            pltpu.VMEM((layers, hidden_width, width), bf16),
            pltpu.VMEM((per_core, packed_rows, width), f32),
            pltpu.VMEM((layers, packed_rows, width), f32),
            pltpu.VMEM((layers, hidden_width // tile, 1, tile), f32),
            pltpu.VMEM((rows, tile), f32),
            pltpu.VMEM((rows, tile), f32),
            pltpu.VMEM((clips, bands, width), f32),
            pltpu.VMEM((10, 8, width), f32),
            pltpu.VMEM((hidden_width // tile, 8, tile), f32),
            pltpu.VMEM((layers, packed_rows, width), f32),
            pltpu.VMEM((2 * layers, clips, frames, width), f32),
            pltpu.VMEM((2, clips, frames, width), f32),
            pltpu.VMEM((2, clips, frames, width), f32),
            pltpu.VMEM((per_core, packed_rows, width), f32),
            pltpu.VMEM((bits + 1, per_core, packed_rows, width), f32),
            *[pltpu.VMEM((2, plan.slot_rows[stage][1], width), f32) for stage in range(bits)],
            dma((2 + 2 * clips,)),
            dma((4 * per_core, 2)),
            dma((4 * per_core, 2)),
            dma((1,)),
            dma((1,)),
            dma((4,)),
            dma((2,)),
            dma((2,)),
            dma((2,)),
            dma((bits, 2, lanes)),
            dma((bits, 2, lanes)),
            dma((layers, lanes)),
            dma((layers, lanes)),
            dma((bits, 2, 2, lanes)),
            dma((bits, 2, 2, lanes)),
            dma((layers, 2, 3)),
            pltpu.SemaphoreType.REGULAR((bits, lanes)),
            dma((bits + 1,)),
            dma((bits + 1,)),
            dma((2, 2)),
            dma((3,)),
        ],
        compiler_params=pltpu.CompilerParams(
            collective_id=0, has_side_effects=True, vmem_limit_bytes=255 * 2**18
        ),
        cost_estimate=pl.CostEstimate(
            flops=24 * rows * width * hidden_width * 2, bytes_accessed=2**26, transcendentals=2**24
        ),
        name="blocks_step",
    )(
        inputs,
        grad_out,
        jnp.transpose(band_ids),
        conv_kernel,
        conv_bias,
        band_scale,
        band_shift,
        up_weight,
        up_bias,
        down_weight,
        down_bias,
        layer_scale,
    )

    def like(array):
        return jax.ShapeDtypeStruct(array.shape, f32)

    outs = pl.pallas_call(
        results_kernel,
        out_shape=[
            ends_shape,
            like(conv_kernel),
            like(conv_bias),
            like(band_scale),
            like(band_shift),
            up_shape,
            like(up_bias),
            down_shape,
            like(down_bias),
            like(layer_scale),
        ],
        in_specs=[hbm, hbm, hbm, vmem],
        out_specs=[hbm, vmem, vmem, vmem, vmem, hbm, vmem, hbm, vmem, vmem],
        scratch_shapes=[
            pltpu.VMEM(ends_shape.shape[1:], f32),
            pltpu.VMEM(up_shape.shape, f32),
            pltpu.VMEM(down_shape.shape, f32),
            dma((8 * per_core + clips,)),
            dma((8 * per_core + clips,)),
        ],
        compiler_params=pltpu.CompilerParams(vmem_limit_bytes=255 * 2**18),
        cost_estimate=pl.CostEstimate(flops=0, bytes_accessed=2**25, transcendentals=0),
        name="results",
    )(ends, up_grad, down_grad, small)
    outs = list(outs)
    outs[1] = jnp.transpose(outs[1], (1, 0, 2))
    outs[5] = outs[5].reshape(up_weight.shape)
    outs[7] = outs[7].reshape(down_weight.shape)
    return tuple(outs)


def solution(mesh):
    in_specs = (
        P(None, "batch", None, None),
        P(None, "batch", None, None),
        P(None, "batch"),
        P("section", None, None),
        P("section", None),
        P("section", None, None),
        P("section", None, None),
        P("section", None, None),
        P("section", None),
        P("section", None, None),
        P("section", None),
        P("section", None),
    )
    out_specs = (
        P("section", None, "batch", None, None),
        P("section", None, None),
        P("section", None),
        P("section", None, None),
        P("section", None, None),
        P("section", None, None),
        P("section", None),
        P("section", None, None),
        P("section", None),
        P("section", None),
    )
    return jax.shard_map(body, mesh=mesh, in_specs=in_specs, out_specs=out_specs, check_vma=False)
```

```python
import functools

import jax
import jax.numpy as jnp
from jax import lax
from jax.experimental import pallas as pl
from jax.experimental.pallas import tpu as pltpu
from jax.sharding import PartitionSpec as P

norm_epsilon = 1e-06
f32 = jnp.float32
bf16 = jnp.bfloat16

log_density = -1.3257480647361593

taps_row, conv_bias_row, scale_row, shift_row, up_bias_row, down_bias_row, gamma_row = 0, 7, 8, 12, 16, 19, 20
packed_rows = 24
pad = 8
chunk = 32


def gelu_and_slope(u):
    cdf = 0.5 * lax.erf(u * 0.7071067811865476) + 0.5
    density = jnp.exp2(u * (u * (-0.5 * 1.4426950408889634)) + log_density)
    return u * cdf, cdf + u * density


def fold(values):
    rows, columns = values.shape
    return jnp.sum(values.reshape(rows // 8, 8, columns), axis=0)


def dot_rows(left, right):
    return lax.dot_general(left, right, (((0,), (0,)), ((), ())), preferred_element_type=f32)


def dot_plain(left, right):
    return lax.dot_general(left, right, (((1,), (0,)), ((), ())), preferred_element_type=f32)


def dot_cols(left, right):
    return lax.dot_general(left, right, (((1,), (1,)), ((), ())), preferred_element_type=f32)


class Plan:
    def __init__(self, batch, rows):
        self.bits = batch.bit_length() - 1
        order = [(bit, bit) for bit in range(self.bits)]
        if self.bits > 1:
            order[:2] = [(0, 1), (1, 0)]
        late = order[:]
        if self.bits > 2:
            late = [order[2]] + order[:2] + order[3:]
        third = rows // 3
        self.lanes = [(0, 2 * third, order), (2 * third, third, late)]
        self.kept = []
        self.halves = []
        self.slot_rows = []
        for _, size, _ in self.lanes:
            kept, halves = [size], []
            for _ in range(self.bits):
                halves.append(kept[-1] // 2 >= 8)
                kept.append(kept[-1] // 2 if halves[-1] else kept[-1])
            self.kept.append(kept)
            self.halves.append(halves)
        for stage in range(self.bits):
            begin, starts = 0, []
            for lane in range(len(self.lanes)):
                starts.append(begin)
                begin += self.kept[lane][stage + 1]
            self.slot_rows.append((starts, begin))


def step_kernel(
    plan,
    inputs,
    grad_out,
    band_ids,
    conv_kernel,
    conv_bias,
    band_scale,
    band_shift,
    up_weight,
    up_bias,
    down_weight,
    down_bias,
    layer_scale,
    ends,
    up_out,
    down_out,
    small_out,
    spill,
    normed_spill,
    inv_spill,
    adapted_spill,
    xs,
    normed,
    inv_std,
    adapted,
    hidden,
    slope,
    gb,
    g,
    gc,
    wup,
    wdn,
    packed,
    params,
    up_bias_row_of,
    upper_even,
    upper_odd,
    onehot,
    sums,
    up_sums,
    small,
    keep,
    outgo,
    income,
    small_sum,
    small_in,
    *rest,
):
    stage_in = rest[: plan.bits]
    (
        load_sem,
        wt_send,
        wt_recv,
        par_send,
        par_recv,
        ends_send,
        ends_recv,
        core_send,
        core_recv,
        rs_send,
        rs_recv,
        deliver_send,
        deliver_recv,
        ag_send,
        ag_recv,
        out_sem,
        credit,
        small_send,
        small_recv,
        spill_sem,
        norm_sem,
    ) = rest[plan.bits :]
    uppers = (upper_even, upper_odd)
    core = lax.axis_index("section")
    other = 1 - core
    batch = lax.axis_index("batch")
    clips, frames, width = g.shape
    rows = clips * frames
    layers = xs.shape[0] - 1
    per_core = layers // 2
    hidden_width = hidden.shape[2]
    tile = 2 * frames
    chunks = frames // chunk
    blocks = hidden_width // tile
    bits = plan.bits
    mesh_id = pl.DeviceIdType.MESH

    def bit_of(bit):
        return (batch // (1 << bit)) % 2

    def partner(bit):
        return batch + (1 - 2 * bit_of(bit)) * (1 << bit)

    def choose(pair, side, value):
        first, second = pair
        if first == second:
            return value(first)
        if isinstance(side, int):
            return value(pair[side])
        return (1 - side) * value(first) + side * value(second)

    def to_core(source, target, send, recv):
        return pltpu.make_async_remote_copy(source, target, send, recv, {"section": other}, mesh_id)

    def to_batch(source, target, send, recv, device):
        return pltpu.make_async_remote_copy(source, target, send, recv, {"batch": device}, mesh_id)

    own_blocks = pl.ds(per_core * core, per_core)
    own_up = pltpu.make_async_copy(up_weight, wup.at[own_blocks], load_sem.at[0])
    own_dn = pltpu.make_async_copy(down_weight, wdn.at[own_blocks], load_sem.at[1])
    own_up.start()
    own_dn.start()
    loads = []
    for source, target in ((inputs, adapted), (grad_out, gb)):
        for clip in range(clips):
            loads.append(
                pltpu.make_async_copy(
                    source.at[clip, core], target.at[pl.ds(clip * frames, frames)], load_sem.at[2 + len(loads)]
                )
            )
    for load in loads:
        load.start()

    for j in range(per_core):
        packed[j, taps_row : taps_row + 7] = conv_kernel[:, j]
        packed[j, conv_bias_row : conv_bias_row + 1] = conv_bias[j : j + 1]
        packed[j, scale_row : scale_row + 4] = band_scale[j]
        packed[j, shift_row : shift_row + 4] = band_shift[j]
        for q in range(3):
            row = up_bias_row + q
            packed[j, row : row + 1] = up_bias[j : j + 1, q * width : (q + 1) * width]
        packed[j, down_bias_row : down_bias_row + 1] = down_bias[j : j + 1]
        packed[j, gamma_row : gamma_row + 1] = layer_scale[j : j + 1]
        packed[j, gamma_row + 1 : packed_rows] = jnp.zeros((packed_rows - gamma_row - 1, width), f32)

    barrier = pltpu.get_barrier_semaphore()
    pl.semaphore_signal(barrier, inc=1, device_id={"section": other}, device_id_type=mesh_id)
    for bit in range(bits):
        pl.semaphore_signal(barrier, inc=1, device_id={"batch": partner(bit)}, device_id_type=mesh_id)

    for load in loads[:clips]:
        load.wait()

    def load_x(clip, carry):
        xs[0, clip, 0:pad, :] = jnp.zeros((pad, width), f32)
        xs[0, clip, pad + frames : 2 * pad + frames, :] = jnp.zeros((pad, width), f32)
        xs[0, clip, pad : pad + frames, :] = adapted[
            pl.ds(pl.multiple_of(clip * frames, frames), frames), :
        ].astype(f32)
        for band in range(4):
            chosen = jnp.where(band_ids[core, clip] == band, 1.0, 0.0).astype(f32)
            onehot[clip, band : band + 1] = jnp.zeros((1, width), f32) + chosen
        return carry

    lax.fori_loop(0, clips, load_x, 0)
    pl.semaphore_wait(barrier, 1 + bits)

    par_copy = to_core(packed, params.at[own_blocks], par_send.at[0], par_recv.at[0])
    par_copy.start()
    params[own_blocks] = packed[...]

    stages = [
        xs.at[1, :, 0:frames],
        xs.at[2, :, 0:frames],
        xs.at[3, :, 0:frames],
        outgo.at[0],
        outgo.at[1],
        xs.at[4, :, 0:frames],
        gc.at[:, 0:frames],
        outgo.at[0],
    ]

    def weight_part(kind, layer, half, part):
        if kind == 0:
            return wup.at[
                layer,
                pl.ds(pl.multiple_of(half * (width // 2) + (part % 2) * frames, frames), frames),
                pl.ds(pl.multiple_of((part // 2) * width, width), width),
            ]
        return wdn.at[layer, pl.ds(pl.multiple_of(half * rows + part * frames, frames), frames), :]

    def weight_copy(stage, k):
        return to_core(stage, keep.at[k], wt_send.at[k], wt_recv.at[k])

    def send_weights(k):
        j, kind, half = k // 4, k // 2 % 2, k % 2

        def cast(part, carry):
            stages[k][part] = weight_part(kind, per_core * core + j, half, part)[...].astype(f32)
            return carry

        lax.fori_loop(0, clips, cast, 0)
        weight_copy(stages[k], k).start()

    def take_weights(layer, kind):
        @pl.when(layer // per_core != core)
        def _():
            for half in range(2):
                k = 4 * (layer % per_core) + 2 * kind + half
                weight_copy(outgo.at[0], k).wait_recv()

                def cast(part, carry, half=half, k=k):
                    weight_part(kind, layer, half, part)[...] = keep[k, part].astype(bf16)
                    return carry

                lax.fori_loop(0, clips, cast, 0)

    own_up.wait()
    for k in range(2):
        send_weights(k)
    own_dn.wait()
    for k in range(2, 4):
        send_weights(k)
    par_copy.wait()
    for layer in range(layers):
        for block in range(blocks):
            row = up_bias_row + block // 2
            place = (block % 2) * tile
            up_bias_row_of[layer, block] = params[layer, row : row + 1, place : place + tile]

    def chosen_row(layer, clip, first):
        return jnp.sum(onehot[clip] * params[layer, first : first + 4], axis=0, keepdims=True)

    def norm_clip(layer, clip):
        table = params[layer]
        scale = chosen_row(layer, clip, scale_row)
        shift = chosen_row(layer, clip, shift_row)
        for j in range(chunks):
            window = xs[layer, clip, j * chunk : (j + 1) * chunk + 2 * pad, :]
            conv = window[pad : pad + chunk] * table[3:4] + table[conv_bias_row : conv_bias_row + 1]
            for k in (0, 1, 2, 4, 5, 6):
                conv = conv + window[pad - 3 + k : pad - 3 + k + chunk] * table[k : k + 1]
            centered = conv - jnp.mean(conv, axis=-1, keepdims=True)
            inv = lax.rsqrt(jnp.mean(centered * centered, axis=-1, keepdims=True) + norm_epsilon)
            value = centered * inv
            at = pl.ds(pl.multiple_of(clip * frames + j * chunk, chunk), chunk)
            normed[at, :] = value
            inv_std[at, :] = inv
            adapted[at, :] = (value * scale + shift).astype(bf16)

    def saved_copy(layer, which, back):
        buffer = (hidden if which == 0 else slope).at[layer % 2]
        away = spill.at[layer % 2, which]
        source, target = (away, buffer) if back else (buffer, away)
        return pltpu.make_async_copy(source, target, spill_sem.at[layer % 2, which])

    def norm_copies(layer, back):
        copies = []
        for i, (near, away) in enumerate(((normed, normed_spill), (inv_std, inv_spill), (adapted, adapted_spill))):
            source, target = (away.at[layer], near) if back else (near, away.at[layer])
            copies.append(pltpu.make_async_copy(source, target, norm_sem.at[i]))
        return copies

    branch_sum = g.reshape(rows, width)

    def forward(layer, carry):
        slot = layer % 2

        @pl.when(layer > 0)
        def _():
            for copy in norm_copies(layer - 1, False):
                copy.wait()

        def norm_body(clip, carry):
            norm_clip(layer, clip)
            return carry

        lax.fori_loop(0, clips, norm_body, 0)

        @pl.when(layer == 0)
        def _():
            for k in range(4, 4 * per_core - 1):
                send_weights(k)

        @pl.when(layer < layers - 1)
        def _():
            for copy in norm_copies(layer, False):
                copy.start()

        take_weights(layer, 0)

        @pl.when(layer >= 2)
        def _():
            for which in range(2):
                saved_copy(layer, which, False).wait()

        def up(block):
            columns = slice(block * tile, (block + 1) * tile)
            uppers[block % 2][...] = dot_plain(adapted[...], wup[layer, :, columns])

        def down(block):
            columns = slice(block * tile, (block + 1) * tile)
            value = dot_plain(hidden[slot, :, columns], wdn[layer, columns, :])
            branch_sum[...] = value if block == 0 else branch_sum[...] + value

        downs = {0: (), 1: (), 2: (), 3: (0, 1), 4: (2, 3), 5: (4,)}
        up(0)
        for block in range(blocks):
            columns = slice(block * tile, (block + 1) * tile)
            if block + 1 < blocks:
                up(block + 1)
            if block == blocks // 2:
                take_weights(layer, 1)
            for earlier in downs[block]:
                down(earlier)
            bias = up_bias_row_of[layer, block]
            for q in range(rows // chunk):
                at = slice(q * chunk, (q + 1) * chunk)
                smooth, steep = gelu_and_slope(uppers[block % 2][at, :] + bias)
                hidden[slot, at, columns] = smooth.astype(bf16)
                slope[slot, at, columns] = steep.astype(bf16)
        down(blocks - 1)

        @pl.when(layer < 2)
        def _():
            for which in range(2):
                saved_copy(layer, which, False).start()

        for step in range(layers):

            @pl.when(layer == step)
            def _(step=step):
                for k in [step] if step < layers - 1 else range(layers, 4 * per_core):
                    weight_copy(outgo.at[0], k).wait_send()
                if step == 0:
                    weight_copy(outgo.at[0], layers - 1).wait_send()
                    send_weights(4 * per_core - 1)

        def residual(clip, carry):
            bias = params[layer, down_bias_row : down_bias_row + 1]
            gamma = params[layer, gamma_row : gamma_row + 1]
            branch = g[clip] + bias
            xs[layer + 1, clip, pad : pad + frames, :] = xs[layer, clip, pad : pad + frames, :] + gamma * branch
            return carry

        lax.fori_loop(0, clips, residual, 0)

        def zero_pads(clip, carry):
            xs[layer + 1, clip, 0:pad, :] = jnp.zeros((pad, width), f32)
            xs[layer + 1, clip, pad + frames : 2 * pad + frames, :] = jnp.zeros((pad, width), f32)
            return carry

        lax.fori_loop(0, clips, zero_pads, 0)
        return carry

    lax.fori_loop(0, layers, forward, 0)

    result = xs.at[layers, :, pad : pad + frames]
    result_remote = to_core(result, ends.at[0, :, 0], ends_send.at[0], ends_recv.at[0])
    result_local = pltpu.make_async_copy(result, ends.at[0, :, 1], ends_send.at[1])

    @pl.when(core == 0)
    def _():
        result_remote.start()

    @pl.when(core == 1)
    def _():
        result_local.start()

    for load in loads[clips:]:
        load.wait()

    def load_g(clip, carry):
        g[clip] = gb[pl.ds(pl.multiple_of(clip * frames, frames), frames), :].astype(f32)
        gc[clip, 0:pad, :] = jnp.zeros((pad, width), f32)
        gc[clip, pad + frames : 2 * pad + frames, :] = jnp.zeros((pad, width), f32)
        return carry

    lax.fori_loop(0, clips, load_g, 0)

    matrices = 2 * layers
    lane_count = len(plan.lanes)

    def core_copy(m, parity):
        return to_core(outgo.at[parity], income.at[parity], core_send.at[parity], core_recv.at[parity])

    keep_rows = keep.reshape(matrices, rows, width)

    def offset(lane, stage, side):
        start = 0
        for s in range(stage):
            if plan.halves[lane][s]:
                start = start + choose(plan.lanes[lane][2][s], side, bit_of) * plan.kept[lane][s + 1]
        return start

    def rs_copy(m, parity, lane, stage):
        begin, _, order = plan.lanes[lane]
        size = plan.kept[lane][stage + 1]
        at = begin + offset(lane, stage, core)
        if plan.halves[lane][stage]:
            at = at + (1 - choose(order[stage], core, bit_of)) * size
        starts, _ = plan.slot_rows[stage]
        return to_batch(
            keep_rows.at[m, pl.ds(pl.multiple_of(at, 8), size)],
            stage_in[stage].at[parity, starts[lane] : starts[lane] + size],
            rs_send.at[stage, parity, lane],
            rs_recv.at[stage, parity, lane],
            choose(order[stage], core, partner),
        )

    def rs_add(m, parity, lane, stage):
        begin, _, _ = plan.lanes[lane]
        size = plan.kept[lane][stage + 1]
        at = begin + offset(lane, stage + 1, core)
        starts, _ = plan.slot_rows[stage]
        step = min(size, 2 * chunk)

        def body(i, carry):
            r = pl.multiple_of(at + i * step, 8)
            keep_rows[m, pl.ds(r, step), :] = (
                keep_rows[m, pl.ds(r, step), :]
                + stage_in[stage][parity, pl.ds(pl.multiple_of(starts[lane] + i * step, 8), step), :]
            )
            return carry

        lax.fori_loop(0, size // step, body, 0)

    half_way = matrices // 2
    xs_rows = xs.reshape(layers + 1, clips * (frames + 2 * pad), width)

    def rows_of(m, owner, own, lane, at, size):
        span = pl.ds(pl.multiple_of(plan.lanes[lane][0] + at, 8), size)
        if own:
            return keep_rows.at[m, span]
        return xs_rows.at[layers - m, span] if owner == 1 else keep_rows.at[m - half_way, span]

    def deliver_copy(m, owner, lane):
        size = plan.kept[lane][bits]
        at = offset(lane, bits, 1 - owner)
        return to_core(
            rows_of(m, owner, True, lane, at, size),
            rows_of(m, owner, False, lane, at, size),
            deliver_send.at[m % half_way, lane],
            deliver_recv.at[m % half_way, lane],
        )

    def ag_copy(m, owner, own, parity, lane, stage):
        size = plan.kept[lane][stage + 1]
        side = owner if own else 1 - owner
        place = rows_of(m, owner, own, lane, offset(lane, stage + 1, side), size)
        return to_batch(
            place,
            place,
            ag_send.at[stage, parity, own, lane],
            ag_recv.at[stage, parity, own, lane],
            choose(plan.lanes[lane][2][stage], side, partner),
        )

    def out_copies(m, kind, local, owner):
        copies = []
        third = rows // 3
        for own in range(2):
            half = owner if own else 1 - owner
            if own:
                source = keep_rows.at[m]
            else:
                source = xs_rows.at[layers - m] if owner == 1 else keep_rows.at[m - half_way]
            sem = out_sem.at[m % half_way, own]
            if kind == 0:
                copies.append(pltpu.make_async_copy(source.at[0:rows], down_out.at[local, half], sem.at[0]))
                continue
            for part in range(3):
                columns = slice(part * width, (part + 1) * width)
                copies.append(
                    pltpu.make_async_copy(
                        source.at[part * third : (part + 1) * third],
                        up_out.at[local, half, :, columns],
                        sem.at[part],
                    )
                )
        return copies

    def owner_of(m):
        return 1 - m // half_way

    def owned_by(owner, m):
        return m < half_way if owner == 1 else m >= half_way

    def tick(pair, phase):
        for s in range(2 * bits + 3, 0, -1):
            m = 2 * pair + phase + 1 - s
            parity = (phase + 1 - s) % 2
            kind = parity
            local = (layers - 1 - (m - kind) // 2) % per_core
            valid = (m >= 0) & (m < matrices)

            if s <= bits + 1:

                @pl.when(valid)
                def _(s=s, m=m, parity=parity):
                    if s == 1:
                        core_copy(m, parity).wait()

                        def body(clip, carry):
                            keep[m, clip] = keep[m, clip] + income[parity, clip]
                            return carry

                        lax.fori_loop(0, clips, body, 0)
                    else:
                        for lane in range(lane_count):
                            rs_copy(m, parity, lane, s - 2).wait()
                            if plan.halves[lane][s - 2]:
                                @pl.when(owner_of(m) == core)
                                def _(lane=lane):
                                    pl.semaphore_signal(
                                        credit.at[s - 2, lane],
                                        inc=1,
                                        device_id={"batch": choose(plan.lanes[lane][2][s - 2], core, partner)},
                                        device_id_type=mesh_id,
                                    )

                            rs_add(m, parity, lane, s - 2)
                    if s <= bits:
                        for lane in range(lane_count):
                            rs_copy(m, parity, lane, s - 1).start()

            for owner in range(2):
                if s == bits + 1:

                    @pl.when(valid & owned_by(owner, m) & (core == 1 - owner))
                    def _(m=m, owner=owner):
                        for lane in range(lane_count):
                            deliver_copy(m, owner, lane).start()

                if s > bits + 1:

                    @pl.when(valid & owned_by(owner, m) & (core == owner))
                    def _(s=s, m=m, parity=parity, kind=kind, local=local, owner=owner):
                        if s == bits + 2:
                            for lane in range(lane_count):
                                deliver_copy(m, owner, lane).wait_recv()
                        elif s <= 2 * bits + 2:
                            stage = 2 * bits + 2 - s
                            for lane in range(lane_count):
                                if plan.halves[lane][stage]:
                                    for own in range(2):
                                        ag_copy(m, owner, own, parity, lane, stage).wait()
                        if s <= 2 * bits + 1:
                            stage = 2 * bits + 1 - s
                            for lane in range(lane_count):
                                if plan.halves[lane][stage]:
                                    pl.semaphore_wait(credit.at[stage, lane], 1)
                                    for own in range(2):
                                        ag_copy(m, owner, own, parity, lane, stage).start()
                        elif s == 2 * bits + 2:
                            for copy in out_copies(m, kind, local, owner):
                                copy.start()
                        else:
                            for copy in out_copies(m, kind, local, owner):
                                copy.wait()

        m = 2 * pair + phase - bits
        for owner in range(2):

            @pl.when((m >= 0) & (m < matrices) & owned_by(owner, m) & (core == 1 - owner))
            def _(m=m, owner=owner):
                for lane in range(lane_count):
                    deliver_copy(m, owner, lane).wait_send()

    def store_block(m, phase, second, block, value):
        for q in range(2):
            piece = value[q * frames : (q + 1) * frames]
            if second == 0:
                outgo[phase, 2 * block + q] = piece
            else:
                keep[m, 2 * block + q] = piece

    def scale_clip(layer, clip):
        gamma = params[layer, gamma_row : gamma_row + 1]
        gamma_sum = bias_sum = jnp.zeros((8, width), f32)
        for j in range(chunks):
            here = g[clip, j * chunk : (j + 1) * chunk, :]
            at = slice(pad + j * chunk, pad + (j + 1) * chunk)
            gamma_sum = gamma_sum + fold(here * (xs[layer + 1, clip, at, :] - xs[layer, clip, at, :]))
            value = (gamma * here).astype(bf16)
            gb[pl.ds(pl.multiple_of(clip * frames + j * chunk, chunk), chunk), :] = value
            bias_sum = bias_sum + fold(value.astype(f32))
        sums[0] += gamma_sum
        sums[1] += bias_sum

    def norm_back(layer, clip):
        scale = chosen_row(layer, clip, scale_row)
        scale_sum = shift_sum = conv_sum = jnp.zeros((8, width), f32)
        for j in range(chunks):
            row = pl.ds(pl.multiple_of(clip * frames + j * chunk, chunk), chunk)
            at = slice(pad + j * chunk, pad + (j + 1) * chunk)
            ga = gc[clip, at, :]
            value = normed[row, :]
            scale_sum = scale_sum + fold(ga * value)
            shift_sum = shift_sum + fold(ga)
            dn = ga * scale
            first = jnp.mean(dn, axis=-1, keepdims=True)
            second = jnp.mean(dn * value, axis=-1, keepdims=True)
            result = inv_std[row, :] * (dn - first - value * second)
            gc[clip, at, :] = result
            conv_sum = conv_sum + fold(result)
        sums[9] += conv_sum
        choice = onehot[clip]
        small[layer, scale_row : scale_row + 4, :] += choice * jnp.sum(scale_sum, axis=0, keepdims=True)
        small[layer, shift_row : shift_row + 4, :] += choice * jnp.sum(shift_sum, axis=0, keepdims=True)

    def conv_back(layer, clip):
        table = params[layer]
        totals = [jnp.zeros((8, width), f32) for _ in range(7)]
        for j in range(chunks):
            grads = gc[clip, j * chunk : (j + 1) * chunk + 2 * pad, :]
            signal = xs[layer, clip, pad + j * chunk : pad + (j + 1) * chunk, :]
            at = slice(j * chunk, (j + 1) * chunk)
            total = g[clip, at, :]
            for k in (3, 0, 1, 2, 4, 5, 6):
                shifted = grads[pad + 3 - k : pad + 3 - k + chunk]
                total = total + shifted * table[k : k + 1]
                totals[k] = totals[k] + fold(signal * shifted)
            g[clip, at, :] = total
        for k in range(7):
            sums[2 + k] += totals[k]

    def backward(pair, carry):
        layer = layers - 1 - pair
        slot = layer % 2

        @pl.when((pair == 1) & (core == 0))
        def _():
            result_remote.wait_send()

        @pl.when((pair == 1) & (core == 1))
        def _():
            result_local.wait()

        sums[...] = jnp.zeros(sums.shape, f32)
        small[layer] = jnp.zeros(small.shape[1:], f32)

        def scale_body(clip, carry):
            scale_clip(layer, clip)
            return carry

        lax.fori_loop(0, clips, scale_body, 0)

        @pl.when(layer < 2)
        def _():
            for which in range(2):
                saved_copy(layer, which, True).wait()

        def up_grad(block):
            columns = pl.ds(pl.multiple_of(block * tile, tile), tile)
            value = dot_cols(gb[...], wdn[layer, columns, :])
            total = jnp.zeros((8, tile), f32)
            for q in range(rows // chunk):
                at = slice(q * chunk, (q + 1) * chunk)
                piece = (value[at] * slope[slot, at, columns].astype(f32)).astype(bf16)
                slope[slot, at, columns] = piece
                total = total + fold(piece.astype(f32))
            up_sums[block] = total

        for second in range(2):
            half = other if second == 0 else core

            def down_body(block, carry, second=second, half=half):
                at = pl.ds(pl.multiple_of(half * rows + block * tile, tile), tile)
                store_block(2 * pair, 0, second, block, dot_rows(hidden[slot, :, at], gb[...]))
                up_grad(block + 3 * second)
                return carry

            lax.fori_loop(0, clips // 2, down_body, 0)
            if second == 0:
                core_copy(2 * pair, 0).start()

        @pl.when(pair > 0)
        def _():
            for copy in norm_copies(layer, True):
                copy.wait()

        tick(pair, 0)

        def up_weight_grad(second, block):
            half = other if second == 0 else core
            at = pl.ds(pl.multiple_of(half * (width // 2), width // 2), width // 2)
            columns = pl.ds(pl.multiple_of(block * width, width), width)
            store_block(2 * pair + 1, 1, second, block, dot_rows(adapted[:, at], slope[slot, :, columns]))

        def adapted_grad(i):
            r = pl.multiple_of(i * tile, tile)
            value = dot_cols(slope[slot, pl.ds(r, tile), :], wup[layer])
            for q in range(2):
                gc[2 * i + q, pad : pad + frames, :] = value[q * frames : (q + 1) * frames]

        def norm_conv_back(i):
            for q in range(2):
                norm_back(layer, 2 * i + q)
                conv_back(layer, 2 * i + q)

        adapted_grad(0)
        up_weight_grad(0, 0)

        def tile_body(i, carry):
            adapted_grad(i + 1)
            up_weight_grad(0, i + 1)
            norm_conv_back(i)
            return carry

        lax.fori_loop(0, rows // tile - 1, tile_body, 0)
        core_copy(2 * pair + 1, 1).start()
        for block in range(3):
            up_weight_grad(1, block)
        norm_conv_back(rows // tile - 1)

        @pl.when(layer > 0)
        def _():
            for copy in norm_copies(layer - 1, True):
                copy.start()

        @pl.when(layer >= 2)
        def _():
            for which in range(2):
                saved_copy(layer, which, True).start()

        gamma = params[layer, gamma_row : gamma_row + 1, :]
        small[layer, gamma_row : gamma_row + 1, :] = jnp.sum(sums[0], axis=0, keepdims=True) / gamma
        small[layer, down_bias_row : down_bias_row + 1, :] = jnp.sum(sums[1], axis=0, keepdims=True)
        for block in range(blocks):
            row = up_bias_row + block // 2
            place = (block % 2) * tile
            small[layer, row : row + 1, place : place + tile] = jnp.sum(up_sums[block], axis=0, keepdims=True)
        for k in range(7):
            small[layer, taps_row + k : taps_row + k + 1, :] = jnp.sum(sums[2 + k], axis=0, keepdims=True)
        small[layer, conv_bias_row : conv_bias_row + 1, :] = jnp.sum(sums[9], axis=0, keepdims=True)
        tick(pair, 1)
        return carry

    lax.fori_loop(0, layers, backward, 0)

    grad_remote = to_core(g, ends.at[0, :, 1], ends_send.at[2], ends_recv.at[1])
    grad_local = pltpu.make_async_copy(g, ends.at[0, :, 0], ends_send.at[3])

    @pl.when(core == 0)
    def _():
        grad_local.start()

    @pl.when(core == 1)
    def _():
        grad_remote.start()

    small_core = to_core(
        small.at[pl.ds(per_core * other, per_core)], small_in.at[bits], small_send.at[bits], small_recv.at[bits]
    )
    small_core.start()

    def small_copy(bit):
        return to_batch(small_sum, small_in.at[bit], small_send.at[bit], small_recv.at[bit], partner(bit))

    def drain(pair, carry):
        for phase in range(2):
            tick(pair, phase)
            for step in range(bits + 1):

                @pl.when(2 * pair + phase - matrices == step)
                def _(step=step):
                    if step == 0:
                        small_core.wait()
                        small_sum[...] = small[pl.ds(per_core * core, per_core)] + small_in[bits]
                    else:
                        small_copy(step - 1).wait()
                        small_sum[...] = small_sum[...] + small_in[step - 1]
                    if step < bits:
                        small_copy(step).start()

        return carry

    lax.fori_loop(layers, layers + bits + 1, drain, 0)
    small_out[...] = small_sum[...]

    @pl.when(core == 0)
    def _():
        grad_local.wait()
        grad_remote.wait_recv()

    @pl.when(core == 1)
    def _():
        result_remote.wait_recv()
        grad_remote.wait_send()


def results_kernel(
    ends,
    up_grad,
    down_grad,
    small,
    ends_out,
    conv_kernel_out,
    conv_bias_out,
    band_scale_out,
    band_shift_out,
    up_out,
    up_bias_out,
    down_out,
    down_bias_out,
    layer_scale_out,
    ends_stage,
    up_stage,
    down_stage,
    in_sem,
    out_sem,
):
    copies = []
    per_core, _, width = small.shape
    for clip in range(ends.shape[1]):
        copies.append((ends.at[0, clip], ends_stage.at[clip], ends_out.at[0, clip]))
    for j in range(per_core):
        for half in range(2):
            for source, stage, target in ((up_grad, up_stage, up_out), (down_grad, down_stage, down_out)):
                size = source.shape[2] // 2
                for part in range(2):
                    at = (j, half, slice(part * size, (part + 1) * size))
                    copies.append((source.at[at], stage.at[at], target.at[at]))
    loads = [pltpu.make_async_copy(a, b, in_sem.at[i]) for i, (a, b, _) in enumerate(copies)]
    stores = [pltpu.make_async_copy(b, c, out_sem.at[i]) for i, (_, b, c) in enumerate(copies)]
    ahead = 6
    for load in loads[:ahead]:
        load.start()
    for i, (load, store) in enumerate(zip(loads, stores)):
        load.wait()
        store.start()
        if i + ahead < len(loads):
            loads[i + ahead].start()
    for j in range(per_core):
        conv_kernel_out[:, j] = small[j, taps_row : taps_row + 7]
        conv_bias_out[j : j + 1] = small[j, conv_bias_row : conv_bias_row + 1]
        band_scale_out[j] = small[j, scale_row : scale_row + 4]
        band_shift_out[j] = small[j, shift_row : shift_row + 4]
        for q in range(3):
            row = up_bias_row + q
            up_bias_out[j : j + 1, q * width : (q + 1) * width] = small[j, row : row + 1]
        down_bias_out[j : j + 1] = small[j, down_bias_row : down_bias_row + 1]
        layer_scale_out[j : j + 1] = small[j, gamma_row : gamma_row + 1]
    for store in stores:
        store.wait()


def body(
    inputs,
    grad_out,
    band_ids,
    conv_kernel,
    conv_bias,
    band_scale,
    band_shift,
    up_weight,
    up_bias,
    down_weight,
    down_bias,
    layer_scale,
):
    sections = lax.axis_size("section")
    batch = lax.axis_size("batch")
    clips, local_clips, frames, width = inputs.shape
    per_core, _, hidden_width = up_weight.shape
    layers = per_core * sections
    bands = band_scale.shape[1]
    rows = clips * frames
    assert sections == 2 and local_clips == 2 and batch & (batch - 1) == 0
    assert hidden_width == 3 * width and bands == 4 and layers == 4 and rows == 3 * width // 2
    plan = Plan(batch, rows)
    bits = plan.bits
    hbm = pl.BlockSpec(memory_space=pl.ANY)
    vmem = pl.BlockSpec(memory_space=pltpu.VMEM)
    smem = pl.BlockSpec(memory_space=pltpu.SMEM)
    padded = frames + 2 * pad
    dma = pltpu.SemaphoreType.DMA
    lanes = len(plan.lanes)
    tile = 2 * frames
    ends_shape = jax.ShapeDtypeStruct((1, clips, local_clips, frames, width), f32)
    up_shape = jax.ShapeDtypeStruct((per_core, 2, width // 2, hidden_width), f32)
    down_shape = jax.ShapeDtypeStruct((per_core, 2, hidden_width // 2, width), f32)
    small_shape = jax.ShapeDtypeStruct((per_core, packed_rows, width), f32)
    conv_kernel = jnp.transpose(conv_kernel, (1, 0, 2))
    ends, up_grad, down_grad, small, *_ = pl.pallas_call(
        functools.partial(step_kernel, plan),
        out_shape=[
            ends_shape,
            up_shape,
            down_shape,
            small_shape,
            jax.ShapeDtypeStruct((2, 2, rows, hidden_width), bf16),
            jax.ShapeDtypeStruct((layers - 1, rows, width), f32),
            jax.ShapeDtypeStruct((layers - 1, rows, 1), f32),
            jax.ShapeDtypeStruct((layers - 1, rows, width), bf16),
        ],
        in_specs=[hbm, hbm, smem, vmem, vmem, vmem, vmem, hbm, vmem, hbm, vmem, vmem],
        out_specs=[hbm, hbm, hbm, vmem, hbm, hbm, hbm, hbm],
        scratch_shapes=[
            pltpu.VMEM((layers + 1, clips, padded, width), f32),
            pltpu.VMEM((rows, width), f32),
            pltpu.VMEM((rows, 1), f32),
            pltpu.VMEM((rows, width), bf16),
            pltpu.VMEM((2, rows, hidden_width), bf16),
            pltpu.VMEM((2, rows, hidden_width), bf16),
            pltpu.VMEM((rows, width), bf16),
            pltpu.VMEM((clips, frames, width), f32),
            pltpu.VMEM((clips, padded, width), f32),
            pltpu.VMEM((layers, width, hidden_width), bf16),
            pltpu.VMEM((layers, hidden_width, width), bf16),
            pltpu.VMEM((per_core, packed_rows, width), f32),
            pltpu.VMEM((layers, packed_rows, width), f32),
            pltpu.VMEM((layers, hidden_width // tile, 1, tile), f32),
            pltpu.VMEM((rows, tile), f32),
            pltpu.VMEM((rows, tile), f32),
            pltpu.VMEM((clips, bands, width), f32),
            pltpu.VMEM((10, 8, width), f32),
            pltpu.VMEM((hidden_width // tile, 8, tile), f32),
            pltpu.VMEM((layers, packed_rows, width), f32),
            pltpu.VMEM((2 * layers, clips, frames, width), f32),
            pltpu.VMEM((2, clips, frames, width), f32),
            pltpu.VMEM((2, clips, frames, width), f32),
            pltpu.VMEM((per_core, packed_rows, width), f32),
            pltpu.VMEM((bits + 1, per_core, packed_rows, width), f32),
            *[pltpu.VMEM((2, plan.slot_rows[stage][1], width), f32) for stage in range(bits)],
            dma((2 + 2 * clips,)),
            dma((4 * per_core,)),
            dma((4 * per_core,)),
            dma((1,)),
            dma((1,)),
            dma((4,)),
            dma((2,)),
            dma((2,)),
            dma((2,)),
            dma((bits, 2, lanes)),
            dma((bits, 2, lanes)),
            dma((layers, lanes)),
            dma((layers, lanes)),
            dma((bits, 2, 2, lanes)),
            dma((bits, 2, 2, lanes)),
            dma((layers, 2, 3)),
            pltpu.SemaphoreType.REGULAR((bits, lanes)),
            dma((bits + 1,)),
            dma((bits + 1,)),
            dma((2, 2)),
            dma((3,)),
        ],
        compiler_params=pltpu.CompilerParams(
            collective_id=0, has_side_effects=True, vmem_limit_bytes=255 * 2**18
        ),
        cost_estimate=pl.CostEstimate(
            flops=24 * rows * width * hidden_width * 2, bytes_accessed=2**26, transcendentals=2**24
        ),
        name="blocks_step",
    )(
        inputs,
        grad_out,
        jnp.transpose(band_ids),
        conv_kernel,
        conv_bias,
        band_scale,
        band_shift,
        up_weight,
        up_bias,
        down_weight,
        down_bias,
        layer_scale,
    )

    def like(array):
        return jax.ShapeDtypeStruct(array.shape, f32)

    outs = pl.pallas_call(
        results_kernel,
        out_shape=[
            ends_shape,
            like(conv_kernel),
            like(conv_bias),
            like(band_scale),
            like(band_shift),
            up_shape,
            like(up_bias),
            down_shape,
            like(down_bias),
            like(layer_scale),
        ],
        in_specs=[hbm, hbm, hbm, vmem],
        out_specs=[hbm, vmem, vmem, vmem, vmem, hbm, vmem, hbm, vmem, vmem],
        scratch_shapes=[
            pltpu.VMEM(ends_shape.shape[1:], f32),
            pltpu.VMEM(up_shape.shape, f32),
            pltpu.VMEM(down_shape.shape, f32),
            dma((8 * per_core + clips,)),
            dma((8 * per_core + clips,)),
        ],
        compiler_params=pltpu.CompilerParams(vmem_limit_bytes=255 * 2**18),
        cost_estimate=pl.CostEstimate(flops=0, bytes_accessed=2**25, transcendentals=0),
        name="results",
    )(ends, up_grad, down_grad, small)
    outs = list(outs)
    outs[1] = jnp.transpose(outs[1], (1, 0, 2))
    outs[5] = outs[5].reshape(up_weight.shape)
    outs[7] = outs[7].reshape(down_weight.shape)
    return tuple(outs)


def solution(mesh):
    in_specs = (
        P(None, "batch", None, None),
        P(None, "batch", None, None),
        P(None, "batch"),
        P("section", None, None),
        P("section", None),
        P("section", None, None),
        P("section", None, None),
        P("section", None, None),
        P("section", None),
        P("section", None, None),
        P("section", None),
        P("section", None),
    )
    out_specs = (
        P("section", None, "batch", None, None),
        P("section", None, None),
        P("section", None),
        P("section", None, None),
        P("section", None, None),
        P("section", None, None),
        P("section", None),
        P("section", None, None),
        P("section", None),
        P("section", None),
    )
    return jax.shard_map(body, mesh=mesh, in_specs=in_specs, out_specs=out_specs, check_vma=False)
```

```python
import functools

import jax
import jax.numpy as jnp
from jax import lax
from jax.experimental import pallas as pl
from jax.experimental.pallas import tpu as pltpu
from jax.sharding import PartitionSpec as P

norm_epsilon = 1e-06
f32 = jnp.float32
bf16 = jnp.bfloat16

log_density = -1.3257480647361593

taps_row, conv_bias_row, scale_row, shift_row, up_bias_row, down_bias_row, gamma_row = 0, 7, 8, 12, 16, 19, 20
packed_rows = 24
pad = 8
chunk = 32


def gelu_and_slope(u):
    cdf = 0.5 * lax.erf(u * 0.7071067811865476) + 0.5
    density = jnp.exp2(u * (u * (-0.5 * 1.4426950408889634)) + log_density)
    return u * cdf, cdf + u * density


def fold(values):
    rows, columns = values.shape
    return jnp.sum(values.reshape(rows // 8, 8, columns), axis=0)


def dot_plain(left, right):
    return lax.dot_general(left, right, (((1,), (0,)), ((), ())), preferred_element_type=f32)


def dot_cols(left, right):
    return lax.dot_general(left, right, (((1,), (1,)), ((), ())), preferred_element_type=f32)


class Plan:
    def __init__(self, batch, rows):
        self.bits = batch.bit_length() - 1
        order = [(bit, bit) for bit in range(self.bits)]
        if self.bits > 1:
            order[:2] = [(0, 1), (1, 0)]
        late = order[:]
        if self.bits > 2:
            late = [order[2]] + order[:2] + order[3:]
        third = rows // 3
        self.lanes = [(0, 2 * third, order), (2 * third, third, late)]
        self.kept = []
        self.halves = []
        self.slot_rows = []
        for _, size, _ in self.lanes:
            kept, halves = [size], []
            for _ in range(self.bits):
                halves.append(kept[-1] // 2 >= 8)
                kept.append(kept[-1] // 2 if halves[-1] else kept[-1])
            self.kept.append(kept)
            self.halves.append(halves)
        for stage in range(self.bits):
            begin, starts = 0, []
            for lane in range(len(self.lanes)):
                starts.append(begin)
                begin += self.kept[lane][stage + 1]
            self.slot_rows.append((starts, begin))


def step_kernel(
    plan,
    inputs,
    grad_out,
    band_ids,
    conv_kernel,
    conv_bias,
    band_scale,
    band_shift,
    up_weight,
    up_bias,
    down_weight,
    down_bias,
    layer_scale,
    ends,
    up_out,
    down_out,
    small_out,
    hidden_spill,
    slope_spill,
    normed_spill,
    inv_spill,
    adapted_spill,
    xs,
    normed,
    inv_std,
    adapted_t,
    hidden_t,
    slope,
    hidden_near,
    gb,
    g,
    gc,
    wup,
    wdn,
    packed,
    params,
    up_bias_row_of,
    upper_even,
    upper_odd,
    onehot,
    sums,
    up_sums,
    small,
    keep,
    outgo,
    income,
    small_sum,
    small_in,
    *rest,
):
    stage_in = rest[: plan.bits]
    (
        load_sem,
        wt_send,
        wt_recv,
        par_send,
        par_recv,
        ends_send,
        ends_recv,
        core_send,
        core_recv,
        rs_send,
        rs_recv,
        deliver_send,
        deliver_recv,
        ag_send,
        ag_recv,
        out_sem,
        credit,
        small_send,
        small_recv,
        spill_sem,
        norm_sem,
    ) = rest[plan.bits :]
    uppers = (upper_even, upper_odd)
    core = lax.axis_index("section")
    other = 1 - core
    batch = lax.axis_index("batch")
    clips, frames, width = g.shape
    rows = clips * frames
    layers = xs.shape[0] - 1
    per_core = layers // 2
    hidden_width = slope.shape[2]
    tile = 2 * frames
    chunks = frames // chunk
    blocks = hidden_width // tile
    bits = plan.bits
    mesh_id = pl.DeviceIdType.MESH

    def bit_of(bit):
        return (batch // (1 << bit)) % 2

    def partner(bit):
        return batch + (1 - 2 * bit_of(bit)) * (1 << bit)

    def choose(pair, side, value):
        first, second = pair
        if first == second:
            return value(first)
        if isinstance(side, int):
            return value(pair[side])
        return (1 - side) * value(first) + side * value(second)

    def to_core(source, target, send, recv):
        return pltpu.make_async_remote_copy(source, target, send, recv, {"section": other}, mesh_id)

    def to_batch(source, target, send, recv, device):
        return pltpu.make_async_remote_copy(source, target, send, recv, {"batch": device}, mesh_id)

    own_blocks = pl.ds(per_core * core, per_core)
    own_up = pltpu.make_async_copy(up_weight, wup.at[own_blocks], load_sem.at[0])
    own_dn = pltpu.make_async_copy(down_weight, wdn.at[own_blocks], load_sem.at[1])
    own_up.start()
    own_dn.start()
    loads = []
    for source, target in ((inputs, slope.at[0, :, 0:width]), (grad_out, gb)):
        for clip in range(clips):
            loads.append(
                pltpu.make_async_copy(
                    source.at[clip, core], target.at[pl.ds(clip * frames, frames)], load_sem.at[2 + len(loads)]
                )
            )
    for load in loads:
        load.start()

    for j in range(per_core):
        packed[j, taps_row : taps_row + 7] = conv_kernel[:, j]
        packed[j, conv_bias_row : conv_bias_row + 1] = conv_bias[j : j + 1]
        packed[j, scale_row : scale_row + 4] = band_scale[j]
        packed[j, shift_row : shift_row + 4] = band_shift[j]
        for q in range(3):
            row = up_bias_row + q
            packed[j, row : row + 1] = up_bias[j : j + 1, q * width : (q + 1) * width]
        packed[j, down_bias_row : down_bias_row + 1] = down_bias[j : j + 1]
        packed[j, gamma_row : gamma_row + 1] = layer_scale[j : j + 1]
        packed[j, gamma_row + 1 : packed_rows] = jnp.zeros((packed_rows - gamma_row - 1, width), f32)

    barrier = pltpu.get_barrier_semaphore()
    pl.semaphore_signal(barrier, inc=1, device_id={"section": other}, device_id_type=mesh_id)
    for bit in range(bits):
        pl.semaphore_signal(barrier, inc=1, device_id={"batch": partner(bit)}, device_id_type=mesh_id)

    for load in loads[:clips]:
        load.wait()

    def load_x(clip, carry):
        xs[0, clip, 0:pad, :] = jnp.zeros((pad, width), f32)
        xs[0, clip, pad + frames : 2 * pad + frames, :] = jnp.zeros((pad, width), f32)
        xs[0, clip, pad : pad + frames, :] = slope[
            0, pl.ds(pl.multiple_of(clip * frames, frames), frames), 0:width
        ].astype(f32)
        for band in range(4):
            chosen = jnp.where(band_ids[core, clip] == band, 1.0, 0.0).astype(f32)
            onehot[clip, band : band + 1] = jnp.zeros((1, width), f32) + chosen
        return carry

    lax.fori_loop(0, clips, load_x, 0)
    pl.semaphore_wait(barrier, 1 + bits)

    par_copy = to_core(packed, params.at[own_blocks], par_send.at[0], par_recv.at[0])
    par_copy.start()
    params[own_blocks] = packed[...]

    stages = [
        xs.at[1, :, 0:frames],
        xs.at[2, :, 0:frames],
        xs.at[3, :, 0:frames],
        outgo.at[0],
        outgo.at[1],
        xs.at[4, :, 0:frames],
        gc.at[:, 0:frames],
        outgo.at[0],
    ]

    def weight_part(kind, layer, half, part):
        if kind == 0:
            return wup.at[
                layer,
                pl.ds(pl.multiple_of(half * (width // 2) + (part % 2) * frames, frames), frames),
                pl.ds(pl.multiple_of((part // 2) * width, width), width),
            ]
        return wdn.at[layer, pl.ds(pl.multiple_of(half * rows + part * frames, frames), frames), :]

    def weight_copy(stage, k):
        return to_core(stage, keep.at[k], wt_send.at[k], wt_recv.at[k])

    def send_weights(k):
        j, kind, half = k // 4, k // 2 % 2, k % 2

        def cast(part, carry):
            stages[k][part] = weight_part(kind, per_core * core + j, half, part)[...].astype(f32)
            return carry

        lax.fori_loop(0, clips, cast, 0)
        weight_copy(stages[k], k).start()

    def take_weights(layer, kind):
        @pl.when(layer // per_core != core)
        def _():
            for half in range(2):
                k = 4 * (layer % per_core) + 2 * kind + half
                weight_copy(outgo.at[0], k).wait_recv()

                def cast(part, carry, half=half, k=k):
                    weight_part(kind, layer, half, part)[...] = keep[k, part].astype(bf16)
                    return carry

                lax.fori_loop(0, clips, cast, 0)

    own_up.wait()
    for k in range(2):
        send_weights(k)
    own_dn.wait()
    for k in range(2, 4):
        send_weights(k)
    par_copy.wait()
    for layer in range(layers):
        for block in range(blocks):
            row = up_bias_row + block // 2
            place = (block % 2) * tile
            up_bias_row_of[layer, block] = params[layer, row : row + 1, place : place + tile]

    def chosen_row(layer, clip, first):
        return jnp.sum(onehot[clip] * params[layer, first : first + 4], axis=0, keepdims=True)

    adapted_place = slice(hidden_width - width, hidden_width)

    def norm_clip(layer, clip):
        table = params[layer]
        scale = chosen_row(layer, clip, scale_row)
        shift = chosen_row(layer, clip, shift_row)
        for j in range(chunks):
            window = xs[layer, clip, j * chunk : (j + 1) * chunk + 2 * pad, :]
            conv = window[pad : pad + chunk] * table[3:4] + table[conv_bias_row : conv_bias_row + 1]
            for k in (0, 1, 2, 4, 5, 6):
                conv = conv + window[pad - 3 + k : pad - 3 + k + chunk] * table[k : k + 1]
            centered = conv - jnp.mean(conv, axis=-1, keepdims=True)
            inv = lax.rsqrt(jnp.mean(centered * centered, axis=-1, keepdims=True) + norm_epsilon)
            value = centered * inv
            at = pl.ds(pl.multiple_of(clip * frames + j * chunk, chunk), chunk)
            normed[at, :] = value
            inv_std[at, :] = inv
            slope[layer % 2, at, adapted_place] = (value * scale + shift).astype(bf16)

    def saved_copy(layer, which, back):
        buffer = (hidden_t if which == 0 else slope).at[layer % 2]
        away = (hidden_spill if which == 0 else slope_spill).at[layer % 2]
        source, target = (away, buffer) if back else (buffer, away)
        return pltpu.make_async_copy(source, target, spill_sem.at[layer % 2, which])

    def norm_copies(layer, back):
        copies = []
        for i, (near, away) in enumerate(((normed, normed_spill), (inv_std, inv_spill), (adapted_t, adapted_spill))):
            source, target = (away.at[layer], near) if back else (near, away.at[layer])
            copies.append(pltpu.make_async_copy(source, target, norm_sem.at[i]))
        return copies

    branch_sum = g.reshape(rows, width)

    def forward(layer, carry):
        slot = layer % 2

        @pl.when(layer > 0)
        def _():
            for copy in norm_copies(layer - 1, False):
                copy.wait()

        @pl.when(layer >= 2)
        def _():
            for which in range(2):
                saved_copy(layer, which, False).wait()

        def norm_body(clip, carry):
            norm_clip(layer, clip)
            return carry

        lax.fori_loop(0, clips, norm_body, 0)

        @pl.when(layer == 0)
        def _():
            for k in range(4, 4 * per_core - 1):
                send_weights(k)

        take_weights(layer, 0)

        def up(block):
            columns = slice(block * tile, (block + 1) * tile)
            uppers[block % 2][...] = dot_plain(slope[slot, :, adapted_place], wup[layer, :, columns])

        def down(block):
            columns = slice(block * tile, (block + 1) * tile)
            here = hidden_near[block % 2]
            value = dot_plain(here, wdn[layer, columns, :])
            branch_sum[...] = value if block == 0 else branch_sum[...] + value
            hidden_t[slot, columns, :] = here.T

        up(0)
        for block in range(blocks):
            columns = slice(block * tile, (block + 1) * tile)
            if block + 1 < blocks:
                up(block + 1)
            if block == 0:
                adapted_t[...] = slope[slot, :, adapted_place].T
            if block == 1:
                take_weights(layer, 1)
            if block > 0:
                down(block - 1)
            bias = up_bias_row_of[layer, block]
            for q in range(rows // chunk):
                at = slice(q * chunk, (q + 1) * chunk)
                smooth, steep = gelu_and_slope(uppers[block % 2][at, :] + bias)
                hidden_near[block % 2, at, :] = smooth.astype(bf16)
                slope[slot, at, columns] = steep.astype(bf16)
        down(blocks - 1)

        @pl.when(layer < layers - 1)
        def _():
            for copy in norm_copies(layer, False):
                copy.start()

        @pl.when(layer < 2)
        def _():
            for which in range(2):
                saved_copy(layer, which, False).start()

        for step in range(layers):

            @pl.when(layer == step)
            def _(step=step):
                for k in [step] if step < layers - 1 else range(layers, 4 * per_core):
                    weight_copy(outgo.at[0], k).wait_send()
                if step == 0:
                    weight_copy(outgo.at[0], layers - 1).wait_send()
                    send_weights(4 * per_core - 1)

        def residual(clip, carry):
            bias = params[layer, down_bias_row : down_bias_row + 1]
            gamma = params[layer, gamma_row : gamma_row + 1]
            branch = g[clip] + bias
            xs[layer + 1, clip, pad : pad + frames, :] = xs[layer, clip, pad : pad + frames, :] + gamma * branch
            return carry

        lax.fori_loop(0, clips, residual, 0)

        def zero_pads(clip, carry):
            xs[layer + 1, clip, 0:pad, :] = jnp.zeros((pad, width), f32)
            xs[layer + 1, clip, pad + frames : 2 * pad + frames, :] = jnp.zeros((pad, width), f32)
            return carry

        lax.fori_loop(0, clips, zero_pads, 0)
        return carry

    lax.fori_loop(0, layers, forward, 0)

    result = xs.at[layers, :, pad : pad + frames]
    result_remote = to_core(result, ends.at[0, :, 0], ends_send.at[0], ends_recv.at[0])
    result_local = pltpu.make_async_copy(result, ends.at[0, :, 1], ends_send.at[1])

    @pl.when(core == 0)
    def _():
        result_remote.start()

    @pl.when(core == 1)
    def _():
        result_local.start()

    for load in loads[clips:]:
        load.wait()

    def load_g(clip, carry):
        g[clip] = gb[pl.ds(pl.multiple_of(clip * frames, frames), frames), :].astype(f32)
        gc[clip, 0:pad, :] = jnp.zeros((pad, width), f32)
        gc[clip, pad + frames : 2 * pad + frames, :] = jnp.zeros((pad, width), f32)
        return carry

    lax.fori_loop(0, clips, load_g, 0)

    matrices = 2 * layers
    lane_count = len(plan.lanes)

    def core_copy(m, parity):
        return to_core(outgo.at[parity], income.at[parity], core_send.at[parity], core_recv.at[parity])

    keep_rows = keep.reshape(matrices, rows, width)

    def offset(lane, stage, side):
        start = 0
        for s in range(stage):
            if plan.halves[lane][s]:
                start = start + choose(plan.lanes[lane][2][s], side, bit_of) * plan.kept[lane][s + 1]
        return start

    def rs_copy(m, parity, lane, stage):
        begin, _, order = plan.lanes[lane]
        size = plan.kept[lane][stage + 1]
        at = begin + offset(lane, stage, core)
        if plan.halves[lane][stage]:
            at = at + (1 - choose(order[stage], core, bit_of)) * size
        starts, _ = plan.slot_rows[stage]
        return to_batch(
            keep_rows.at[m, pl.ds(pl.multiple_of(at, 8), size)],
            stage_in[stage].at[parity, starts[lane] : starts[lane] + size],
            rs_send.at[stage, parity, lane],
            rs_recv.at[stage, parity, lane],
            choose(order[stage], core, partner),
        )

    def rs_add(m, parity, lane, stage):
        begin, _, _ = plan.lanes[lane]
        size = plan.kept[lane][stage + 1]
        at = begin + offset(lane, stage + 1, core)
        starts, _ = plan.slot_rows[stage]
        step = min(size, 2 * chunk)

        def body(i, carry):
            r = pl.multiple_of(at + i * step, 8)
            keep_rows[m, pl.ds(r, step), :] = (
                keep_rows[m, pl.ds(r, step), :]
                + stage_in[stage][parity, pl.ds(pl.multiple_of(starts[lane] + i * step, 8), step), :]
            )
            return carry

        lax.fori_loop(0, size // step, body, 0)

    half_way = matrices // 2
    xs_rows = xs.reshape(layers + 1, clips * (frames + 2 * pad), width)

    def rows_of(m, owner, own, lane, at, size):
        span = pl.ds(pl.multiple_of(plan.lanes[lane][0] + at, 8), size)
        if own:
            return keep_rows.at[m, span]
        return xs_rows.at[layers - m, span] if owner == 1 else keep_rows.at[m - half_way, span]

    def deliver_copy(m, owner, lane):
        size = plan.kept[lane][bits]
        at = offset(lane, bits, 1 - owner)
        return to_core(
            rows_of(m, owner, True, lane, at, size),
            rows_of(m, owner, False, lane, at, size),
            deliver_send.at[m % half_way, lane],
            deliver_recv.at[m % half_way, lane],
        )

    def ag_copy(m, owner, own, parity, lane, stage):
        size = plan.kept[lane][stage + 1]
        side = owner if own else 1 - owner
        place = rows_of(m, owner, own, lane, offset(lane, stage + 1, side), size)
        return to_batch(
            place,
            place,
            ag_send.at[stage, parity, own, lane],
            ag_recv.at[stage, parity, own, lane],
            choose(plan.lanes[lane][2][stage], side, partner),
        )

    def out_copies(m, kind, local, owner):
        copies = []
        third = rows // 3
        for own in range(2):
            half = owner if own else 1 - owner
            if own:
                source = keep_rows.at[m]
            else:
                source = xs_rows.at[layers - m] if owner == 1 else keep_rows.at[m - half_way]
            sem = out_sem.at[m % half_way, own]
            if kind == 0:
                copies.append(pltpu.make_async_copy(source.at[0:rows], down_out.at[local, half], sem.at[0]))
                continue
            for part in range(3):
                columns = slice(part * width, (part + 1) * width)
                copies.append(
                    pltpu.make_async_copy(
                        source.at[part * third : (part + 1) * third],
                        up_out.at[local, half, :, columns],
                        sem.at[part],
                    )
                )
        return copies

    def owner_of(m):
        return 1 - m // half_way

    def owned_by(owner, m):
        return m < half_way if owner == 1 else m >= half_way

    def tick(pair, phase):
        for s in range(2 * bits + 3, 0, -1):
            m = 2 * pair + phase + 1 - s
            parity = (phase + 1 - s) % 2
            kind = parity
            local = (layers - 1 - (m - kind) // 2) % per_core
            valid = (m >= 0) & (m < matrices)

            if s <= bits + 1:

                @pl.when(valid)
                def _(s=s, m=m, parity=parity):
                    if s == 1:
                        core_copy(m, parity).wait()

                        def body(clip, carry):
                            keep[m, clip] = keep[m, clip] + income[parity, clip]
                            return carry

                        lax.fori_loop(0, clips, body, 0)
                    else:
                        for lane in range(lane_count):
                            rs_copy(m, parity, lane, s - 2).wait()
                            if plan.halves[lane][s - 2]:
                                @pl.when(owner_of(m) == core)
                                def _(lane=lane):
                                    pl.semaphore_signal(
                                        credit.at[s - 2, lane],
                                        inc=1,
                                        device_id={"batch": choose(plan.lanes[lane][2][s - 2], core, partner)},
                                        device_id_type=mesh_id,
                                    )

                            rs_add(m, parity, lane, s - 2)
                    if s <= bits:
                        for lane in range(lane_count):
                            rs_copy(m, parity, lane, s - 1).start()

            for owner in range(2):
                if s == bits + 1:

                    @pl.when(valid & owned_by(owner, m) & (core == 1 - owner))
                    def _(m=m, owner=owner):
                        for lane in range(lane_count):
                            deliver_copy(m, owner, lane).start()

                if s > bits + 1:

                    @pl.when(valid & owned_by(owner, m) & (core == owner))
                    def _(s=s, m=m, parity=parity, kind=kind, local=local, owner=owner):
                        if s == bits + 2:
                            for lane in range(lane_count):
                                deliver_copy(m, owner, lane).wait_recv()
                        elif s <= 2 * bits + 2:
                            stage = 2 * bits + 2 - s
                            for lane in range(lane_count):
                                if plan.halves[lane][stage]:
                                    for own in range(2):
                                        ag_copy(m, owner, own, parity, lane, stage).wait()
                        if s <= 2 * bits + 1:
                            stage = 2 * bits + 1 - s
                            for lane in range(lane_count):
                                if plan.halves[lane][stage]:
                                    pl.semaphore_wait(credit.at[stage, lane], 1)
                                    for own in range(2):
                                        ag_copy(m, owner, own, parity, lane, stage).start()
                        elif s == 2 * bits + 2:
                            for copy in out_copies(m, kind, local, owner):
                                copy.start()
                        else:
                            for copy in out_copies(m, kind, local, owner):
                                copy.wait()

        m = 2 * pair + phase - bits
        for owner in range(2):

            @pl.when((m >= 0) & (m < matrices) & owned_by(owner, m) & (core == 1 - owner))
            def _(m=m, owner=owner):
                for lane in range(lane_count):
                    deliver_copy(m, owner, lane).wait_send()

    def store_block(m, phase, second, block, value):
        for q in range(2):
            piece = value[q * frames : (q + 1) * frames]
            if second == 0:
                outgo[phase, 2 * block + q] = piece
            else:
                keep[m, 2 * block + q] = piece

    def scale_clip(layer, clip):
        gamma = params[layer, gamma_row : gamma_row + 1]
        gamma_sum = bias_sum = jnp.zeros((8, width), f32)
        for j in range(chunks):
            here = g[clip, j * chunk : (j + 1) * chunk, :]
            at = slice(pad + j * chunk, pad + (j + 1) * chunk)
            gamma_sum = gamma_sum + fold(here * (xs[layer + 1, clip, at, :] - xs[layer, clip, at, :]))
            value = (gamma * here).astype(bf16)
            gb[pl.ds(pl.multiple_of(clip * frames + j * chunk, chunk), chunk), :] = value
            bias_sum = bias_sum + fold(value.astype(f32))
        sums[0] += gamma_sum
        sums[1] += bias_sum

    def norm_back(layer, clip):
        scale = chosen_row(layer, clip, scale_row)
        scale_sum = shift_sum = conv_sum = jnp.zeros((8, width), f32)
        for j in range(chunks):
            row = pl.ds(pl.multiple_of(clip * frames + j * chunk, chunk), chunk)
            at = slice(pad + j * chunk, pad + (j + 1) * chunk)
            ga = gc[clip, at, :]
            value = normed[row, :]
            scale_sum = scale_sum + fold(ga * value)
            shift_sum = shift_sum + fold(ga)
            dn = ga * scale
            first = jnp.mean(dn, axis=-1, keepdims=True)
            second = jnp.mean(dn * value, axis=-1, keepdims=True)
            result = inv_std[row, :] * (dn - first - value * second)
            gc[clip, at, :] = result
            conv_sum = conv_sum + fold(result)
        sums[9] += conv_sum
        choice = onehot[clip]
        small[layer, scale_row : scale_row + 4, :] += choice * jnp.sum(scale_sum, axis=0, keepdims=True)
        small[layer, shift_row : shift_row + 4, :] += choice * jnp.sum(shift_sum, axis=0, keepdims=True)

    def conv_back(layer, clip):
        table = params[layer]
        totals = [jnp.zeros((8, width), f32) for _ in range(7)]
        for j in range(chunks):
            grads = gc[clip, j * chunk : (j + 1) * chunk + 2 * pad, :]
            signal = xs[layer, clip, pad + j * chunk : pad + (j + 1) * chunk, :]
            at = slice(j * chunk, (j + 1) * chunk)
            total = g[clip, at, :]
            for k in (3, 0, 1, 2, 4, 5, 6):
                shifted = grads[pad + 3 - k : pad + 3 - k + chunk]
                total = total + shifted * table[k : k + 1]
                totals[k] = totals[k] + fold(signal * shifted)
            g[clip, at, :] = total
        for k in range(7):
            sums[2 + k] += totals[k]

    def backward(pair, carry):
        layer = layers - 1 - pair
        slot = layer % 2

        @pl.when((pair == 1) & (core == 0))
        def _():
            result_remote.wait_send()

        @pl.when((pair == 1) & (core == 1))
        def _():
            result_local.wait()

        sums[...] = jnp.zeros(sums.shape, f32)
        small[layer] = jnp.zeros(small.shape[1:], f32)

        def scale_body(clip, carry):
            scale_clip(layer, clip)
            return carry

        lax.fori_loop(0, clips, scale_body, 0)

        @pl.when(layer < 2)
        def _():
            for which in range(2):
                saved_copy(layer, which, True).wait()

        def up_grad(block):
            columns = pl.ds(pl.multiple_of(block * tile, tile), tile)
            value = dot_cols(gb[...], wdn[layer, columns, :])
            total = jnp.zeros((8, tile), f32)
            for q in range(rows // chunk):
                at = slice(q * chunk, (q + 1) * chunk)
                piece = (value[at] * slope[slot, at, columns].astype(f32)).astype(bf16)
                slope[slot, at, columns] = piece
                total = total + fold(piece.astype(f32))
            up_sums[block] = total

        for second in range(2):
            half = other if second == 0 else core

            def down_body(block, carry, second=second, half=half):
                at = pl.ds(pl.multiple_of(half * rows + block * tile, tile), tile)
                store_block(2 * pair, 0, second, block, dot_plain(hidden_t[slot, at, :], gb[...]))
                up_grad(block + 3 * second)
                return carry

            lax.fori_loop(0, clips // 2, down_body, 0)
            if second == 0:
                core_copy(2 * pair, 0).start()

        @pl.when(pair > 0)
        def _():
            for copy in norm_copies(layer, True):
                copy.wait()

        tick(pair, 0)

        def up_weight_grad(second, block):
            half = other if second == 0 else core
            at = pl.ds(pl.multiple_of(half * (width // 2), width // 2), width // 2)
            columns = pl.ds(pl.multiple_of(block * width, width), width)
            store_block(2 * pair + 1, 1, second, block, dot_plain(adapted_t[at, :], slope[slot, :, columns]))

        def adapted_grad(i):
            r = pl.multiple_of(i * tile, tile)
            value = dot_cols(slope[slot, pl.ds(r, tile), :], wup[layer])
            for q in range(2):
                gc[2 * i + q, pad : pad + frames, :] = value[q * frames : (q + 1) * frames]

        def norm_conv_back(i):
            for q in range(2):
                norm_back(layer, 2 * i + q)
                conv_back(layer, 2 * i + q)

        adapted_grad(0)
        up_weight_grad(0, 0)

        def tile_body(i, carry):
            adapted_grad(i + 1)
            up_weight_grad(0, i + 1)
            norm_conv_back(i)
            return carry

        lax.fori_loop(0, rows // tile - 1, tile_body, 0)
        core_copy(2 * pair + 1, 1).start()
        for block in range(3):
            up_weight_grad(1, block)
        norm_conv_back(rows // tile - 1)

        @pl.when(layer > 0)
        def _():
            for copy in norm_copies(layer - 1, True):
                copy.start()

        @pl.when(layer >= 2)
        def _():
            for which in range(2):
                saved_copy(layer, which, True).start()

        gamma = params[layer, gamma_row : gamma_row + 1, :]
        small[layer, gamma_row : gamma_row + 1, :] = jnp.sum(sums[0], axis=0, keepdims=True) / gamma
        small[layer, down_bias_row : down_bias_row + 1, :] = jnp.sum(sums[1], axis=0, keepdims=True)
        for block in range(blocks):
            row = up_bias_row + block // 2
            place = (block % 2) * tile
            small[layer, row : row + 1, place : place + tile] = jnp.sum(up_sums[block], axis=0, keepdims=True)
        for k in range(7):
            small[layer, taps_row + k : taps_row + k + 1, :] = jnp.sum(sums[2 + k], axis=0, keepdims=True)
        small[layer, conv_bias_row : conv_bias_row + 1, :] = jnp.sum(sums[9], axis=0, keepdims=True)
        tick(pair, 1)
        return carry

    lax.fori_loop(0, layers, backward, 0)

    grad_remote = to_core(g, ends.at[0, :, 1], ends_send.at[2], ends_recv.at[1])
    grad_local = pltpu.make_async_copy(g, ends.at[0, :, 0], ends_send.at[3])

    @pl.when(core == 0)
    def _():
        grad_local.start()

    @pl.when(core == 1)
    def _():
        grad_remote.start()

    small_core = to_core(
        small.at[pl.ds(per_core * other, per_core)], small_in.at[bits], small_send.at[bits], small_recv.at[bits]
    )
    small_core.start()

    def small_copy(bit):
        return to_batch(small_sum, small_in.at[bit], small_send.at[bit], small_recv.at[bit], partner(bit))

    def drain(pair, carry):
        for phase in range(2):
            tick(pair, phase)
            for step in range(bits + 1):

                @pl.when(2 * pair + phase - matrices == step)
                def _(step=step):
                    if step == 0:
                        small_core.wait()
                        small_sum[...] = small[pl.ds(per_core * core, per_core)] + small_in[bits]
                    else:
                        small_copy(step - 1).wait()
                        small_sum[...] = small_sum[...] + small_in[step - 1]
                    if step < bits:
                        small_copy(step).start()

        return carry

    lax.fori_loop(layers, layers + bits + 1, drain, 0)
    small_out[...] = small_sum[...]

    @pl.when(core == 0)
    def _():
        grad_local.wait()
        grad_remote.wait_recv()

    @pl.when(core == 1)
    def _():
        result_remote.wait_recv()
        grad_remote.wait_send()


def results_kernel(
    ends,
    up_grad,
    down_grad,
    small,
    ends_out,
    conv_kernel_out,
    conv_bias_out,
    band_scale_out,
    band_shift_out,
    up_out,
    up_bias_out,
    down_out,
    down_bias_out,
    layer_scale_out,
    ends_stage,
    up_stage,
    down_stage,
    in_sem,
    out_sem,
):
    copies = []
    per_core, _, width = small.shape
    for clip in range(ends.shape[1]):
        copies.append((ends.at[0, clip], ends_stage.at[clip], ends_out.at[0, clip]))
    for j in range(per_core):
        for half in range(2):
            for source, stage, target in ((up_grad, up_stage, up_out), (down_grad, down_stage, down_out)):
                size = source.shape[2] // 2
                for part in range(2):
                    at = (j, half, slice(part * size, (part + 1) * size))
                    copies.append((source.at[at], stage.at[at], target.at[at]))
    loads = [pltpu.make_async_copy(a, b, in_sem.at[i]) for i, (a, b, _) in enumerate(copies)]
    stores = [pltpu.make_async_copy(b, c, out_sem.at[i]) for i, (_, b, c) in enumerate(copies)]
    ahead = 6
    for load in loads[:ahead]:
        load.start()
    for i, (load, store) in enumerate(zip(loads, stores)):
        load.wait()
        store.start()
        if i + ahead < len(loads):
            loads[i + ahead].start()
    for j in range(per_core):
        conv_kernel_out[:, j] = small[j, taps_row : taps_row + 7]
        conv_bias_out[j : j + 1] = small[j, conv_bias_row : conv_bias_row + 1]
        band_scale_out[j] = small[j, scale_row : scale_row + 4]
        band_shift_out[j] = small[j, shift_row : shift_row + 4]
        for q in range(3):
            row = up_bias_row + q
            up_bias_out[j : j + 1, q * width : (q + 1) * width] = small[j, row : row + 1]
        down_bias_out[j : j + 1] = small[j, down_bias_row : down_bias_row + 1]
        layer_scale_out[j : j + 1] = small[j, gamma_row : gamma_row + 1]
    for store in stores:
        store.wait()


def body(
    inputs,
    grad_out,
    band_ids,
    conv_kernel,
    conv_bias,
    band_scale,
    band_shift,
    up_weight,
    up_bias,
    down_weight,
    down_bias,
    layer_scale,
):
    sections = lax.axis_size("section")
    batch = lax.axis_size("batch")
    clips, local_clips, frames, width = inputs.shape
    per_core, _, hidden_width = up_weight.shape
    layers = per_core * sections
    bands = band_scale.shape[1]
    rows = clips * frames
    assert sections == 2 and local_clips == 2 and batch & (batch - 1) == 0
    assert hidden_width == 3 * width and bands == 4 and layers == 4 and rows == 3 * width // 2
    plan = Plan(batch, rows)
    bits = plan.bits
    hbm = pl.BlockSpec(memory_space=pl.ANY)
    vmem = pl.BlockSpec(memory_space=pltpu.VMEM)
    smem = pl.BlockSpec(memory_space=pltpu.SMEM)
    padded = frames + 2 * pad
    dma = pltpu.SemaphoreType.DMA
    lanes = len(plan.lanes)
    tile = 2 * frames
    ends_shape = jax.ShapeDtypeStruct((1, clips, local_clips, frames, width), f32)
    up_shape = jax.ShapeDtypeStruct((per_core, 2, width // 2, hidden_width), f32)
    down_shape = jax.ShapeDtypeStruct((per_core, 2, hidden_width // 2, width), f32)
    small_shape = jax.ShapeDtypeStruct((per_core, packed_rows, width), f32)
    conv_kernel = jnp.transpose(conv_kernel, (1, 0, 2))
    ends, up_grad, down_grad, small, *_ = pl.pallas_call(
        functools.partial(step_kernel, plan),
        out_shape=[
            ends_shape,
            up_shape,
            down_shape,
            small_shape,
            jax.ShapeDtypeStruct((2, hidden_width, rows), bf16),
            jax.ShapeDtypeStruct((2, rows, hidden_width), bf16),
            jax.ShapeDtypeStruct((layers - 1, rows, width), f32),
            jax.ShapeDtypeStruct((layers - 1, rows, 1), f32),
            jax.ShapeDtypeStruct((layers - 1, width, rows), bf16),
        ],
        in_specs=[hbm, hbm, smem, vmem, vmem, vmem, vmem, hbm, vmem, hbm, vmem, vmem],
        out_specs=[hbm, hbm, hbm, vmem, hbm, hbm, hbm, hbm, hbm],
        scratch_shapes=[
            pltpu.VMEM((layers + 1, clips, padded, width), f32),
            pltpu.VMEM((rows, width), f32),
            pltpu.VMEM((rows, 1), f32),
            pltpu.VMEM((width, rows), bf16),
            pltpu.VMEM((2, hidden_width, rows), bf16),
            pltpu.VMEM((2, rows, hidden_width), bf16),
            pltpu.VMEM((2, rows, tile), bf16),
            pltpu.VMEM((rows, width), bf16),
            pltpu.VMEM((clips, frames, width), f32),
            pltpu.VMEM((clips, padded, width), f32),
            pltpu.VMEM((layers, width, hidden_width), bf16),
            pltpu.VMEM((layers, hidden_width, width), bf16),
            pltpu.VMEM((per_core, packed_rows, width), f32),
            pltpu.VMEM((layers, packed_rows, width), f32),
            pltpu.VMEM((layers, hidden_width // tile, 1, tile), f32),
            pltpu.VMEM((rows, tile), f32),
            pltpu.VMEM((rows, tile), f32),
            pltpu.VMEM((clips, bands, width), f32),
            pltpu.VMEM((10, 8, width), f32),
            pltpu.VMEM((hidden_width // tile, 8, tile), f32),
            pltpu.VMEM((layers, packed_rows, width), f32),
            pltpu.VMEM((2 * layers, clips, frames, width), f32),
            pltpu.VMEM((2, clips, frames, width), f32),
            pltpu.VMEM((2, clips, frames, width), f32),
            pltpu.VMEM((per_core, packed_rows, width), f32),
            pltpu.VMEM((bits + 1, per_core, packed_rows, width), f32),
            *[pltpu.VMEM((2, plan.slot_rows[stage][1], width), f32) for stage in range(bits)],
            dma((2 + 2 * clips,)),
            dma((4 * per_core,)),
            dma((4 * per_core,)),
            dma((1,)),
            dma((1,)),
            dma((4,)),
            dma((2,)),
            dma((2,)),
            dma((2,)),
            dma((bits, 2, lanes)),
            dma((bits, 2, lanes)),
            dma((layers, lanes)),
            dma((layers, lanes)),
            dma((bits, 2, 2, lanes)),
            dma((bits, 2, 2, lanes)),
            dma((layers, 2, 3)),
            pltpu.SemaphoreType.REGULAR((bits, lanes)),
            dma((bits + 1,)),
            dma((bits + 1,)),
            dma((2, 2)),
            dma((3,)),
        ],
        compiler_params=pltpu.CompilerParams(
            collective_id=0, has_side_effects=True, vmem_limit_bytes=255 * 2**18
        ),
        cost_estimate=pl.CostEstimate(
            flops=24 * rows * width * hidden_width * 2, bytes_accessed=2**26, transcendentals=2**24
        ),
        name="blocks_step",
    )(
        inputs,
        grad_out,
        jnp.transpose(band_ids),
        conv_kernel,
        conv_bias,
        band_scale,
        band_shift,
        up_weight,
        up_bias,
        down_weight,
        down_bias,
        layer_scale,
    )

    def like(array):
        return jax.ShapeDtypeStruct(array.shape, f32)

    outs = pl.pallas_call(
        results_kernel,
        out_shape=[
            ends_shape,
            like(conv_kernel),
            like(conv_bias),
            like(band_scale),
            like(band_shift),
            up_shape,
            like(up_bias),
            down_shape,
            like(down_bias),
            like(layer_scale),
        ],
        in_specs=[hbm, hbm, hbm, vmem],
        out_specs=[hbm, vmem, vmem, vmem, vmem, hbm, vmem, hbm, vmem, vmem],
        scratch_shapes=[
            pltpu.VMEM(ends_shape.shape[1:], f32),
            pltpu.VMEM(up_shape.shape, f32),
            pltpu.VMEM(down_shape.shape, f32),
            dma((8 * per_core + clips,)),
            dma((8 * per_core + clips,)),
        ],
        compiler_params=pltpu.CompilerParams(vmem_limit_bytes=255 * 2**18),
        cost_estimate=pl.CostEstimate(flops=0, bytes_accessed=2**25, transcendentals=0),
        name="results",
    )(ends, up_grad, down_grad, small)
    outs = list(outs)
    outs[1] = jnp.transpose(outs[1], (1, 0, 2))
    outs[5] = outs[5].reshape(up_weight.shape)
    outs[7] = outs[7].reshape(down_weight.shape)
    return tuple(outs)


def solution(mesh):
    in_specs = (
        P(None, "batch", None, None),
        P(None, "batch", None, None),
        P(None, "batch"),
        P("section", None, None),
        P("section", None),
        P("section", None, None),
        P("section", None, None),
        P("section", None, None),
        P("section", None),
        P("section", None, None),
        P("section", None),
        P("section", None),
    )
    out_specs = (
        P("section", None, "batch", None, None),
        P("section", None, None),
        P("section", None),
        P("section", None, None),
        P("section", None, None),
        P("section", None, None),
        P("section", None),
        P("section", None, None),
        P("section", None),
        P("section", None),
    )
    return jax.shard_map(body, mesh=mesh, in_specs=in_specs, out_specs=out_specs, check_vma=False)
```

```python
import functools

import jax
import jax.numpy as jnp
from jax import lax
from jax.experimental import pallas as pl
from jax.experimental.pallas import tpu as pltpu
from jax.sharding import PartitionSpec as P

norm_epsilon = 1e-06
f32 = jnp.float32
bf16 = jnp.bfloat16

log_density = -1.3257480647361593

taps_row, conv_bias_row, scale_row, shift_row, up_bias_row, down_bias_row, gamma_row = 0, 7, 8, 12, 16, 19, 20
packed_rows = 24
pad = 8
chunk = 32


def gelu_and_slope(u):
    cdf = 0.5 * lax.erf(u * 0.7071067811865476) + 0.5
    density = jnp.exp2(u * (u * (-0.5 * 1.4426950408889634)) + log_density)
    return u * cdf, cdf + u * density


def fold(values):
    rows, columns = values.shape
    return jnp.sum(values.reshape(rows // 8, 8, columns), axis=0)


def dot_plain(left, right):
    return lax.dot_general(left, right, (((1,), (0,)), ((), ())), preferred_element_type=f32)


def dot_cols(left, right):
    return lax.dot_general(left, right, (((1,), (1,)), ((), ())), preferred_element_type=f32)


class Plan:
    def __init__(self, batch, rows):
        self.bits = batch.bit_length() - 1
        order = [(bit, bit) for bit in range(self.bits)]
        if self.bits > 1:
            order[:2] = [(0, 1), (1, 0)]
        late = order[:]
        if self.bits > 2:
            late = [order[2]] + order[:2] + order[3:]
        third = rows // 3
        self.lanes = [(0, 2 * third, order), (2 * third, third, late)]
        self.kept = []
        self.halves = []
        self.slot_rows = []
        for _, size, _ in self.lanes:
            kept, halves = [size], []
            for stage in range(self.bits):
                halves.append(stage < self.bits - 1 and kept[-1] // 2 % 8 == 0)
                kept.append(kept[-1] // 2 if halves[-1] else kept[-1])
            self.kept.append(kept)
            self.halves.append(halves)
        self.doublings = max(sum(halves) for halves in self.halves)
        for stage in range(self.bits):
            begin, starts = 0, []
            for lane in range(len(self.lanes)):
                starts.append(begin)
                begin += self.kept[lane][stage + 1]
            self.slot_rows.append((starts, begin))


def step_kernel(
    plan,
    inputs,
    grad_out,
    band_ids,
    conv_kernel,
    conv_bias,
    band_scale,
    band_shift,
    up_weight,
    up_bias,
    down_weight,
    down_bias,
    layer_scale,
    ends,
    up_out,
    down_out,
    small_out,
    hidden_spill,
    slope_spill,
    normed_spill,
    inv_spill,
    adapted_spill,
    xs,
    normed,
    inv_std,
    adapted_t,
    hidden_t,
    slope,
    hidden_near,
    gb,
    g,
    gc,
    wup,
    wdn,
    packed,
    params,
    up_bias_row_of,
    upper_even,
    upper_odd,
    onehot,
    sums,
    up_sums,
    small,
    keep,
    outgo,
    income,
    small_sum,
    small_in,
    *rest,
):
    stage_in = rest[: plan.bits]
    (
        load_sem,
        own_sem,
        wt_send,
        wt_recv,
        par_send,
        par_recv,
        ends_send,
        ends_recv,
        core_send,
        core_recv,
        rs_send,
        rs_recv,
        deliver_send,
        deliver_recv,
        ag_send,
        ag_recv,
        out_sem,
        credit,
        small_send,
        small_recv,
        spill_sem,
        norm_sem,
    ) = rest[plan.bits :]
    uppers = (upper_even, upper_odd)
    core = lax.axis_index("section")
    other = 1 - core
    batch = lax.axis_index("batch")
    clips, frames, width = g.shape
    rows = clips * frames
    layers = xs.shape[0] - 1
    per_core = layers // 2
    hidden_width = slope.shape[2]
    tile = 2 * frames
    chunks = frames // chunk
    blocks = hidden_width // tile
    bits = plan.bits
    mesh_id = pl.DeviceIdType.MESH

    def bit_of(bit):
        return (batch // (1 << bit)) % 2

    def partner(bit):
        return batch + (1 - 2 * bit_of(bit)) * (1 << bit)

    def choose(pair, side, value):
        first, second = pair
        if first == second:
            return value(first)
        if isinstance(side, int):
            return value(pair[side])
        return (1 - side) * value(first) + side * value(second)

    def to_core(source, target, send, recv):
        return pltpu.make_async_remote_copy(source, target, send, recv, {"section": other}, mesh_id)

    def to_batch(source, target, send, recv, device):
        return pltpu.make_async_remote_copy(source, target, send, recv, {"batch": device}, mesh_id)

    own_blocks = pl.ds(per_core * core, per_core)
    own = []
    for j in range(per_core):
        for source, target in ((up_weight, wup), (down_weight, wdn)):
            own.append(pltpu.make_async_copy(source.at[j], target.at[per_core * core + j], own_sem.at[len(own)]))
    own[0].start()
    loads = []
    for source, target in ((inputs, slope.at[0, :, 0:width]), (grad_out, gb)):
        for clip in range(clips):
            loads.append(
                pltpu.make_async_copy(
                    source.at[clip, core], target.at[pl.ds(clip * frames, frames)], load_sem.at[len(loads)]
                )
            )
    for load in loads[:clips]:
        load.start()
    for load in own[1:] + loads[clips:]:
        load.start()

    for j in range(per_core):
        packed[j, taps_row : taps_row + 7] = conv_kernel[:, j]
        packed[j, conv_bias_row : conv_bias_row + 1] = conv_bias[j : j + 1]
        packed[j, scale_row : scale_row + 4] = band_scale[j]
        packed[j, shift_row : shift_row + 4] = band_shift[j]
        for q in range(3):
            row = up_bias_row + q
            packed[j, row : row + 1] = up_bias[j : j + 1, q * width : (q + 1) * width]
        packed[j, down_bias_row : down_bias_row + 1] = down_bias[j : j + 1]
        packed[j, gamma_row : gamma_row + 1] = layer_scale[j : j + 1]
        packed[j, gamma_row + 1 : packed_rows] = jnp.zeros((packed_rows - gamma_row - 1, width), f32)

    barrier = pltpu.get_barrier_semaphore()
    pl.semaphore_signal(barrier, inc=1, device_id={"section": other}, device_id_type=mesh_id)
    for bit in range(bits):
        pl.semaphore_signal(barrier, inc=1, device_id={"batch": partner(bit)}, device_id_type=mesh_id)

    for load in loads[:clips]:
        load.wait()

    def load_x(clip, carry):
        xs[0, clip, 0:pad, :] = jnp.zeros((pad, width), f32)
        xs[0, clip, pad + frames : 2 * pad + frames, :] = jnp.zeros((pad, width), f32)
        xs[0, clip, pad : pad + frames, :] = slope[
            0, pl.ds(pl.multiple_of(clip * frames, frames), frames), 0:width
        ].astype(f32)
        for band in range(4):
            chosen = jnp.where(band_ids[core, clip] == band, 1.0, 0.0).astype(f32)
            onehot[clip, band : band + 1] = jnp.zeros((1, width), f32) + chosen
        return carry

    lax.fori_loop(0, clips, load_x, 0)
    pl.semaphore_wait(barrier, 1 + bits)

    par_copy = to_core(packed, params.at[own_blocks], par_send.at[0], par_recv.at[0])
    par_copy.start()
    params[own_blocks] = packed[...]

    stages = [
        xs.at[1, :, 0:frames],
        xs.at[2, :, 0:frames],
        xs.at[3, :, 0:frames],
        outgo.at[0],
        outgo.at[1],
        xs.at[4, :, 0:frames],
        gc.at[:, 0:frames],
        outgo.at[0],
    ]

    def weight_part(kind, layer, half, part):
        if kind == 0:
            return wup.at[
                layer,
                pl.ds(pl.multiple_of(half * (width // 2) + (part % 2) * frames, frames), frames),
                pl.ds(pl.multiple_of((part // 2) * width, width), width),
            ]
        return wdn.at[layer, pl.ds(pl.multiple_of(half * rows + part * frames, frames), frames), :]

    def weight_copy(stage, k):
        return to_core(stage, keep.at[k], wt_send.at[k], wt_recv.at[k])

    def send_weights(k):
        j, kind, half = k // 4, k // 2 % 2, k % 2

        def cast(part, carry):
            stages[k][part] = weight_part(kind, per_core * core + j, half, part)[...].astype(f32)
            return carry

        lax.fori_loop(0, clips, cast, 0)
        weight_copy(stages[k], k).start()

    def take_weights(layer, kind):
        @pl.when(layer // per_core != core)
        def _():
            for half in range(2):
                k = 4 * (layer % per_core) + 2 * kind + half
                weight_copy(outgo.at[0], k).wait_recv()

                def cast(part, carry, half=half, k=k):
                    weight_part(kind, layer, half, part)[...] = keep[k, part].astype(bf16)
                    return carry

                lax.fori_loop(0, clips, cast, 0)

    for kind in range(2):
        own[kind].wait()
        for half in range(2):
            send_weights(2 * kind + half)
    par_copy.wait()
    for layer in range(layers):
        for block in range(blocks):
            row = up_bias_row + block // 2
            place = (block % 2) * tile
            up_bias_row_of[layer, block] = params[layer, row : row + 1, place : place + tile]

    def chosen_row(layer, clip, first):
        return jnp.sum(onehot[clip] * params[layer, first : first + 4], axis=0, keepdims=True)

    adapted_place = slice(hidden_width - width, hidden_width)

    def norm_clip(layer, clip):
        table = params[layer]
        scale = chosen_row(layer, clip, scale_row)
        shift = chosen_row(layer, clip, shift_row)
        for j in range(chunks):
            window = xs[layer, clip, j * chunk : (j + 1) * chunk + 2 * pad, :]
            conv = window[pad : pad + chunk] * table[3:4] + table[conv_bias_row : conv_bias_row + 1]
            for k in (0, 1, 2, 4, 5, 6):
                conv = conv + window[pad - 3 + k : pad - 3 + k + chunk] * table[k : k + 1]
            centered = conv - jnp.mean(conv, axis=-1, keepdims=True)
            inv = lax.rsqrt(jnp.mean(centered * centered, axis=-1, keepdims=True) + norm_epsilon)
            value = centered * inv
            at = pl.ds(pl.multiple_of(clip * frames + j * chunk, chunk), chunk)
            normed[at, :] = value
            inv_std[at, :] = inv
            slope[layer % 2, at, adapted_place] = (value * scale + shift).astype(bf16)

    def saved_copy(layer, which, back):
        buffer = (hidden_t if which == 0 else slope).at[layer % 2]
        away = (hidden_spill if which == 0 else slope_spill).at[layer % 2]
        source, target = (away, buffer) if back else (buffer, away)
        return pltpu.make_async_copy(source, target, spill_sem.at[layer % 2, which])

    def norm_copies(layer, back):
        copies = []
        for i, (near, away) in enumerate(((normed, normed_spill), (inv_std, inv_spill), (adapted_t, adapted_spill))):
            source, target = (away.at[layer], near) if back else (near, away.at[layer])
            copies.append(pltpu.make_async_copy(source, target, norm_sem.at[i]))
        return copies

    branch_sum = g.reshape(rows, width)

    def forward(layer, carry):
        slot = layer % 2

        @pl.when(layer > 0)
        def _():
            for copy in norm_copies(layer - 1, False):
                copy.wait()

        @pl.when(layer >= 2)
        def _():
            for which in range(2):
                saved_copy(layer, which, False).wait()

        def norm_body(clip, carry):
            norm_clip(layer, clip)
            return carry

        lax.fori_loop(0, clips, norm_body, 0)

        @pl.when(layer == 0)
        def _():
            for load in own[2:]:
                load.wait()
            for k in range(4, 4 * per_core - 1):
                send_weights(k)

        take_weights(layer, 0)

        def up(block):
            columns = slice(block * tile, (block + 1) * tile)
            uppers[block % 2][...] = dot_plain(slope[slot, :, adapted_place], wup[layer, :, columns])

        def down(block):
            columns = slice(block * tile, (block + 1) * tile)
            here = hidden_near[block % 2]
            value = dot_plain(here, wdn[layer, columns, :])
            branch_sum[...] = value if block == 0 else branch_sum[...] + value
            hidden_t[slot, columns, :] = here.T

        up(0)
        for block in range(blocks):
            columns = slice(block * tile, (block + 1) * tile)
            if block + 1 < blocks:
                up(block + 1)
            if block == 0:
                adapted_t[...] = slope[slot, :, adapted_place].T
            if block == 1:
                take_weights(layer, 1)
            if block > 0:
                down(block - 1)
            bias = up_bias_row_of[layer, block]
            for q in range(rows // chunk):
                at = slice(q * chunk, (q + 1) * chunk)
                smooth, steep = gelu_and_slope(uppers[block % 2][at, :] + bias)
                hidden_near[block % 2, at, :] = smooth.astype(bf16)
                slope[slot, at, columns] = steep.astype(bf16)
        down(blocks - 1)

        @pl.when(layer < layers - 1)
        def _():
            for copy in norm_copies(layer, False):
                copy.start()

        @pl.when(layer < 2)
        def _():
            for which in range(2):
                saved_copy(layer, which, False).start()

        for step in range(layers):

            @pl.when(layer == step)
            def _(step=step):
                for k in [step] if step < layers - 1 else range(layers, 4 * per_core):
                    weight_copy(outgo.at[0], k).wait_send()
                if step == 0:
                    weight_copy(outgo.at[0], layers - 1).wait_send()
                    send_weights(4 * per_core - 1)

        def residual(clip, carry):
            bias = params[layer, down_bias_row : down_bias_row + 1]
            gamma = params[layer, gamma_row : gamma_row + 1]
            branch = g[clip] + bias
            xs[layer + 1, clip, pad : pad + frames, :] = xs[layer, clip, pad : pad + frames, :] + gamma * branch
            return carry

        lax.fori_loop(0, clips, residual, 0)

        def zero_pads(clip, carry):
            xs[layer + 1, clip, 0:pad, :] = jnp.zeros((pad, width), f32)
            xs[layer + 1, clip, pad + frames : 2 * pad + frames, :] = jnp.zeros((pad, width), f32)
            return carry

        lax.fori_loop(0, clips, zero_pads, 0)
        return carry

    lax.fori_loop(0, layers, forward, 0)

    result = xs.at[layers, :, pad : pad + frames]
    result_remote = to_core(result, ends.at[0, :, 0], ends_send.at[0], ends_recv.at[0])
    result_local = pltpu.make_async_copy(result, ends.at[0, :, 1], ends_send.at[1])

    @pl.when(core == 0)
    def _():
        result_remote.start()

    @pl.when(core == 1)
    def _():
        result_local.start()

    for load in loads[clips:]:
        load.wait()

    def load_g(clip, carry):
        g[clip] = gb[pl.ds(pl.multiple_of(clip * frames, frames), frames), :].astype(f32)
        gc[clip, 0:pad, :] = jnp.zeros((pad, width), f32)
        gc[clip, pad + frames : 2 * pad + frames, :] = jnp.zeros((pad, width), f32)
        return carry

    lax.fori_loop(0, clips, load_g, 0)

    matrices = 2 * layers
    lane_count = len(plan.lanes)

    def core_copy(m, parity):
        return to_core(outgo.at[parity], income.at[parity], core_send.at[parity], core_recv.at[parity])

    keep_rows = keep.reshape(matrices, rows, width)

    def offset(lane, stage, side):
        start = 0
        for s in range(stage):
            if plan.halves[lane][s]:
                start = start + choose(plan.lanes[lane][2][s], side, bit_of) * plan.kept[lane][s + 1]
        return start

    def rs_copy(m, parity, lane, stage):
        begin, _, order = plan.lanes[lane]
        size = plan.kept[lane][stage + 1]
        at = begin + offset(lane, stage, core)
        if plan.halves[lane][stage]:
            at = at + (1 - choose(order[stage], core, bit_of)) * size
        starts, _ = plan.slot_rows[stage]
        return to_batch(
            keep_rows.at[m, pl.ds(pl.multiple_of(at, 8), size)],
            stage_in[stage].at[parity, starts[lane] : starts[lane] + size],
            rs_send.at[stage, parity, lane],
            rs_recv.at[stage, parity, lane],
            choose(order[stage], core, partner),
        )

    def rs_add(m, parity, lane, stage):
        begin, _, _ = plan.lanes[lane]
        size = plan.kept[lane][stage + 1]
        at = begin + offset(lane, stage + 1, core)
        starts, _ = plan.slot_rows[stage]
        step = min(size, 2 * chunk)

        def body(i, carry):
            r = pl.multiple_of(at + i * step, 8)
            keep_rows[m, pl.ds(r, step), :] = (
                keep_rows[m, pl.ds(r, step), :]
                + stage_in[stage][parity, pl.ds(pl.multiple_of(starts[lane] + i * step, 8), step), :]
            )
            return carry

        lax.fori_loop(0, size // step, body, 0)

    half_way = matrices // 2
    xs_rows = xs.reshape(layers + 1, clips * (frames + 2 * pad), width)

    def rows_of(m, owner, own, lane, at, size):
        span = pl.ds(pl.multiple_of(plan.lanes[lane][0] + at, 8), size)
        if own:
            return keep_rows.at[m, span]
        return xs_rows.at[layers - m, span] if owner == 1 else keep_rows.at[m - half_way, span]

    def deliver_copy(m, owner, lane):
        size = plan.kept[lane][bits]
        at = offset(lane, bits, 1 - owner)
        return to_core(
            rows_of(m, owner, True, lane, at, size),
            rows_of(m, owner, False, lane, at, size),
            deliver_send.at[m % half_way, lane],
            deliver_recv.at[m % half_way, lane],
        )

    def ag_copy(m, owner, own, parity, lane, stage):
        size = plan.kept[lane][stage + 1]
        side = owner if own else 1 - owner
        place = rows_of(m, owner, own, lane, offset(lane, stage + 1, side), size)
        return to_batch(
            place,
            place,
            ag_send.at[stage, parity, own, lane],
            ag_recv.at[stage, parity, own, lane],
            choose(plan.lanes[lane][2][stage], side, partner),
        )

    def out_copies(m, kind, local, owner):
        copies = []
        third = rows // 3
        for own in range(2):
            half = owner if own else 1 - owner
            if own:
                source = keep_rows.at[m]
            else:
                source = xs_rows.at[layers - m] if owner == 1 else keep_rows.at[m - half_way]
            sem = out_sem.at[m % half_way, own]
            if kind == 0:
                copies.append(pltpu.make_async_copy(source.at[0:rows], down_out.at[local, half], sem.at[0]))
                continue
            for part in range(3):
                columns = slice(part * width, (part + 1) * width)
                copies.append(
                    pltpu.make_async_copy(
                        source.at[part * third : (part + 1) * third],
                        up_out.at[local, half, :, columns],
                        sem.at[part],
                    )
                )
        return copies

    def owner_of(m):
        return 1 - m // half_way

    def owned_by(owner, m):
        return m < half_way if owner == 1 else m >= half_way

    last_step = bits + plan.doublings + 3

    def tick(pair, phase):
        for s in range(last_step, 0, -1):
            m = 2 * pair + phase + 1 - s
            parity = (phase + 1 - s) % 2
            kind = parity
            local = (layers - 1 - (m - kind) // 2) % per_core
            valid = (m >= 0) & (m < matrices)

            if s <= bits + 1:

                @pl.when(valid)
                def _(s=s, m=m, parity=parity):
                    if s == 1:
                        core_copy(m, parity).wait()

                        def body(clip, carry):
                            keep[m, clip] = keep[m, clip] + income[parity, clip]
                            return carry

                        lax.fori_loop(0, clips, body, 0)
                    else:
                        for lane in range(lane_count):
                            rs_copy(m, parity, lane, s - 2).wait()
                            if plan.halves[lane][s - 2]:
                                @pl.when(owner_of(m) == core)
                                def _(lane=lane):
                                    pl.semaphore_signal(
                                        credit.at[s - 2, lane],
                                        inc=1,
                                        device_id={"batch": choose(plan.lanes[lane][2][s - 2], core, partner)},
                                        device_id_type=mesh_id,
                                    )

                            rs_add(m, parity, lane, s - 2)
                    if s <= bits:
                        for lane in range(lane_count):
                            rs_copy(m, parity, lane, s - 1).start()

            for owner in range(2):
                if s == bits + 1:

                    @pl.when(valid & owned_by(owner, m) & (core == 1 - owner))
                    def _(m=m, owner=owner):
                        for lane in range(lane_count):
                            deliver_copy(m, owner, lane).start()

                if s > bits + 1:

                    @pl.when(valid & owned_by(owner, m) & (core == owner))
                    def _(s=s, m=m, parity=parity, kind=kind, local=local, owner=owner):
                        if s == bits + 2:
                            for lane in range(lane_count):
                                deliver_copy(m, owner, lane).wait_recv()
                        elif s < last_step:
                            stage = last_step - 1 - s
                            for lane in range(lane_count):
                                if plan.halves[lane][stage]:
                                    for own in range(2):
                                        ag_copy(m, owner, own, parity, lane, stage).wait()
                        if s < last_step - 1:
                            stage = last_step - 2 - s
                            for lane in range(lane_count):
                                if plan.halves[lane][stage]:
                                    pl.semaphore_wait(credit.at[stage, lane], 1)
                                    for own in range(2):
                                        ag_copy(m, owner, own, parity, lane, stage).start()
                        elif s == last_step - 1:
                            for copy in out_copies(m, kind, local, owner):
                                copy.start()
                        else:
                            for copy in out_copies(m, kind, local, owner):
                                copy.wait()

        m = 2 * pair + phase - bits
        for owner in range(2):

            @pl.when((m >= 0) & (m < matrices) & owned_by(owner, m) & (core == 1 - owner))
            def _(m=m, owner=owner):
                for lane in range(lane_count):
                    deliver_copy(m, owner, lane).wait_send()

    def store_block(m, phase, second, block, value):
        for q in range(2):
            piece = value[q * frames : (q + 1) * frames]
            if second == 0:
                outgo[phase, 2 * block + q] = piece
            else:
                keep[m, 2 * block + q] = piece

    def scale_clip(layer, clip):
        gamma = params[layer, gamma_row : gamma_row + 1]
        gamma_sum = bias_sum = jnp.zeros((8, width), f32)
        for j in range(chunks):
            here = g[clip, j * chunk : (j + 1) * chunk, :]
            at = slice(pad + j * chunk, pad + (j + 1) * chunk)
            gamma_sum = gamma_sum + fold(here * (xs[layer + 1, clip, at, :] - xs[layer, clip, at, :]))
            value = (gamma * here).astype(bf16)
            gb[pl.ds(pl.multiple_of(clip * frames + j * chunk, chunk), chunk), :] = value
            bias_sum = bias_sum + fold(value.astype(f32))
        sums[0] += gamma_sum
        sums[1] += bias_sum

    def norm_back(layer, clip):
        scale = chosen_row(layer, clip, scale_row)
        scale_sum = shift_sum = conv_sum = jnp.zeros((8, width), f32)
        for j in range(chunks):
            row = pl.ds(pl.multiple_of(clip * frames + j * chunk, chunk), chunk)
            at = slice(pad + j * chunk, pad + (j + 1) * chunk)
            ga = gc[clip, at, :]
            value = normed[row, :]
            scale_sum = scale_sum + fold(ga * value)
            shift_sum = shift_sum + fold(ga)
            dn = ga * scale
            first = jnp.mean(dn, axis=-1, keepdims=True)
            second = jnp.mean(dn * value, axis=-1, keepdims=True)
            result = inv_std[row, :] * (dn - first - value * second)
            gc[clip, at, :] = result
            conv_sum = conv_sum + fold(result)
        sums[9] += conv_sum
        choice = onehot[clip]
        small[layer, scale_row : scale_row + 4, :] += choice * jnp.sum(scale_sum, axis=0, keepdims=True)
        small[layer, shift_row : shift_row + 4, :] += choice * jnp.sum(shift_sum, axis=0, keepdims=True)

    def conv_back(layer, clip):
        table = params[layer]
        totals = [jnp.zeros((8, width), f32) for _ in range(7)]
        for j in range(chunks):
            grads = gc[clip, j * chunk : (j + 1) * chunk + 2 * pad, :]
            signal = xs[layer, clip, pad + j * chunk : pad + (j + 1) * chunk, :]
            at = slice(j * chunk, (j + 1) * chunk)
            total = g[clip, at, :]
            for k in (3, 0, 1, 2, 4, 5, 6):
                shifted = grads[pad + 3 - k : pad + 3 - k + chunk]
                total = total + shifted * table[k : k + 1]
                totals[k] = totals[k] + fold(signal * shifted)
            g[clip, at, :] = total
        for k in range(7):
            sums[2 + k] += totals[k]

    def backward(pair, carry):
        layer = layers - 1 - pair
        slot = layer % 2

        @pl.when((pair == 1) & (core == 0))
        def _():
            result_remote.wait_send()

        @pl.when((pair == 1) & (core == 1))
        def _():
            result_local.wait()

        sums[...] = jnp.zeros(sums.shape, f32)
        small[layer] = jnp.zeros(small.shape[1:], f32)

        def scale_body(clip, carry):
            scale_clip(layer, clip)
            return carry

        lax.fori_loop(0, clips, scale_body, 0)

        @pl.when(layer < 2)
        def _():
            for which in range(2):
                saved_copy(layer, which, True).wait()

        def up_grad(block):
            columns = pl.ds(pl.multiple_of(block * tile, tile), tile)
            value = dot_cols(gb[...], wdn[layer, columns, :])
            total = jnp.zeros((8, tile), f32)
            for q in range(rows // chunk):
                at = slice(q * chunk, (q + 1) * chunk)
                piece = (value[at] * slope[slot, at, columns].astype(f32)).astype(bf16)
                slope[slot, at, columns] = piece
                total = total + fold(piece.astype(f32))
            up_sums[block] = total

        for second in range(2):
            half = other if second == 0 else core

            def down_body(block, carry, second=second, half=half):
                at = pl.ds(pl.multiple_of(half * rows + block * tile, tile), tile)
                store_block(2 * pair, 0, second, block, dot_plain(hidden_t[slot, at, :], gb[...]))
                up_grad(block + 3 * second)
                return carry

            lax.fori_loop(0, clips // 2, down_body, 0)
            if second == 0:
                core_copy(2 * pair, 0).start()

        @pl.when(pair > 0)
        def _():
            for copy in norm_copies(layer, True):
                copy.wait()

        tick(pair, 0)

        def up_weight_grad(second, block):
            half = other if second == 0 else core
            at = pl.ds(pl.multiple_of(half * (width // 2), width // 2), width // 2)
            columns = pl.ds(pl.multiple_of(block * width, width), width)
            store_block(2 * pair + 1, 1, second, block, dot_plain(adapted_t[at, :], slope[slot, :, columns]))

        def adapted_grad(i):
            r = pl.multiple_of(i * tile, tile)
            value = dot_cols(slope[slot, pl.ds(r, tile), :], wup[layer])
            for q in range(2):
                gc[2 * i + q, pad : pad + frames, :] = value[q * frames : (q + 1) * frames]

        def norm_conv_back(i):
            for q in range(2):
                norm_back(layer, 2 * i + q)
                conv_back(layer, 2 * i + q)

        adapted_grad(0)
        up_weight_grad(0, 0)

        def tile_body(i, carry):
            adapted_grad(i + 1)
            up_weight_grad(0, i + 1)
            norm_conv_back(i)
            return carry

        lax.fori_loop(0, rows // tile - 1, tile_body, 0)
        core_copy(2 * pair + 1, 1).start()
        for block in range(3):
            up_weight_grad(1, block)
        norm_conv_back(rows // tile - 1)

        @pl.when(layer > 0)
        def _():
            for copy in norm_copies(layer - 1, True):
                copy.start()

        @pl.when(layer >= 2)
        def _():
            for which in range(2):
                saved_copy(layer, which, True).start()

        gamma = params[layer, gamma_row : gamma_row + 1, :]
        small[layer, gamma_row : gamma_row + 1, :] = jnp.sum(sums[0], axis=0, keepdims=True) / gamma
        small[layer, down_bias_row : down_bias_row + 1, :] = jnp.sum(sums[1], axis=0, keepdims=True)
        for block in range(blocks):
            row = up_bias_row + block // 2
            place = (block % 2) * tile
            small[layer, row : row + 1, place : place + tile] = jnp.sum(up_sums[block], axis=0, keepdims=True)
        for k in range(7):
            small[layer, taps_row + k : taps_row + k + 1, :] = jnp.sum(sums[2 + k], axis=0, keepdims=True)
        small[layer, conv_bias_row : conv_bias_row + 1, :] = jnp.sum(sums[9], axis=0, keepdims=True)
        tick(pair, 1)
        return carry

    lax.fori_loop(0, layers, backward, 0)

    grad_remote = to_core(g, ends.at[0, :, 1], ends_send.at[2], ends_recv.at[1])
    grad_local = pltpu.make_async_copy(g, ends.at[0, :, 0], ends_send.at[3])

    @pl.when(core == 0)
    def _():
        grad_local.start()

    @pl.when(core == 1)
    def _():
        grad_remote.start()

    small_core = to_core(
        small.at[pl.ds(per_core * other, per_core)], small_in.at[bits], small_send.at[bits], small_recv.at[bits]
    )
    small_core.start()

    def small_copy(bit):
        return to_batch(small_sum, small_in.at[bit], small_send.at[bit], small_recv.at[bit], partner(bit))

    def drain(pair, carry):
        for phase in range(2):
            tick(pair, phase)
            for step in range(bits + 1):

                @pl.when(2 * pair + phase - matrices == step)
                def _(step=step):
                    if step == 0:
                        small_core.wait()
                        small_sum[...] = small[pl.ds(per_core * core, per_core)] + small_in[bits]
                    else:
                        small_copy(step - 1).wait()
                        small_sum[...] = small_sum[...] + small_in[step - 1]
                    if step < bits:
                        small_copy(step).start()

        return carry

    lax.fori_loop(layers, (matrices - 2 + last_step) // 2 + 1, drain, 0)
    small_out[...] = small_sum[...]

    @pl.when(core == 0)
    def _():
        grad_local.wait()
        grad_remote.wait_recv()

    @pl.when(core == 1)
    def _():
        result_remote.wait_recv()
        grad_remote.wait_send()


def results_kernel(
    small,
    conv_kernel_out,
    conv_bias_out,
    band_scale_out,
    band_shift_out,
    up_bias_out,
    down_bias_out,
    layer_scale_out,
):
    per_core, _, width = small.shape
    for j in range(per_core):
        conv_kernel_out[:, j] = small[j, taps_row : taps_row + 7]
        conv_bias_out[j : j + 1] = small[j, conv_bias_row : conv_bias_row + 1]
        band_scale_out[j] = small[j, scale_row : scale_row + 4]
        band_shift_out[j] = small[j, shift_row : shift_row + 4]
        for q in range(3):
            row = up_bias_row + q
            up_bias_out[j : j + 1, q * width : (q + 1) * width] = small[j, row : row + 1]
        down_bias_out[j : j + 1] = small[j, down_bias_row : down_bias_row + 1]
        layer_scale_out[j : j + 1] = small[j, gamma_row : gamma_row + 1]


def body(
    inputs,
    grad_out,
    band_ids,
    conv_kernel,
    conv_bias,
    band_scale,
    band_shift,
    up_weight,
    up_bias,
    down_weight,
    down_bias,
    layer_scale,
):
    sections = lax.axis_size("section")
    batch = lax.axis_size("batch")
    clips, local_clips, frames, width = inputs.shape
    per_core, _, hidden_width = up_weight.shape
    layers = per_core * sections
    bands = band_scale.shape[1]
    rows = clips * frames
    assert sections == 2 and local_clips == 2 and batch & (batch - 1) == 0
    assert hidden_width == 3 * width and bands == 4 and layers == 4 and rows == 3 * width // 2
    plan = Plan(batch, rows)
    bits = plan.bits
    hbm = pl.BlockSpec(memory_space=pl.ANY)
    vmem = pl.BlockSpec(memory_space=pltpu.VMEM)
    smem = pl.BlockSpec(memory_space=pltpu.SMEM)
    padded = frames + 2 * pad
    dma = pltpu.SemaphoreType.DMA
    lanes = len(plan.lanes)
    tile = 2 * frames
    ends_shape = jax.ShapeDtypeStruct((1, clips, local_clips, frames, width), f32)
    up_shape = jax.ShapeDtypeStruct((per_core, 2, width // 2, hidden_width), f32)
    down_shape = jax.ShapeDtypeStruct((per_core, 2, hidden_width // 2, width), f32)
    small_shape = jax.ShapeDtypeStruct((per_core, packed_rows, width), f32)
    conv_kernel = jnp.transpose(conv_kernel, (1, 0, 2))
    ends, up_grad, down_grad, small, *_ = pl.pallas_call(
        functools.partial(step_kernel, plan),
        out_shape=[
            ends_shape,
            up_shape,
            down_shape,
            small_shape,
            jax.ShapeDtypeStruct((2, hidden_width, rows), bf16),
            jax.ShapeDtypeStruct((2, rows, hidden_width), bf16),
            jax.ShapeDtypeStruct((layers - 1, rows, width), f32),
            jax.ShapeDtypeStruct((layers - 1, rows, 1), f32),
            jax.ShapeDtypeStruct((layers - 1, width, rows), bf16),
        ],
        in_specs=[hbm, hbm, smem, vmem, vmem, vmem, vmem, hbm, vmem, hbm, vmem, vmem],
        out_specs=[hbm, hbm, hbm, vmem, hbm, hbm, hbm, hbm, hbm],
        scratch_shapes=[
            pltpu.VMEM((layers + 1, clips, padded, width), f32),
            pltpu.VMEM((rows, width), f32),
            pltpu.VMEM((rows, 1), f32),
            pltpu.VMEM((width, rows), bf16),
            pltpu.VMEM((2, hidden_width, rows), bf16),
            pltpu.VMEM((2, rows, hidden_width), bf16),
            pltpu.VMEM((2, rows, tile), bf16),
            pltpu.VMEM((rows, width), bf16),
            pltpu.VMEM((clips, frames, width), f32),
            pltpu.VMEM((clips, padded, width), f32),
            pltpu.VMEM((layers, width, hidden_width), bf16),
            pltpu.VMEM((layers, hidden_width, width), bf16),
            pltpu.VMEM((per_core, packed_rows, width), f32),
            pltpu.VMEM((layers, packed_rows, width), f32),
            pltpu.VMEM((layers, hidden_width // tile, 1, tile), f32),
            pltpu.VMEM((rows, tile), f32),
            pltpu.VMEM((rows, tile), f32),
            pltpu.VMEM((clips, bands, width), f32),
            pltpu.VMEM((10, 8, width), f32),
            pltpu.VMEM((hidden_width // tile, 8, tile), f32),
            pltpu.VMEM((layers, packed_rows, width), f32),
            pltpu.VMEM((2 * layers, clips, frames, width), f32),
            pltpu.VMEM((2, clips, frames, width), f32),
            pltpu.VMEM((2, clips, frames, width), f32),
            pltpu.VMEM((per_core, packed_rows, width), f32),
            pltpu.VMEM((bits + 1, per_core, packed_rows, width), f32),
            *[pltpu.VMEM((2, plan.slot_rows[stage][1], width), f32) for stage in range(bits)],
            dma((2 * clips,)),
            dma((2 * per_core,)),
            dma((4 * per_core,)),
            dma((4 * per_core,)),
            dma((1,)),
            dma((1,)),
            dma((4,)),
            dma((2,)),
            dma((2,)),
            dma((2,)),
            dma((bits, 2, lanes)),
            dma((bits, 2, lanes)),
            dma((layers, lanes)),
            dma((layers, lanes)),
            dma((bits, 2, 2, lanes)),
            dma((bits, 2, 2, lanes)),
            dma((layers, 2, 3)),
            pltpu.SemaphoreType.REGULAR((bits, lanes)),
            dma((bits + 1,)),
            dma((bits + 1,)),
            dma((2, 2)),
            dma((3,)),
        ],
        compiler_params=pltpu.CompilerParams(
            collective_id=0, has_side_effects=True, vmem_limit_bytes=255 * 2**18
        ),
        cost_estimate=pl.CostEstimate(
            flops=24 * rows * width * hidden_width * 2, bytes_accessed=2**26, transcendentals=2**24
        ),
        name="blocks_step",
    )(
        inputs,
        grad_out,
        jnp.transpose(band_ids),
        conv_kernel,
        conv_bias,
        band_scale,
        band_shift,
        up_weight,
        up_bias,
        down_weight,
        down_bias,
        layer_scale,
    )

    def like(array):
        return jax.ShapeDtypeStruct(array.shape, f32)

    taps_grad, conv_bias_grad, scale_grad, shift_grad, up_bias_grad, down_bias_grad, gamma_grad = pl.pallas_call(
        results_kernel,
        out_shape=[
            like(array)
            for array in (conv_kernel, conv_bias, band_scale, band_shift, up_bias, down_bias, layer_scale)
        ],
        in_specs=[vmem],
        out_specs=[vmem] * 7,
        cost_estimate=pl.CostEstimate(flops=0, bytes_accessed=2**18, transcendentals=0),
        name="results",
    )(small)
    return (
        ends,
        jnp.transpose(taps_grad, (1, 0, 2)),
        conv_bias_grad,
        scale_grad,
        shift_grad,
        up_grad.reshape(up_weight.shape),
        up_bias_grad,
        down_grad.reshape(down_weight.shape),
        down_bias_grad,
        gamma_grad,
    )


def solution(mesh):
    in_specs = (
        P(None, "batch", None, None),
        P(None, "batch", None, None),
        P(None, "batch"),
        P("section", None, None),
        P("section", None),
        P("section", None, None),
        P("section", None, None),
        P("section", None, None),
        P("section", None),
        P("section", None, None),
        P("section", None),
        P("section", None),
    )
    out_specs = (
        P("section", None, "batch", None, None),
        P("section", None, None),
        P("section", None),
        P("section", None, None),
        P("section", None, None),
        P("section", None, None),
        P("section", None),
        P("section", None, None),
        P("section", None),
        P("section", None),
    )
    return jax.shard_map(body, mesh=mesh, in_specs=in_specs, out_specs=out_specs, check_vma=False)
```

```python
import functools

import jax
import jax.numpy as jnp
from jax import lax
from jax.experimental import pallas as pl
from jax.experimental.pallas import tpu as pltpu
from jax.sharding import PartitionSpec as P

norm_epsilon = 1e-06
f32 = jnp.float32
bf16 = jnp.bfloat16

log_density = -1.3257480647361593

taps_row, conv_bias_row, scale_row, shift_row, up_bias_row, down_bias_row, gamma_row = 0, 7, 8, 12, 16, 19, 20
packed_rows = 24
pad = 8
chunk = 32


def gelu_and_slope(u):
    cdf = 0.5 * lax.erf(u * 0.7071067811865476) + 0.5
    density = jnp.exp2(u * (u * (-0.5 * 1.4426950408889634)) + log_density)
    return u * cdf, cdf + u * density


def fold(values):
    rows, columns = values.shape
    return jnp.sum(values.reshape(rows // 8, 8, columns), axis=0)


def dot_plain(left, right):
    return lax.dot_general(left, right, (((1,), (0,)), ((), ())), preferred_element_type=f32)


def dot_cols(left, right):
    return lax.dot_general(left, right, (((1,), (1,)), ((), ())), preferred_element_type=f32)


class Plan:
    def __init__(self, batch, rows):
        self.bits = batch.bit_length() - 1
        order = [(bit, bit) for bit in range(self.bits)]
        if self.bits > 1:
            order[:2] = [(0, 1), (1, 0)]
        late = order[:]
        if self.bits > 2:
            late = [order[2]] + order[:2] + order[3:]
        third = rows // 3
        self.lanes = [(0, 2 * third, order), (2 * third, third, late)]
        self.kept = []
        self.halves = []
        self.slot_rows = []
        for _, size, _ in self.lanes:
            kept, halves = [size], []
            for stage in range(self.bits):
                halves.append(stage < self.bits - 1 and kept[-1] // 2 % 8 == 0)
                kept.append(kept[-1] // 2 if halves[-1] else kept[-1])
            self.kept.append(kept)
            self.halves.append(halves)
        self.doublings = max(sum(halves) for halves in self.halves)
        for stage in range(self.bits):
            begin, starts = 0, []
            for lane in range(len(self.lanes)):
                starts.append(begin)
                begin += self.kept[lane][stage + 1]
            self.slot_rows.append((starts, begin))


def step_kernel(
    plan,
    inputs,
    grad_out,
    band_ids,
    conv_kernel,
    conv_bias,
    band_scale,
    band_shift,
    up_weight,
    up_bias,
    down_weight,
    down_bias,
    layer_scale,
    ends,
    up_out,
    down_out,
    small_out,
    hidden_spill,
    slope_spill,
    normed_spill,
    inv_spill,
    adapted_spill,
    xs,
    normed,
    inv_std,
    adapted_t,
    hidden_t,
    slope,
    hidden_near,
    gb,
    g,
    gc,
    wup,
    wdn,
    packed,
    params,
    up_bias_row_of,
    upper_even,
    upper_odd,
    onehot,
    sums,
    up_sums,
    small,
    keep,
    outgo,
    income,
    small_sum,
    small_in,
    *rest,
):
    stage_in = rest[: plan.bits]
    (
        load_sem,
        own_sem,
        wt_send,
        wt_recv,
        par_send,
        par_recv,
        ends_send,
        ends_recv,
        core_send,
        core_recv,
        rs_send,
        rs_recv,
        deliver_send,
        deliver_recv,
        ag_send,
        ag_recv,
        out_sem,
        credit,
        small_send,
        small_recv,
        spill_sem,
        norm_sem,
    ) = rest[plan.bits :]
    uppers = (upper_even, upper_odd)
    core = lax.axis_index("section")
    other = 1 - core
    batch = lax.axis_index("batch")
    clips, frames, width = g.shape
    rows = clips * frames
    layers = xs.shape[0] - 1
    per_core = layers // 2
    hidden_width = slope.shape[2]
    tile = 2 * frames
    chunks = frames // chunk
    blocks = hidden_width // tile
    bits = plan.bits
    mesh_id = pl.DeviceIdType.MESH

    def bit_of(bit):
        return (batch // (1 << bit)) % 2

    def partner(bit):
        return batch + (1 - 2 * bit_of(bit)) * (1 << bit)

    def choose(pair, side, value):
        first, second = pair
        if first == second:
            return value(first)
        if isinstance(side, int):
            return value(pair[side])
        return (1 - side) * value(first) + side * value(second)

    def to_core(source, target, send, recv):
        return pltpu.make_async_remote_copy(source, target, send, recv, {"section": other}, mesh_id)

    def to_batch(source, target, send, recv, device):
        return pltpu.make_async_remote_copy(source, target, send, recv, {"batch": device}, mesh_id)

    own_blocks = pl.ds(per_core * core, per_core)
    own = []
    for j in range(per_core):
        for source, target in ((up_weight, wup), (down_weight, wdn)):
            own.append(pltpu.make_async_copy(source.at[j], target.at[per_core * core + j], own_sem.at[len(own)]))
    own[0].start()
    loads = []
    for source, target in ((inputs, slope.at[0, :, 0:width]), (grad_out, gb)):
        for clip in range(clips):
            loads.append(
                pltpu.make_async_copy(
                    source.at[clip, core], target.at[pl.ds(clip * frames, frames)], load_sem.at[len(loads)]
                )
            )
    for load in loads[:clips]:
        load.start()
    for load in own[1:] + loads[clips:]:
        load.start()

    for j in range(per_core):
        packed[j, taps_row : taps_row + 7] = conv_kernel[:, j]
        packed[j, conv_bias_row : conv_bias_row + 1] = conv_bias[j : j + 1]
        packed[j, scale_row : scale_row + 4] = band_scale[j]
        packed[j, shift_row : shift_row + 4] = band_shift[j]
        for q in range(3):
            row = up_bias_row + q
            packed[j, row : row + 1] = up_bias[j : j + 1, q * width : (q + 1) * width]
        packed[j, down_bias_row : down_bias_row + 1] = down_bias[j : j + 1]
        packed[j, gamma_row : gamma_row + 1] = layer_scale[j : j + 1]
        packed[j, gamma_row + 1 : packed_rows] = jnp.zeros((packed_rows - gamma_row - 1, width), f32)

    barrier = pltpu.get_barrier_semaphore()
    pl.semaphore_signal(barrier, inc=1, device_id={"section": other}, device_id_type=mesh_id)
    for bit in range(bits):
        pl.semaphore_signal(barrier, inc=1, device_id={"batch": partner(bit)}, device_id_type=mesh_id)

    for load in loads[:clips]:
        load.wait()

    def load_x(clip, carry):
        xs[0, clip, 0:pad, :] = jnp.zeros((pad, width), f32)
        xs[0, clip, pad + frames : 2 * pad + frames, :] = jnp.zeros((pad, width), f32)
        xs[0, clip, pad : pad + frames, :] = slope[
            0, pl.ds(pl.multiple_of(clip * frames, frames), frames), 0:width
        ].astype(f32)
        for band in range(4):
            chosen = jnp.where(band_ids[core, clip] == band, 1.0, 0.0).astype(f32)
            onehot[clip, band : band + 1] = jnp.zeros((1, width), f32) + chosen
        return carry

    lax.fori_loop(0, clips, load_x, 0)
    pl.semaphore_wait(barrier, 1 + bits)

    par_copy = to_core(packed, params.at[own_blocks], par_send.at[0], par_recv.at[0])
    par_copy.start()
    params[own_blocks] = packed[...]

    stages = [
        xs.at[1, :, 0:frames],
        xs.at[2, :, 0:frames],
        xs.at[3, :, 0:frames],
        outgo.at[0],
        outgo.at[1],
        xs.at[4, :, 0:frames],
        gc.at[:, 0:frames],
        outgo.at[0],
    ]

    def weight_part(kind, layer, half, part):
        if kind == 0:
            return wup.at[
                layer,
                pl.ds(pl.multiple_of(half * (width // 2) + (part % 2) * frames, frames), frames),
                pl.ds(pl.multiple_of((part // 2) * width, width), width),
            ]
        return wdn.at[layer, pl.ds(pl.multiple_of(half * rows + part * frames, frames), frames), :]

    def weight_copy(stage, k):
        return to_core(stage, keep.at[k], wt_send.at[k], wt_recv.at[k])

    def send_weights(k):
        j, kind, half = k // 4, k // 2 % 2, k % 2

        def cast(i, carry):
            for part in (2 * i, 2 * i + 1):
                stages[k][part] = weight_part(kind, per_core * core + j, half, part)[...].astype(f32)
            return carry

        lax.fori_loop(0, clips // 2, cast, 0)
        weight_copy(stages[k], k).start()

    def take_weights(layer, kind):
        @pl.when(layer // per_core != core)
        def _():
            for half in range(2):
                k = 4 * (layer % per_core) + 2 * kind + half
                weight_copy(outgo.at[0], k).wait_recv()

                def cast(i, carry, half=half, k=k):
                    for part in (2 * i, 2 * i + 1):
                        weight_part(kind, layer, half, part)[...] = keep[k, part].astype(bf16)
                    return carry

                lax.fori_loop(0, clips // 2, cast, 0)

    for kind in range(2):
        own[kind].wait()
        for half in range(2):
            send_weights(2 * kind + half)
    par_copy.wait()
    for layer in range(layers):
        for block in range(blocks):
            row = up_bias_row + block // 2
            place = (block % 2) * tile
            up_bias_row_of[layer, block] = params[layer, row : row + 1, place : place + tile]

    def chosen_row(layer, clip, first):
        return jnp.sum(onehot[clip] * params[layer, first : first + 4], axis=0, keepdims=True)

    adapted_place = slice(hidden_width - width, hidden_width)

    def norm_clip(layer, clip):
        table = params[layer]
        scale = chosen_row(layer, clip, scale_row)
        shift = chosen_row(layer, clip, shift_row)
        for j in range(chunks):
            window = xs[layer, clip, j * chunk : (j + 1) * chunk + 2 * pad, :]
            conv = window[pad : pad + chunk] * table[3:4] + table[conv_bias_row : conv_bias_row + 1]
            for k in (0, 1, 2, 4, 5, 6):
                conv = conv + window[pad - 3 + k : pad - 3 + k + chunk] * table[k : k + 1]
            centered = conv - jnp.mean(conv, axis=-1, keepdims=True)
            inv = lax.rsqrt(jnp.mean(centered * centered, axis=-1, keepdims=True) + norm_epsilon)
            value = centered * inv
            at = pl.ds(pl.multiple_of(clip * frames + j * chunk, chunk), chunk)
            normed[at, :] = value
            inv_std[at, :] = inv
            slope[layer % 2, at, adapted_place] = (value * scale + shift).astype(bf16)

    def saved_copy(layer, which, back):
        buffer = (hidden_t if which == 0 else slope).at[layer % 2]
        away = (hidden_spill if which == 0 else slope_spill).at[layer % 2]
        source, target = (away, buffer) if back else (buffer, away)
        return pltpu.make_async_copy(source, target, spill_sem.at[layer % 2, which])

    def norm_copies(layer, back, which=(0, 1, 2)):
        copies = []
        kept = ((normed, normed_spill), (inv_std, inv_spill), (adapted_t, adapted_spill))
        for i in which:
            near, away = kept[i]
            source, target = (away.at[layer], near) if back else (near, away.at[layer])
            copies.append(pltpu.make_async_copy(source, target, norm_sem.at[i]))
        return copies

    branch_sum = g.reshape(rows, width)

    def norm_pair(i, carry):
        for q in range(2):
            norm_clip(0, 2 * i + q)
        return carry

    lax.fori_loop(0, clips // 2, norm_pair, 0)
    for copy in norm_copies(0, False, (0, 1)):
        copy.start()
    for load in own[2:]:
        load.wait()
    for k in range(4, 4 * per_core - 1):
        send_weights(k)

    def forward(layer, carry):
        slot = layer % 2

        @pl.when(layer > 0)
        def _():
            norm_copies(layer - 1, False, (2,))[0].wait()

        take_weights(layer, 0)

        def up(block):
            columns = slice(block * tile, (block + 1) * tile)
            uppers[block % 2][...] = dot_plain(slope[slot, :, adapted_place], wup[layer, :, columns])

        def down(block):
            columns = slice(block * tile, (block + 1) * tile)
            here = hidden_near[block % 2]
            value = dot_plain(here, wdn[layer, columns, :])
            branch_sum[...] = value if block == 0 else branch_sum[...] + value
            hidden_t[slot, columns, :] = here.T

        up(0)
        for block in range(blocks):
            columns = slice(block * tile, (block + 1) * tile)
            if block + 1 < blocks:
                up(block + 1)
            if block == 0:
                adapted_t[...] = slope[slot, :, adapted_place].T
            if block == 1:
                take_weights(layer, 1)
            if block > 0:
                down(block - 1)
            bias = up_bias_row_of[layer, block]
            for q in range(rows // chunk):
                at = slice(q * chunk, (q + 1) * chunk)
                smooth, steep = gelu_and_slope(uppers[block % 2][at, :] + bias)
                hidden_near[block % 2, at, :] = smooth.astype(bf16)
                slope[slot, at, columns] = steep.astype(bf16)
        down(blocks - 1)

        @pl.when(layer < layers - 1)
        def _():
            norm_copies(layer, False, (2,))[0].start()

        @pl.when(layer < 2)
        def _():
            for which in range(2):
                saved_copy(layer, which, False).start()

        for step in range(layers):

            @pl.when(layer == step)
            def _(step=step):
                for k in [step] if step < layers - 1 else range(layers, 4 * per_core):
                    weight_copy(outgo.at[0], k).wait_send()
                if step == 0:
                    weight_copy(outgo.at[0], layers - 1).wait_send()
                    send_weights(4 * per_core - 1)

        def residual(clip):
            bias = params[layer, down_bias_row : down_bias_row + 1]
            gamma = params[layer, gamma_row : gamma_row + 1]
            xs[layer + 1, clip, 0:pad, :] = jnp.zeros((pad, width), f32)
            xs[layer + 1, clip, pad + frames : 2 * pad + frames, :] = jnp.zeros((pad, width), f32)
            xs[layer + 1, clip, pad : pad + frames, :] = xs[layer, clip, pad : pad + frames, :] + gamma * (
                g[clip] + bias
            )

        def residual_pair(i, carry):
            for q in range(2):
                residual(2 * i + q)
            return carry

        def residual_norm_pair(i, carry):
            for q in range(2):
                residual(2 * i + q)
            for q in range(2):
                norm_clip(layer + 1, 2 * i + q)
            return carry

        @pl.when((layer >= 1) & (layer < layers - 1))
        def _():
            for which in range(2):
                saved_copy(layer - 1, which, False).wait()

        @pl.when(layer < layers - 1)
        def _():
            for copy in norm_copies(layer, False, (0, 1)):
                copy.wait()
            lax.fori_loop(0, clips // 2, residual_norm_pair, 0)

        @pl.when(layer < layers - 2)
        def _():
            for copy in norm_copies(layer + 1, False, (0, 1)):
                copy.start()

        @pl.when(layer == layers - 1)
        def _():
            lax.fori_loop(0, clips // 2, residual_pair, 0)

        return carry

    lax.fori_loop(0, layers, forward, 0)

    result = xs.at[layers, :, pad : pad + frames]
    result_remote = to_core(result, ends.at[0, :, 0], ends_send.at[0], ends_recv.at[0])
    result_local = pltpu.make_async_copy(result, ends.at[0, :, 1], ends_send.at[1])

    @pl.when(core == 0)
    def _():
        result_remote.start()

    @pl.when(core == 1)
    def _():
        result_local.start()

    for load in loads[clips:]:
        load.wait()

    def load_g(clip, carry):
        g[clip] = gb[pl.ds(pl.multiple_of(clip * frames, frames), frames), :].astype(f32)
        gc[clip, 0:pad, :] = jnp.zeros((pad, width), f32)
        gc[clip, pad + frames : 2 * pad + frames, :] = jnp.zeros((pad, width), f32)
        return carry

    lax.fori_loop(0, clips, load_g, 0)

    matrices = 2 * layers
    lane_count = len(plan.lanes)

    def core_copy(m, parity):
        return to_core(outgo.at[parity], income.at[parity], core_send.at[parity], core_recv.at[parity])

    keep_rows = keep.reshape(matrices, rows, width)

    def offset(lane, stage, side):
        start = 0
        for s in range(stage):
            if plan.halves[lane][s]:
                start = start + choose(plan.lanes[lane][2][s], side, bit_of) * plan.kept[lane][s + 1]
        return start

    def rs_copy(m, parity, lane, stage):
        begin, _, order = plan.lanes[lane]
        size = plan.kept[lane][stage + 1]
        at = begin + offset(lane, stage, core)
        if plan.halves[lane][stage]:
            at = at + (1 - choose(order[stage], core, bit_of)) * size
        starts, _ = plan.slot_rows[stage]
        return to_batch(
            keep_rows.at[m, pl.ds(pl.multiple_of(at, 8), size)],
            stage_in[stage].at[parity, starts[lane] : starts[lane] + size],
            rs_send.at[stage, parity, lane],
            rs_recv.at[stage, parity, lane],
            choose(order[stage], core, partner),
        )

    def rs_add(m, parity, lane, stage):
        begin, _, _ = plan.lanes[lane]
        size = plan.kept[lane][stage + 1]
        at = begin + offset(lane, stage + 1, core)
        starts, _ = plan.slot_rows[stage]
        step = min(size, 2 * chunk)

        def body(i, carry):
            r = pl.multiple_of(at + i * step, 8)
            keep_rows[m, pl.ds(r, step), :] = (
                keep_rows[m, pl.ds(r, step), :]
                + stage_in[stage][parity, pl.ds(pl.multiple_of(starts[lane] + i * step, 8), step), :]
            )
            return carry

        lax.fori_loop(0, size // step, body, 0)

    half_way = matrices // 2
    xs_rows = xs.reshape(layers + 1, clips * (frames + 2 * pad), width)

    def rows_of(m, owner, own, lane, at, size):
        span = pl.ds(pl.multiple_of(plan.lanes[lane][0] + at, 8), size)
        if own:
            return keep_rows.at[m, span]
        return xs_rows.at[layers - m, span] if owner == 1 else keep_rows.at[m - half_way, span]

    def deliver_copy(m, owner, lane):
        size = plan.kept[lane][bits]
        at = offset(lane, bits, 1 - owner)
        return to_core(
            rows_of(m, owner, True, lane, at, size),
            rows_of(m, owner, False, lane, at, size),
            deliver_send.at[m % half_way, lane],
            deliver_recv.at[m % half_way, lane],
        )

    def ag_copy(m, owner, own, parity, lane, stage):
        size = plan.kept[lane][stage + 1]
        side = owner if own else 1 - owner
        place = rows_of(m, owner, own, lane, offset(lane, stage + 1, side), size)
        return to_batch(
            place,
            place,
            ag_send.at[stage, parity, own, lane],
            ag_recv.at[stage, parity, own, lane],
            choose(plan.lanes[lane][2][stage], side, partner),
        )

    def out_copies(m, kind, local, owner):
        copies = []
        third = rows // 3
        for own in range(2):
            half = owner if own else 1 - owner
            if own:
                source = keep_rows.at[m]
            else:
                source = xs_rows.at[layers - m] if owner == 1 else keep_rows.at[m - half_way]
            sem = out_sem.at[m % half_way, own]
            if kind == 0:
                copies.append(pltpu.make_async_copy(source.at[0:rows], down_out.at[local, half], sem.at[0]))
                continue
            for part in range(3):
                columns = slice(part * width, (part + 1) * width)
                copies.append(
                    pltpu.make_async_copy(
                        source.at[part * third : (part + 1) * third],
                        up_out.at[local, half, :, columns],
                        sem.at[part],
                    )
                )
        return copies

    def owner_of(m):
        return 1 - m // half_way

    def owned_by(owner, m):
        return m < half_way if owner == 1 else m >= half_way

    last_step = bits + plan.doublings + 3

    def tick(pair, phase):
        for s in range(last_step, 0, -1):
            m = 2 * pair + phase + 1 - s
            parity = (phase + 1 - s) % 2
            kind = parity
            local = (layers - 1 - (m - kind) // 2) % per_core
            valid = (m >= 0) & (m < matrices)

            if s <= bits + 1:

                @pl.when(valid)
                def _(s=s, m=m, parity=parity):
                    if s == 1:
                        core_copy(m, parity).wait()

                        def body(clip, carry):
                            keep[m, clip] = keep[m, clip] + income[parity, clip]
                            return carry

                        lax.fori_loop(0, clips, body, 0)
                    else:
                        for lane in range(lane_count):
                            rs_copy(m, parity, lane, s - 2).wait()
                            if plan.halves[lane][s - 2]:
                                @pl.when(owner_of(m) == core)
                                def _(lane=lane):
                                    pl.semaphore_signal(
                                        credit.at[s - 2, lane],
                                        inc=1,
                                        device_id={"batch": choose(plan.lanes[lane][2][s - 2], core, partner)},
                                        device_id_type=mesh_id,
                                    )

                            rs_add(m, parity, lane, s - 2)
                    if s <= bits:
                        for lane in range(lane_count):
                            rs_copy(m, parity, lane, s - 1).start()

            for owner in range(2):
                if s == bits + 1:

                    @pl.when(valid & owned_by(owner, m) & (core == 1 - owner))
                    def _(m=m, owner=owner):
                        for lane in range(lane_count):
                            deliver_copy(m, owner, lane).start()

                if s > bits + 1:

                    @pl.when(valid & owned_by(owner, m) & (core == owner))
                    def _(s=s, m=m, parity=parity, kind=kind, local=local, owner=owner):
                        if s == bits + 2:
                            for lane in range(lane_count):
                                deliver_copy(m, owner, lane).wait_recv()
                        elif s < last_step:
                            stage = last_step - 1 - s
                            for lane in range(lane_count):
                                if plan.halves[lane][stage]:
                                    for own in range(2):
                                        ag_copy(m, owner, own, parity, lane, stage).wait()
                        if s < last_step - 1:
                            stage = last_step - 2 - s
                            for lane in range(lane_count):
                                if plan.halves[lane][stage]:
                                    pl.semaphore_wait(credit.at[stage, lane], 1)
                                    for own in range(2):
                                        ag_copy(m, owner, own, parity, lane, stage).start()
                        elif s == last_step - 1:
                            for copy in out_copies(m, kind, local, owner):
                                copy.start()
                        else:
                            for copy in out_copies(m, kind, local, owner):
                                copy.wait()

        m = 2 * pair + phase - bits
        for owner in range(2):

            @pl.when((m >= 0) & (m < matrices) & owned_by(owner, m) & (core == 1 - owner))
            def _(m=m, owner=owner):
                for lane in range(lane_count):
                    deliver_copy(m, owner, lane).wait_send()

    def store_block(m, phase, second, block, value):
        for q in range(2):
            piece = value[q * frames : (q + 1) * frames]
            if second == 0:
                outgo[phase, 2 * block + q] = piece
            else:
                keep[m, 2 * block + q] = piece

    def scale_clip(layer, clip):
        gamma = params[layer, gamma_row : gamma_row + 1]
        gamma_sum = bias_sum = jnp.zeros((8, width), f32)
        for j in range(chunks):
            here = g[clip, j * chunk : (j + 1) * chunk, :]
            at = slice(pad + j * chunk, pad + (j + 1) * chunk)
            gamma_sum = gamma_sum + fold(here * (xs[layer + 1, clip, at, :] - xs[layer, clip, at, :]))
            value = (gamma * here).astype(bf16)
            gb[pl.ds(pl.multiple_of(clip * frames + j * chunk, chunk), chunk), :] = value
            bias_sum = bias_sum + fold(value.astype(f32))
        sums[0] += gamma_sum
        sums[1] += bias_sum

    def norm_back(layer, clip):
        scale = chosen_row(layer, clip, scale_row)
        scale_sum = shift_sum = conv_sum = jnp.zeros((8, width), f32)
        for j in range(chunks):
            row = pl.ds(pl.multiple_of(clip * frames + j * chunk, chunk), chunk)
            at = slice(pad + j * chunk, pad + (j + 1) * chunk)
            ga = gc[clip, at, :]
            value = normed[row, :]
            scale_sum = scale_sum + fold(ga * value)
            shift_sum = shift_sum + fold(ga)
            dn = ga * scale
            first = jnp.mean(dn, axis=-1, keepdims=True)
            second = jnp.mean(dn * value, axis=-1, keepdims=True)
            result = inv_std[row, :] * (dn - first - value * second)
            gc[clip, at, :] = result
            conv_sum = conv_sum + fold(result)
        sums[9] += conv_sum
        choice = onehot[clip]
        small[layer, scale_row : scale_row + 4, :] += choice * jnp.sum(scale_sum, axis=0, keepdims=True)
        small[layer, shift_row : shift_row + 4, :] += choice * jnp.sum(shift_sum, axis=0, keepdims=True)

    def conv_back(layer, clip):
        table = params[layer]
        totals = [jnp.zeros((8, width), f32) for _ in range(7)]
        for j in range(chunks):
            grads = gc[clip, j * chunk : (j + 1) * chunk + 2 * pad, :]
            signal = xs[layer, clip, pad + j * chunk : pad + (j + 1) * chunk, :]
            at = slice(j * chunk, (j + 1) * chunk)
            total = g[clip, at, :]
            for k in (3, 0, 1, 2, 4, 5, 6):
                shifted = grads[pad + 3 - k : pad + 3 - k + chunk]
                total = total + shifted * table[k : k + 1]
                totals[k] = totals[k] + fold(signal * shifted)
            g[clip, at, :] = total
        for k in range(7):
            sums[2 + k] += totals[k]

    def backward(pair, carry):
        layer = layers - 1 - pair
        slot = layer % 2

        @pl.when((pair == 1) & (core == 0))
        def _():
            result_remote.wait_send()

        @pl.when((pair == 1) & (core == 1))
        def _():
            result_local.wait()

        sums[...] = jnp.zeros(sums.shape, f32)
        small[layer] = jnp.zeros(small.shape[1:], f32)

        def scale_body(clip, carry):
            scale_clip(layer, clip)
            return carry

        lax.fori_loop(0, clips, scale_body, 0)

        @pl.when(layer < 2)
        def _():
            for which in range(2):
                saved_copy(layer, which, True).wait()

        def up_grad(block):
            columns = pl.ds(pl.multiple_of(block * tile, tile), tile)
            value = dot_cols(gb[...], wdn[layer, columns, :])
            total = jnp.zeros((8, tile), f32)
            for q in range(rows // chunk):
                at = slice(q * chunk, (q + 1) * chunk)
                piece = (value[at] * slope[slot, at, columns].astype(f32)).astype(bf16)
                slope[slot, at, columns] = piece
                total = total + fold(piece.astype(f32))
            up_sums[block] = total

        for second in range(2):
            half = other if second == 0 else core

            def down_body(block, carry, second=second, half=half):
                at = pl.ds(pl.multiple_of(half * rows + block * tile, tile), tile)
                store_block(2 * pair, 0, second, block, dot_plain(hidden_t[slot, at, :], gb[...]))
                up_grad(block + 3 * second)
                return carry

            lax.fori_loop(0, clips // 2, down_body, 0)
            if second == 0:
                core_copy(2 * pair, 0).start()

        @pl.when(pair > 0)
        def _():
            for copy in norm_copies(layer, True):
                copy.wait()

        tick(pair, 0)

        def up_weight_grad(second, block):
            half = other if second == 0 else core
            at = pl.ds(pl.multiple_of(half * (width // 2), width // 2), width // 2)
            columns = pl.ds(pl.multiple_of(block * width, width), width)
            store_block(2 * pair + 1, 1, second, block, dot_plain(adapted_t[at, :], slope[slot, :, columns]))

        def adapted_grad(i):
            r = pl.multiple_of(i * tile, tile)
            value = dot_cols(slope[slot, pl.ds(r, tile), :], wup[layer])
            for q in range(2):
                gc[2 * i + q, pad : pad + frames, :] = value[q * frames : (q + 1) * frames]

        def norm_conv_back(i):
            for q in range(2):
                norm_back(layer, 2 * i + q)
                conv_back(layer, 2 * i + q)

        adapted_grad(0)
        up_weight_grad(0, 0)

        def tile_body(i, carry):
            adapted_grad(i + 1)
            up_weight_grad(0, i + 1)
            norm_conv_back(i)
            return carry

        lax.fori_loop(0, rows // tile - 1, tile_body, 0)
        core_copy(2 * pair + 1, 1).start()
        for block in range(3):
            up_weight_grad(1, block)
        norm_conv_back(rows // tile - 1)

        @pl.when(layer > 0)
        def _():
            for copy in norm_copies(layer - 1, True):
                copy.start()

        @pl.when(layer >= 2)
        def _():
            for which in range(2):
                saved_copy(layer, which, True).start()

        gamma = params[layer, gamma_row : gamma_row + 1, :]
        small[layer, gamma_row : gamma_row + 1, :] = jnp.sum(sums[0], axis=0, keepdims=True) / gamma
        small[layer, down_bias_row : down_bias_row + 1, :] = jnp.sum(sums[1], axis=0, keepdims=True)
        for block in range(blocks):
            row = up_bias_row + block // 2
            place = (block % 2) * tile
            small[layer, row : row + 1, place : place + tile] = jnp.sum(up_sums[block], axis=0, keepdims=True)
        for k in range(7):
            small[layer, taps_row + k : taps_row + k + 1, :] = jnp.sum(sums[2 + k], axis=0, keepdims=True)
        small[layer, conv_bias_row : conv_bias_row + 1, :] = jnp.sum(sums[9], axis=0, keepdims=True)
        tick(pair, 1)
        return carry

    lax.fori_loop(0, layers, backward, 0)

    grad_remote = to_core(g, ends.at[0, :, 1], ends_send.at[2], ends_recv.at[1])
    grad_local = pltpu.make_async_copy(g, ends.at[0, :, 0], ends_send.at[3])

    @pl.when(core == 0)
    def _():
        grad_local.start()

    @pl.when(core == 1)
    def _():
        grad_remote.start()

    small_core = to_core(
        small.at[pl.ds(per_core * other, per_core)], small_in.at[bits], small_send.at[bits], small_recv.at[bits]
    )
    small_core.start()

    def small_copy(bit):
        return to_batch(small_sum, small_in.at[bit], small_send.at[bit], small_recv.at[bit], partner(bit))

    def drain(pair, carry):
        for phase in range(2):
            tick(pair, phase)
            for step in range(bits + 1):

                @pl.when(2 * pair + phase - matrices == step)
                def _(step=step):
                    if step == 0:
                        small_core.wait()
                        small_sum[...] = small[pl.ds(per_core * core, per_core)] + small_in[bits]
                    else:
                        small_copy(step - 1).wait()
                        small_sum[...] = small_sum[...] + small_in[step - 1]
                    if step < bits:
                        small_copy(step).start()

        return carry

    lax.fori_loop(layers, (matrices - 2 + last_step) // 2 + 1, drain, 0)
    small_out[...] = small_sum[...]

    @pl.when(core == 0)
    def _():
        grad_local.wait()
        grad_remote.wait_recv()

    @pl.when(core == 1)
    def _():
        result_remote.wait_recv()
        grad_remote.wait_send()


def results_kernel(
    ends,
    small,
    ends_out,
    conv_kernel_out,
    conv_bias_out,
    band_scale_out,
    band_shift_out,
    up_bias_out,
    down_bias_out,
    layer_scale_out,
    stage,
    in_sem,
    out_sem,
):
    per_core, _, width = small.shape
    pieces = [(0, i, j) for i in range(ends.shape[1]) for j in range(ends.shape[2])]
    loads = [pltpu.make_async_copy(ends.at[at], stage.at[i], in_sem.at[i]) for i, at in enumerate(pieces)]
    stores = [pltpu.make_async_copy(stage.at[i], ends_out.at[at], out_sem.at[i]) for i, at in enumerate(pieces)]
    for load in loads:
        load.start()
    for load, store in zip(loads, stores):
        load.wait()
        store.start()
    for j in range(per_core):
        conv_kernel_out[:, j] = small[j, taps_row : taps_row + 7]
        conv_bias_out[j : j + 1] = small[j, conv_bias_row : conv_bias_row + 1]
        band_scale_out[j] = small[j, scale_row : scale_row + 4]
        band_shift_out[j] = small[j, shift_row : shift_row + 4]
        for q in range(3):
            row = up_bias_row + q
            up_bias_out[j : j + 1, q * width : (q + 1) * width] = small[j, row : row + 1]
        down_bias_out[j : j + 1] = small[j, down_bias_row : down_bias_row + 1]
        layer_scale_out[j : j + 1] = small[j, gamma_row : gamma_row + 1]
    for store in stores:
        store.wait()


def body(
    inputs,
    grad_out,
    band_ids,
    conv_kernel,
    conv_bias,
    band_scale,
    band_shift,
    up_weight,
    up_bias,
    down_weight,
    down_bias,
    layer_scale,
):
    sections = lax.axis_size("section")
    batch = lax.axis_size("batch")
    clips, local_clips, frames, width = inputs.shape
    per_core, _, hidden_width = up_weight.shape
    layers = per_core * sections
    bands = band_scale.shape[1]
    rows = clips * frames
    assert sections == 2 and local_clips == 2 and batch & (batch - 1) == 0
    assert hidden_width == 3 * width and bands == 4 and layers == 4 and rows == 3 * width // 2
    plan = Plan(batch, rows)
    bits = plan.bits
    hbm = pl.BlockSpec(memory_space=pl.ANY)
    vmem = pl.BlockSpec(memory_space=pltpu.VMEM)
    smem = pl.BlockSpec(memory_space=pltpu.SMEM)
    padded = frames + 2 * pad
    dma = pltpu.SemaphoreType.DMA
    lanes = len(plan.lanes)
    tile = 2 * frames
    ends_shape = jax.ShapeDtypeStruct((1, clips, local_clips, frames, width), f32)
    up_shape = jax.ShapeDtypeStruct((per_core, 2, width // 2, hidden_width), f32)
    down_shape = jax.ShapeDtypeStruct((per_core, 2, hidden_width // 2, width), f32)
    small_shape = jax.ShapeDtypeStruct((per_core, packed_rows, width), f32)
    conv_kernel = jnp.transpose(conv_kernel, (1, 0, 2))
    ends, up_grad, down_grad, small, *_ = pl.pallas_call(
        functools.partial(step_kernel, plan),
        out_shape=[
            ends_shape,
            up_shape,
            down_shape,
            small_shape,
            jax.ShapeDtypeStruct((2, hidden_width, rows), bf16),
            jax.ShapeDtypeStruct((2, rows, hidden_width), bf16),
            jax.ShapeDtypeStruct((layers - 1, rows, width), f32),
            jax.ShapeDtypeStruct((layers - 1, rows, 1), f32),
            jax.ShapeDtypeStruct((layers - 1, width, rows), bf16),
        ],
        in_specs=[hbm, hbm, smem, vmem, vmem, vmem, vmem, hbm, vmem, hbm, vmem, vmem],
        out_specs=[hbm, hbm, hbm, vmem, hbm, hbm, hbm, hbm, hbm],
        scratch_shapes=[
            pltpu.VMEM((layers + 1, clips, padded, width), f32),
            pltpu.VMEM((rows, width), f32),
            pltpu.VMEM((rows, 1), f32),
            pltpu.VMEM((width, rows), bf16),
            pltpu.VMEM((2, hidden_width, rows), bf16),
            pltpu.VMEM((2, rows, hidden_width), bf16),
            pltpu.VMEM((2, rows, tile), bf16),
            pltpu.VMEM((rows, width), bf16),
            pltpu.VMEM((clips, frames, width), f32),
            pltpu.VMEM((clips, padded, width), f32),
            pltpu.VMEM((layers, width, hidden_width), bf16),
            pltpu.VMEM((layers, hidden_width, width), bf16),
            pltpu.VMEM((per_core, packed_rows, width), f32),
            pltpu.VMEM((layers, packed_rows, width), f32),
            pltpu.VMEM((layers, hidden_width // tile, 1, tile), f32),
            pltpu.VMEM((rows, tile), f32),
            pltpu.VMEM((rows, tile), f32),
            pltpu.VMEM((clips, bands, width), f32),
            pltpu.VMEM((10, 8, width), f32),
            pltpu.VMEM((hidden_width // tile, 8, tile), f32),
            pltpu.VMEM((layers, packed_rows, width), f32),
            pltpu.VMEM((2 * layers, clips, frames, width), f32),
            pltpu.VMEM((2, clips, frames, width), f32),
            pltpu.VMEM((2, clips, frames, width), f32),
            pltpu.VMEM((per_core, packed_rows, width), f32),
            pltpu.VMEM((bits + 1, per_core, packed_rows, width), f32),
            *[pltpu.VMEM((2, plan.slot_rows[stage][1], width), f32) for stage in range(bits)],
            dma((2 * clips,)),
            dma((2 * per_core,)),
            dma((4 * per_core,)),
            dma((4 * per_core,)),
            dma((1,)),
            dma((1,)),
            dma((4,)),
            dma((2,)),
            dma((2,)),
            dma((2,)),
            dma((bits, 2, lanes)),
            dma((bits, 2, lanes)),
            dma((layers, lanes)),
            dma((layers, lanes)),
            dma((bits, 2, 2, lanes)),
            dma((bits, 2, 2, lanes)),
            dma((layers, 2, 3)),
            pltpu.SemaphoreType.REGULAR((bits, lanes)),
            dma((bits + 1,)),
            dma((bits + 1,)),
            dma((2, 2)),
            dma((3,)),
        ],
        compiler_params=pltpu.CompilerParams(
            collective_id=0, has_side_effects=True, vmem_limit_bytes=255 * 2**18
        ),
        cost_estimate=pl.CostEstimate(
            flops=24 * rows * width * hidden_width * 2, bytes_accessed=2**26, transcendentals=2**24
        ),
        name="blocks_step",
    )(
        inputs,
        grad_out,
        jnp.transpose(band_ids),
        conv_kernel,
        conv_bias,
        band_scale,
        band_shift,
        up_weight,
        up_bias,
        down_weight,
        down_bias,
        layer_scale,
    )

    def like(array):
        return jax.ShapeDtypeStruct(array.shape, f32)

    ends, taps_grad, conv_bias_grad, scale_grad, shift_grad, up_bias_grad, down_bias_grad, gamma_grad = (
        pl.pallas_call(
            results_kernel,
            out_shape=[
                like(array)
                for array in (ends, conv_kernel, conv_bias, band_scale, band_shift, up_bias, down_bias, layer_scale)
            ],
            in_specs=[hbm, vmem],
            out_specs=[hbm] + [vmem] * 7,
            scratch_shapes=[
                pltpu.VMEM((clips * local_clips, frames, width), f32),
                dma((clips * local_clips,)),
                dma((clips * local_clips,)),
            ],
            cost_estimate=pl.CostEstimate(flops=0, bytes_accessed=2**23, transcendentals=0),
            compiler_params=pltpu.CompilerParams(vmem_limit_bytes=255 * 2**18),
            name="results",
        )(ends, small)
    )
    return (
        ends,
        jnp.transpose(taps_grad, (1, 0, 2)),
        conv_bias_grad,
        scale_grad,
        shift_grad,
        up_grad.reshape(up_weight.shape),
        up_bias_grad,
        down_grad.reshape(down_weight.shape),
        down_bias_grad,
        gamma_grad,
    )


def solution(mesh):
    in_specs = (
        P(None, "batch", None, None),
        P(None, "batch", None, None),
        P(None, "batch"),
        P("section", None, None),
        P("section", None),
        P("section", None, None),
        P("section", None, None),
        P("section", None, None),
        P("section", None),
        P("section", None, None),
        P("section", None),
        P("section", None),
    )
    out_specs = (
        P("section", None, "batch", None, None),
        P("section", None, None),
        P("section", None),
        P("section", None, None),
        P("section", None, None),
        P("section", None, None),
        P("section", None),
        P("section", None, None),
        P("section", None),
        P("section", None),
    )
    return jax.shard_map(body, mesh=mesh, in_specs=in_specs, out_specs=out_specs, check_vma=False)
```

```python
import functools

import jax
import jax.numpy as jnp
from jax import lax
from jax.experimental import pallas as pl
from jax.experimental.pallas import tpu as pltpu
from jax.sharding import PartitionSpec as P

norm_epsilon = 1e-06
f32 = jnp.float32
bf16 = jnp.bfloat16

log_density = -1.3257480647361593

taps_row, conv_bias_row, scale_row, shift_row, up_bias_row, down_bias_row, gamma_row = 0, 7, 8, 12, 16, 19, 20
packed_rows = 24
pad = 8
chunk = 32


def gelu_and_slope(u):
    cdf = 0.5 * lax.erf(u * 0.7071067811865476) + 0.5
    density = jnp.exp2(u * (u * (-0.5 * 1.4426950408889634)) + log_density)
    return u * cdf, cdf + u * density


def fold(values):
    rows, columns = values.shape
    return jnp.sum(values.reshape(rows // 8, 8, columns), axis=0)


def dot_plain(left, right):
    return lax.dot_general(left, right, (((1,), (0,)), ((), ())), preferred_element_type=f32)


def dot_cols(left, right):
    return lax.dot_general(left, right, (((1,), (1,)), ((), ())), preferred_element_type=f32)


class Plan:
    def __init__(self, batch, rows):
        self.bits = batch.bit_length() - 1
        order = [(bit, bit) for bit in range(self.bits)]
        if self.bits > 1:
            order[:2] = [(0, 1), (1, 0)]
        late = order[:]
        if self.bits > 2:
            late = [order[2]] + order[:2] + order[3:]
        third = rows // 3
        self.lanes = [(0, 2 * third, order), (2 * third, third, late)]
        self.kept = []
        self.halves = []
        self.slot_rows = []
        for _, size, _ in self.lanes:
            kept, halves = [size], []
            for stage in range(self.bits):
                halves.append(stage < self.bits - 1 and kept[-1] // 2 % 8 == 0)
                kept.append(kept[-1] // 2 if halves[-1] else kept[-1])
            self.kept.append(kept)
            self.halves.append(halves)
        self.doublings = max(sum(halves) for halves in self.halves)
        for stage in range(self.bits):
            begin, starts = 0, []
            for lane in range(len(self.lanes)):
                starts.append(begin)
                begin += self.kept[lane][stage + 1]
            self.slot_rows.append((starts, begin))


def step_kernel(
    plan,
    inputs,
    grad_out,
    band_ids,
    conv_kernel,
    conv_bias,
    band_scale,
    band_shift,
    up_weight,
    up_bias,
    down_weight,
    down_bias,
    layer_scale,
    ends,
    up_out,
    down_out,
    small_out,
    hidden_spill,
    slope_spill,
    normed_spill,
    inv_spill,
    adapted_spill,
    xs,
    normed,
    inv_std,
    adapted_t,
    hidden_t,
    slope,
    hidden_near,
    gb,
    g,
    gc,
    wup,
    wdn,
    packed,
    params,
    up_bias_row_of,
    upper_even,
    upper_odd,
    onehot,
    sums,
    up_sums,
    small,
    keep,
    outgo,
    income,
    small_sum,
    small_in,
    *rest,
):
    stage_in = rest[: plan.bits]
    (
        load_sem,
        own_sem,
        wt_send,
        wt_recv,
        par_send,
        par_recv,
        ends_send,
        ends_recv,
        core_send,
        core_recv,
        rs_send,
        rs_recv,
        deliver_send,
        deliver_recv,
        ag_send,
        ag_recv,
        out_sem,
        credit,
        small_send,
        small_recv,
        spill_sem,
        norm_sem,
    ) = rest[plan.bits :]
    uppers = (upper_even, upper_odd)
    core = lax.axis_index("section")
    other = 1 - core
    batch = lax.axis_index("batch")
    clips, frames, width = g.shape
    rows = clips * frames
    layers = xs.shape[0] - 1
    per_core = layers // 2
    hidden_width = slope.shape[2]
    tile = 2 * frames
    chunks = frames // chunk
    blocks = hidden_width // tile
    bits = plan.bits
    mesh_id = pl.DeviceIdType.MESH

    def bit_of(bit):
        return (batch // (1 << bit)) % 2

    def partner(bit):
        return batch + (1 - 2 * bit_of(bit)) * (1 << bit)

    def choose(pair, side, value):
        first, second = pair
        if first == second:
            return value(first)
        if isinstance(side, int):
            return value(pair[side])
        return (1 - side) * value(first) + side * value(second)

    def to_core(source, target, send, recv):
        return pltpu.make_async_remote_copy(source, target, send, recv, {"section": other}, mesh_id)

    def to_batch(source, target, send, recv, device):
        return pltpu.make_async_remote_copy(source, target, send, recv, {"batch": device}, mesh_id)

    own_blocks = pl.ds(per_core * core, per_core)
    own = []
    for j in range(per_core):
        for source, target in ((up_weight, wup), (down_weight, wdn)):
            own.append(pltpu.make_async_copy(source.at[j], target.at[per_core * core + j], own_sem.at[len(own)]))
    own[0].start()
    loads = []
    for source, target in ((inputs, slope.at[0, :, 0:width]), (grad_out, gb)):
        for clip in range(clips):
            loads.append(
                pltpu.make_async_copy(
                    source.at[clip, core], target.at[pl.ds(clip * frames, frames)], load_sem.at[len(loads)]
                )
            )
    for load in loads[:clips]:
        load.start()
    for load in own[1:] + loads[clips:]:
        load.start()

    for j in range(per_core):
        packed[j, taps_row : taps_row + 7] = conv_kernel[:, j]
        packed[j, conv_bias_row : conv_bias_row + 1] = conv_bias[j : j + 1]
        packed[j, scale_row : scale_row + 4] = band_scale[j]
        packed[j, shift_row : shift_row + 4] = band_shift[j]
        for q in range(3):
            row = up_bias_row + q
            packed[j, row : row + 1] = up_bias[j : j + 1, q * width : (q + 1) * width]
        packed[j, down_bias_row : down_bias_row + 1] = down_bias[j : j + 1]
        packed[j, gamma_row : gamma_row + 1] = layer_scale[j : j + 1]
        packed[j, gamma_row + 1 : packed_rows] = jnp.zeros((packed_rows - gamma_row - 1, width), f32)

    barrier = pltpu.get_barrier_semaphore()
    pl.semaphore_signal(barrier, inc=1, device_id={"section": other}, device_id_type=mesh_id)
    for bit in range(bits):
        pl.semaphore_signal(barrier, inc=1, device_id={"batch": partner(bit)}, device_id_type=mesh_id)

    for load in loads[:clips]:
        load.wait()

    def load_x(clip, carry):
        xs[0, clip, 0:pad, :] = jnp.zeros((pad, width), f32)
        xs[0, clip, pad + frames : 2 * pad + frames, :] = jnp.zeros((pad, width), f32)
        xs[0, clip, pad : pad + frames, :] = slope[
            0, pl.ds(pl.multiple_of(clip * frames, frames), frames), 0:width
        ].astype(f32)
        for band in range(4):
            chosen = jnp.where(band_ids[core, clip] == band, 1.0, 0.0).astype(f32)
            onehot[clip, band : band + 1] = jnp.zeros((1, width), f32) + chosen
        return carry

    lax.fori_loop(0, clips, load_x, 0)
    pl.semaphore_wait(barrier, 1 + bits)

    par_copy = to_core(packed, params.at[own_blocks], par_send.at[0], par_recv.at[0])
    par_copy.start()
    params[own_blocks] = packed[...]

    stages = [
        xs.at[1, :, 0:frames],
        xs.at[2, :, 0:frames],
        xs.at[3, :, 0:frames],
        outgo.at[0],
        outgo.at[1],
        xs.at[4, :, 0:frames],
        gc.at[:, 0:frames],
        outgo.at[0],
    ]

    def weight_part(kind, layer, half, part):
        if kind == 0:
            return wup.at[
                layer,
                pl.ds(pl.multiple_of(half * (width // 2) + (part % 2) * frames, frames), frames),
                pl.ds(pl.multiple_of((part // 2) * width, width), width),
            ]
        return wdn.at[layer, pl.ds(pl.multiple_of(half * rows + part * frames, frames), frames), :]

    def weight_copy(stage, k):
        return to_core(stage, keep.at[k], wt_send.at[k], wt_recv.at[k])

    def send_weights(k):
        j, kind, half = k // 4, k // 2 % 2, k % 2

        def cast(i, carry):
            for part in (2 * i, 2 * i + 1):
                stages[k][part] = weight_part(kind, per_core * core + j, half, part)[...].astype(f32)
            return carry

        lax.fori_loop(0, clips // 2, cast, 0)
        weight_copy(stages[k], k).start()

    def take_weights(layer, kind):
        @pl.when(layer // per_core != core)
        def _():
            for half in range(2):
                k = 4 * (layer % per_core) + 2 * kind + half
                weight_copy(outgo.at[0], k).wait_recv()

                def cast(i, carry, half=half, k=k):
                    for part in (2 * i, 2 * i + 1):
                        weight_part(kind, layer, half, part)[...] = keep[k, part].astype(bf16)
                    return carry

                lax.fori_loop(0, clips // 2, cast, 0)

    for kind in range(2):
        own[kind].wait()
        for half in range(2):
            send_weights(2 * kind + half)
    par_copy.wait()
    for layer in range(layers):
        for block in range(blocks):
            row = up_bias_row + block // 2
            place = (block % 2) * tile
            up_bias_row_of[layer, block] = params[layer, row : row + 1, place : place + tile]

    def chosen_row(layer, clip, first):
        return jnp.sum(onehot[clip] * params[layer, first : first + 4], axis=0, keepdims=True)

    adapted_place = slice(hidden_width - width, hidden_width)

    def norm_clip(layer, clip):
        table = params[layer]
        scale = chosen_row(layer, clip, scale_row)
        shift = chosen_row(layer, clip, shift_row)
        for j in range(chunks):
            window = xs[layer, clip, j * chunk : (j + 1) * chunk + 2 * pad, :]
            conv = window[pad : pad + chunk] * table[3:4] + table[conv_bias_row : conv_bias_row + 1]
            for k in (0, 1, 2, 4, 5, 6):
                conv = conv + window[pad - 3 + k : pad - 3 + k + chunk] * table[k : k + 1]
            centered = conv - jnp.mean(conv, axis=-1, keepdims=True)
            inv = lax.rsqrt(jnp.mean(centered * centered, axis=-1, keepdims=True) + norm_epsilon)
            value = centered * inv
            at = pl.ds(pl.multiple_of(clip * frames + j * chunk, chunk), chunk)
            normed[at, :] = value
            inv_std[at, :] = inv
            slope[layer % 2, at, adapted_place] = (value * scale + shift).astype(bf16)

    def saved_copy(layer, which, back):
        buffer = (hidden_t if which == 0 else slope).at[layer % 2]
        away = (hidden_spill if which == 0 else slope_spill).at[layer % 2]
        source, target = (away, buffer) if back else (buffer, away)
        return pltpu.make_async_copy(source, target, spill_sem.at[layer % 2, which])

    def norm_copies(layer, back, which=(0, 1, 2)):
        copies = []
        kept = ((normed, normed_spill), (inv_std, inv_spill), (adapted_t, adapted_spill))
        for i in which:
            near, away = kept[i]
            source, target = (away.at[layer], near) if back else (near, away.at[layer])
            copies.append(pltpu.make_async_copy(source, target, norm_sem.at[i]))
        return copies

    branch_sum = g.reshape(rows, width)

    def norm_pair(i, carry):
        for q in range(2):
            norm_clip(0, 2 * i + q)
        return carry

    lax.fori_loop(0, clips // 2, norm_pair, 0)
    for copy in norm_copies(0, False, (0, 1)):
        copy.start()
    for load in own[2:]:
        load.wait()
    for k in range(4, 4 * per_core - 1):
        send_weights(k)

    def forward(layer, carry):
        slot = layer % 2

        @pl.when(layer > 0)
        def _():
            norm_copies(layer - 1, False, (2,))[0].wait()

        take_weights(layer, 0)

        def up(block):
            columns = slice(block * tile, (block + 1) * tile)
            uppers[block % 2][...] = dot_plain(slope[slot, :, adapted_place], wup[layer, :, columns])

        def down(block):
            columns = slice(block * tile, (block + 1) * tile)
            here = hidden_near[block % 2]
            value = dot_plain(here, wdn[layer, columns, :])
            branch_sum[...] = value if block == 0 else branch_sum[...] + value
            hidden_t[slot, columns, :] = here.T

        up(0)
        for block in range(blocks):
            columns = slice(block * tile, (block + 1) * tile)
            if block + 1 < blocks:
                up(block + 1)
            if block == 0:
                adapted_t[...] = slope[slot, :, adapted_place].T
            if block == 1:
                take_weights(layer, 1)
            if block > 0:
                down(block - 1)
            bias = up_bias_row_of[layer, block]
            for q in range(rows // chunk):
                at = slice(q * chunk, (q + 1) * chunk)
                smooth, steep = gelu_and_slope(uppers[block % 2][at, :] + bias)
                hidden_near[block % 2, at, :] = smooth.astype(bf16)
                slope[slot, at, columns] = steep.astype(bf16)
        down(blocks - 1)

        @pl.when(layer < layers - 1)
        def _():
            norm_copies(layer, False, (2,))[0].start()

        @pl.when(layer < 2)
        def _():
            for which in range(2):
                saved_copy(layer, which, False).start()

        for step in range(layers):

            @pl.when(layer == step)
            def _(step=step):
                for k in [step] if step < layers - 1 else range(layers, 4 * per_core):
                    weight_copy(outgo.at[0], k).wait_send()
                if step == 0:
                    weight_copy(outgo.at[0], layers - 1).wait_send()
                    send_weights(4 * per_core - 1)

        def residual(clip):
            bias = params[layer, down_bias_row : down_bias_row + 1]
            gamma = params[layer, gamma_row : gamma_row + 1]
            xs[layer + 1, clip, 0:pad, :] = jnp.zeros((pad, width), f32)
            xs[layer + 1, clip, pad + frames : 2 * pad + frames, :] = jnp.zeros((pad, width), f32)
            xs[layer + 1, clip, pad : pad + frames, :] = xs[layer, clip, pad : pad + frames, :] + gamma * (
                g[clip] + bias
            )

        def residual_pair(i, carry):
            for q in range(2):
                residual(2 * i + q)
            return carry

        def residual_norm_pair(i, carry):
            for q in range(2):
                residual(2 * i + q)
            for q in range(2):
                norm_clip(layer + 1, 2 * i + q)
            return carry

        @pl.when((layer >= 1) & (layer < layers - 1))
        def _():
            for which in range(2):
                saved_copy(layer - 1, which, False).wait()

        @pl.when(layer < layers - 1)
        def _():
            for copy in norm_copies(layer, False, (0, 1)):
                copy.wait()
            lax.fori_loop(0, clips // 2, residual_norm_pair, 0)

        @pl.when(layer < layers - 2)
        def _():
            for copy in norm_copies(layer + 1, False, (0, 1)):
                copy.start()

        @pl.when(layer == layers - 1)
        def _():
            lax.fori_loop(0, clips // 2, residual_pair, 0)

        return carry

    lax.fori_loop(0, layers, forward, 0)

    result = xs.at[layers, :, pad : pad + frames]
    result_remote = to_core(result, ends.at[0, :, 0], ends_send.at[0], ends_recv.at[0])
    result_local = pltpu.make_async_copy(result, ends.at[0, :, 1], ends_send.at[1])

    @pl.when(core == 0)
    def _():
        result_remote.start()

    @pl.when(core == 1)
    def _():
        result_local.start()

    for load in loads[clips:]:
        load.wait()

    def load_g(clip, carry):
        g[clip] = gb[pl.ds(pl.multiple_of(clip * frames, frames), frames), :].astype(f32)
        gc[clip, 0:pad, :] = jnp.zeros((pad, width), f32)
        gc[clip, pad + frames : 2 * pad + frames, :] = jnp.zeros((pad, width), f32)
        return carry

    lax.fori_loop(0, clips, load_g, 0)

    matrices = 2 * layers
    lane_count = len(plan.lanes)

    def core_copy(m, parity):
        return to_core(outgo.at[parity], income.at[parity], core_send.at[parity], core_recv.at[parity])

    keep_rows = keep.reshape(matrices, rows, width)

    def offset(lane, stage, side):
        start = 0
        for s in range(stage):
            if plan.halves[lane][s]:
                start = start + choose(plan.lanes[lane][2][s], side, bit_of) * plan.kept[lane][s + 1]
        return start

    def rs_copy(m, parity, lane, stage):
        begin, _, order = plan.lanes[lane]
        size = plan.kept[lane][stage + 1]
        at = begin + offset(lane, stage, core)
        if plan.halves[lane][stage]:
            at = at + (1 - choose(order[stage], core, bit_of)) * size
        starts, _ = plan.slot_rows[stage]
        return to_batch(
            keep_rows.at[m, pl.ds(pl.multiple_of(at, 8), size)],
            stage_in[stage].at[parity, starts[lane] : starts[lane] + size],
            rs_send.at[stage, parity, lane],
            rs_recv.at[stage, parity, lane],
            choose(order[stage], core, partner),
        )

    def rs_add(m, parity, lane, stage):
        begin, _, _ = plan.lanes[lane]
        size = plan.kept[lane][stage + 1]
        at = begin + offset(lane, stage + 1, core)
        starts, _ = plan.slot_rows[stage]
        step = min(size, 2 * chunk)

        def body(i, carry):
            r = pl.multiple_of(at + i * step, 8)
            keep_rows[m, pl.ds(r, step), :] = (
                keep_rows[m, pl.ds(r, step), :]
                + stage_in[stage][parity, pl.ds(pl.multiple_of(starts[lane] + i * step, 8), step), :]
            )
            return carry

        lax.fori_loop(0, size // step, body, 0)

    half_way = matrices // 2
    xs_rows = xs.reshape(layers + 1, clips * (frames + 2 * pad), width)

    def rows_of(m, owner, own, lane, at, size):
        span = pl.ds(pl.multiple_of(plan.lanes[lane][0] + at, 8), size)
        if own:
            return keep_rows.at[m, span]
        return xs_rows.at[layers - m, span] if owner == 1 else keep_rows.at[m - half_way, span]

    def deliver_copy(m, owner, lane):
        size = plan.kept[lane][bits]
        at = offset(lane, bits, 1 - owner)
        return to_core(
            rows_of(m, owner, True, lane, at, size),
            rows_of(m, owner, False, lane, at, size),
            deliver_send.at[m % half_way, lane],
            deliver_recv.at[m % half_way, lane],
        )

    def ag_copy(m, owner, own, parity, lane, stage):
        size = plan.kept[lane][stage + 1]
        side = owner if own else 1 - owner
        place = rows_of(m, owner, own, lane, offset(lane, stage + 1, side), size)
        return to_batch(
            place,
            place,
            ag_send.at[stage, parity, own, lane],
            ag_recv.at[stage, parity, own, lane],
            choose(plan.lanes[lane][2][stage], side, partner),
        )

    def last_copies(m, kind, local, owner, own, parity, lane):
        side = owner if own else 1 - owner
        size = plan.kept[lane][1]
        at = offset(lane, 1, side)
        source = rows_of(m, owner, own, lane, at, size)
        row = plan.lanes[lane][0] + at
        if kind == 0:
            target = down_out.at[local, side, pl.ds(pl.multiple_of(row, 8), size), :]
        else:
            part = row // tile
            target = up_out.at[
                local,
                side,
                pl.ds(pl.multiple_of(row - part * tile, 8), size),
                pl.ds(pl.multiple_of(part * width, width), width),
            ]
        far = to_batch(
            source,
            target,
            ag_send.at[0, parity, own, lane],
            ag_recv.at[0, parity, own, lane],
            choose(plan.lanes[lane][2][0], side, partner),
        )
        return far, pltpu.make_async_copy(source, target, out_sem.at[m % half_way, own, lane])

    def owner_of(m):
        return 1 - m // half_way

    def owned_by(owner, m):
        return m < half_way if owner == 1 else m >= half_way

    last_step = bits + plan.doublings + 2

    def tick(pair, phase):
        for s in range(last_step, 0, -1):
            m = 2 * pair + phase + 1 - s
            parity = (phase + 1 - s) % 2
            kind = parity
            local = (layers - 1 - (m - kind) // 2) % per_core
            valid = (m >= 0) & (m < matrices)

            if s <= bits + 1:

                @pl.when(valid)
                def _(s=s, m=m, parity=parity):
                    if s == 1:
                        core_copy(m, parity).wait()

                        def body(clip, carry):
                            keep[m, clip] = keep[m, clip] + income[parity, clip]
                            return carry

                        lax.fori_loop(0, clips, body, 0)
                    else:
                        for lane in range(lane_count):
                            rs_copy(m, parity, lane, s - 2).wait()
                            if plan.halves[lane][s - 2] and s > 2:
                                @pl.when(owner_of(m) == core)
                                def _(lane=lane):
                                    pl.semaphore_signal(
                                        credit.at[s - 2, lane],
                                        inc=1,
                                        device_id={"batch": choose(plan.lanes[lane][2][s - 2], core, partner)},
                                        device_id_type=mesh_id,
                                    )

                            rs_add(m, parity, lane, s - 2)
                    if s <= bits:
                        for lane in range(lane_count):
                            rs_copy(m, parity, lane, s - 1).start()

            for owner in range(2):
                if s == bits + 1:

                    @pl.when(valid & owned_by(owner, m) & (core == 1 - owner))
                    def _(m=m, owner=owner):
                        for lane in range(lane_count):
                            deliver_copy(m, owner, lane).start()

                if s > bits + 1:

                    @pl.when(valid & owned_by(owner, m) & (core == owner))
                    def _(s=s, m=m, parity=parity, kind=kind, local=local, owner=owner):
                        if s == bits + 2:
                            for lane in range(lane_count):
                                deliver_copy(m, owner, lane).wait_recv()
                        else:
                            stage = last_step - s
                            for lane in range(lane_count):
                                for own in range(2):
                                    if stage == 0:
                                        for copy in last_copies(m, kind, local, owner, own, parity, lane):
                                            copy.wait()
                                    elif plan.halves[lane][stage]:
                                        ag_copy(m, owner, own, parity, lane, stage).wait()
                        if s < last_step:
                            stage = last_step - 1 - s
                            for lane in range(lane_count):
                                if plan.halves[lane][stage] and stage > 0:
                                    pl.semaphore_wait(credit.at[stage, lane], 1)
                                for own in range(2):
                                    if stage == 0:
                                        for copy in last_copies(m, kind, local, owner, own, parity, lane):
                                            copy.start()
                                    elif plan.halves[lane][stage]:
                                        ag_copy(m, owner, own, parity, lane, stage).start()

        m = 2 * pair + phase - bits
        for owner in range(2):

            @pl.when((m >= 0) & (m < matrices) & owned_by(owner, m) & (core == 1 - owner))
            def _(m=m, owner=owner):
                for lane in range(lane_count):
                    deliver_copy(m, owner, lane).wait_send()

    def store_block(m, phase, second, block, value):
        for q in range(2):
            piece = value[q * frames : (q + 1) * frames]
            if second == 0:
                outgo[phase, 2 * block + q] = piece
            else:
                keep[m, 2 * block + q] = piece

    def scale_clip(layer, clip):
        gamma = params[layer, gamma_row : gamma_row + 1]
        gamma_sum = bias_sum = jnp.zeros((8, width), f32)
        for j in range(chunks):
            here = g[clip, j * chunk : (j + 1) * chunk, :]
            at = slice(pad + j * chunk, pad + (j + 1) * chunk)
            gamma_sum = gamma_sum + fold(here * (xs[layer + 1, clip, at, :] - xs[layer, clip, at, :]))
            value = (gamma * here).astype(bf16)
            gb[pl.ds(pl.multiple_of(clip * frames + j * chunk, chunk), chunk), :] = value
            bias_sum = bias_sum + fold(value.astype(f32))
        sums[0] += gamma_sum
        sums[1] += bias_sum

    def norm_back(layer, clip):
        scale = chosen_row(layer, clip, scale_row)
        scale_sum = shift_sum = conv_sum = jnp.zeros((8, width), f32)
        for j in range(chunks):
            row = pl.ds(pl.multiple_of(clip * frames + j * chunk, chunk), chunk)
            at = slice(pad + j * chunk, pad + (j + 1) * chunk)
            ga = gc[clip, at, :]
            value = normed[row, :]
            scale_sum = scale_sum + fold(ga * value)
            shift_sum = shift_sum + fold(ga)
            dn = ga * scale
            first = jnp.mean(dn, axis=-1, keepdims=True)
            second = jnp.mean(dn * value, axis=-1, keepdims=True)
            result = inv_std[row, :] * (dn - first - value * second)
            gc[clip, at, :] = result
            conv_sum = conv_sum + fold(result)
        sums[9] += conv_sum
        choice = onehot[clip]
        small[layer, scale_row : scale_row + 4, :] += choice * jnp.sum(scale_sum, axis=0, keepdims=True)
        small[layer, shift_row : shift_row + 4, :] += choice * jnp.sum(shift_sum, axis=0, keepdims=True)

    def conv_back(layer, clip):
        table = params[layer]
        totals = [jnp.zeros((8, width), f32) for _ in range(7)]
        for j in range(chunks):
            grads = gc[clip, j * chunk : (j + 1) * chunk + 2 * pad, :]
            signal = xs[layer, clip, pad + j * chunk : pad + (j + 1) * chunk, :]
            at = slice(j * chunk, (j + 1) * chunk)
            total = g[clip, at, :]
            for k in (3, 0, 1, 2, 4, 5, 6):
                shifted = grads[pad + 3 - k : pad + 3 - k + chunk]
                total = total + shifted * table[k : k + 1]
                totals[k] = totals[k] + fold(signal * shifted)
            g[clip, at, :] = total
        for k in range(7):
            sums[2 + k] += totals[k]

    def backward(pair, carry):
        layer = layers - 1 - pair
        slot = layer % 2

        @pl.when((pair == 1) & (core == 0))
        def _():
            result_remote.wait_send()

        @pl.when((pair == 1) & (core == 1))
        def _():
            result_local.wait()

        sums[...] = jnp.zeros(sums.shape, f32)
        small[layer] = jnp.zeros(small.shape[1:], f32)

        def scale_body(clip, carry):
            scale_clip(layer, clip)
            return carry

        lax.fori_loop(0, clips, scale_body, 0)

        @pl.when(layer < 2)
        def _():
            for which in range(2):
                saved_copy(layer, which, True).wait()

        def up_grad(block):
            columns = pl.ds(pl.multiple_of(block * tile, tile), tile)
            value = dot_cols(gb[...], wdn[layer, columns, :])
            total = jnp.zeros((8, tile), f32)
            for q in range(rows // chunk):
                at = slice(q * chunk, (q + 1) * chunk)
                piece = (value[at] * slope[slot, at, columns].astype(f32)).astype(bf16)
                slope[slot, at, columns] = piece
                total = total + fold(piece.astype(f32))
            up_sums[block] = total

        for second in range(2):
            half = other if second == 0 else core

            def down_body(block, carry, second=second, half=half):
                at = pl.ds(pl.multiple_of(half * rows + block * tile, tile), tile)
                store_block(2 * pair, 0, second, block, dot_plain(hidden_t[slot, at, :], gb[...]))
                up_grad(block + 3 * second)
                return carry

            lax.fori_loop(0, clips // 2, down_body, 0)
            if second == 0:
                core_copy(2 * pair, 0).start()

        @pl.when(pair > 0)
        def _():
            for copy in norm_copies(layer, True):
                copy.wait()

        tick(pair, 0)

        def up_weight_grad(second, block):
            half = other if second == 0 else core
            at = pl.ds(pl.multiple_of(half * (width // 2), width // 2), width // 2)
            columns = pl.ds(pl.multiple_of(block * width, width), width)
            store_block(2 * pair + 1, 1, second, block, dot_plain(adapted_t[at, :], slope[slot, :, columns]))

        def adapted_grad(i):
            r = pl.multiple_of(i * tile, tile)
            value = dot_cols(slope[slot, pl.ds(r, tile), :], wup[layer])
            for q in range(2):
                gc[2 * i + q, pad : pad + frames, :] = value[q * frames : (q + 1) * frames]

        def norm_conv_back(i):
            for q in range(2):
                norm_back(layer, 2 * i + q)
                conv_back(layer, 2 * i + q)

        adapted_grad(0)
        up_weight_grad(0, 0)

        def tile_body(i, carry):
            adapted_grad(i + 1)
            up_weight_grad(0, i + 1)
            norm_conv_back(i)
            return carry

        lax.fori_loop(0, rows // tile - 1, tile_body, 0)
        core_copy(2 * pair + 1, 1).start()
        for block in range(3):
            up_weight_grad(1, block)
        norm_conv_back(rows // tile - 1)

        @pl.when(layer > 0)
        def _():
            for copy in norm_copies(layer - 1, True):
                copy.start()

        @pl.when(layer >= 2)
        def _():
            for which in range(2):
                saved_copy(layer, which, True).start()

        gamma = params[layer, gamma_row : gamma_row + 1, :]
        small[layer, gamma_row : gamma_row + 1, :] = jnp.sum(sums[0], axis=0, keepdims=True) / gamma
        small[layer, down_bias_row : down_bias_row + 1, :] = jnp.sum(sums[1], axis=0, keepdims=True)
        for block in range(blocks):
            row = up_bias_row + block // 2
            place = (block % 2) * tile
            small[layer, row : row + 1, place : place + tile] = jnp.sum(up_sums[block], axis=0, keepdims=True)
        for k in range(7):
            small[layer, taps_row + k : taps_row + k + 1, :] = jnp.sum(sums[2 + k], axis=0, keepdims=True)
        small[layer, conv_bias_row : conv_bias_row + 1, :] = jnp.sum(sums[9], axis=0, keepdims=True)
        tick(pair, 1)
        return carry

    lax.fori_loop(0, layers, backward, 0)

    grad_remote = to_core(g, ends.at[0, :, 1], ends_send.at[2], ends_recv.at[1])
    grad_local = pltpu.make_async_copy(g, ends.at[0, :, 0], ends_send.at[3])

    @pl.when(core == 0)
    def _():
        grad_local.start()

    @pl.when(core == 1)
    def _():
        grad_remote.start()

    small_core = to_core(
        small.at[pl.ds(per_core * other, per_core)], small_in.at[bits], small_send.at[bits], small_recv.at[bits]
    )
    small_core.start()

    def small_copy(bit):
        return to_batch(small_sum, small_in.at[bit], small_send.at[bit], small_recv.at[bit], partner(bit))

    def drain(pair, carry):
        for phase in range(2):
            tick(pair, phase)
            for step in range(bits + 1):

                @pl.when(2 * pair + phase - matrices == step)
                def _(step=step):
                    if step == 0:
                        small_core.wait()
                        small_sum[...] = small[pl.ds(per_core * core, per_core)] + small_in[bits]
                    else:
                        small_copy(step - 1).wait()
                        small_sum[...] = small_sum[...] + small_in[step - 1]
                    if step < bits:
                        small_copy(step).start()

        return carry

    lax.fori_loop(layers, (matrices - 2 + last_step) // 2 + 1, drain, 0)
    small_out[...] = small_sum[...]

    @pl.when(core == 0)
    def _():
        grad_local.wait()
        grad_remote.wait_recv()

    @pl.when(core == 1)
    def _():
        result_remote.wait_recv()
        grad_remote.wait_send()


def results_kernel(
    ends,
    small,
    ends_out,
    conv_kernel_out,
    conv_bias_out,
    band_scale_out,
    band_shift_out,
    up_bias_out,
    down_bias_out,
    layer_scale_out,
    stage,
    in_sem,
    out_sem,
):
    per_core, _, width = small.shape
    pieces = [(0, i, j) for i in range(ends.shape[1]) for j in range(ends.shape[2])]
    loads = [pltpu.make_async_copy(ends.at[at], stage.at[i], in_sem.at[i]) for i, at in enumerate(pieces)]
    stores = [pltpu.make_async_copy(stage.at[i], ends_out.at[at], out_sem.at[i]) for i, at in enumerate(pieces)]
    for load in loads:
        load.start()
    for load, store in zip(loads, stores):
        load.wait()
        store.start()
    for j in range(per_core):
        conv_kernel_out[:, j] = small[j, taps_row : taps_row + 7]
        conv_bias_out[j : j + 1] = small[j, conv_bias_row : conv_bias_row + 1]
        band_scale_out[j] = small[j, scale_row : scale_row + 4]
        band_shift_out[j] = small[j, shift_row : shift_row + 4]
        for q in range(3):
            row = up_bias_row + q
            up_bias_out[j : j + 1, q * width : (q + 1) * width] = small[j, row : row + 1]
        down_bias_out[j : j + 1] = small[j, down_bias_row : down_bias_row + 1]
        layer_scale_out[j : j + 1] = small[j, gamma_row : gamma_row + 1]
    for store in stores:
        store.wait()


def body(
    inputs,
    grad_out,
    band_ids,
    conv_kernel,
    conv_bias,
    band_scale,
    band_shift,
    up_weight,
    up_bias,
    down_weight,
    down_bias,
    layer_scale,
):
    sections = lax.axis_size("section")
    batch = lax.axis_size("batch")
    clips, local_clips, frames, width = inputs.shape
    per_core, _, hidden_width = up_weight.shape
    layers = per_core * sections
    bands = band_scale.shape[1]
    rows = clips * frames
    assert sections == 2 and local_clips == 2 and batch & (batch - 1) == 0
    assert hidden_width == 3 * width and bands == 4 and layers == 4 and rows == 3 * width // 2
    plan = Plan(batch, rows)
    bits = plan.bits
    hbm = pl.BlockSpec(memory_space=pl.ANY)
    vmem = pl.BlockSpec(memory_space=pltpu.VMEM)
    smem = pl.BlockSpec(memory_space=pltpu.SMEM)
    padded = frames + 2 * pad
    dma = pltpu.SemaphoreType.DMA
    lanes = len(plan.lanes)
    tile = 2 * frames
    ends_shape = jax.ShapeDtypeStruct((1, clips, local_clips, frames, width), f32)
    up_shape = jax.ShapeDtypeStruct((per_core, 2, width // 2, hidden_width), f32)
    down_shape = jax.ShapeDtypeStruct((per_core, 2, hidden_width // 2, width), f32)
    small_shape = jax.ShapeDtypeStruct((per_core, packed_rows, width), f32)
    conv_kernel = jnp.transpose(conv_kernel, (1, 0, 2))
    ends, up_grad, down_grad, small, *_ = pl.pallas_call(
        functools.partial(step_kernel, plan),
        out_shape=[
            ends_shape,
            up_shape,
            down_shape,
            small_shape,
            jax.ShapeDtypeStruct((2, hidden_width, rows), bf16),
            jax.ShapeDtypeStruct((2, rows, hidden_width), bf16),
            jax.ShapeDtypeStruct((layers - 1, rows, width), f32),
            jax.ShapeDtypeStruct((layers - 1, rows, 1), f32),
            jax.ShapeDtypeStruct((layers - 1, width, rows), bf16),
        ],
        in_specs=[hbm, hbm, smem, vmem, vmem, vmem, vmem, hbm, vmem, hbm, vmem, vmem],
        out_specs=[hbm, hbm, hbm, vmem, hbm, hbm, hbm, hbm, hbm],
        scratch_shapes=[
            pltpu.VMEM((layers + 1, clips, padded, width), f32),
            pltpu.VMEM((rows, width), f32),
            pltpu.VMEM((rows, 1), f32),
            pltpu.VMEM((width, rows), bf16),
            pltpu.VMEM((2, hidden_width, rows), bf16),
            pltpu.VMEM((2, rows, hidden_width), bf16),
            pltpu.VMEM((2, rows, tile), bf16),
            pltpu.VMEM((rows, width), bf16),
            pltpu.VMEM((clips, frames, width), f32),
            pltpu.VMEM((clips, padded, width), f32),
            pltpu.VMEM((layers, width, hidden_width), bf16),
            pltpu.VMEM((layers, hidden_width, width), bf16),
            pltpu.VMEM((per_core, packed_rows, width), f32),
            pltpu.VMEM((layers, packed_rows, width), f32),
            pltpu.VMEM((layers, hidden_width // tile, 1, tile), f32),
            pltpu.VMEM((rows, tile), f32),
            pltpu.VMEM((rows, tile), f32),
            pltpu.VMEM((clips, bands, width), f32),
            pltpu.VMEM((10, 8, width), f32),
            pltpu.VMEM((hidden_width // tile, 8, tile), f32),
            pltpu.VMEM((layers, packed_rows, width), f32),
            pltpu.VMEM((2 * layers, clips, frames, width), f32),
            pltpu.VMEM((2, clips, frames, width), f32),
            pltpu.VMEM((2, clips, frames, width), f32),
            pltpu.VMEM((per_core, packed_rows, width), f32),
            pltpu.VMEM((bits + 1, per_core, packed_rows, width), f32),
            *[pltpu.VMEM((2, plan.slot_rows[stage][1], width), f32) for stage in range(bits)],
            dma((2 * clips,)),
            dma((2 * per_core,)),
            dma((4 * per_core,)),
            dma((4 * per_core,)),
            dma((1,)),
            dma((1,)),
            dma((4,)),
            dma((2,)),
            dma((2,)),
            dma((2,)),
            dma((bits, 2, lanes)),
            dma((bits, 2, lanes)),
            dma((layers, lanes)),
            dma((layers, lanes)),
            dma((bits, 2, 2, lanes)),
            dma((bits, 2, 2, lanes)),
            dma((layers, 2, lanes)),
            pltpu.SemaphoreType.REGULAR((bits, lanes)),
            dma((bits + 1,)),
            dma((bits + 1,)),
            dma((2, 2)),
            dma((3,)),
        ],
        compiler_params=pltpu.CompilerParams(
            collective_id=0, has_side_effects=True, vmem_limit_bytes=255 * 2**18
        ),
        cost_estimate=pl.CostEstimate(
            flops=24 * rows * width * hidden_width * 2, bytes_accessed=2**26, transcendentals=2**24
        ),
        name="blocks_step",
    )(
        inputs,
        grad_out,
        jnp.transpose(band_ids),
        conv_kernel,
        conv_bias,
        band_scale,
        band_shift,
        up_weight,
        up_bias,
        down_weight,
        down_bias,
        layer_scale,
    )

    def like(array):
        return jax.ShapeDtypeStruct(array.shape, f32)

    ends, taps_grad, conv_bias_grad, scale_grad, shift_grad, up_bias_grad, down_bias_grad, gamma_grad = (
        pl.pallas_call(
            results_kernel,
            out_shape=[
                like(array)
                for array in (ends, conv_kernel, conv_bias, band_scale, band_shift, up_bias, down_bias, layer_scale)
            ],
            in_specs=[hbm, vmem],
            out_specs=[hbm] + [vmem] * 7,
            scratch_shapes=[
                pltpu.VMEM((clips * local_clips, frames, width), f32),
                dma((clips * local_clips,)),
                dma((clips * local_clips,)),
            ],
            cost_estimate=pl.CostEstimate(flops=0, bytes_accessed=2**23, transcendentals=0),
            compiler_params=pltpu.CompilerParams(vmem_limit_bytes=2**23),
            name="results",
        )(ends, small)
    )
    return (
        ends,
        jnp.transpose(taps_grad, (1, 0, 2)),
        conv_bias_grad,
        scale_grad,
        shift_grad,
        up_grad.reshape(up_weight.shape),
        up_bias_grad,
        down_grad.reshape(down_weight.shape),
        down_bias_grad,
        gamma_grad,
    )


def solution(mesh):
    in_specs = (
        P(None, "batch", None, None),
        P(None, "batch", None, None),
        P(None, "batch"),
        P("section", None, None),
        P("section", None),
        P("section", None, None),
        P("section", None, None),
        P("section", None, None),
        P("section", None),
        P("section", None, None),
        P("section", None),
        P("section", None),
    )
    out_specs = (
        P("section", None, "batch", None, None),
        P("section", None, None),
        P("section", None),
        P("section", None, None),
        P("section", None, None),
        P("section", None, None),
        P("section", None),
        P("section", None, None),
        P("section", None),
        P("section", None),
    )
    return jax.shard_map(body, mesh=mesh, in_specs=in_specs, out_specs=out_specs, check_vma=False)
```

```python
import functools

import jax
import jax.numpy as jnp
from jax import lax
from jax.experimental import pallas as pl
from jax.experimental.pallas import tpu as pltpu
from jax.sharding import PartitionSpec as P

norm_epsilon = 1e-06
f32 = jnp.float32
bf16 = jnp.bfloat16

log_density = -1.3257480647361593

taps_row, conv_bias_row, scale_row, shift_row, up_bias_row, down_bias_row, gamma_row = 0, 7, 8, 12, 16, 19, 20
packed_rows = 24
pad = 8
chunk = 32


def gelu_and_slope(u):
    cdf = 0.5 * lax.erf(u * 0.7071067811865476) + 0.5
    density = jnp.exp2(u * (u * (-0.5 * 1.4426950408889634)) + log_density)
    return u * cdf, cdf + u * density


def fold(values):
    rows, columns = values.shape
    return jnp.sum(values.reshape(rows // 8, 8, columns), axis=0)


def dot_plain(left, right):
    return lax.dot_general(left, right, (((1,), (0,)), ((), ())), preferred_element_type=f32)


def dot_cols(left, right):
    return lax.dot_general(left, right, (((1,), (1,)), ((), ())), preferred_element_type=f32)


class Plan:
    def __init__(self, batch, rows):
        self.bits = batch.bit_length() - 1
        order = [(bit, bit) for bit in range(self.bits)]
        if self.bits > 1:
            order[:2] = [(0, 1), (1, 0)]
        late = order[:]
        if self.bits > 2:
            late = [order[2]] + order[:2] + order[3:]
        third = rows // 3
        self.lanes = [(0, 2 * third, order), (2 * third, third, late)]
        self.kept = []
        self.halves = []
        self.slot_rows = []
        for _, size, _ in self.lanes:
            kept, halves = [size], []
            for stage in range(self.bits):
                halves.append(stage < self.bits - 1 and kept[-1] // 2 % 8 == 0)
                kept.append(kept[-1] // 2 if halves[-1] else kept[-1])
            self.kept.append(kept)
            self.halves.append(halves)
        self.doublings = max(sum(halves) for halves in self.halves)
        for stage in range(self.bits):
            begin, starts = 0, []
            for lane in range(len(self.lanes)):
                starts.append(begin)
                begin += self.kept[lane][stage + 1]
            self.slot_rows.append((starts, begin))


def step_kernel(
    plan,
    inputs,
    grad_out,
    band_ids,
    conv_kernel,
    conv_bias,
    band_scale,
    band_shift,
    up_weight,
    up_bias,
    down_weight,
    down_bias,
    layer_scale,
    ends,
    up_out,
    down_out,
    small_out,
    hidden_spill,
    slope_spill,
    normed_spill,
    inv_spill,
    adapted_spill,
    xs,
    normed,
    inv_std,
    adapted_t,
    hidden_t,
    slope,
    hidden_near,
    gb,
    g,
    gc,
    wup,
    wdn,
    packed,
    params,
    up_bias_row_of,
    upper_even,
    upper_odd,
    onehot,
    sums,
    up_sums,
    small,
    keep,
    outgo,
    income,
    small_sum,
    small_in,
    *rest,
):
    stage_in = rest[: plan.bits]
    (
        load_sem,
        own_sem,
        wt_send,
        wt_recv,
        par_send,
        par_recv,
        ends_send,
        ends_recv,
        core_send,
        core_recv,
        rs_send,
        rs_recv,
        deliver_send,
        deliver_recv,
        ag_send,
        ag_recv,
        out_sem,
        credit,
        small_send,
        small_recv,
        spill_sem,
        norm_sem,
    ) = rest[plan.bits :]
    uppers = (upper_even, upper_odd)
    core = lax.axis_index("section")
    other = 1 - core
    batch = lax.axis_index("batch")
    clips, frames, width = g.shape
    rows = clips * frames
    layers = xs.shape[0] - 1
    per_core = layers // 2
    hidden_width = slope.shape[2]
    tile = 2 * frames
    chunks = frames // chunk
    blocks = hidden_width // tile
    bits = plan.bits
    mesh_id = pl.DeviceIdType.MESH

    def bit_of(bit):
        return (batch // (1 << bit)) % 2

    def partner(bit):
        return batch + (1 - 2 * bit_of(bit)) * (1 << bit)

    def choose(pair, side, value):
        first, second = pair
        if first == second:
            return value(first)
        if isinstance(side, int):
            return value(pair[side])
        return (1 - side) * value(first) + side * value(second)

    def to_core(source, target, send, recv):
        return pltpu.make_async_remote_copy(source, target, send, recv, {"section": other}, mesh_id)

    def to_batch(source, target, send, recv, device):
        return pltpu.make_async_remote_copy(source, target, send, recv, {"batch": device}, mesh_id)

    own_blocks = pl.ds(per_core * core, per_core)
    own = []
    for j in range(per_core):
        for source, target in ((up_weight, wup), (down_weight, wdn)):
            own.append(pltpu.make_async_copy(source.at[j], target.at[per_core * core + j], own_sem.at[len(own)]))
    own[0].start()
    loads = []
    for source, target in ((inputs, slope.at[0, :, 0:width]), (grad_out, gb)):
        for clip in range(clips):
            loads.append(
                pltpu.make_async_copy(
                    source.at[clip, core], target.at[pl.ds(clip * frames, frames)], load_sem.at[len(loads)]
                )
            )
    for load in loads[:clips]:
        load.start()
    for load in own[1:] + loads[clips:]:
        load.start()

    for j in range(per_core):
        packed[j, taps_row : taps_row + 7] = conv_kernel[:, j]
        packed[j, conv_bias_row : conv_bias_row + 1] = conv_bias[j : j + 1]
        packed[j, scale_row : scale_row + 4] = band_scale[j]
        packed[j, shift_row : shift_row + 4] = band_shift[j]
        for q in range(3):
            row = up_bias_row + q
            packed[j, row : row + 1] = up_bias[j : j + 1, q * width : (q + 1) * width]
        packed[j, down_bias_row : down_bias_row + 1] = down_bias[j : j + 1]
        packed[j, gamma_row : gamma_row + 1] = layer_scale[j : j + 1]
        packed[j, gamma_row + 1 : packed_rows] = jnp.zeros((packed_rows - gamma_row - 1, width), f32)

    barrier = pltpu.get_barrier_semaphore()
    pl.semaphore_signal(barrier, inc=1, device_id={"section": other}, device_id_type=mesh_id)
    for bit in range(bits):
        pl.semaphore_signal(barrier, inc=1, device_id={"batch": partner(bit)}, device_id_type=mesh_id)

    for load in loads[:clips]:
        load.wait()

    def load_x(clip, carry):
        xs[0, clip, 0:pad, :] = jnp.zeros((pad, width), f32)
        xs[0, clip, pad + frames : 2 * pad + frames, :] = jnp.zeros((pad, width), f32)
        xs[0, clip, pad : pad + frames, :] = slope[
            0, pl.ds(pl.multiple_of(clip * frames, frames), frames), 0:width
        ].astype(f32)
        for band in range(4):
            chosen = jnp.where(band_ids[core, clip] == band, 1.0, 0.0).astype(f32)
            onehot[clip, band : band + 1] = jnp.zeros((1, width), f32) + chosen
        return carry

    lax.fori_loop(0, clips, load_x, 0)
    pl.semaphore_wait(barrier, 1 + bits)

    par_copy = to_core(packed, params.at[own_blocks], par_send.at[0], par_recv.at[0])
    par_copy.start()
    params[own_blocks] = packed[...]

    stages = [
        xs.at[1, :, 0:frames],
        xs.at[2, :, 0:frames],
        xs.at[3, :, 0:frames],
        outgo.at[0],
        outgo.at[1],
        xs.at[4, :, 0:frames],
        gc.at[:, 0:frames],
        outgo.at[0],
    ]

    def weight_part(kind, layer, half, part):
        if kind == 0:
            return wup.at[
                layer,
                pl.ds(pl.multiple_of(half * (width // 2) + (part % 2) * frames, frames), frames),
                pl.ds(pl.multiple_of((part // 2) * width, width), width),
            ]
        return wdn.at[layer, pl.ds(pl.multiple_of(half * rows + part * frames, frames), frames), :]

    def weight_copy(stage, k):
        return to_core(stage, keep.at[k], wt_send.at[k], wt_recv.at[k])

    def send_weights(k):
        j, kind, half = k // 4, k // 2 % 2, k % 2

        def cast(i, carry):
            for part in (2 * i, 2 * i + 1):
                stages[k][part] = weight_part(kind, per_core * core + j, half, part)[...].astype(f32)
            return carry

        lax.fori_loop(0, clips // 2, cast, 0)
        weight_copy(stages[k], k).start()

    def take_weights(layer, kind):
        @pl.when(layer // per_core != core)
        def _():
            for half in range(2):
                k = 4 * (layer % per_core) + 2 * kind + half
                weight_copy(outgo.at[0], k).wait_recv()

                def cast(i, carry, half=half, k=k):
                    for part in (2 * i, 2 * i + 1):
                        weight_part(kind, layer, half, part)[...] = keep[k, part].astype(bf16)
                    return carry

                lax.fori_loop(0, clips // 2, cast, 0)

    for kind in range(2):
        own[kind].wait()
        for half in range(2):
            send_weights(2 * kind + half)
    par_copy.wait()
    for layer in range(layers):
        for block in range(blocks):
            row = up_bias_row + block // 2
            place = (block % 2) * tile
            up_bias_row_of[layer, block] = params[layer, row : row + 1, place : place + tile]

    def chosen_row(layer, clip, first):
        return jnp.sum(onehot[clip] * params[layer, first : first + 4], axis=0, keepdims=True)

    adapted_place = slice(hidden_width - width, hidden_width)

    def norm_clip(layer, clip):
        table = params[layer]
        scale = chosen_row(layer, clip, scale_row)
        shift = chosen_row(layer, clip, shift_row)
        for j in range(chunks):
            window = xs[layer, clip, j * chunk : (j + 1) * chunk + 2 * pad, :]
            conv = window[pad : pad + chunk] * table[3:4] + table[conv_bias_row : conv_bias_row + 1]
            for k in (0, 1, 2, 4, 5, 6):
                conv = conv + window[pad - 3 + k : pad - 3 + k + chunk] * table[k : k + 1]
            centered = conv - jnp.mean(conv, axis=-1, keepdims=True)
            inv = lax.rsqrt(jnp.mean(centered * centered, axis=-1, keepdims=True) + norm_epsilon)
            value = centered * inv
            at = pl.ds(pl.multiple_of(clip * frames + j * chunk, chunk), chunk)
            normed[at, :] = value
            inv_std[at, :] = inv
            slope[layer % 2, at, adapted_place] = (value * scale + shift).astype(bf16)

    def saved_copy(layer, which, back):
        buffer = (hidden_t if which == 0 else slope).at[layer % 2]
        away = (hidden_spill if which == 0 else slope_spill).at[layer % 2]
        source, target = (away, buffer) if back else (buffer, away)
        return pltpu.make_async_copy(source, target, spill_sem.at[layer % 2, which])

    def norm_copies(layer, back, which=(0, 1, 2)):
        copies = []
        kept = ((normed, normed_spill), (inv_std, inv_spill), (adapted_t, adapted_spill))
        for i in which:
            near, away = kept[i]
            source, target = (away.at[layer], near) if back else (near, away.at[layer])
            copies.append(pltpu.make_async_copy(source, target, norm_sem.at[i]))
        return copies

    branch_sum = g.reshape(rows, width)

    def norm_pair(i, carry):
        for q in range(2):
            norm_clip(0, 2 * i + q)
        return carry

    lax.fori_loop(0, clips // 2, norm_pair, 0)
    for copy in norm_copies(0, False, (0, 1)):
        copy.start()
    for load in own[2:]:
        load.wait()
    for k in range(4, 4 * per_core - 1):
        send_weights(k)

    def forward(layer, carry):
        slot = layer % 2

        @pl.when(layer > 0)
        def _():
            norm_copies(layer - 1, False, (2,))[0].wait()

        take_weights(layer, 0)

        def up(block):
            columns = slice(block * tile, (block + 1) * tile)
            uppers[block % 2][...] = dot_plain(slope[slot, :, adapted_place], wup[layer, :, columns])

        def down(block):
            columns = slice(block * tile, (block + 1) * tile)
            here = hidden_near[block % 2]
            value = dot_plain(here, wdn[layer, columns, :])
            branch_sum[...] = value if block == 0 else branch_sum[...] + value
            hidden_t[slot, columns, :] = here.T

        up(0)
        for block in range(blocks):
            columns = slice(block * tile, (block + 1) * tile)
            if block + 1 < blocks:
                up(block + 1)
            if block == 0:
                adapted_t[...] = slope[slot, :, adapted_place].T
            if block == 1:
                take_weights(layer, 1)
            if block > 0:
                down(block - 1)
            bias = up_bias_row_of[layer, block]
            for q in range(rows // chunk):
                at = slice(q * chunk, (q + 1) * chunk)
                smooth, steep = gelu_and_slope(uppers[block % 2][at, :] + bias)
                hidden_near[block % 2, at, :] = smooth.astype(bf16)
                slope[slot, at, columns] = steep.astype(bf16)
        down(blocks - 1)

        @pl.when(layer < layers - 1)
        def _():
            norm_copies(layer, False, (2,))[0].start()

        @pl.when(layer < 2)
        def _():
            for which in range(2):
                saved_copy(layer, which, False).start()

        for step in range(layers):

            @pl.when(layer == step)
            def _(step=step):
                for k in [step] if step < layers - 1 else range(layers, 4 * per_core):
                    weight_copy(outgo.at[0], k).wait_send()
                if step == 0:
                    weight_copy(outgo.at[0], layers - 1).wait_send()
                    send_weights(4 * per_core - 1)

        def residual(clip):
            bias = params[layer, down_bias_row : down_bias_row + 1]
            gamma = params[layer, gamma_row : gamma_row + 1]
            xs[layer + 1, clip, 0:pad, :] = jnp.zeros((pad, width), f32)
            xs[layer + 1, clip, pad + frames : 2 * pad + frames, :] = jnp.zeros((pad, width), f32)
            xs[layer + 1, clip, pad : pad + frames, :] = xs[layer, clip, pad : pad + frames, :] + gamma * (
                g[clip] + bias
            )

        def residual_pair(i, carry):
            for q in range(2):
                residual(2 * i + q)
            return carry

        def residual_norm_pair(i, carry):
            for q in range(2):
                residual(2 * i + q)
            for q in range(2):
                norm_clip(layer + 1, 2 * i + q)
            return carry

        @pl.when((layer >= 1) & (layer < layers - 1))
        def _():
            for which in range(2):
                saved_copy(layer - 1, which, False).wait()

        @pl.when(layer < layers - 1)
        def _():
            for copy in norm_copies(layer, False, (0, 1)):
                copy.wait()
            lax.fori_loop(0, clips // 2, residual_norm_pair, 0)

        @pl.when(layer < layers - 2)
        def _():
            for copy in norm_copies(layer + 1, False, (0, 1)):
                copy.start()

        @pl.when(layer == layers - 1)
        def _():
            lax.fori_loop(0, clips // 2, residual_pair, 0)

        return carry

    lax.fori_loop(0, layers, forward, 0)

    result = xs.at[layers, :, pad : pad + frames]
    result_remote = to_core(result, ends.at[0, :, 0], ends_send.at[0], ends_recv.at[0])
    result_local = pltpu.make_async_copy(result, ends.at[0, :, 1], ends_send.at[1])

    @pl.when(core == 0)
    def _():
        result_remote.start()

    @pl.when(core == 1)
    def _():
        result_local.start()

    for load in loads[clips:]:
        load.wait()

    def load_g(clip, carry):
        g[clip] = gb[pl.ds(pl.multiple_of(clip * frames, frames), frames), :].astype(f32)
        gc[clip, 0:pad, :] = jnp.zeros((pad, width), f32)
        gc[clip, pad + frames : 2 * pad + frames, :] = jnp.zeros((pad, width), f32)
        return carry

    lax.fori_loop(0, clips, load_g, 0)

    matrices = 2 * layers
    lane_count = len(plan.lanes)

    def core_copy(m, parity):
        return to_core(outgo.at[parity], income.at[parity], core_send.at[parity], core_recv.at[parity])

    keep_rows = keep.reshape(matrices, rows, width)

    def offset(lane, stage, side):
        start = 0
        for s in range(stage):
            if plan.halves[lane][s]:
                start = start + choose(plan.lanes[lane][2][s], side, bit_of) * plan.kept[lane][s + 1]
        return start

    def rs_copy(m, parity, lane, stage):
        begin, _, order = plan.lanes[lane]
        size = plan.kept[lane][stage + 1]
        at = begin + offset(lane, stage, core)
        if plan.halves[lane][stage]:
            at = at + (1 - choose(order[stage], core, bit_of)) * size
        starts, _ = plan.slot_rows[stage]
        return to_batch(
            keep_rows.at[m, pl.ds(pl.multiple_of(at, 8), size)],
            stage_in[stage].at[parity, starts[lane] : starts[lane] + size],
            rs_send.at[stage, parity, lane],
            rs_recv.at[stage, parity, lane],
            choose(order[stage], core, partner),
        )

    def rs_add(m, parity, lane, stage):
        begin, _, _ = plan.lanes[lane]
        size = plan.kept[lane][stage + 1]
        at = begin + offset(lane, stage + 1, core)
        starts, _ = plan.slot_rows[stage]
        step = min(size, 2 * chunk)

        def body(i, carry):
            r = pl.multiple_of(at + i * step, 8)
            keep_rows[m, pl.ds(r, step), :] = (
                keep_rows[m, pl.ds(r, step), :]
                + stage_in[stage][parity, pl.ds(pl.multiple_of(starts[lane] + i * step, 8), step), :]
            )
            return carry

        lax.fori_loop(0, size // step, body, 0)

    half_way = matrices // 2
    xs_rows = xs.reshape(layers + 1, clips * (frames + 2 * pad), width)

    def rows_of(m, owner, own, lane, at, size):
        span = pl.ds(pl.multiple_of(plan.lanes[lane][0] + at, 8), size)
        if own:
            return keep_rows.at[m, span]
        return xs_rows.at[layers - m, span] if owner == 1 else keep_rows.at[m - half_way, span]

    def deliver_copy(m, owner, lane):
        size = plan.kept[lane][bits]
        at = offset(lane, bits, 1 - owner)
        return to_core(
            rows_of(m, owner, True, lane, at, size),
            rows_of(m, owner, False, lane, at, size),
            deliver_send.at[m % half_way, lane],
            deliver_recv.at[m % half_way, lane],
        )

    def ag_copy(m, owner, own, parity, lane, stage):
        size = plan.kept[lane][stage + 1]
        side = owner if own else 1 - owner
        place = rows_of(m, owner, own, lane, offset(lane, stage + 1, side), size)
        return to_batch(
            place,
            place,
            ag_send.at[stage, parity, own, lane],
            ag_recv.at[stage, parity, own, lane],
            choose(plan.lanes[lane][2][stage], side, partner),
        )

    def last_copies(m, kind, local, owner, own, parity, lane):
        side = owner if own else 1 - owner
        size = plan.kept[lane][1]
        at = offset(lane, 1, side)
        source = rows_of(m, owner, own, lane, at, size)
        row = plan.lanes[lane][0] + at
        if kind == 0:
            target = down_out.at[local, side, pl.ds(pl.multiple_of(row, 8), size), :]
        else:
            part = row // tile
            target = up_out.at[
                local,
                side,
                pl.ds(pl.multiple_of(row - part * tile, 8), size),
                pl.ds(pl.multiple_of(part * width, width), width),
            ]
        far = to_batch(
            source,
            target,
            ag_send.at[0, parity, own, lane],
            ag_recv.at[0, parity, own, lane],
            choose(plan.lanes[lane][2][0], side, partner),
        )
        return far, pltpu.make_async_copy(source, target, out_sem.at[m % half_way, own, lane])

    def owner_of(m):
        return 1 - m // half_way

    def owned_by(owner, m):
        return m < half_way if owner == 1 else m >= half_way

    last_step = bits + plan.doublings + 2

    def tick(pair, phase):
        for s in range(last_step, 0, -1):
            m = 2 * pair + phase + 1 - s
            parity = (phase + 1 - s) % 2
            kind = parity
            local = (layers - 1 - (m - kind) // 2) % per_core
            valid = (m >= 0) & (m < matrices)

            if s <= bits + 1:

                @pl.when(valid)
                def _(s=s, m=m, parity=parity):
                    if s == 1:
                        core_copy(m, parity).wait()

                        def body(clip, carry):
                            keep[m, clip] = keep[m, clip] + income[parity, clip]
                            return carry

                        lax.fori_loop(0, clips, body, 0)
                    else:
                        for lane in range(lane_count):
                            rs_copy(m, parity, lane, s - 2).wait()
                            if plan.halves[lane][s - 2] and s > 2:
                                @pl.when(owner_of(m) == core)
                                def _(lane=lane):
                                    pl.semaphore_signal(
                                        credit.at[s - 2, lane],
                                        inc=1,
                                        device_id={"batch": choose(plan.lanes[lane][2][s - 2], core, partner)},
                                        device_id_type=mesh_id,
                                    )

                            rs_add(m, parity, lane, s - 2)
                    if s <= bits:
                        for lane in range(lane_count):
                            rs_copy(m, parity, lane, s - 1).start()

            for owner in range(2):
                if s == bits + 1:

                    @pl.when(valid & owned_by(owner, m) & (core == 1 - owner))
                    def _(m=m, owner=owner):
                        for lane in range(lane_count):
                            deliver_copy(m, owner, lane).start()

                if s > bits + 1:

                    @pl.when(valid & owned_by(owner, m) & (core == owner))
                    def _(s=s, m=m, parity=parity, kind=kind, local=local, owner=owner):
                        if s == bits + 2:
                            for lane in range(lane_count):
                                deliver_copy(m, owner, lane).wait_recv()
                        else:
                            stage = last_step - s
                            for lane in range(lane_count):
                                for own in range(2):
                                    if stage == 0:
                                        for copy in last_copies(m, kind, local, owner, own, parity, lane):
                                            copy.wait()
                                    elif plan.halves[lane][stage]:
                                        ag_copy(m, owner, own, parity, lane, stage).wait()
                        if s < last_step:
                            stage = last_step - 1 - s
                            for lane in range(lane_count):
                                if plan.halves[lane][stage] and stage > 0:
                                    pl.semaphore_wait(credit.at[stage, lane], 1)
                                for own in range(2):
                                    if stage == 0:
                                        for copy in last_copies(m, kind, local, owner, own, parity, lane):
                                            copy.start()
                                    elif plan.halves[lane][stage]:
                                        ag_copy(m, owner, own, parity, lane, stage).start()

        m = 2 * pair + phase - bits
        for owner in range(2):

            @pl.when((m >= 0) & (m < matrices) & owned_by(owner, m) & (core == 1 - owner))
            def _(m=m, owner=owner):
                for lane in range(lane_count):
                    deliver_copy(m, owner, lane).wait_send()

    def store_block(m, phase, second, block, value):
        for q in range(2):
            piece = value[q * frames : (q + 1) * frames]
            if second == 0:
                outgo[phase, 2 * block + q] = piece
            else:
                keep[m, 2 * block + q] = piece

    def scale_clip(layer, clip):
        gamma = params[layer, gamma_row : gamma_row + 1]
        gamma_sum = bias_sum = jnp.zeros((8, width), f32)
        for j in range(chunks):
            here = g[clip, j * chunk : (j + 1) * chunk, :]
            at = slice(pad + j * chunk, pad + (j + 1) * chunk)
            gamma_sum = gamma_sum + fold(here * (xs[layer + 1, clip, at, :] - xs[layer, clip, at, :]))
            value = (gamma * here).astype(bf16)
            gb[pl.ds(pl.multiple_of(clip * frames + j * chunk, chunk), chunk), :] = value
            bias_sum = bias_sum + fold(value.astype(f32))
        sums[0] += gamma_sum
        sums[1] += bias_sum

    def norm_back(layer, clip):
        scale = chosen_row(layer, clip, scale_row)
        scale_sum = shift_sum = conv_sum = jnp.zeros((8, width), f32)
        for j in range(chunks):
            row = pl.ds(pl.multiple_of(clip * frames + j * chunk, chunk), chunk)
            at = slice(pad + j * chunk, pad + (j + 1) * chunk)
            ga = gc[clip, at, :]
            value = normed[row, :]
            scale_sum = scale_sum + fold(ga * value)
            shift_sum = shift_sum + fold(ga)
            dn = ga * scale
            first = jnp.mean(dn, axis=-1, keepdims=True)
            second = jnp.mean(dn * value, axis=-1, keepdims=True)
            result = inv_std[row, :] * (dn - first - value * second)
            gc[clip, at, :] = result
            conv_sum = conv_sum + fold(result)
        sums[9] += conv_sum
        choice = onehot[clip]
        small[layer, scale_row : scale_row + 4, :] += choice * jnp.sum(scale_sum, axis=0, keepdims=True)
        small[layer, shift_row : shift_row + 4, :] += choice * jnp.sum(shift_sum, axis=0, keepdims=True)

    def conv_back(layer, clip):
        table = params[layer]
        totals = [jnp.zeros((8, width), f32) for _ in range(7)]
        for j in range(chunks):
            grads = gc[clip, j * chunk : (j + 1) * chunk + 2 * pad, :]
            signal = xs[layer, clip, pad + j * chunk : pad + (j + 1) * chunk, :]
            at = slice(j * chunk, (j + 1) * chunk)
            total = g[clip, at, :]
            for k in (3, 0, 1, 2, 4, 5, 6):
                shifted = grads[pad + 3 - k : pad + 3 - k + chunk]
                total = total + shifted * table[k : k + 1]
                totals[k] = totals[k] + fold(signal * shifted)
            g[clip, at, :] = total
        for k in range(7):
            sums[2 + k] += totals[k]

    def backward(pair, carry):
        layer = layers - 1 - pair
        slot = layer % 2

        @pl.when((pair == 1) & (core == 0))
        def _():
            result_remote.wait_send()

        @pl.when((pair == 1) & (core == 1))
        def _():
            result_local.wait()

        sums[...] = jnp.zeros(sums.shape, f32)
        small[layer] = jnp.zeros(small.shape[1:], f32)

        def scale_body(i, carry):
            for q in range(2):
                scale_clip(layer, 2 * i + q)
            return carry

        lax.fori_loop(0, clips // 2, scale_body, 0)

        @pl.when(layer < 2)
        def _():
            for which in range(2):
                saved_copy(layer, which, True).wait()

        def up_grad(block):
            columns = pl.ds(pl.multiple_of(block * tile, tile), tile)
            value = dot_cols(gb[...], wdn[layer, columns, :])
            total = jnp.zeros((8, tile), f32)
            for q in range(rows // chunk):
                at = slice(q * chunk, (q + 1) * chunk)
                piece = (value[at] * slope[slot, at, columns].astype(f32)).astype(bf16)
                slope[slot, at, columns] = piece
                total = total + fold(piece.astype(f32))
            up_sums[block] = total

        def down_weight_grad(second, block):
            half = other if second == 0 else core
            at = pl.ds(pl.multiple_of(half * rows + block * tile, tile), tile)
            store_block(2 * pair, 0, second, block, dot_plain(hidden_t[slot, at, :], gb[...]))

        for block in range(3):
            down_weight_grad(0, block)
        core_copy(2 * pair, 0).start()

        def down_body(block, carry):
            down_weight_grad(1, block)
            up_grad(2 * block)
            up_grad(2 * block + 1)
            return carry

        lax.fori_loop(0, clips // 2, down_body, 0)

        @pl.when(pair > 0)
        def _():
            for copy in norm_copies(layer, True):
                copy.wait()

        tick(pair, 0)

        def up_weight_grad(second, block):
            half = other if second == 0 else core
            at = pl.ds(pl.multiple_of(half * (width // 2), width // 2), width // 2)
            columns = pl.ds(pl.multiple_of(block * width, width), width)
            store_block(2 * pair + 1, 1, second, block, dot_plain(adapted_t[at, :], slope[slot, :, columns]))

        def adapted_grad(i):
            r = pl.multiple_of(i * tile, tile)
            value = dot_cols(slope[slot, pl.ds(r, tile), :], wup[layer])
            for q in range(2):
                gc[2 * i + q, pad : pad + frames, :] = value[q * frames : (q + 1) * frames]

        def norm_conv_back(i):
            for q in range(2):
                norm_back(layer, 2 * i + q)
                conv_back(layer, 2 * i + q)

        adapted_grad(0)
        up_weight_grad(0, 0)

        def tile_body(i, carry):
            adapted_grad(i + 1)
            up_weight_grad(0, i + 1)
            norm_conv_back(i)
            return carry

        lax.fori_loop(0, rows // tile - 1, tile_body, 0)
        core_copy(2 * pair + 1, 1).start()
        for block in range(3):
            up_weight_grad(1, block)
        norm_conv_back(rows // tile - 1)

        @pl.when(layer > 0)
        def _():
            for copy in norm_copies(layer - 1, True):
                copy.start()

        @pl.when(layer >= 2)
        def _():
            for which in range(2):
                saved_copy(layer, which, True).start()

        gamma = params[layer, gamma_row : gamma_row + 1, :]
        small[layer, gamma_row : gamma_row + 1, :] = jnp.sum(sums[0], axis=0, keepdims=True) / gamma
        small[layer, down_bias_row : down_bias_row + 1, :] = jnp.sum(sums[1], axis=0, keepdims=True)
        for block in range(blocks):
            row = up_bias_row + block // 2
            place = (block % 2) * tile
            small[layer, row : row + 1, place : place + tile] = jnp.sum(up_sums[block], axis=0, keepdims=True)
        for k in range(7):
            small[layer, taps_row + k : taps_row + k + 1, :] = jnp.sum(sums[2 + k], axis=0, keepdims=True)
        small[layer, conv_bias_row : conv_bias_row + 1, :] = jnp.sum(sums[9], axis=0, keepdims=True)
        tick(pair, 1)
        return carry

    lax.fori_loop(0, layers, backward, 0)

    grad_remote = to_core(g, ends.at[0, :, 1], ends_send.at[2], ends_recv.at[1])
    grad_local = pltpu.make_async_copy(g, ends.at[0, :, 0], ends_send.at[3])

    @pl.when(core == 0)
    def _():
        grad_local.start()

    @pl.when(core == 1)
    def _():
        grad_remote.start()

    small_core = to_core(
        small.at[pl.ds(per_core * other, per_core)], small_in.at[bits], small_send.at[bits], small_recv.at[bits]
    )
    small_core.start()

    def small_copy(bit):
        return to_batch(small_sum, small_in.at[bit], small_send.at[bit], small_recv.at[bit], partner(bit))

    def drain(pair, carry):
        for phase in range(2):
            tick(pair, phase)
            for step in range(bits + 1):

                @pl.when(2 * pair + phase - matrices == step)
                def _(step=step):
                    if step == 0:
                        small_core.wait()
                        small_sum[...] = small[pl.ds(per_core * core, per_core)] + small_in[bits]
                    else:
                        small_copy(step - 1).wait()
                        small_sum[...] = small_sum[...] + small_in[step - 1]
                    if step < bits:
                        small_copy(step).start()

        return carry

    lax.fori_loop(layers, (matrices - 2 + last_step) // 2 + 1, drain, 0)
    small_out[...] = small_sum[...]

    @pl.when(core == 0)
    def _():
        grad_local.wait()
        grad_remote.wait_recv()

    @pl.when(core == 1)
    def _():
        result_remote.wait_recv()
        grad_remote.wait_send()


def results_kernel(
    ends,
    small,
    ends_out,
    conv_kernel_out,
    conv_bias_out,
    band_scale_out,
    band_shift_out,
    up_bias_out,
    down_bias_out,
    layer_scale_out,
    stage,
    in_sem,
    out_sem,
):
    per_core, _, width = small.shape
    pieces = [(0, i, j) for i in range(ends.shape[1]) for j in range(ends.shape[2])]
    loads = [pltpu.make_async_copy(ends.at[at], stage.at[i], in_sem.at[i]) for i, at in enumerate(pieces)]
    stores = [pltpu.make_async_copy(stage.at[i], ends_out.at[at], out_sem.at[i]) for i, at in enumerate(pieces)]
    for load in loads:
        load.start()
    for load, store in zip(loads, stores):
        load.wait()
        store.start()
    for j in range(per_core):
        conv_kernel_out[:, j] = small[j, taps_row : taps_row + 7]
        conv_bias_out[j : j + 1] = small[j, conv_bias_row : conv_bias_row + 1]
        band_scale_out[j] = small[j, scale_row : scale_row + 4]
        band_shift_out[j] = small[j, shift_row : shift_row + 4]
        for q in range(3):
            row = up_bias_row + q
            up_bias_out[j : j + 1, q * width : (q + 1) * width] = small[j, row : row + 1]
        down_bias_out[j : j + 1] = small[j, down_bias_row : down_bias_row + 1]
        layer_scale_out[j : j + 1] = small[j, gamma_row : gamma_row + 1]
    for store in stores:
        store.wait()


def body(
    inputs,
    grad_out,
    band_ids,
    conv_kernel,
    conv_bias,
    band_scale,
    band_shift,
    up_weight,
    up_bias,
    down_weight,
    down_bias,
    layer_scale,
):
    sections = lax.axis_size("section")
    batch = lax.axis_size("batch")
    clips, local_clips, frames, width = inputs.shape
    per_core, _, hidden_width = up_weight.shape
    layers = per_core * sections
    bands = band_scale.shape[1]
    rows = clips * frames
    assert sections == 2 and local_clips == 2 and batch & (batch - 1) == 0
    assert hidden_width == 3 * width and bands == 4 and layers == 4 and rows == 3 * width // 2
    plan = Plan(batch, rows)
    bits = plan.bits
    hbm = pl.BlockSpec(memory_space=pl.ANY)
    vmem = pl.BlockSpec(memory_space=pltpu.VMEM)
    smem = pl.BlockSpec(memory_space=pltpu.SMEM)
    padded = frames + 2 * pad
    dma = pltpu.SemaphoreType.DMA
    lanes = len(plan.lanes)
    tile = 2 * frames
    ends_shape = jax.ShapeDtypeStruct((1, clips, local_clips, frames, width), f32)
    up_shape = jax.ShapeDtypeStruct((per_core, 2, width // 2, hidden_width), f32)
    down_shape = jax.ShapeDtypeStruct((per_core, 2, hidden_width // 2, width), f32)
    small_shape = jax.ShapeDtypeStruct((per_core, packed_rows, width), f32)
    conv_kernel = jnp.transpose(conv_kernel, (1, 0, 2))
    ends, up_grad, down_grad, small, *_ = pl.pallas_call(
        functools.partial(step_kernel, plan),
        out_shape=[
            ends_shape,
            up_shape,
            down_shape,
            small_shape,
            jax.ShapeDtypeStruct((2, hidden_width, rows), bf16),
            jax.ShapeDtypeStruct((2, rows, hidden_width), bf16),
            jax.ShapeDtypeStruct((layers - 1, rows, width), f32),
            jax.ShapeDtypeStruct((layers - 1, rows, 1), f32),
            jax.ShapeDtypeStruct((layers - 1, width, rows), bf16),
        ],
        in_specs=[hbm, hbm, smem, vmem, vmem, vmem, vmem, hbm, vmem, hbm, vmem, vmem],
        out_specs=[hbm, hbm, hbm, vmem, hbm, hbm, hbm, hbm, hbm],
        scratch_shapes=[
            pltpu.VMEM((layers + 1, clips, padded, width), f32),
            pltpu.VMEM((rows, width), f32),
            pltpu.VMEM((rows, 1), f32),
            pltpu.VMEM((width, rows), bf16),
            pltpu.VMEM((2, hidden_width, rows), bf16),
            pltpu.VMEM((2, rows, hidden_width), bf16),
            pltpu.VMEM((2, rows, tile), bf16),
            pltpu.VMEM((rows, width), bf16),
            pltpu.VMEM((clips, frames, width), f32),
            pltpu.VMEM((clips, padded, width), f32),
            pltpu.VMEM((layers, width, hidden_width), bf16),
            pltpu.VMEM((layers, hidden_width, width), bf16),
            pltpu.VMEM((per_core, packed_rows, width), f32),
            pltpu.VMEM((layers, packed_rows, width), f32),
            pltpu.VMEM((layers, hidden_width // tile, 1, tile), f32),
            pltpu.VMEM((rows, tile), f32),
            pltpu.VMEM((rows, tile), f32),
            pltpu.VMEM((clips, bands, width), f32),
            pltpu.VMEM((10, 8, width), f32),
            pltpu.VMEM((hidden_width // tile, 8, tile), f32),
            pltpu.VMEM((layers, packed_rows, width), f32),
            pltpu.VMEM((2 * layers, clips, frames, width), f32),
            pltpu.VMEM((2, clips, frames, width), f32),
            pltpu.VMEM((2, clips, frames, width), f32),
            pltpu.VMEM((per_core, packed_rows, width), f32),
            pltpu.VMEM((bits + 1, per_core, packed_rows, width), f32),
            *[pltpu.VMEM((2, plan.slot_rows[stage][1], width), f32) for stage in range(bits)],
            dma((2 * clips,)),
            dma((2 * per_core,)),
            dma((4 * per_core,)),
            dma((4 * per_core,)),
            dma((1,)),
            dma((1,)),
            dma((4,)),
            dma((2,)),
            dma((2,)),
            dma((2,)),
            dma((bits, 2, lanes)),
            dma((bits, 2, lanes)),
            dma((layers, lanes)),
            dma((layers, lanes)),
            dma((bits, 2, 2, lanes)),
            dma((bits, 2, 2, lanes)),
            dma((layers, 2, lanes)),
            pltpu.SemaphoreType.REGULAR((bits, lanes)),
            dma((bits + 1,)),
            dma((bits + 1,)),
            dma((2, 2)),
            dma((3,)),
        ],
        compiler_params=pltpu.CompilerParams(
            collective_id=0, has_side_effects=True, vmem_limit_bytes=255 * 2**18
        ),
        cost_estimate=pl.CostEstimate(
            flops=24 * rows * width * hidden_width * 2, bytes_accessed=2**26, transcendentals=2**24
        ),
        name="blocks_step",
    )(
        inputs,
        grad_out,
        jnp.transpose(band_ids),
        conv_kernel,
        conv_bias,
        band_scale,
        band_shift,
        up_weight,
        up_bias,
        down_weight,
        down_bias,
        layer_scale,
    )

    def like(array):
        return jax.ShapeDtypeStruct(array.shape, f32)

    ends, taps_grad, conv_bias_grad, scale_grad, shift_grad, up_bias_grad, down_bias_grad, gamma_grad = (
        pl.pallas_call(
            results_kernel,
            out_shape=[
                like(array)
                for array in (ends, conv_kernel, conv_bias, band_scale, band_shift, up_bias, down_bias, layer_scale)
            ],
            in_specs=[hbm, vmem],
            out_specs=[hbm] + [vmem] * 7,
            scratch_shapes=[
                pltpu.VMEM((clips * local_clips, frames, width), f32),
                dma((clips * local_clips,)),
                dma((clips * local_clips,)),
            ],
            cost_estimate=pl.CostEstimate(flops=0, bytes_accessed=2**23, transcendentals=0),
            compiler_params=pltpu.CompilerParams(vmem_limit_bytes=255 * 2**18),
            name="results",
        )(ends, small)
    )
    return (
        ends,
        jnp.transpose(taps_grad, (1, 0, 2)),
        conv_bias_grad,
        scale_grad,
        shift_grad,
        up_grad.reshape(up_weight.shape),
        up_bias_grad,
        down_grad.reshape(down_weight.shape),
        down_bias_grad,
        gamma_grad,
    )


def solution(mesh):
    in_specs = (
        P(None, "batch", None, None),
        P(None, "batch", None, None),
        P(None, "batch"),
        P("section", None, None),
        P("section", None),
        P("section", None, None),
        P("section", None, None),
        P("section", None, None),
        P("section", None),
        P("section", None, None),
        P("section", None),
        P("section", None),
    )
    out_specs = (
        P("section", None, "batch", None, None),
        P("section", None, None),
        P("section", None),
        P("section", None, None),
        P("section", None, None),
        P("section", None, None),
        P("section", None),
        P("section", None, None),
        P("section", None),
        P("section", None),
    )
    return jax.shard_map(body, mesh=mesh, in_specs=in_specs, out_specs=out_specs, check_vma=False)
```

```python
import functools

import jax
import jax.numpy as jnp
from jax import lax
from jax.experimental import pallas as pl
from jax.experimental.pallas import tpu as pltpu
from jax.sharding import PartitionSpec as P

norm_epsilon = 1e-06
f32 = jnp.float32
bf16 = jnp.bfloat16

log_density = -1.3257480647361593

taps_row, conv_bias_row, scale_row, shift_row, up_bias_row, down_bias_row, gamma_row = 0, 7, 8, 12, 16, 19, 20
packed_rows = 24
pad = 8
chunk = 32


def gelu_and_slope(u):
    cdf = 0.5 * lax.erf(u * 0.7071067811865476) + 0.5
    density = jnp.exp2(u * (u * (-0.5 * 1.4426950408889634)) + log_density)
    return u * cdf, cdf + u * density


def fold(values):
    rows, columns = values.shape
    return jnp.sum(values.reshape(rows // 8, 8, columns), axis=0)


def dot_plain(left, right):
    return lax.dot_general(left, right, (((1,), (0,)), ((), ())), preferred_element_type=f32)


def dot_cols(left, right):
    return lax.dot_general(left, right, (((1,), (1,)), ((), ())), preferred_element_type=f32)


class Plan:
    def __init__(self, batch, rows):
        self.bits = batch.bit_length() - 1
        order = [(bit, bit) for bit in range(self.bits)]
        if self.bits > 1:
            order[:2] = [(0, 1), (1, 0)]
        late = order[:]
        if self.bits > 2:
            late = [order[2]] + order[:2] + order[3:]
        third = rows // 3
        self.lanes = [(0, 2 * third, order), (2 * third, third, late)]
        self.kept = []
        self.halves = []
        self.slot_rows = []
        for _, size, _ in self.lanes:
            kept, halves = [size], []
            for stage in range(self.bits):
                halves.append(stage < self.bits - 1 and kept[-1] // 2 % 8 == 0)
                kept.append(kept[-1] // 2 if halves[-1] else kept[-1])
            self.kept.append(kept)
            self.halves.append(halves)
        self.doublings = max(sum(halves) for halves in self.halves)
        for stage in range(self.bits):
            begin, starts = 0, []
            for lane in range(len(self.lanes)):
                starts.append(begin)
                begin += self.kept[lane][stage + 1]
            self.slot_rows.append((starts, begin))


def step_kernel(
    plan,
    inputs,
    grad_out,
    band_ids,
    conv_kernel,
    conv_bias,
    band_scale,
    band_shift,
    up_weight,
    up_bias,
    down_weight,
    down_bias,
    layer_scale,
    ends,
    up_out,
    down_out,
    small_out,
    hidden_spill,
    slope_spill,
    normed_spill,
    inv_spill,
    adapted_spill,
    xs,
    normed,
    inv_std,
    adapted_t,
    hidden_t,
    slope,
    hidden_near,
    gb,
    g,
    gc,
    wup,
    wdn,
    packed,
    params,
    up_bias_row_of,
    upper_even,
    upper_odd,
    onehot,
    sums,
    up_sums,
    small,
    keep,
    outgo,
    income,
    small_sum,
    small_in,
    *rest,
):
    stage_in = rest[: plan.bits]
    (
        load_sem,
        own_sem,
        wt_send,
        wt_recv,
        par_send,
        par_recv,
        ends_send,
        ends_recv,
        core_send,
        core_recv,
        rs_send,
        rs_recv,
        deliver_send,
        deliver_recv,
        ag_send,
        ag_recv,
        out_sem,
        credit,
        small_send,
        small_recv,
        spill_sem,
        norm_sem,
    ) = rest[plan.bits :]
    uppers = (upper_even, upper_odd)
    core = lax.axis_index("section")
    other = 1 - core
    batch = lax.axis_index("batch")
    clips, frames, width = g.shape
    rows = clips * frames
    layers = xs.shape[0] - 1
    per_core = layers // 2
    hidden_width = slope.shape[2]
    tile = 2 * frames
    chunks = frames // chunk
    blocks = hidden_width // tile
    bits = plan.bits
    mesh_id = pl.DeviceIdType.MESH

    def bit_of(bit):
        return (batch // (1 << bit)) % 2

    def partner(bit):
        return batch + (1 - 2 * bit_of(bit)) * (1 << bit)

    def choose(pair, side, value):
        first, second = pair
        if first == second:
            return value(first)
        if isinstance(side, int):
            return value(pair[side])
        return (1 - side) * value(first) + side * value(second)

    def to_core(source, target, send, recv):
        return pltpu.make_async_remote_copy(source, target, send, recv, {"section": other}, mesh_id)

    def to_batch(source, target, send, recv, device):
        return pltpu.make_async_remote_copy(source, target, send, recv, {"batch": device}, mesh_id)

    own_blocks = pl.ds(per_core * core, per_core)
    own = []
    for j in range(per_core):
        for source, target in ((up_weight, wup), (down_weight, wdn)):
            own.append(pltpu.make_async_copy(source.at[j], target.at[per_core * core + j], own_sem.at[len(own)]))
    own[0].start()
    loads = []
    for source, target in ((inputs, slope.at[0, :, 0:width]), (grad_out, gb)):
        for clip in range(clips):
            loads.append(
                pltpu.make_async_copy(
                    source.at[clip, core], target.at[pl.ds(clip * frames, frames)], load_sem.at[len(loads)]
                )
            )
    for load in loads[:clips]:
        load.start()
    for load in own[1:] + loads[clips:]:
        load.start()

    for j in range(per_core):
        packed[j, taps_row : taps_row + 7] = conv_kernel[:, j]
        packed[j, conv_bias_row : conv_bias_row + 1] = conv_bias[j : j + 1]
        packed[j, scale_row : scale_row + 4] = band_scale[j]
        packed[j, shift_row : shift_row + 4] = band_shift[j]
        for q in range(3):
            row = up_bias_row + q
            packed[j, row : row + 1] = up_bias[j : j + 1, q * width : (q + 1) * width]
        packed[j, down_bias_row : down_bias_row + 1] = down_bias[j : j + 1]
        packed[j, gamma_row : gamma_row + 1] = layer_scale[j : j + 1]
        packed[j, gamma_row + 1 : packed_rows] = jnp.zeros((packed_rows - gamma_row - 1, width), f32)

    barrier = pltpu.get_barrier_semaphore()
    pl.semaphore_signal(barrier, inc=1, device_id={"section": other}, device_id_type=mesh_id)
    for bit in range(bits):
        pl.semaphore_signal(barrier, inc=1, device_id={"batch": partner(bit)}, device_id_type=mesh_id)

    for load in loads[:clips]:
        load.wait()

    def load_x(clip, carry):
        xs[0, clip, 0:pad, :] = jnp.zeros((pad, width), f32)
        xs[0, clip, pad + frames : 2 * pad + frames, :] = jnp.zeros((pad, width), f32)
        xs[0, clip, pad : pad + frames, :] = slope[
            0, pl.ds(pl.multiple_of(clip * frames, frames), frames), 0:width
        ].astype(f32)
        for band in range(4):
            chosen = jnp.where(band_ids[core, clip] == band, 1.0, 0.0).astype(f32)
            onehot[clip, band : band + 1] = jnp.zeros((1, width), f32) + chosen
        return carry

    lax.fori_loop(0, clips, load_x, 0)
    pl.semaphore_wait(barrier, 1 + bits)

    par_copy = to_core(packed, params.at[own_blocks], par_send.at[0], par_recv.at[0])
    par_copy.start()
    params[own_blocks] = packed[...]

    stages = [
        xs.at[1, :, 0:frames],
        xs.at[2, :, 0:frames],
        xs.at[3, :, 0:frames],
        outgo.at[0],
        outgo.at[1],
        xs.at[4, :, 0:frames],
        gc.at[:, 0:frames],
        outgo.at[0],
    ]

    def weight_part(kind, layer, half, part):
        if kind == 0:
            return wup.at[
                layer,
                pl.ds(pl.multiple_of(half * (width // 2) + (part % 2) * frames, frames), frames),
                pl.ds(pl.multiple_of((part // 2) * width, width), width),
            ]
        return wdn.at[layer, pl.ds(pl.multiple_of(half * rows + part * frames, frames), frames), :]

    def weight_copy(stage, k):
        return to_core(stage, keep.at[k], wt_send.at[k], wt_recv.at[k])

    def send_weights(k):
        j, kind, half = k // 4, k // 2 % 2, k % 2

        def cast(i, carry):
            for part in (2 * i, 2 * i + 1):
                stages[k][part] = weight_part(kind, per_core * core + j, half, part)[...].astype(f32)
            return carry

        lax.fori_loop(0, clips // 2, cast, 0)
        weight_copy(stages[k], k).start()

    def take_weights(layer, kind):
        @pl.when(layer // per_core != core)
        def _():
            for half in range(2):
                k = 4 * (layer % per_core) + 2 * kind + half
                weight_copy(outgo.at[0], k).wait_recv()

                def cast(i, carry, half=half, k=k):
                    for part in (2 * i, 2 * i + 1):
                        weight_part(kind, layer, half, part)[...] = keep[k, part].astype(bf16)
                    return carry

                lax.fori_loop(0, clips // 2, cast, 0)

    for kind in range(2):
        own[kind].wait()
        for half in range(2):
            send_weights(2 * kind + half)
    par_copy.wait()
    for layer in range(layers):
        for block in range(blocks):
            row = up_bias_row + block // 2
            place = (block % 2) * tile
            up_bias_row_of[layer, block] = params[layer, row : row + 1, place : place + tile]

    def chosen_row(layer, clip, first):
        return jnp.sum(onehot[clip] * params[layer, first : first + 4], axis=0, keepdims=True)

    adapted_place = slice(hidden_width - width, hidden_width)

    def norm_clip(layer, clip):
        table = params[layer]
        scale = chosen_row(layer, clip, scale_row)
        shift = chosen_row(layer, clip, shift_row)
        for j in range(chunks):
            window = xs[layer, clip, j * chunk : (j + 1) * chunk + 2 * pad, :]
            conv = window[pad : pad + chunk] * table[3:4] + table[conv_bias_row : conv_bias_row + 1]
            for k in (0, 1, 2, 4, 5, 6):
                conv = conv + window[pad - 3 + k : pad - 3 + k + chunk] * table[k : k + 1]
            centered = conv - jnp.mean(conv, axis=-1, keepdims=True)
            inv = lax.rsqrt(jnp.mean(centered * centered, axis=-1, keepdims=True) + norm_epsilon)
            value = centered * inv
            at = pl.ds(pl.multiple_of(clip * frames + j * chunk, chunk), chunk)
            normed[at, :] = value
            inv_std[at, :] = inv
            slope[layer % 2, at, adapted_place] = (value * scale + shift).astype(bf16)

    def saved_copy(layer, which, back):
        buffer = (hidden_t if which == 0 else slope).at[layer % 2]
        away = (hidden_spill if which == 0 else slope_spill).at[layer % 2]
        source, target = (away, buffer) if back else (buffer, away)
        return pltpu.make_async_copy(source, target, spill_sem.at[layer % 2, which])

    def norm_copies(layer, back, which=(0, 1, 2)):
        copies = []
        kept = ((normed, normed_spill), (inv_std, inv_spill), (adapted_t, adapted_spill))
        for i in which:
            near, away = kept[i]
            source, target = (away.at[layer], near) if back else (near, away.at[layer])
            copies.append(pltpu.make_async_copy(source, target, norm_sem.at[i]))
        return copies

    branch_sum = g.reshape(rows, width)

    def norm_pair(i, carry):
        for q in range(2):
            norm_clip(0, 2 * i + q)
        return carry

    lax.fori_loop(0, clips // 2, norm_pair, 0)
    for copy in norm_copies(0, False, (0, 1)):
        copy.start()
    for load in own[2:]:
        load.wait()
    for k in range(4, 4 * per_core - 1):
        send_weights(k)

    def forward(layer, carry):
        slot = layer % 2

        @pl.when(layer > 0)
        def _():
            norm_copies(layer - 1, False, (2,))[0].wait()

        take_weights(layer, 0)

        def up(block):
            columns = slice(block * tile, (block + 1) * tile)
            uppers[block % 2][...] = dot_plain(slope[slot, :, adapted_place], wup[layer, :, columns])

        def down(block):
            columns = slice(block * tile, (block + 1) * tile)
            here = hidden_near[block % 2]
            value = dot_plain(here, wdn[layer, columns, :])
            branch_sum[...] = value if block == 0 else branch_sum[...] + value
            hidden_t[slot, columns, :] = here.T

        up(0)
        for block in range(blocks):
            columns = slice(block * tile, (block + 1) * tile)
            if block + 1 < blocks:
                up(block + 1)
            if block == 0:
                adapted_t[...] = slope[slot, :, adapted_place].T
            if block == 1:
                take_weights(layer, 1)
            if block > 0:
                down(block - 1)
            bias = up_bias_row_of[layer, block]
            for q in range(rows // chunk):
                at = slice(q * chunk, (q + 1) * chunk)
                smooth, steep = gelu_and_slope(uppers[block % 2][at, :] + bias)
                hidden_near[block % 2, at, :] = smooth.astype(bf16)
                slope[slot, at, columns] = steep.astype(bf16)
        down(blocks - 1)

        @pl.when(layer < layers - 1)
        def _():
            norm_copies(layer, False, (2,))[0].start()

        @pl.when(layer < 2)
        def _():
            for which in range(2):
                saved_copy(layer, which, False).start()

        for step in range(layers):

            @pl.when(layer == step)
            def _(step=step):
                for k in [step] if step < layers - 1 else range(layers, 4 * per_core):
                    weight_copy(outgo.at[0], k).wait_send()
                if step == 0:
                    weight_copy(outgo.at[0], layers - 1).wait_send()
                    send_weights(4 * per_core - 1)

        def residual(clip):
            bias = params[layer, down_bias_row : down_bias_row + 1]
            gamma = params[layer, gamma_row : gamma_row + 1]
            xs[layer + 1, clip, 0:pad, :] = jnp.zeros((pad, width), f32)
            xs[layer + 1, clip, pad + frames : 2 * pad + frames, :] = jnp.zeros((pad, width), f32)
            xs[layer + 1, clip, pad : pad + frames, :] = xs[layer, clip, pad : pad + frames, :] + gamma * (
                g[clip] + bias
            )

        def residual_pair(i, carry):
            for q in range(2):
                residual(2 * i + q)
            return carry

        def residual_norm_pair(i, carry):
            for q in range(2):
                residual(2 * i + q)
            for q in range(2):
                norm_clip(layer + 1, 2 * i + q)
            return carry

        @pl.when((layer >= 1) & (layer < layers - 1))
        def _():
            for which in range(2):
                saved_copy(layer - 1, which, False).wait()

        @pl.when(layer < layers - 1)
        def _():
            for copy in norm_copies(layer, False, (0, 1)):
                copy.wait()
            lax.fori_loop(0, clips // 2, residual_norm_pair, 0)

        @pl.when(layer < layers - 2)
        def _():
            for copy in norm_copies(layer + 1, False, (0, 1)):
                copy.start()

        @pl.when(layer == layers - 1)
        def _():
            lax.fori_loop(0, clips // 2, residual_pair, 0)

        return carry

    lax.fori_loop(0, layers, forward, 0)

    result = xs.at[layers, :, pad : pad + frames]
    result_remote = to_core(result, ends.at[0, :, 0], ends_send.at[0], ends_recv.at[0])
    result_local = pltpu.make_async_copy(result, ends.at[0, :, 1], ends_send.at[1])

    @pl.when(core == 0)
    def _():
        result_remote.start()

    @pl.when(core == 1)
    def _():
        result_local.start()

    for load in loads[clips:]:
        load.wait()

    def load_g(clip, carry):
        g[clip] = gb[pl.ds(pl.multiple_of(clip * frames, frames), frames), :].astype(f32)
        gc[clip, 0:pad, :] = jnp.zeros((pad, width), f32)
        gc[clip, pad + frames : 2 * pad + frames, :] = jnp.zeros((pad, width), f32)
        return carry

    lax.fori_loop(0, clips, load_g, 0)

    matrices = 2 * layers
    lane_count = len(plan.lanes)

    def core_copy(m, parity):
        return to_core(outgo.at[parity], income.at[parity], core_send.at[parity], core_recv.at[parity])

    keep_rows = keep.reshape(matrices, rows, width)

    def offset(lane, stage, side):
        start = 0
        for s in range(stage):
            if plan.halves[lane][s]:
                start = start + choose(plan.lanes[lane][2][s], side, bit_of) * plan.kept[lane][s + 1]
        return start

    def rs_copy(m, parity, lane, stage):
        begin, _, order = plan.lanes[lane]
        size = plan.kept[lane][stage + 1]
        at = begin + offset(lane, stage, core)
        if plan.halves[lane][stage]:
            at = at + (1 - choose(order[stage], core, bit_of)) * size
        starts, _ = plan.slot_rows[stage]
        return to_batch(
            keep_rows.at[m, pl.ds(pl.multiple_of(at, 8), size)],
            stage_in[stage].at[parity, starts[lane] : starts[lane] + size],
            rs_send.at[stage, parity, lane],
            rs_recv.at[stage, parity, lane],
            choose(order[stage], core, partner),
        )

    def rs_add(m, parity, lane, stage):
        begin, _, _ = plan.lanes[lane]
        size = plan.kept[lane][stage + 1]
        at = begin + offset(lane, stage + 1, core)
        starts, _ = plan.slot_rows[stage]
        step = min(size, 2 * chunk)

        def body(i, carry):
            r = pl.multiple_of(at + i * step, 8)
            keep_rows[m, pl.ds(r, step), :] = (
                keep_rows[m, pl.ds(r, step), :]
                + stage_in[stage][parity, pl.ds(pl.multiple_of(starts[lane] + i * step, 8), step), :]
            )
            return carry

        lax.fori_loop(0, size // step, body, 0)

    half_way = matrices // 2
    xs_rows = xs.reshape(layers + 1, clips * (frames + 2 * pad), width)

    def rows_of(m, owner, own, lane, at, size):
        span = pl.ds(pl.multiple_of(plan.lanes[lane][0] + at, 8), size)
        if own:
            return keep_rows.at[m, span]
        return xs_rows.at[layers - m, span] if owner == 1 else keep_rows.at[m - half_way, span]

    def deliver_copy(m, owner, lane):
        size = plan.kept[lane][bits]
        at = offset(lane, bits, 1 - owner)
        return to_core(
            rows_of(m, owner, True, lane, at, size),
            rows_of(m, owner, False, lane, at, size),
            deliver_send.at[m % half_way, lane],
            deliver_recv.at[m % half_way, lane],
        )

    def ag_copy(m, owner, own, parity, lane, stage):
        size = plan.kept[lane][stage + 1]
        side = owner if own else 1 - owner
        place = rows_of(m, owner, own, lane, offset(lane, stage + 1, side), size)
        return to_batch(
            place,
            place,
            ag_send.at[stage, parity, own, lane],
            ag_recv.at[stage, parity, own, lane],
            choose(plan.lanes[lane][2][stage], side, partner),
        )

    def last_copies(m, kind, local, owner, own, parity, lane):
        side = owner if own else 1 - owner
        size = plan.kept[lane][1]
        at = offset(lane, 1, side)
        source = rows_of(m, owner, own, lane, at, size)
        row = plan.lanes[lane][0] + at
        if kind == 0:
            target = down_out.at[local, side, pl.ds(pl.multiple_of(row, 8), size), :]
        else:
            part = row // tile
            target = up_out.at[
                local,
                side,
                pl.ds(pl.multiple_of(row - part * tile, 8), size),
                pl.ds(pl.multiple_of(part * width, width), width),
            ]
        far = to_batch(
            source,
            target,
            ag_send.at[0, parity, own, lane],
            ag_recv.at[0, parity, own, lane],
            choose(plan.lanes[lane][2][0], side, partner),
        )
        return far, pltpu.make_async_copy(source, target, out_sem.at[m % half_way, own, lane])

    def owner_of(m):
        return 1 - m // half_way

    def owned_by(owner, m):
        return m < half_way if owner == 1 else m >= half_way

    last_step = bits + plan.doublings + 2

    def tick(pair, phase):
        for s in range(last_step, 0, -1):
            m = 2 * pair + phase + 1 - s
            parity = (phase + 1 - s) % 2
            kind = parity
            local = (layers - 1 - (m - kind) // 2) % per_core
            valid = (m >= 0) & (m < matrices)

            if s <= bits + 1:

                @pl.when(valid)
                def _(s=s, m=m, parity=parity):
                    if s == 1:
                        core_copy(m, parity).wait()

                        def body(clip, carry):
                            keep[m, clip] = keep[m, clip] + income[parity, clip]
                            return carry

                        lax.fori_loop(0, clips, body, 0)
                    else:
                        for lane in range(lane_count):
                            rs_copy(m, parity, lane, s - 2).wait()
                            if plan.halves[lane][s - 2] and s > 2:
                                @pl.when(owner_of(m) == core)
                                def _(lane=lane):
                                    pl.semaphore_signal(
                                        credit.at[s - 2, lane],
                                        inc=1,
                                        device_id={"batch": choose(plan.lanes[lane][2][s - 2], core, partner)},
                                        device_id_type=mesh_id,
                                    )

                            rs_add(m, parity, lane, s - 2)
                    if s <= bits:
                        for lane in range(lane_count):
                            rs_copy(m, parity, lane, s - 1).start()

            for owner in range(2):
                if s == bits + 1:

                    @pl.when(valid & owned_by(owner, m) & (core == 1 - owner))
                    def _(m=m, owner=owner):
                        for lane in range(lane_count):
                            deliver_copy(m, owner, lane).start()

                if s > bits + 1:

                    @pl.when(valid & owned_by(owner, m) & (core == owner))
                    def _(s=s, m=m, parity=parity, kind=kind, local=local, owner=owner):
                        if s == bits + 2:
                            for lane in range(lane_count):
                                deliver_copy(m, owner, lane).wait_recv()
                        else:
                            stage = last_step - s
                            for lane in range(lane_count):
                                for own in range(2):
                                    if stage == 0:
                                        for copy in last_copies(m, kind, local, owner, own, parity, lane):
                                            copy.wait()
                                    elif plan.halves[lane][stage]:
                                        ag_copy(m, owner, own, parity, lane, stage).wait()
                        if s < last_step:
                            stage = last_step - 1 - s
                            for lane in range(lane_count):
                                if plan.halves[lane][stage] and stage > 0:
                                    pl.semaphore_wait(credit.at[stage, lane], 1)
                                for own in range(2):
                                    if stage == 0:
                                        for copy in last_copies(m, kind, local, owner, own, parity, lane):
                                            copy.start()
                                    elif plan.halves[lane][stage]:
                                        ag_copy(m, owner, own, parity, lane, stage).start()

        m = 2 * pair + phase - bits
        for owner in range(2):

            @pl.when((m >= 0) & (m < matrices) & owned_by(owner, m) & (core == 1 - owner))
            def _(m=m, owner=owner):
                for lane in range(lane_count):
                    deliver_copy(m, owner, lane).wait_send()

    def store_block(m, phase, second, block, value):
        for q in range(2):
            piece = value[q * frames : (q + 1) * frames]
            if second == 0:
                outgo[phase, 2 * block + q] = piece
            else:
                keep[m, 2 * block + q] = piece

    def scale_clip(layer, clip):
        gamma = params[layer, gamma_row : gamma_row + 1]
        gamma_sum = bias_sum = jnp.zeros((8, width), f32)
        for j in range(chunks):
            here = g[clip, j * chunk : (j + 1) * chunk, :]
            at = slice(pad + j * chunk, pad + (j + 1) * chunk)
            gamma_sum = gamma_sum + fold(here * (xs[layer + 1, clip, at, :] - xs[layer, clip, at, :]))
            value = (gamma * here).astype(bf16)
            gb[pl.ds(pl.multiple_of(clip * frames + j * chunk, chunk), chunk), :] = value
            bias_sum = bias_sum + fold(value.astype(f32))
        sums[0] += gamma_sum
        sums[1] += bias_sum

    def norm_back(layer, clip):
        scale = chosen_row(layer, clip, scale_row)
        scale_sum = shift_sum = conv_sum = jnp.zeros((8, width), f32)
        for j in range(chunks):
            row = pl.ds(pl.multiple_of(clip * frames + j * chunk, chunk), chunk)
            at = slice(pad + j * chunk, pad + (j + 1) * chunk)
            ga = gc[clip, at, :]
            value = normed[row, :]
            scale_sum = scale_sum + fold(ga * value)
            shift_sum = shift_sum + fold(ga)
            dn = ga * scale
            first = jnp.mean(dn, axis=-1, keepdims=True)
            second = jnp.mean(dn * value, axis=-1, keepdims=True)
            result = inv_std[row, :] * (dn - first - value * second)
            gc[clip, at, :] = result
            conv_sum = conv_sum + fold(result)
        sums[9] += conv_sum
        choice = onehot[clip]
        small[layer, scale_row : scale_row + 4, :] += choice * jnp.sum(scale_sum, axis=0, keepdims=True)
        small[layer, shift_row : shift_row + 4, :] += choice * jnp.sum(shift_sum, axis=0, keepdims=True)

    def conv_back(layer, clip):
        table = params[layer]
        totals = [jnp.zeros((8, width), f32) for _ in range(7)]
        for j in range(chunks):
            grads = gc[clip, j * chunk : (j + 1) * chunk + 2 * pad, :]
            signal = xs[layer, clip, pad + j * chunk : pad + (j + 1) * chunk, :]
            at = slice(j * chunk, (j + 1) * chunk)
            total = g[clip, at, :]
            for k in (3, 0, 1, 2, 4, 5, 6):
                shifted = grads[pad + 3 - k : pad + 3 - k + chunk]
                total = total + shifted * table[k : k + 1]
                totals[k] = totals[k] + fold(signal * shifted)
            g[clip, at, :] = total
        for k in range(7):
            sums[2 + k] += totals[k]

    def backward(pair, carry):
        layer = layers - 1 - pair
        slot = layer % 2

        @pl.when((pair == 1) & (core == 0))
        def _():
            result_remote.wait_send()

        @pl.when((pair == 1) & (core == 1))
        def _():
            result_local.wait()

        sums[...] = jnp.zeros(sums.shape, f32)
        small[layer] = jnp.zeros(small.shape[1:], f32)

        def scale_body(i, carry):
            for q in range(2):
                scale_clip(layer, 2 * i + q)
            return carry

        lax.fori_loop(0, clips // 2, scale_body, 0)

        @pl.when(layer < 2)
        def _():
            for which in range(2):
                saved_copy(layer, which, True).wait()

        def up_grad(block):
            columns = pl.ds(pl.multiple_of(block * tile, tile), tile)
            value = dot_cols(gb[...], wdn[layer, columns, :])
            total = jnp.zeros((8, tile), f32)
            for q in range(rows // chunk):
                at = slice(q * chunk, (q + 1) * chunk)
                piece = (value[at] * slope[slot, at, columns].astype(f32)).astype(bf16)
                slope[slot, at, columns] = piece
                total = total + fold(piece.astype(f32))
            up_sums[block] = total

        def down_weight_grad(second, block):
            half = other if second == 0 else core
            at = pl.ds(pl.multiple_of(half * rows + block * tile, tile), tile)
            store_block(2 * pair, 0, second, block, dot_plain(hidden_t[slot, at, :], gb[...]))

        for block in range(3):
            down_weight_grad(0, block)
        core_copy(2 * pair, 0).start()

        def down_body(block, carry):
            down_weight_grad(1, block)
            up_grad(2 * block)
            up_grad(2 * block + 1)
            return carry

        lax.fori_loop(0, clips // 2, down_body, 0)

        @pl.when(pair > 0)
        def _():
            for copy in norm_copies(layer, True):
                copy.wait()

        tick(pair, 0)

        def up_weight_grad(second, block):
            half = other if second == 0 else core
            at = pl.ds(pl.multiple_of(half * (width // 2), width // 2), width // 2)
            columns = pl.ds(pl.multiple_of(block * width, width), width)
            store_block(2 * pair + 1, 1, second, block, dot_plain(adapted_t[at, :], slope[slot, :, columns]))

        def adapted_grad(i):
            r = pl.multiple_of(i * tile, tile)
            value = dot_cols(slope[slot, pl.ds(r, tile), :], wup[layer])
            for q in range(2):
                gc[2 * i + q, pad : pad + frames, :] = value[q * frames : (q + 1) * frames]

        def norm_conv_back(i):
            for q in range(2):
                norm_back(layer, 2 * i + q)
                conv_back(layer, 2 * i + q)

        def up_body(i, carry):
            up_weight_grad(0, i)
            adapted_grad(i)
            return carry

        lax.fori_loop(0, rows // tile, up_body, 0)
        core_copy(2 * pair + 1, 1).start()
        for block in range(3):
            up_weight_grad(1, block)
        tick(pair, 1)

        def back_body(i, carry):
            norm_conv_back(i)
            return carry

        lax.fori_loop(0, rows // tile, back_body, 0)

        @pl.when(layer > 0)
        def _():
            for copy in norm_copies(layer - 1, True):
                copy.start()

        @pl.when(layer >= 2)
        def _():
            for which in range(2):
                saved_copy(layer, which, True).start()

        gamma = params[layer, gamma_row : gamma_row + 1, :]
        small[layer, gamma_row : gamma_row + 1, :] = jnp.sum(sums[0], axis=0, keepdims=True) / gamma
        small[layer, down_bias_row : down_bias_row + 1, :] = jnp.sum(sums[1], axis=0, keepdims=True)
        for block in range(blocks):
            row = up_bias_row + block // 2
            place = (block % 2) * tile
            small[layer, row : row + 1, place : place + tile] = jnp.sum(up_sums[block], axis=0, keepdims=True)
        for k in range(7):
            small[layer, taps_row + k : taps_row + k + 1, :] = jnp.sum(sums[2 + k], axis=0, keepdims=True)
        small[layer, conv_bias_row : conv_bias_row + 1, :] = jnp.sum(sums[9], axis=0, keepdims=True)
        return carry

    lax.fori_loop(0, layers, backward, 0)

    grad_remote = to_core(g, ends.at[0, :, 1], ends_send.at[2], ends_recv.at[1])
    grad_local = pltpu.make_async_copy(g, ends.at[0, :, 0], ends_send.at[3])

    @pl.when(core == 0)
    def _():
        grad_local.start()

    @pl.when(core == 1)
    def _():
        grad_remote.start()

    small_core = to_core(
        small.at[pl.ds(per_core * other, per_core)], small_in.at[bits], small_send.at[bits], small_recv.at[bits]
    )
    small_core.start()

    def small_copy(bit):
        return to_batch(small_sum, small_in.at[bit], small_send.at[bit], small_recv.at[bit], partner(bit))

    def drain(pair, carry):
        for phase in range(2):
            tick(pair, phase)
            for step in range(bits + 1):

                @pl.when(2 * pair + phase - matrices == step)
                def _(step=step):
                    if step == 0:
                        small_core.wait()
                        small_sum[...] = small[pl.ds(per_core * core, per_core)] + small_in[bits]
                    else:
                        small_copy(step - 1).wait()
                        small_sum[...] = small_sum[...] + small_in[step - 1]
                    if step < bits:
                        small_copy(step).start()

        return carry

    lax.fori_loop(layers, (matrices - 2 + last_step) // 2 + 1, drain, 0)
    small_out[...] = small_sum[...]

    @pl.when(core == 0)
    def _():
        grad_local.wait()
        grad_remote.wait_recv()

    @pl.when(core == 1)
    def _():
        result_remote.wait_recv()
        grad_remote.wait_send()


def results_kernel(
    ends,
    small,
    ends_out,
    conv_kernel_out,
    conv_bias_out,
    band_scale_out,
    band_shift_out,
    up_bias_out,
    down_bias_out,
    layer_scale_out,
    stage,
    in_sem,
    out_sem,
):
    per_core, _, width = small.shape
    pieces = [(0, i, j) for i in range(ends.shape[1]) for j in range(ends.shape[2])]
    loads = [pltpu.make_async_copy(ends.at[at], stage.at[i], in_sem.at[i]) for i, at in enumerate(pieces)]
    stores = [pltpu.make_async_copy(stage.at[i], ends_out.at[at], out_sem.at[i]) for i, at in enumerate(pieces)]
    for load in loads:
        load.start()
    for load, store in zip(loads, stores):
        load.wait()
        store.start()
    for j in range(per_core):
        conv_kernel_out[:, j] = small[j, taps_row : taps_row + 7]
        conv_bias_out[j : j + 1] = small[j, conv_bias_row : conv_bias_row + 1]
        band_scale_out[j] = small[j, scale_row : scale_row + 4]
        band_shift_out[j] = small[j, shift_row : shift_row + 4]
        for q in range(3):
            row = up_bias_row + q
            up_bias_out[j : j + 1, q * width : (q + 1) * width] = small[j, row : row + 1]
        down_bias_out[j : j + 1] = small[j, down_bias_row : down_bias_row + 1]
        layer_scale_out[j : j + 1] = small[j, gamma_row : gamma_row + 1]
    for store in stores:
        store.wait()


def body(
    inputs,
    grad_out,
    band_ids,
    conv_kernel,
    conv_bias,
    band_scale,
    band_shift,
    up_weight,
    up_bias,
    down_weight,
    down_bias,
    layer_scale,
):
    sections = lax.axis_size("section")
    batch = lax.axis_size("batch")
    clips, local_clips, frames, width = inputs.shape
    per_core, _, hidden_width = up_weight.shape
    layers = per_core * sections
    bands = band_scale.shape[1]
    rows = clips * frames
    assert sections == 2 and local_clips == 2 and batch & (batch - 1) == 0
    assert hidden_width == 3 * width and bands == 4 and layers == 4 and rows == 3 * width // 2
    plan = Plan(batch, rows)
    bits = plan.bits
    hbm = pl.BlockSpec(memory_space=pl.ANY)
    vmem = pl.BlockSpec(memory_space=pltpu.VMEM)
    smem = pl.BlockSpec(memory_space=pltpu.SMEM)
    padded = frames + 2 * pad
    dma = pltpu.SemaphoreType.DMA
    lanes = len(plan.lanes)
    tile = 2 * frames
    ends_shape = jax.ShapeDtypeStruct((1, clips, local_clips, frames, width), f32)
    up_shape = jax.ShapeDtypeStruct((per_core, 2, width // 2, hidden_width), f32)
    down_shape = jax.ShapeDtypeStruct((per_core, 2, hidden_width // 2, width), f32)
    small_shape = jax.ShapeDtypeStruct((per_core, packed_rows, width), f32)
    conv_kernel = jnp.transpose(conv_kernel, (1, 0, 2))
    ends, up_grad, down_grad, small, *_ = pl.pallas_call(
        functools.partial(step_kernel, plan),
        out_shape=[
            ends_shape,
            up_shape,
            down_shape,
            small_shape,
            jax.ShapeDtypeStruct((2, hidden_width, rows), bf16),
            jax.ShapeDtypeStruct((2, rows, hidden_width), bf16),
            jax.ShapeDtypeStruct((layers - 1, rows, width), f32),
            jax.ShapeDtypeStruct((layers - 1, rows, 1), f32),
            jax.ShapeDtypeStruct((layers - 1, width, rows), bf16),
        ],
        in_specs=[hbm, hbm, smem, vmem, vmem, vmem, vmem, hbm, vmem, hbm, vmem, vmem],
        out_specs=[hbm, hbm, hbm, vmem, hbm, hbm, hbm, hbm, hbm],
        scratch_shapes=[
            pltpu.VMEM((layers + 1, clips, padded, width), f32),
            pltpu.VMEM((rows, width), f32),
            pltpu.VMEM((rows, 1), f32),
            pltpu.VMEM((width, rows), bf16),
            pltpu.VMEM((2, hidden_width, rows), bf16),
            pltpu.VMEM((2, rows, hidden_width), bf16),
            pltpu.VMEM((2, rows, tile), bf16),
            pltpu.VMEM((rows, width), bf16),
            pltpu.VMEM((clips, frames, width), f32),
            pltpu.VMEM((clips, padded, width), f32),
            pltpu.VMEM((layers, width, hidden_width), bf16),
            pltpu.VMEM((layers, hidden_width, width), bf16),
            pltpu.VMEM((per_core, packed_rows, width), f32),
            pltpu.VMEM((layers, packed_rows, width), f32),
            pltpu.VMEM((layers, hidden_width // tile, 1, tile), f32),
            pltpu.VMEM((rows, tile), f32),
            pltpu.VMEM((rows, tile), f32),
            pltpu.VMEM((clips, bands, width), f32),
            pltpu.VMEM((10, 8, width), f32),
            pltpu.VMEM((hidden_width // tile, 8, tile), f32),
            pltpu.VMEM((layers, packed_rows, width), f32),
            pltpu.VMEM((2 * layers, clips, frames, width), f32),
            pltpu.VMEM((2, clips, frames, width), f32),
            pltpu.VMEM((2, clips, frames, width), f32),
            pltpu.VMEM((per_core, packed_rows, width), f32),
            pltpu.VMEM((bits + 1, per_core, packed_rows, width), f32),
            *[pltpu.VMEM((2, plan.slot_rows[stage][1], width), f32) for stage in range(bits)],
            dma((2 * clips,)),
            dma((2 * per_core,)),
            dma((4 * per_core,)),
            dma((4 * per_core,)),
            dma((1,)),
            dma((1,)),
            dma((4,)),
            dma((2,)),
            dma((2,)),
            dma((2,)),
            dma((bits, 2, lanes)),
            dma((bits, 2, lanes)),
            dma((layers, lanes)),
            dma((layers, lanes)),
            dma((bits, 2, 2, lanes)),
            dma((bits, 2, 2, lanes)),
            dma((layers, 2, lanes)),
            pltpu.SemaphoreType.REGULAR((bits, lanes)),
            dma((bits + 1,)),
            dma((bits + 1,)),
            dma((2, 2)),
            dma((3,)),
        ],
        compiler_params=pltpu.CompilerParams(
            collective_id=0, has_side_effects=True, vmem_limit_bytes=255 * 2**18
        ),
        cost_estimate=pl.CostEstimate(
            flops=24 * rows * width * hidden_width * 2, bytes_accessed=2**26, transcendentals=2**24
        ),
        name="blocks_step",
    )(
        inputs,
        grad_out,
        jnp.transpose(band_ids),
        conv_kernel,
        conv_bias,
        band_scale,
        band_shift,
        up_weight,
        up_bias,
        down_weight,
        down_bias,
        layer_scale,
    )

    def like(array):
        return jax.ShapeDtypeStruct(array.shape, f32)

    ends, taps_grad, conv_bias_grad, scale_grad, shift_grad, up_bias_grad, down_bias_grad, gamma_grad = (
        pl.pallas_call(
            results_kernel,
            out_shape=[
                like(array)
                for array in (ends, conv_kernel, conv_bias, band_scale, band_shift, up_bias, down_bias, layer_scale)
            ],
            in_specs=[hbm, vmem],
            out_specs=[hbm] + [vmem] * 7,
            scratch_shapes=[
                pltpu.VMEM((clips * local_clips, frames, width), f32),
                dma((clips * local_clips,)),
                dma((clips * local_clips,)),
            ],
            cost_estimate=pl.CostEstimate(flops=0, bytes_accessed=2**23, transcendentals=0),
            compiler_params=pltpu.CompilerParams(vmem_limit_bytes=255 * 2**18),
            name="results",
        )(ends, small)
    )
    return (
        ends,
        jnp.transpose(taps_grad, (1, 0, 2)),
        conv_bias_grad,
        scale_grad,
        shift_grad,
        up_grad.reshape(up_weight.shape),
        up_bias_grad,
        down_grad.reshape(down_weight.shape),
        down_bias_grad,
        gamma_grad,
    )


def solution(mesh):
    in_specs = (
        P(None, "batch", None, None),
        P(None, "batch", None, None),
        P(None, "batch"),
        P("section", None, None),
        P("section", None),
        P("section", None, None),
        P("section", None, None),
        P("section", None, None),
        P("section", None),
        P("section", None, None),
        P("section", None),
        P("section", None),
    )
    out_specs = (
        P("section", None, "batch", None, None),
        P("section", None, None),
        P("section", None),
        P("section", None, None),
        P("section", None, None),
        P("section", None, None),
        P("section", None),
        P("section", None, None),
        P("section", None),
        P("section", None),
    )
    return jax.shard_map(body, mesh=mesh, in_specs=in_specs, out_specs=out_specs, check_vma=False)
```
